32 devices in a mesh: ta: 4 (over z), ha: 2 (over x), wa: 4 (over y, core).
Axes of the slice: x: 2, y: 2, z: 4, core: 2. Of those that a mesh axis runs over, the one named last changes fastest.
Arguments:
- query_in: bfloat16 [12, 16, 32, 256], P('ta', 'ha', 'wa'), may hold values from -24 to 24
- key_in: bfloat16 [12, 16, 32, 256], P('ta', 'ha', 'wa'), may hold values from -24 to 24
- value_in: bfloat16 [12, 16, 32, 256], P('ta', 'ha', 'wa'), may hold values from -6 to 6
- cotangent: bfloat16 [12, 16, 32, 256], P('ta', 'ha', 'wa'), may hold values from -6 to 6
Outputs:
- attended: bfloat16 [12, 16, 32, 256], P('ta', 'ha', 'wa')
- grad_query: bfloat16 [12, 16, 32, 256], P('ta', 'ha', 'wa')
- grad_key: bfloat16 [12, 16, 32, 256], P('ta', 'ha', 'wa')
- grad_value: bfloat16 [12, 16, 32, 256], P('ta', 'ha', 'wa')
The draws below stay inside these ranges and needn't reach their ends.
All inputs are finite; a program needn't handle non-finite values.
Results may differ from the reference program's by a relative error of at most 0.035.
Values may be sent and summed in bfloat16 or wider, within the bound.
No kernel may reach another device: no remote copies, remote signals or barrier semaphores. Data moves between devices by JAX's collectives and lax.ppermute only.
A program may use at most 128 MiB of HBM per device.

```python
import jax
import jax.numpy as jnp
from jax import lax

DH = 128
HEADS = 2
TILE_T = 6
TILE_H = 8
TILE_W = 8
NT = 12
NH = 16
NW = 32


def drawn_pair(key):
    shape_all = (NT, NH, NW, HEADS * DH)
    query_base = jnp.clip(jax.random.normal(jax.random.fold_in(key, 11), shape_all, jnp.float32), -6.0, 6.0)
    key_base = jnp.clip(jax.random.normal(jax.random.fold_in(key, 12), shape_all, jnp.float32), -6.0, 6.0)
    return (query_base, key_base)


def draw_query_in(key, part):
    return drawn_pair(key)[0].astype(jnp.bfloat16)


def draw_key_in(key, part):
    return drawn_pair(key)[1].astype(jnp.bfloat16)


def block_levels(rng, dims, pieces, low, top_value):
    loudness = 1.0
    for axis_at, parts in pieces:
        heights = jax.random.uniform(jax.random.fold_in(jax.random.fold_in(rng, 6), axis_at), (parts,), jnp.float32, low / len(pieces), top_value / len(pieces))
        loudness = loudness * jnp.repeat(jnp.exp(heights), dims[axis_at] // parts).reshape((-1,) + (1,) * (len(dims) - 1 - axis_at))
    return loudness


def gaussian(stream_key, dims, width, bound, split=(), kind=jnp.bfloat16):
    values = jax.random.normal(stream_key, dims, jnp.float32) * width
    if len(split) > 0:
        values = block_levels(stream_key, dims, split, -0.22, 0.18) * values
    return jnp.clip(values, min=-bound, max=bound).astype(kind)


def setup_inputs(seed: int = 0) -> dict:
    key_of = jax.random.split(jax.random.key(seed), 5)
    query_in = draw_query_in(jax.random.fold_in(key_of[4], 71), 0)
    key_in = draw_key_in(jax.random.fold_in(key_of[4], 71), 0)
    value_in = gaussian(key_of[2], (NT, NH, NW, HEADS * DH), 1.0, 6.0, ((0, 4), (1, 2), (2, 4)))
    cotangent = gaussian(key_of[3], (NT, NH, NW, HEADS * DH), 1.0, 6.0, ((0, 4), (1, 2), (2, 4)))
    return {"query_in": query_in, "key_in": key_in, "value_in": value_in, "cotangent": cotangent}


NEGATIVE = -1e+30

def rope_tables(time_pos, row_pos, col_pos):
    time_dims = DH // 8
    space_dims = (DH - time_dims) // 2
    slower = 256.0 ** (-jnp.arange(0, time_dims, 2, dtype=jnp.float32) / time_dims)
    faster = 256.0 ** (-jnp.arange(0, space_dims, 2, dtype=jnp.float32) / space_dims)
    angles = jnp.concatenate([time_pos[:, None] * slower, row_pos[:, None] * faster, col_pos[:, None] * faster], axis=1)
    return (jnp.cos(angles), jnp.sin(angles))

def rotate(flat_in, cosine, sine_tab, direction):
    row_total = flat_in.shape[0]
    paired = flat_in.reshape(row_total, HEADS, DH // 2, 2)
    real_part = paired[..., 0]
    imag_part = paired[..., 1]
    cos_rows = cosine[:, None, :]
    sin_rows = direction * sine_tab[:, None, :]
    turned = jnp.stack([real_part * cos_rows - imag_part * sin_rows, real_part * sin_rows + imag_part * cos_rows], axis=-1)
    return turned.reshape(row_total, HEADS * DH)

def reference(query_in, key_in, value_in, cotangent):
    frame_all, row_all, col_all, chan_count = query_in.shape
    cell_all = frame_all * row_all * col_all
    scale_factor = DH ** (-0.5)
    tiles_t = frame_all // TILE_T
    tiles_h = row_all // TILE_H
    tiles_w = col_all // TILE_W
    tile_count = tiles_t * tiles_h * tiles_w
    tile_cells = TILE_T * TILE_H * TILE_W
    per_frame = 9 * TILE_H * TILE_W
    shape_all = (frame_all, row_all, col_all)
    frame_grid = jnp.broadcast_to(jnp.arange(frame_all, dtype=jnp.int32)[:, None, None], shape_all).reshape(-1)
    row_grid = jnp.broadcast_to(jnp.arange(row_all, dtype=jnp.int32)[None, :, None], shape_all).reshape(-1)
    col_grid = jnp.broadcast_to(jnp.arange(col_all, dtype=jnp.int32)[None, None, :], shape_all).reshape(-1)
    cosine, sine_tab = rope_tables(frame_grid.astype(jnp.float32), row_grid.astype(jnp.float32), col_grid.astype(jnp.float32))
    query_rot = rotate(query_in.reshape(cell_all, chan_count).astype(jnp.float32), cosine, sine_tab, 1.0).astype(jnp.bfloat16).reshape(frame_all, row_all, col_all, chan_count)
    key_rot = rotate(key_in.reshape(cell_all, chan_count).astype(jnp.float32), cosine, sine_tab, 1.0).astype(jnp.bfloat16).reshape(frame_all, row_all, col_all, chan_count)

    def pad_space(grid_in):
        return jnp.pad(grid_in, ((0, 0), (TILE_H, TILE_H), (TILE_W, TILE_W), (0, 0)))

    def split_index(tile_idx):
        return (tile_idx // (tiles_h * tiles_w), tile_idx // tiles_w % tiles_h, tile_idx % tiles_w)

    def tile_of(grid_in, tile_idx):
        pos_t, pos_h, pos_w = split_index(tile_idx)
        block = lax.dynamic_slice(grid_in, (pos_t * TILE_T, pos_h * TILE_H, pos_w * TILE_W, jnp.int32(0)), (TILE_T, TILE_H, TILE_W, grid_in.shape[3]))
        return block.reshape(tile_cells, grid_in.shape[3])

    def window_of(grid_in, tile_idx):
        pos_t, pos_h, pos_w = split_index(tile_idx)
        block = lax.dynamic_slice(grid_in, (jnp.int32(0), pos_h * TILE_H, pos_w * TILE_W, jnp.int32(0)), (frame_all, 3 * TILE_H, 3 * TILE_W, grid_in.shape[3]))
        return block.reshape(frame_all * per_frame, grid_in.shape[3])

    def window_mask(tile_idx):
        pos_t, pos_h, pos_w = split_index(tile_idx)
        frame_ok = jnp.abs(pos_t - jnp.arange(frame_all, dtype=jnp.int32) // TILE_T) <= 1
        row_ids = pos_h * TILE_H - TILE_H + jnp.arange(3 * TILE_H, dtype=jnp.int32)
        col_ids = pos_w * TILE_W - TILE_W + jnp.arange(3 * TILE_W, dtype=jnp.int32)
        row_ok = (row_ids >= 0) & (row_ids < row_all)
        col_ok = (col_ids >= 0) & (col_ids < col_all)
        return (frame_ok[:, None, None] & row_ok[None, :, None] & col_ok[None, None, :]).reshape(-1)

    def heads_of(matrix):
        return matrix.reshape(matrix.shape[0], HEADS, DH).astype(jnp.float32)

    def ungrid(blocks):
        channels = blocks.shape[2]
        shaped = blocks.reshape(tiles_t, tiles_h, tiles_w, TILE_T, TILE_H, TILE_W, channels)
        return shaped.transpose(0, 3, 1, 4, 2, 5, 6).reshape(frame_all, row_all, col_all, channels)
    key_wide = pad_space(key_rot)
    value_wide = pad_space(value_in)
    tile_ids = jnp.arange(tile_count, dtype=jnp.int32)

    def forward_tile(tile_idx):
        query_tile = heads_of(tile_of(query_rot, tile_idx))
        key_window = heads_of(window_of(key_wide, tile_idx))
        value_window = heads_of(window_of(value_wide, tile_idx))
        visible = window_mask(tile_idx).reshape(frame_all, per_frame)
        scores = jnp.einsum('qhd,khd->hqk', query_tile, key_window) * scale_factor
        scores = scores.reshape(HEADS, tile_cells, frame_all, per_frame)
        frame_max = lax.optimization_barrier(jnp.max(jnp.where(visible, scores, NEGATIVE), axis=3))
        weights = jnp.where(visible, jnp.exp(scores - frame_max[..., None]), 0.0)
        frame_sum = lax.optimization_barrier(jnp.sum(weights, axis=3))
        frame_part = jnp.einsum('hqfk,fkhd->hqfd', weights.astype(jnp.bfloat16).astype(jnp.float32), value_window.reshape(frame_all, per_frame, HEADS, DH))
        highest = lax.optimization_barrier(jnp.max(frame_max, axis=2))
        factor = jnp.exp(frame_max - highest[..., None])
        denom = lax.optimization_barrier(jnp.sum(factor * frame_sum, axis=2))
        output = lax.optimization_barrier(jnp.sum(factor[..., None] * frame_part, axis=2)) / denom[..., None]
        return (jnp.transpose(output, (1, 0, 2)).reshape(tile_cells, chan_count), highest + jnp.log(denom))
    out_tiles, lse_tiles = lax.map(forward_tile, tile_ids)
    attended = ungrid(out_tiles).astype(jnp.bfloat16)
    lse_grid = ungrid(jnp.transpose(lse_tiles, (0, 2, 1)))
    delta_grid = lax.optimization_barrier(jnp.sum(cotangent.reshape(frame_all, row_all, col_all, HEADS, DH).astype(jnp.float32) * attended.reshape(frame_all, row_all, col_all, HEADS, DH).astype(jnp.float32), axis=4))

    def query_tile_grad(tile_idx):
        query_tile = heads_of(tile_of(query_rot, tile_idx))
        grad_tile = heads_of(tile_of(cotangent, tile_idx))
        lse_tile = tile_of(lse_grid, tile_idx)
        delta_tile = tile_of(delta_grid, tile_idx)
        key_window = heads_of(window_of(key_wide, tile_idx))
        value_window = heads_of(window_of(value_wide, tile_idx))
        visible = window_mask(tile_idx)
        scores = jnp.einsum('qhd,khd->hqk', query_tile, key_window) * scale_factor
        prob_rows = jnp.where(visible[None, None, :], jnp.exp(scores - lse_tile.T[:, :, None]), 0.0)
        prob_grad = jnp.einsum('qhd,khd->hqk', grad_tile, value_window)
        dscore = (prob_rows * (prob_grad - delta_tile.T[:, :, None])).astype(jnp.bfloat16).astype(jnp.float32)
        result = jnp.einsum('hqk,khd->qhd', dscore, key_window) * scale_factor
        return result.reshape(tile_cells, chan_count)
    query_wide = pad_space(query_rot)
    grad_wide = pad_space(cotangent)
    lse_wide = pad_space(lse_grid)
    delta_wide = pad_space(delta_grid)

    def key_tile_grad(tile_idx):
        key_tile = heads_of(tile_of(key_rot, tile_idx))
        value_tile = heads_of(tile_of(value_in, tile_idx))
        query_window = heads_of(window_of(query_wide, tile_idx))
        grad_window = heads_of(window_of(grad_wide, tile_idx))
        lse_window = window_of(lse_wide, tile_idx)
        delta_window = window_of(delta_wide, tile_idx)
        visible = window_mask(tile_idx)
        scores = jnp.einsum('khd,qhd->hkq', key_tile, query_window) * scale_factor
        prob_rows = jnp.where(visible[None, None, :], jnp.exp(scores - lse_window.T[:, None, :]), 0.0)
        value_grad = jnp.einsum('hkq,qhd->khd', prob_rows.astype(jnp.bfloat16).astype(jnp.float32), grad_window)
        prob_grad = jnp.einsum('khd,qhd->hkq', value_tile, grad_window)
        dscore = (prob_rows * (prob_grad - delta_window.T[:, None, :])).astype(jnp.bfloat16).astype(jnp.float32)
        key_grad = jnp.einsum('hkq,qhd->khd', dscore, query_window) * scale_factor
        return (key_grad.reshape(tile_cells, chan_count), value_grad.reshape(tile_cells, chan_count))
    dq_tiles = lax.map(query_tile_grad, tile_ids)
    dk_tiles, dv_tiles = lax.map(key_tile_grad, tile_ids)
    grad_query = rotate(ungrid(dq_tiles).reshape(cell_all, chan_count), cosine, sine_tab, -1.0).astype(jnp.bfloat16).reshape(frame_all, row_all, col_all, chan_count)
    grad_key = rotate(ungrid(dk_tiles).reshape(cell_all, chan_count), cosine, sine_tab, -1.0).astype(jnp.bfloat16).reshape(frame_all, row_all, col_all, chan_count)
    grad_value = ungrid(dv_tiles).astype(jnp.bfloat16)
    return (attended, grad_query, grad_key, grad_value)
```

```python
import functools
import math

import jax
import jax.numpy as jnp
import numpy as np
from jax import lax
from jax.experimental import pallas as pl
from jax.experimental.pallas import tpu as pltpu
from jax.sharding import PartitionSpec as P

DH = 128
HEADS = 2
TILE_T = 6
TILE_H = 8
TILE_W = 8

NEGATIVE = -1e30
SCALE = DH**-0.5
SCALE_LOG2 = SCALE * math.log2(math.e)
F32 = jnp.float32
BF16 = jnp.bfloat16
VMEM_LIMIT = 48 * 1024 * 1024


def near_pairs(count):
    return [(i, i ^ 1) for i in range(count)]


def far_pairs(count):
    pairs = []
    for i in range(count):
        j = i + 1 if i % 2 else i - 1
        pairs.append((i, j if 0 <= j < count else i))
    return pairs


def far_exists(axis, count):
    pos = lax.axis_index(axis)
    other = jnp.where(pos % 2 == 1, pos + 1, pos - 1)
    return (other >= 0) & (other < count)


def side_pairs(count):
    sides = []
    if count > 1:
        sides.append(near_pairs(count))
    if count > 2:
        sides.append(far_pairs(count))
    return sides


def rope_table(frame_total, row_total, col_total):
    time_dims = DH // 8
    space_dims = (DH - time_dims) // 2
    slower = 256.0 ** (-np.arange(0, time_dims, 2) / time_dims)
    faster = 256.0 ** (-np.arange(0, space_dims, 2) / space_dims)
    starts = (0, time_dims, time_dims + space_dims)
    pieces = []
    for total, rates, start in zip(
        (frame_total, row_total, col_total), (slower, faster, faster), starts
    ):
        padded = -(-total // 8) * 8
        piece = np.zeros((3, padded, DH), np.float32)
        angles = np.arange(padded)[:, None] * rates[None, :]
        stop = start + 2 * len(rates)
        piece[0, :, start:stop:2] = np.cos(angles)
        piece[0, :, start + 1 : stop : 2] = np.cos(angles)
        piece[1, :, start:stop:2] = -np.sin(angles)
        piece[2, :, start + 1 : stop : 2] = np.sin(angles)
        pieces.append(piece)
    return tuple(pieces)


def local_table(plane, time_ref, row_ref, col_ref, frames, rows, cols):
    frame_lo = lax.axis_index("ta") * frames
    row_lo = pl.multiple_of(lax.axis_index("ha") * rows, rows)
    col_lo = pl.multiple_of(lax.axis_index("wa") * cols, cols)
    row_part = row_ref[plane, pl.ds(row_lo, rows), :]
    col_part = col_ref[plane, pl.ds(col_lo, cols), :]
    grids = []
    for i in range(frames):
        lead = row_part + time_ref[plane, pl.ds(frame_lo + i, 1), :]
        grid = lead[:, None, :] + col_part[None, :, :]
        grids.append(grid.reshape(rows * cols, DH))
    return jnp.concatenate(grids, axis=0)


def turn(x, cosine, sin_even, sin_odd, sign):
    follow = pltpu.roll(x, DH - 1, 1)
    lead = pltpu.roll(x, 1, 1)
    return x * cosine + sign * (follow * sin_even + lead * sin_odd)


def head_slice(head):
    return slice(head * DH, (head + 1) * DH)


def rotate_kernel(dims, q_ref, k_ref, v_ref, g_ref, tt_ref, rt_ref, ct_ref, kv_ref, qg_ref):
    tables = [local_table(plane, tt_ref, rt_ref, ct_ref, *dims) for plane in range(3)]
    for head in range(HEADS):
        cut = head_slice(head)
        kv_ref[0, :, cut] = turn(k_ref[:, cut].astype(F32), *tables, 1.0).astype(BF16)
        qg_ref[0, :, cut] = turn(q_ref[:, cut].astype(F32), *tables, 1.0).astype(BF16)
    kv_ref[1] = v_ref[...]
    qg_ref[1] = g_ref[...]


def dot_nt(a, b):
    return lax.dot_general(a, b, (((1,), (1,)), ((), ())), preferred_element_type=F32)


def dot_nn(a, b):
    return lax.dot_general(a, b, (((1,), (0,)), ((), ())), preferred_element_type=F32)


def dot_tn(a, b):
    return lax.dot_general(a, b, (((0,), (0,)), ((), ())), preferred_element_type=F32)


def group_bias(flags, sizes):
    valid = None
    for axis, is_far in zip(("ha", "wa"), flags):
        if is_far:
            here = far_exists(axis, sizes[axis])
            valid = here if valid is None else valid & here
    return None if valid is None else jnp.where(valid, 0.0, NEGATIVE).astype(F32)


def forward_kernel(groups, sizes, cells, with_first, *refs):
    tile_count = sum(len(members) for _, members in groups)
    qa_ref, qb_ref = refs[0], refs[1]
    kv_refs = refs[2 : 2 + tile_count]
    rest = refs[2 + tile_count :]
    if with_first:
        first_ref, oa_ref, ob_ref, stat_ref, key_buf, value_buf = rest
    else:
        oa_ref, ob_ref, stat_ref, key_buf, value_buf = rest
    at = 0
    spans = []
    for flags, members in groups:
        begin = at
        for member in members:
            key_buf[at : at + cells] = kv_refs[member][0]
            value_buf[at : at + cells] = kv_refs[member][1]
            at += cells
        spans.append((begin, at, group_bias(flags, sizes)))
    lane = lax.broadcasted_iota(jnp.int32, (2 * cells, DH), 1)
    stat = jnp.zeros((2 * cells, DH), F32)
    for head in range(HEADS):
        cut = head_slice(head)
        query = jnp.concatenate([qa_ref[0, :, cut], qb_ref[0, :, cut]], axis=0)
        grad = jnp.concatenate([qa_ref[1, :, cut], qb_ref[1, :, cut]], axis=0)
        scores = [dot_nt(query, key_buf[lo:hi, cut]) for lo, hi, _ in spans]
        best = None
        for raw, (_, _, bias) in zip(scores, spans):
            top = jnp.max(raw, axis=1, keepdims=True) * SCALE_LOG2
            if bias is not None:
                top = top + bias
            best = top if best is None else jnp.maximum(best, top)
        total = None
        out = None
        for raw, (lo, hi, bias) in zip(scores, spans):
            shift = best if bias is None else best - bias
            weights = jnp.exp2(raw * SCALE_LOG2 - shift)
            part = jnp.sum(weights, axis=1, keepdims=True)
            piece = dot_nn(weights.astype(BF16), value_buf[lo:hi, cut])
            total = part if total is None else total + part
            out = piece if out is None else out + piece
        out = out * (1.0 / total)
        dotted = jnp.sum(out * grad.astype(F32), axis=1, keepdims=True)
        out = out.astype(BF16)
        oa_ref[:, cut] = out[:cells]
        ob_ref[:, cut] = out[cells:]
        stat = jnp.where(lane == head, best + jnp.log2(total), stat)
        stat = jnp.where(lane == HEADS + head, dotted, stat)
    flipped = stat.T[: stat_ref.shape[-2]]
    if with_first:
        stat_ref[0] = first_ref[...]
        stat_ref[1] = flipped
    else:
        stat_ref[...] = flipped


def merged_stats(own_ref, s1_ref, s2_ref, s3_ref, half, cells):
    parts = [
        own_ref[half],
        s1_ref[1 - half],
        pltpu.roll(s2_ref[half], cells, 1),
        pltpu.roll(s3_ref[1 - half], cells, 1),
    ]
    top = functools.reduce(jnp.maximum, parts)
    shares = [jnp.exp2(part - top) for part in parts]
    total = functools.reduce(jnp.add, shares)
    lse = top + jnp.log2(total)
    shares = [share / total for share in shares]
    rows_lse = [lse[head : head + 1] for head in range(HEADS)]
    rows_delta = []
    for head in range(HEADS):
        terms = [
            share[head : head + 1] * part[HEADS + head : HEADS + head + 1]
            for share, part in zip(shares, parts)
        ]
        rows_delta.append(functools.reduce(jnp.add, terms))
    return rows_lse, rows_delta, shares


def backward_kernel(groups, grid_rows, grid_cols, sizes, cells, *refs):
    tile_count = sum(len(members) for _, members in groups)
    qg_refs = refs[:4]
    kv_refs = refs[4 : 4 + tile_count]
    rest = refs[4 + tile_count :]
    stat_refs = rest[:4]
    dq_refs = rest[4:8]
    share_ref = rest[8]
    col_refs = rest[9 : 9 + grid_cols]
    half_rows = 2 * cells
    halves = [(qg_refs[0], qg_refs[1]), (qg_refs[2], qg_refs[3])]
    stats = [merged_stats(*stat_refs, half, cells) for half in range(2)]

    own_shares = stats[0][2]
    rows = [own_shares[d][head : head + 1] for head in range(HEADS) for d in range(4)]
    wide = jnp.concatenate(rows + [jnp.zeros((DH - len(rows), half_rows), F32)], axis=0)
    share_ref[...] = wide.T[:cells]

    for head in range(HEADS):
        cut = head_slice(head)
        queries = [
            jnp.concatenate([a[0, :, cut], b[0, :, cut]], axis=0) for a, b in halves
        ]
        grads = [jnp.concatenate([a[1, :, cut], b[1, :, cut]], axis=0) for a, b in halves]
        dq = [None, None]
        for flags, members in groups:
            bias = group_bias(flags, sizes)
            for member in members:
                row, col = member // grid_cols, member % grid_cols
                key = kv_refs[member][0, :, cut]
                value = kv_refs[member][1, :, cut]
                dk, dv = None, None
                for half in range(2):
                    lse = stats[half][0][head]
                    delta = stats[half][1][head]
                    if bias is not None:
                        lse = lse - bias
                    raw = dot_nt(key, queries[half])
                    probs = jnp.exp2(raw * SCALE_LOG2 - lse)
                    prob_grad = dot_nt(value, grads[half])
                    dscore = (probs * (prob_grad - delta)).astype(BF16)
                    dv_part = dot_nn(probs.astype(BF16), grads[half])
                    dk_part = dot_nn(dscore, queries[half])
                    dq_part = dot_tn(dscore, key)
                    dv = dv_part if dv is None else dv + dv_part
                    dk = dk_part if dk is None else dk + dk_part
                    dq[half] = dq_part if dq[half] is None else dq[half] + dq_part
                col_refs[col][row, 0, :, cut] = (dk * SCALE).astype(BF16)
                col_refs[col][row, 1, :, cut] = dv.astype(BF16)
        for half in range(2):
            scaled = (dq[half] * SCALE).astype(BF16)
            dq_refs[2 * half][:, cut] = scaled[:cells]
            dq_refs[2 * half + 1][:, cut] = scaled[cells:]


def finish_query_kernel(dims, *refs):
    o_refs, dq_refs = refs[:4], refs[4:8]
    share_ref, tt_ref, rt_ref, ct_ref, out_ref, dq_out = refs[8:]
    tables = [local_table(plane, tt_ref, rt_ref, ct_ref, *dims) for plane in range(3)]
    for head in range(HEADS):
        cut = head_slice(head)
        out, dq = None, None
        for d in range(4):
            weight = share_ref[:, 4 * head + d : 4 * head + d + 1]
            piece = o_refs[d][:, cut].astype(F32) * weight
            out = piece if out is None else out + piece
            grad = dq_refs[d][:, cut].astype(F32)
            dq = grad if dq is None else dq + grad
        out_ref[:, cut] = out.astype(BF16)
        dq_out[:, cut] = turn(dq, *tables, -1.0).astype(BF16)


def finish_key_kernel(dims, cols, rows, *refs):
    col_refs, row_refs = refs[:cols], refs[cols : cols + rows]
    tt_ref, rt_ref, ct_ref, dk_out, dv_out = refs[cols + rows :]
    tables = [local_table(plane, tt_ref, rt_ref, ct_ref, *dims) for plane in range(3)]
    for head in range(HEADS):
        cut = head_slice(head)
        sums = []
        for which in range(2):
            terms = [ref[0, which, :, cut].astype(F32) for ref in col_refs]
            terms += [ref[which, :, cut].astype(F32) for ref in row_refs]
            sums.append(functools.reduce(jnp.add, terms))
        dk_out[:, cut] = turn(sums[0], *tables, -1.0).astype(BF16)
        dv_out[:, cut] = sums[1].astype(BF16)


def call(kernel, out_shape, args, flops=0, exps=0, scratch=()):
    shapes = jax.tree.leaves(out_shape)
    moved = sum(math.prod(x.shape) * x.dtype.itemsize for x in list(args) + shapes)
    return pl.pallas_call(
        kernel,
        out_shape=out_shape,
        scratch_shapes=list(scratch),
        compiler_params=pltpu.CompilerParams(vmem_limit_bytes=VMEM_LIMIT),
        cost_estimate=pl.CostEstimate(flops=flops, bytes_accessed=moved, transcendentals=exps),
    )(*args)


def shards(query_in, key_in, value_in, cotangent):
    frames, rows, cols, chan = query_in.shape
    cells = frames * rows * cols
    sizes = {axis: lax.axis_size(axis) for axis in ("ta", "ha", "wa")}
    assert rows == TILE_H and cols == TILE_W and chan == HEADS * DH
    assert TILE_T % frames == 0 and frames * sizes["ta"] <= 2 * TILE_T
    assert sizes["ta"] == 4 and sizes["ha"] % 2 == 0 and sizes["wa"] % 2 == 0
    dims = (frames, rows, cols)
    tables = tuple(
        jnp.asarray(x)
        for x in rope_table(frames * sizes["ta"], rows * sizes["ha"], cols * sizes["wa"])
    )
    flat = [x.reshape(cells, chan) for x in (query_in, key_in, value_in, cotangent)]
    pair = jax.ShapeDtypeStruct((2, cells, chan), BF16)
    plain = jax.ShapeDtypeStruct((cells, chan), BF16)

    with jax.named_scope("rotate"):
        kv, qg = call(
            functools.partial(rotate_kernel, dims), (pair, pair), (*flat, *tables)
        )

    def other_frames(x, distance):
        return lax.ppermute(x, "ta", [(i, i ^ distance) for i in range(sizes["ta"])])

    row_sides = side_pairs(sizes["ha"])
    col_sides = side_pairs(sizes["wa"])
    with jax.named_scope("halo"):
        kv_rows = [kv] + [lax.ppermute(kv, "ha", pairs) for pairs in row_sides]
        qg2 = other_frames(qg, 2)
        qg1 = other_frames(qg, 1)
        tiles = []
        for block in kv_rows:
            tiles += [block] + [lax.ppermute(block, "wa", pairs) for pairs in col_sides]
        qg3 = other_frames(qg2, 1)
    grid_rows, grid_cols = 1 + len(row_sides), 1 + len(col_sides)
    groups = {}
    for row in range(grid_rows):
        for col in range(grid_cols):
            groups.setdefault((row == 2, col == 2), []).append(row * grid_cols + col)
    groups = list(groups.items())

    key_count = len(tiles) * cells
    product = 2 * 2 * cells * key_count * DH * HEADS
    keys = [pltpu.VMEM((key_count, chan), BF16)] * 2
    stat_shape = (8, 2 * cells)

    def forward(qa, qb, first):
        args = (qa, qb, *tiles) + (() if first is None else (first,))
        stat = stat_shape if first is None else (2, *stat_shape)
        return call(
            functools.partial(forward_kernel, groups, sizes, cells, first is not None),
            (plain, plain, jax.ShapeDtypeStruct(stat, F32)),
            args,
            2 * product,
            2 * cells * key_count * HEADS,
            keys,
        )

    with jax.named_scope("attend"):
        o0, o2, first = forward(qg, qg2, None)
        o1, o3, stat = forward(qg1, qg3, first)
    with jax.named_scope("merge"):
        stats = [stat] + [other_frames(stat, d) for d in (1, 2, 3)]
        outs = [o0] + [other_frames(o, d) for d, o in ((1, o1), (2, o2), (3, o3))]

    with jax.named_scope("gradients"):
        results = call(
            functools.partial(backward_kernel, groups, grid_rows, grid_cols, sizes, cells),
            (
                *[plain] * 4,
                jax.ShapeDtypeStruct((cells, DH), F32),
                *[jax.ShapeDtypeStruct((grid_rows, 2, cells, chan), BF16)] * grid_cols,
            ),
            (qg, qg2, qg1, qg3, *tiles, *stats),
            10 * product,
            4 * cells * key_count * HEADS,
        )
    d0, d2, d1, d3, shares = results[:5]
    by_col = results[5:]
    with jax.named_scope("return"):
        col_parts = [by_col[0]] + [
            lax.ppermute(x, "wa", pairs) for x, pairs in zip(by_col[1:], col_sides)
        ]
        dqs = [d0] + [other_frames(x, d) for d, x in ((1, d1), (2, d2), (3, d3))]
        row_parts = []
        for row, pairs in enumerate(row_sides, start=1):
            partial_sum = sum(x[row].astype(F32) for x in col_parts).astype(BF16)
            row_parts.append(lax.ppermute(partial_sum, "ha", pairs))

    with jax.named_scope("finish"):
        attended, grad_query = call(
            functools.partial(finish_query_kernel, dims),
            (plain, plain),
            (*outs, *dqs, shares, *tables),
        )
        grad_key, grad_value = call(
            functools.partial(finish_key_kernel, dims, grid_cols, len(row_parts)),
            (plain, plain),
            (*col_parts, *row_parts, *tables),
        )
    return tuple(x.reshape(query_in.shape) for x in (attended, grad_query, grad_key, grad_value))


def solution(mesh):
    spec = P("ta", "ha", "wa", None)
    return jax.shard_map(
        shards, mesh=mesh, in_specs=(spec,) * 4, out_specs=(spec,) * 4, check_vma=False
    )
```

```python
import functools
import math

import jax
import jax.numpy as jnp
import numpy as np
from jax import lax
from jax.experimental import pallas as pl
from jax.experimental.pallas import tpu as pltpu
from jax.sharding import PartitionSpec as P

DH = 128
HEADS = 2
TILE_T = 6
TILE_H = 8
TILE_W = 8

NEGATIVE = -1e30
SCALE = DH**-0.5
SCALE_LOG2 = SCALE * math.log2(math.e)
F32 = jnp.float32
BF16 = jnp.bfloat16
VMEM_LIMIT = 48 * 1024 * 1024


def near_pairs(count):
    return [(i, i ^ 1) for i in range(count)]


def far_pairs(count):
    pairs = []
    for i in range(count):
        j = i + 1 if i % 2 else i - 1
        pairs.append((i, j if 0 <= j < count else i))
    return pairs


def far_exists(axis, count):
    pos = lax.axis_index(axis)
    other = jnp.where(pos % 2 == 1, pos + 1, pos - 1)
    return (other >= 0) & (other < count)


def side_pairs(count):
    sides = []
    if count > 1:
        sides.append(near_pairs(count))
    if count > 2:
        sides.append(far_pairs(count))
    return sides


def rope_table(frame_total, row_total, col_total):
    time_dims = DH // 8
    space_dims = (DH - time_dims) // 2
    slower = 256.0 ** (-np.arange(0, time_dims, 2) / time_dims)
    faster = 256.0 ** (-np.arange(0, space_dims, 2) / space_dims)
    starts = (0, time_dims, time_dims + space_dims)
    pieces = []
    for total, rates, start in zip(
        (frame_total, row_total, col_total), (slower, faster, faster), starts
    ):
        padded = -(-total // 8) * 8
        piece = np.zeros((3, padded, DH), np.float32)
        angles = np.arange(padded)[:, None] * rates[None, :]
        stop = start + 2 * len(rates)
        piece[0, :, start:stop:2] = np.cos(angles)
        piece[0, :, start + 1 : stop : 2] = np.cos(angles)
        piece[1, :, start:stop:2] = -np.sin(angles)
        piece[2, :, start + 1 : stop : 2] = np.sin(angles)
        pieces.append(piece)
    begins = np.cumsum([0] + [piece.shape[1] for piece in pieces])
    return np.concatenate(pieces, axis=1), tuple(int(x) for x in begins[:3])


def local_table(plane, table_ref, begins, frames, rows, cols):
    frame_lo = begins[0] + lax.axis_index("ta") * frames
    row_lo = pl.multiple_of(begins[1] + lax.axis_index("ha") * rows, 8)
    col_lo = pl.multiple_of(begins[2] + lax.axis_index("wa") * cols, 8)
    row_part = table_ref[plane, pl.ds(row_lo, rows), :]
    col_part = table_ref[plane, pl.ds(col_lo, cols), :]
    grids = []
    for i in range(frames):
        lead = row_part + table_ref[plane, pl.ds(frame_lo + i, 1), :]
        grid = lead[:, None, :] + col_part[None, :, :]
        grids.append(grid.reshape(rows * cols, DH))
    return jnp.concatenate(grids, axis=0)


def turn(x, cosine, sin_even, sin_odd, sign):
    follow = pltpu.roll(x, DH - 1, 1)
    lead = pltpu.roll(x, 1, 1)
    return x * cosine + sign * (follow * sin_even + lead * sin_odd)


def head_slice(head):
    return slice(head * DH, (head + 1) * DH)


def rotate_kernel(
    dims, begins, q_hbm, k_hbm, v_hbm, g_hbm, table_hbm, kv_ref, qg_ref, rope_ref, q_ref, k_ref,
    table_ref, sems,
):
    moves = [
        (table_hbm, table_ref),
        (k_hbm, k_ref),
        (q_hbm, q_ref),
        (v_hbm, kv_ref.at[1]),
        (g_hbm, qg_ref.at[1]),
    ]
    copies = [pltpu.make_async_copy(*move, sems.at[i]) for i, move in enumerate(moves)]
    for copy in copies:
        copy.start()
    copies[0].wait()
    tables = [local_table(plane, table_ref, begins, *dims) for plane in range(3)]
    for plane in range(3):
        rope_ref[plane] = tables[plane]
    for copy, source, target in ((copies[1], k_ref, kv_ref), (copies[2], q_ref, qg_ref)):
        copy.wait()
        for head in range(HEADS):
            cut = head_slice(head)
            target[0, :, cut] = turn(source[:, cut].astype(F32), *tables, 1.0).astype(BF16)
    copies[3].wait()
    copies[4].wait()


def dot_nt(a, b):
    return lax.dot_general(a, b, (((1,), (1,)), ((), ())), preferred_element_type=F32)


def dot_nn(a, b):
    return lax.dot_general(a, b, (((1,), (0,)), ((), ())), preferred_element_type=F32)


def dot_tn(a, b):
    return lax.dot_general(a, b, (((0,), (0,)), ((), ())), preferred_element_type=F32)


def group_bias(flags, sizes):
    valid = None
    for axis, is_far in zip(("ha", "wa"), flags):
        if is_far:
            here = far_exists(axis, sizes[axis])
            valid = here if valid is None else valid & here
    return None if valid is None else jnp.where(valid, 0.0, NEGATIVE).astype(F32)


def forward_kernel(groups, sizes, cells, with_first, *refs):
    tile_count = sum(len(members) for _, members in groups)
    qa_ref, qb_ref = refs[0], refs[1]
    kv_refs = refs[2 : 2 + tile_count]
    rest = refs[2 + tile_count :]
    if with_first:
        first_ref, oa_ref, ob_ref, stat_ref, key_buf, value_buf = rest
    else:
        oa_ref, ob_ref, stat_ref, key_buf, value_buf = rest
    at = 0
    spans = []
    for flags, members in groups:
        begin = at
        for member in members:
            key_buf[at : at + cells] = kv_refs[member][0]
            value_buf[at : at + cells] = kv_refs[member][1]
            at += cells
        spans.append((begin, at, group_bias(flags, sizes)))
    lane = lax.broadcasted_iota(jnp.int32, (2 * cells, DH), 1)
    stat = jnp.zeros((2 * cells, DH), F32)
    for head in range(HEADS):
        cut = head_slice(head)
        query = jnp.concatenate([qa_ref[0, :, cut], qb_ref[0, :, cut]], axis=0)
        grad = jnp.concatenate([qa_ref[1, :, cut], qb_ref[1, :, cut]], axis=0)
        scores = [dot_nt(query, key_buf[lo:hi, cut]) for lo, hi, _ in spans]
        best = None
        for raw, (_, _, bias) in zip(scores, spans):
            top = jnp.max(raw, axis=1, keepdims=True) * SCALE_LOG2
            if bias is not None:
                top = top + bias
            best = top if best is None else jnp.maximum(best, top)
        total = None
        out = None
        for raw, (lo, hi, bias) in zip(scores, spans):
            shift = best if bias is None else best - bias
            weights = jnp.exp2(raw * SCALE_LOG2 - shift)
            part = jnp.sum(weights, axis=1, keepdims=True)
            piece = dot_nn(weights.astype(BF16), value_buf[lo:hi, cut])
            total = part if total is None else total + part
            out = piece if out is None else out + piece
        out = out * (1.0 / total)
        dotted = jnp.sum(out * grad.astype(F32), axis=1, keepdims=True)
        out = out.astype(BF16)
        oa_ref[:, cut] = out[:cells]
        ob_ref[:, cut] = out[cells:]
        stat = jnp.where(lane == head, best + jnp.log2(total), stat)
        stat = jnp.where(lane == HEADS + head, dotted, stat)
    flipped = stat.T[: stat_ref.shape[-2]]
    if with_first:
        stat_ref[0] = first_ref[...]
        stat_ref[1] = flipped
    else:
        stat_ref[...] = flipped


def merged_stats(own_ref, s1_ref, s2_ref, s3_ref, half, cells):
    parts = [
        own_ref[half],
        pltpu.roll(s1_ref[half], cells, 1),
        s2_ref[1 - half],
        pltpu.roll(s3_ref[1 - half], cells, 1),
    ]
    top = functools.reduce(jnp.maximum, parts)
    shares = [jnp.exp2(part - top) for part in parts]
    total = functools.reduce(jnp.add, shares)
    lse = top + jnp.log2(total)
    shares = [share / total for share in shares]
    delta = functools.reduce(
        jnp.add,
        [share[:HEADS] * part[HEADS : 2 * HEADS] for share, part in zip(shares, parts)],
    )
    return lse[:HEADS], delta, shares


def gradient_blocks(cols, flags_of, sizes, key_buf, value_buf, queries, grads, lse, delta, span):
    dq = None
    results = []
    for slot, col in enumerate(cols):
        lo = slot * span
        key = key_buf[lo : lo + span]
        value = value_buf[lo : lo + span]
        raw = dot_nt(key, queries)
        prob_grad = dot_nt(value, grads)
        cells = span // len(flags_of)
        probs = []
        for row, row_far in enumerate(flags_of):
            bias = group_bias((row_far, col == 2), sizes)
            shift = lse if bias is None else lse - bias
            probs.append(jnp.exp2(raw[row * cells : (row + 1) * cells] * SCALE_LOG2 - shift))
        probs = jnp.concatenate(probs, axis=0)
        dscore = (probs * (prob_grad - delta)).astype(BF16)
        dv = dot_nn(probs.astype(BF16), grads)
        dk = dot_nn(dscore, queries) * SCALE
        results.append((dk, dv))
        part = dot_nn(key.T, dscore)
        dq = part if dq is None else dq + part
    return results, dq


def backward_kernel(cols, grid_rows, sizes, cells, last, *refs):
    tile_count = grid_rows * len(cols)
    qg_refs = refs[:4]
    kv_refs = refs[4 : 4 + tile_count]
    rest = refs[4 + tile_count :]
    if last:
        lse_ref, delta_ref, share_ref, dq_ref = rest[:4]
        o_refs = rest[4:8]
        dq_outs, out_ref = rest[8:12], rest[12]
        col_refs = rest[13 : 13 + len(cols)]
        key_buf, value_buf = rest[13 + len(cols) :]
        lse, delta = lse_ref[...], delta_ref[...]
        for head in range(HEADS):
            cut = head_slice(head)
            out = None
            for d in range(4):
                weight = share_ref[:, 4 * head + d : 4 * head + d + 1]
                piece = o_refs[d][:, cut].astype(F32) * weight
                out = piece if out is None else out + piece
            out_ref[:, cut] = out.astype(BF16)
    else:
        stat_refs = rest[:4]
        lse_ref, delta_ref, share_ref, dq_ref = rest[4:8]
        col_refs = rest[8 : 8 + len(cols)]
        key_buf, value_buf = rest[8 + len(cols) :]
        stats = [merged_stats(*stat_refs, half, cells) for half in range(2)]
        lse = jnp.concatenate([stats[0][0], stats[1][0]], axis=1)
        delta = jnp.concatenate([stats[0][1], stats[1][1]], axis=1)
        lse_ref[...] = lse
        delta_ref[...] = delta
        shares = stats[0][2]
        rows = [shares[d][head : head + 1] for head in range(HEADS) for d in range(4)]
        wide = jnp.concatenate(rows + [jnp.zeros((DH - len(rows), 2 * cells), F32)], axis=0)
        share_ref[...] = wide.T[:cells]

    span = grid_rows * cells
    for i, ref in enumerate(kv_refs):
        key_buf[i * cells : (i + 1) * cells] = ref[0]
        value_buf[i * cells : (i + 1) * cells] = ref[1]
    row_flags = [row == 2 for row in range(grid_rows)]
    for head in range(HEADS):
        cut = head_slice(head)
        queries = jnp.concatenate([ref[0, :, cut] for ref in qg_refs], axis=0)
        grads = jnp.concatenate([ref[1, :, cut] for ref in qg_refs], axis=0)
        results, dq = gradient_blocks(
            cols, row_flags, sizes, key_buf.at[:, cut], value_buf.at[:, cut], queries, grads,
            lse[head : head + 1], delta[head : head + 1], span,
        )
        for (dk, dv), ref in zip(results, col_refs):
            for row in range(grid_rows):
                at = slice(row * cells, (row + 1) * cells)
                ref[row, 0, :, cut] = dk[at].astype(BF16)
                ref[row, 1, :, cut] = dv[at].astype(BF16)
        if last:
            dq = ((dq + dq_ref[head]) * SCALE).T.astype(BF16)
            for i, ref in enumerate(dq_outs):
                ref[:, cut] = dq[i * cells : (i + 1) * cells]
        else:
            dq_ref[head] = dq


def finish_query_kernel(*refs):
    dq_refs = refs[:4]
    rope_ref, dq_out = refs[4:]
    for head in range(HEADS):
        cut = head_slice(head)
        dq = functools.reduce(jnp.add, [ref[:, cut].astype(F32) for ref in dq_refs])
        dq_out[:, cut] = turn(dq, rope_ref[0], rope_ref[1], rope_ref[2], -1.0).astype(BF16)


def finish_key_kernel(cols, rows, *refs):
    col_refs, row_refs = refs[:cols], refs[cols : cols + rows]
    rope_ref, dk_out, dv_out = refs[cols + rows :]
    for head in range(HEADS):
        cut = head_slice(head)
        sums = []
        for which in range(2):
            terms = [ref[0, which, :, cut].astype(F32) for ref in col_refs]
            terms += [ref[which, :, cut].astype(F32) for ref in row_refs]
            sums.append(functools.reduce(jnp.add, terms))
        dk_out[:, cut] = turn(
            sums[0], rope_ref[0], rope_ref[1], rope_ref[2], -1.0
        ).astype(BF16)
        dv_out[:, cut] = sums[1].astype(BF16)


def call(kernel, out_shape, args, flops=0, exps=0, scratch=(), space=pltpu.VMEM, limit=VMEM_LIMIT):
    shapes = jax.tree.leaves(out_shape)
    moved = sum(math.prod(x.shape) * x.dtype.itemsize for x in list(args) + shapes)
    return pl.pallas_call(
        kernel,
        out_shape=out_shape,
        in_specs=[pl.BlockSpec(memory_space=space)] * len(args),
        scratch_shapes=list(scratch),
        compiler_params=pltpu.CompilerParams(vmem_limit_bytes=limit),
        cost_estimate=pl.CostEstimate(flops=flops, bytes_accessed=moved, transcendentals=exps),
    )(*args)


def shards(query_in, key_in, value_in, cotangent):
    frames, rows, cols, chan = query_in.shape
    cells = frames * rows * cols
    sizes = {axis: lax.axis_size(axis) for axis in ("ta", "ha", "wa")}
    assert rows == TILE_H and cols == TILE_W and chan == HEADS * DH
    assert TILE_T % frames == 0 and frames * sizes["ta"] <= 2 * TILE_T
    assert sizes["ta"] == 4 and sizes["ha"] % 2 == 0 and sizes["wa"] % 2 == 0
    dims = (frames, rows, cols)
    table, begins = rope_table(frames * sizes["ta"], rows * sizes["ha"], cols * sizes["wa"])
    flat = [x.reshape(cells, chan) for x in (query_in, key_in, value_in, cotangent)]
    pair = jax.ShapeDtypeStruct((2, cells, chan), BF16)
    plain = jax.ShapeDtypeStruct((cells, chan), BF16)

    def real(*shape):
        return jax.ShapeDtypeStruct(shape, F32)

    with jax.named_scope("rotate"):
        kv, qg, rope = call(
            functools.partial(rotate_kernel, dims, begins),
            (pair, pair, real(3, cells, DH)),
            [pltpu.with_memory_space_constraint(x, pltpu.HBM) for x in (*flat, jnp.asarray(table))],
            scratch=[pltpu.VMEM((cells, chan), BF16)] * 2
            + [pltpu.VMEM(table.shape, F32), pltpu.SemaphoreType.DMA((5,))],
            space=pltpu.HBM,
        )

    def other_frames(x, distance):
        return lax.ppermute(x, "ta", [(i, i ^ distance) for i in range(sizes["ta"])])

    row_sides = side_pairs(sizes["ha"])
    col_sides = side_pairs(sizes["wa"])
    with jax.named_scope("halo"):
        kv_rows = [kv] + [lax.ppermute(kv, "ha", pairs) for pairs in row_sides]
        qg2 = other_frames(qg, 2)
        qg1 = other_frames(qg, 1)
        tiles = []
        for block in kv_rows:
            tiles.append([block] + [lax.ppermute(block, "wa", pairs) for pairs in col_sides])
        qg3 = other_frames(qg2, 1)
    grid_rows, grid_cols = 1 + len(row_sides), 1 + len(col_sides)
    flat_tiles = [tiles[row][col] for row in range(grid_rows) for col in range(grid_cols)]
    groups = {}
    for row in range(grid_rows):
        for col in range(grid_cols):
            groups.setdefault((row == 2, col == 2), []).append(row * grid_cols + col)
    groups = list(groups.items())

    key_count = len(flat_tiles) * cells
    product = 2 * 2 * cells * key_count * DH * HEADS

    def forward(qa, qb, first):
        args = (qa, qb, *flat_tiles) + (() if first is None else (first,))
        stat = (8, 2 * cells) if first is None else (2, 8, 2 * cells)
        return call(
            functools.partial(forward_kernel, groups, sizes, cells, first is not None),
            (plain, plain, real(*stat)),
            args,
            2 * product,
            2 * cells * key_count * HEADS,
            [pltpu.VMEM((key_count, chan), BF16)] * 2,
        )

    with jax.named_scope("attend"):
        o0, o1, first = forward(qg, qg1, None)
        o2, o3, stat = forward(qg2, qg3, first)
    with jax.named_scope("merge"):
        stats = [stat] + [other_frames(stat, d) for d in (1, 2, 3)]
        outs = [o0] + [other_frames(o, d) for d, o in ((1, o1), (2, o2), (3, o3))]

    queries = (qg, qg1, qg2, qg3)
    col_shape = jax.ShapeDtypeStruct((grid_rows, 2, cells, chan), BF16)

    def gradients(which, last, extra_out, extra_in):
        count = len(which)
        return call(
            functools.partial(backward_kernel, which, grid_rows, sizes, cells, last),
            (*extra_out, *[col_shape] * count),
            (*queries, *[tiles[row][col] for col in which for row in range(grid_rows)], *extra_in),
            10 * product * count // grid_cols,
            4 * cells * key_count * HEADS * count // grid_cols,
            [pltpu.VMEM((count * grid_rows * cells, chan), BF16)] * 2,
        )

    with jax.named_scope("gradients"):
        lse, delta, shares, dq, *sides = gradients(
            tuple(range(1, grid_cols)),
            False,
            (
                real(HEADS, 4 * cells),
                real(HEADS, 4 * cells),
                real(cells, DH),
                real(HEADS, DH, 4 * cells),
            ),
            stats,
        )
        sides = [lax.ppermute(x, "wa", pairs) for x, pairs in zip(sides, col_sides)]
        d0, d1, d2, d3, attended, own = gradients(
            (0,), True, [plain] * 5, (lse, delta, shares, dq, *outs)
        )
    with jax.named_scope("return"):
        col_parts = [own, *sides]
        dqs = [d0] + [other_frames(x, d) for d, x in ((1, d1), (2, d2), (3, d3))]
        row_parts = []
        for row, pairs in enumerate(row_sides, start=1):
            partial_sum = sum(x[row].astype(F32) for x in col_parts).astype(BF16)
            row_parts.append(lax.ppermute(partial_sum, "ha", pairs))

    with jax.named_scope("finish"):
        grad_query = call(finish_query_kernel, plain, (*dqs, rope))
        grad_key, grad_value = call(
            functools.partial(finish_key_kernel, grid_cols, len(row_parts)),
            (plain, plain),
            (*col_parts, *row_parts, rope),
        )
    return tuple(x.reshape(query_in.shape) for x in (attended, grad_query, grad_key, grad_value))


def solution(mesh):
    spec = P("ta", "ha", "wa", None)
    return jax.shard_map(
        shards, mesh=mesh, in_specs=(spec,) * 4, out_specs=(spec,) * 4, check_vma=False
    )
```

```python
import functools
import math

import jax
import jax.numpy as jnp
import numpy as np
from jax import lax
from jax.experimental import pallas as pl
from jax.experimental.pallas import tpu as pltpu
from jax.sharding import PartitionSpec as P

DH = 128
HEADS = 2
TILE_T = 6
TILE_H = 8
TILE_W = 8

NEGATIVE = -1e30
SCALE = DH**-0.5
SCALE_LOG2 = SCALE * math.log2(math.e)
F32 = jnp.float32
BF16 = jnp.bfloat16
VMEM_LIMIT = 48 * 1024 * 1024


def near_pairs(count):
    return [(i, i ^ 1) for i in range(count)]


def far_pairs(count):
    pairs = []
    for i in range(count):
        j = i + 1 if i % 2 else i - 1
        pairs.append((i, j if 0 <= j < count else i))
    return pairs


def far_exists(axis, count):
    pos = lax.axis_index(axis)
    other = jnp.where(pos % 2 == 1, pos + 1, pos - 1)
    return (other >= 0) & (other < count)


def side_pairs(count):
    sides = []
    if count > 1:
        sides.append(near_pairs(count))
    if count > 2:
        sides.append(far_pairs(count))
    return sides


def rope_table(frame_total, row_total, col_total):
    time_dims = DH // 8
    space_dims = (DH - time_dims) // 2
    slower = 256.0 ** (-np.arange(0, time_dims, 2) / time_dims)
    faster = 256.0 ** (-np.arange(0, space_dims, 2) / space_dims)
    starts = (0, time_dims, time_dims + space_dims)
    pieces = []
    for total, rates, start in zip(
        (frame_total, row_total, col_total), (slower, faster, faster), starts
    ):
        padded = -(-total // 8) * 8
        piece = np.zeros((3, padded, DH), np.float32)
        angles = np.arange(padded)[:, None] * rates[None, :]
        stop = start + 2 * len(rates)
        piece[0, :, start:stop:2] = np.cos(angles)
        piece[0, :, start + 1 : stop : 2] = np.cos(angles)
        piece[1, :, start:stop:2] = -np.sin(angles)
        piece[2, :, start + 1 : stop : 2] = np.sin(angles)
        pieces.append(piece)
    begins = np.cumsum([0] + [piece.shape[1] for piece in pieces])
    return np.concatenate(pieces, axis=1), tuple(int(x) for x in begins[:3])


def local_table(plane, table_ref, begins, frames, rows, cols):
    frame_lo = begins[0] + lax.axis_index("ta") * frames
    row_lo = pl.multiple_of(begins[1] + lax.axis_index("ha") * rows, 8)
    col_lo = pl.multiple_of(begins[2] + lax.axis_index("wa") * cols, 8)
    row_part = table_ref[plane, pl.ds(row_lo, rows), :]
    col_part = table_ref[plane, pl.ds(col_lo, cols), :]
    grids = []
    for i in range(frames):
        lead = row_part + table_ref[plane, pl.ds(frame_lo + i, 1), :]
        grid = lead[:, None, :] + col_part[None, :, :]
        grids.append(grid.reshape(rows * cols, DH))
    return jnp.concatenate(grids, axis=0)


def turn(x, cosine, sin_even, sin_odd, sign):
    follow = pltpu.roll(x, DH - 1, 1)
    lead = pltpu.roll(x, 1, 1)
    return x * cosine + sign * (follow * sin_even + lead * sin_odd)


def head_slice(head):
    return slice(head * DH, (head + 1) * DH)


def rotate_kernel(
    dims, begins, q_hbm, k_hbm, v_hbm, g_hbm, table_hbm, kv_ref, qg_ref, rope_ref, q_ref, k_ref,
    table_ref, sems,
):
    moves = [
        (table_hbm, table_ref),
        (k_hbm, k_ref),
        (q_hbm, q_ref),
        (v_hbm, kv_ref.at[1]),
        (g_hbm, qg_ref.at[1]),
    ]
    copies = [pltpu.make_async_copy(*move, sems.at[i]) for i, move in enumerate(moves)]
    for copy in copies:
        copy.start()
    copies[0].wait()
    tables = [local_table(plane, table_ref, begins, *dims) for plane in range(3)]
    for plane in range(3):
        rope_ref[plane] = tables[plane]
    for copy, source, target in ((copies[1], k_ref, kv_ref), (copies[2], q_ref, qg_ref)):
        copy.wait()
        for head in range(HEADS):
            cut = head_slice(head)
            target[0, :, cut] = turn(source[:, cut].astype(F32), *tables, 1.0).astype(BF16)
    copies[3].wait()
    copies[4].wait()


def dot_nt(a, b):
    return lax.dot_general(a, b, (((1,), (1,)), ((), ())), preferred_element_type=F32)


def dot_nn(a, b):
    return lax.dot_general(a, b, (((1,), (0,)), ((), ())), preferred_element_type=F32)


def dot_tn(a, b):
    return lax.dot_general(a, b, (((0,), (0,)), ((), ())), preferred_element_type=F32)


def group_bias(flags, sizes):
    valid = None
    for axis, is_far in zip(("ha", "wa"), flags):
        if is_far:
            here = far_exists(axis, sizes[axis])
            valid = here if valid is None else valid & here
    return None if valid is None else jnp.where(valid, 0.0, NEGATIVE).astype(F32)


def forward_kernel(groups, sizes, cells, with_first, *refs):
    tile_count = sum(len(members) for _, members in groups)
    qa_ref, qb_ref = refs[0], refs[1]
    kv_refs = refs[2 : 2 + tile_count]
    rest = refs[2 + tile_count :]
    if with_first:
        first_ref, oa_ref, ob_ref, stat_ref, key_buf, value_buf = rest
    else:
        oa_ref, ob_ref, stat_ref, key_buf, value_buf = rest
    at = 0
    spans = []
    for flags, members in groups:
        begin = at
        for member in members:
            key_buf[at : at + cells] = kv_refs[member][0]
            value_buf[at : at + cells] = kv_refs[member][1]
            at += cells
        spans.append((begin, at, group_bias(flags, sizes)))
    lane = lax.broadcasted_iota(jnp.int32, (2 * cells, DH), 1)
    stat = jnp.zeros((2 * cells, DH), F32)
    for head in range(HEADS):
        cut = head_slice(head)
        query = jnp.concatenate([qa_ref[0, :, cut], qb_ref[0, :, cut]], axis=0)
        grad = jnp.concatenate([qa_ref[1, :, cut], qb_ref[1, :, cut]], axis=0)
        scores = [dot_nt(query, key_buf[lo:hi, cut]) for lo, hi, _ in spans]
        best = None
        for raw, (_, _, bias) in zip(scores, spans):
            top = jnp.max(raw, axis=1, keepdims=True) * SCALE_LOG2
            if bias is not None:
                top = top + bias
            best = top if best is None else jnp.maximum(best, top)
        total = None
        out = None
        for raw, (lo, hi, bias) in zip(scores, spans):
            shift = best if bias is None else best - bias
            weights = jnp.exp2(raw * SCALE_LOG2 - shift)
            part = jnp.sum(weights, axis=1, keepdims=True)
            piece = dot_nn(weights.astype(BF16), value_buf[lo:hi, cut])
            total = part if total is None else total + part
            out = piece if out is None else out + piece
        out = out * (1.0 / total)
        dotted = jnp.sum(out * grad.astype(F32), axis=1, keepdims=True)
        out = out.astype(BF16)
        oa_ref[:, cut] = out[:cells]
        ob_ref[:, cut] = out[cells:]
        stat = jnp.where(lane == head, best + jnp.log2(total), stat)
        stat = jnp.where(lane == HEADS + head, dotted, stat)
    flipped = stat.T[: stat_ref.shape[-2]]
    if with_first:
        stat_ref[0] = first_ref[...]
        stat_ref[1] = flipped
    else:
        stat_ref[...] = flipped


def merged_stats(own_ref, s1_ref, s2_ref, s3_ref, half, cells):
    parts = [
        own_ref[half],
        pltpu.roll(s1_ref[half], cells, 1),
        s2_ref[1 - half],
        pltpu.roll(s3_ref[1 - half], cells, 1),
    ]
    top = functools.reduce(jnp.maximum, parts)
    shares = [jnp.exp2(part - top) for part in parts]
    total = functools.reduce(jnp.add, shares)
    lse = top + jnp.log2(total)
    shares = [share / total for share in shares]
    delta = functools.reduce(
        jnp.add,
        [share[:HEADS] * part[HEADS : 2 * HEADS] for share, part in zip(shares, parts)],
    )
    return lse[:HEADS], delta, shares


def gradient_blocks(cols, flags_of, sizes, key_buf, value_buf, queries, grads, lse, delta, span):
    dq = None
    results = []
    for slot, col in enumerate(cols):
        lo = slot * span
        key = key_buf[lo : lo + span]
        value = value_buf[lo : lo + span]
        raw = dot_nt(key, queries)
        prob_grad = dot_nt(value, grads)
        cells = span // len(flags_of)
        probs = []
        for row, row_far in enumerate(flags_of):
            bias = group_bias((row_far, col == 2), sizes)
            shift = lse if bias is None else lse - bias
            probs.append(jnp.exp2(raw[row * cells : (row + 1) * cells] * SCALE_LOG2 - shift))
        probs = jnp.concatenate(probs, axis=0)
        dscore = (probs * (prob_grad - delta)).astype(BF16)
        dv = dot_nn(probs.astype(BF16), grads)
        dk = dot_nn(dscore, queries) * SCALE
        results.append((dk, dv))
        part = dot_nn(key.T, dscore)
        dq = part if dq is None else dq + part
    return results, dq


def backward_kernel(cols, grid_rows, sizes, cells, last, *refs):
    tile_count = grid_rows * len(cols)
    qg_refs = refs[:4]
    kv_refs = refs[4 : 4 + tile_count]
    rest = refs[4 + tile_count :]
    if last:
        lse_ref, delta_ref, share_ref, dq_ref = rest[:4]
        o_refs = rest[4:8]
        dq_outs, out_ref = rest[8:12], rest[12]
        col_refs = rest[13 : 13 + len(cols)]
        key_buf, value_buf = rest[13 + len(cols) :]
        lse, delta = lse_ref[...], delta_ref[...]
        for head in range(HEADS):
            cut = head_slice(head)
            out = None
            for d in range(4):
                weight = share_ref[:, 4 * head + d : 4 * head + d + 1]
                piece = o_refs[d][:, cut].astype(F32) * weight
                out = piece if out is None else out + piece
            out_ref[:, cut] = out.astype(BF16)
    else:
        stat_refs = rest[:4]
        lse_ref, delta_ref, share_ref, dq_ref = rest[4:8]
        col_refs = rest[8 : 8 + len(cols)]
        key_buf, value_buf = rest[8 + len(cols) :]
        stats = [merged_stats(*stat_refs, half, cells) for half in range(2)]
        lse = jnp.concatenate([stats[0][0], stats[1][0]], axis=1)
        delta = jnp.concatenate([stats[0][1], stats[1][1]], axis=1)
        lse_ref[...] = lse
        delta_ref[...] = delta
        shares = stats[0][2]
        rows = [shares[d][head : head + 1] for head in range(HEADS) for d in range(4)]
        wide = jnp.concatenate(rows + [jnp.zeros((DH - len(rows), 2 * cells), F32)], axis=0)
        share_ref[...] = wide.T[:cells]

    span = grid_rows * cells
    for i, ref in enumerate(kv_refs):
        key_buf[i * cells : (i + 1) * cells] = ref[0]
        value_buf[i * cells : (i + 1) * cells] = ref[1]
    row_flags = [row == 2 for row in range(grid_rows)]
    for head in range(HEADS):
        cut = head_slice(head)
        queries = jnp.concatenate([ref[0, :, cut] for ref in qg_refs], axis=0)
        grads = jnp.concatenate([ref[1, :, cut] for ref in qg_refs], axis=0)
        results, dq = gradient_blocks(
            cols, row_flags, sizes, key_buf.at[:, cut], value_buf.at[:, cut], queries, grads,
            lse[head : head + 1], delta[head : head + 1], span,
        )
        for (dk, dv), ref in zip(results, col_refs):
            for row in range(grid_rows):
                at = slice(row * cells, (row + 1) * cells)
                ref[row, 0, :, cut] = dk[at].astype(BF16)
                ref[row, 1, :, cut] = dv[at].astype(BF16)
        if last:
            dq = ((dq + dq_ref[head]) * SCALE).T.astype(BF16)
            for i, ref in enumerate(dq_outs):
                ref[:, cut] = dq[i * cells : (i + 1) * cells]
        else:
            dq_ref[head] = dq


def finish_query_kernel(*refs):
    dq_refs = refs[:4]
    rope_ref, dq_out = refs[4:]
    for head in range(HEADS):
        cut = head_slice(head)
        dq = functools.reduce(jnp.add, [ref[:, cut].astype(F32) for ref in dq_refs])
        dq_out[:, cut] = turn(dq, rope_ref[0], rope_ref[1], rope_ref[2], -1.0).astype(BF16)


def finish_key_kernel(cols, rows, *refs):
    col_refs, row_refs = refs[:cols], refs[cols : cols + rows]
    rope_ref, dk_out, dv_out = refs[cols + rows :]
    for head in range(HEADS):
        cut = head_slice(head)
        sums = []
        for which in range(2):
            terms = [ref[0, which, :, cut].astype(F32) for ref in col_refs]
            terms += [ref[which, :, cut].astype(F32) for ref in row_refs]
            sums.append(functools.reduce(jnp.add, terms))
        dk_out[:, cut] = turn(
            sums[0], rope_ref[0], rope_ref[1], rope_ref[2], -1.0
        ).astype(BF16)
        dv_out[:, cut] = sums[1].astype(BF16)


def call(kernel, out_shape, args, flops=0, exps=0, scratch=(), space=pltpu.VMEM, limit=VMEM_LIMIT):
    shapes = jax.tree.leaves(out_shape)
    flops *= 8
    moved = sum(math.prod(x.shape) * x.dtype.itemsize for x in list(args) + shapes)
    return pl.pallas_call(
        kernel,
        out_shape=out_shape,
        in_specs=[pl.BlockSpec(memory_space=space)] * len(args),
        scratch_shapes=list(scratch),
        compiler_params=pltpu.CompilerParams(vmem_limit_bytes=limit),
        cost_estimate=pl.CostEstimate(flops=flops, bytes_accessed=moved, transcendentals=exps),
    )(*args)


def shards(query_in, key_in, value_in, cotangent):
    frames, rows, cols, chan = query_in.shape
    cells = frames * rows * cols
    sizes = {axis: lax.axis_size(axis) for axis in ("ta", "ha", "wa")}
    assert rows == TILE_H and cols == TILE_W and chan == HEADS * DH
    assert TILE_T % frames == 0 and frames * sizes["ta"] <= 2 * TILE_T
    assert sizes["ta"] == 4 and sizes["ha"] % 2 == 0 and sizes["wa"] % 2 == 0
    dims = (frames, rows, cols)
    table, begins = rope_table(frames * sizes["ta"], rows * sizes["ha"], cols * sizes["wa"])
    flat = [x.reshape(cells, chan) for x in (query_in, key_in, value_in, cotangent)]
    pair = jax.ShapeDtypeStruct((2, cells, chan), BF16)
    plain = jax.ShapeDtypeStruct((cells, chan), BF16)

    def real(*shape):
        return jax.ShapeDtypeStruct(shape, F32)

    with jax.named_scope("rotate"):
        kv, qg, rope = call(
            functools.partial(rotate_kernel, dims, begins),
            (pair, pair, real(3, cells, DH)),
            [pltpu.with_memory_space_constraint(x, pltpu.HBM) for x in (*flat, jnp.asarray(table))],
            scratch=[pltpu.VMEM((cells, chan), BF16)] * 2
            + [pltpu.VMEM(table.shape, F32), pltpu.SemaphoreType.DMA((5,))],
            space=pltpu.HBM,
        )

    def other_frames(x, distance):
        return lax.ppermute(x, "ta", [(i, i ^ distance) for i in range(sizes["ta"])])

    row_sides = side_pairs(sizes["ha"])
    col_sides = side_pairs(sizes["wa"])
    with jax.named_scope("halo"):
        kv_rows = [kv] + [lax.ppermute(kv, "ha", pairs) for pairs in row_sides]
        qg2 = other_frames(qg, 2)
        qg1 = other_frames(qg, 1)
        tiles = []
        for block in kv_rows:
            tiles.append([block] + [lax.ppermute(block, "wa", pairs) for pairs in col_sides])
        qg3 = other_frames(qg2, 1)
    grid_rows, grid_cols = 1 + len(row_sides), 1 + len(col_sides)
    flat_tiles = [tiles[row][col] for row in range(grid_rows) for col in range(grid_cols)]
    groups = {}
    for row in range(grid_rows):
        for col in range(grid_cols):
            groups.setdefault((row == 2, col == 2), []).append(row * grid_cols + col)
    groups = list(groups.items())

    key_count = len(flat_tiles) * cells
    product = 2 * 2 * cells * key_count * DH * HEADS

    def forward(qa, qb, first):
        args = (qa, qb, *flat_tiles) + (() if first is None else (first,))
        stat = (8, 2 * cells) if first is None else (2, 8, 2 * cells)
        return call(
            functools.partial(forward_kernel, groups, sizes, cells, first is not None),
            (plain, plain, real(*stat)),
            args,
            2 * product,
            2 * cells * key_count * HEADS,
            [pltpu.VMEM((key_count, chan), BF16)] * 2,
        )

    with jax.named_scope("attend"):
        o0, o1, first = forward(qg, qg1, None)
        o2, o3, stat = forward(qg2, qg3, first)
    with jax.named_scope("merge"):
        stats = [stat] + [other_frames(stat, d) for d in (1, 2, 3)]
        outs = [o0] + [other_frames(o, d) for d, o in ((1, o1), (2, o2), (3, o3))]

    queries = (qg, qg1, qg2, qg3)
    col_shape = jax.ShapeDtypeStruct((grid_rows, 2, cells, chan), BF16)

    def gradients(which, last, extra_out, extra_in):
        count = len(which)
        return call(
            functools.partial(backward_kernel, which, grid_rows, sizes, cells, last),
            (*extra_out, *[col_shape] * count),
            (*queries, *[tiles[row][col] for col in which for row in range(grid_rows)], *extra_in),
            10 * product * count // grid_cols,
            4 * cells * key_count * HEADS * count // grid_cols,
            [pltpu.VMEM((count * grid_rows * cells, chan), BF16)] * 2,
        )

    with jax.named_scope("gradients"):
        lse, delta, shares, dq, *sides = gradients(
            tuple(range(1, grid_cols)),
            False,
            (
                real(HEADS, 4 * cells),
                real(HEADS, 4 * cells),
                real(cells, DH),
                real(HEADS, DH, 4 * cells),
            ),
            stats,
        )
        sides = [lax.ppermute(x, "wa", pairs) for x, pairs in zip(sides, col_sides)]
        d0, d1, d2, d3, attended, own = gradients(
            (0,), True, [plain] * 5, (lse, delta, shares, dq, *outs)
        )
    with jax.named_scope("return"):
        col_parts = [own, *sides]
        dqs = [d0] + [other_frames(x, d) for d, x in ((1, d1), (2, d2), (3, d3))]
        row_parts = []
        for row, pairs in enumerate(row_sides, start=1):
            partial_sum = sum(x[row].astype(F32) for x in col_parts).astype(BF16)
            row_parts.append(lax.ppermute(partial_sum, "ha", pairs))

    with jax.named_scope("finish"):
        grad_query = call(finish_query_kernel, plain, (*dqs, rope))
        grad_key, grad_value = call(
            functools.partial(finish_key_kernel, grid_cols, len(row_parts)),
            (plain, plain),
            (*col_parts, *row_parts, rope),
        )
    return tuple(x.reshape(query_in.shape) for x in (attended, grad_query, grad_key, grad_value))


def solution(mesh):
    spec = P("ta", "ha", "wa", None)
    return jax.shard_map(
        shards, mesh=mesh, in_specs=(spec,) * 4, out_specs=(spec,) * 4, check_vma=False
    )
```

```python
import functools
import math

import jax
import jax.numpy as jnp
import numpy as np
from jax import lax
from jax.experimental import pallas as pl
from jax.experimental.pallas import tpu as pltpu
from jax.sharding import PartitionSpec as P

DH = 128
HEADS = 2
TILE_T = 6
TILE_H = 8
TILE_W = 8

NEGATIVE = -1e30
SCALE = DH**-0.5
SCALE_LOG2 = SCALE * math.log2(math.e)
F32 = jnp.float32
BF16 = jnp.bfloat16
VMEM_LIMIT = 48 * 1024 * 1024


def near_pairs(count):
    return [(i, i ^ 1) for i in range(count)]


def far_pairs(count):
    pairs = []
    for i in range(count):
        j = i + 1 if i % 2 else i - 1
        pairs.append((i, j if 0 <= j < count else i))
    return pairs


def far_exists(axis, count):
    pos = lax.axis_index(axis)
    other = jnp.where(pos % 2 == 1, pos + 1, pos - 1)
    return (other >= 0) & (other < count)


def side_pairs(count):
    sides = []
    if count > 1:
        sides.append(near_pairs(count))
    if count > 2:
        sides.append(far_pairs(count))
    return sides


def rope_table(frame_total, row_total, col_total):
    time_dims = DH // 8
    space_dims = (DH - time_dims) // 2
    slower = 256.0 ** (-np.arange(0, time_dims, 2) / time_dims)
    faster = 256.0 ** (-np.arange(0, space_dims, 2) / space_dims)
    starts = (0, time_dims, time_dims + space_dims)
    pieces = []
    for total, rates, start in zip(
        (frame_total, row_total, col_total), (slower, faster, faster), starts
    ):
        padded = -(-total // 8) * 8
        piece = np.zeros((3, padded, DH), np.float32)
        angles = np.arange(padded)[:, None] * rates[None, :]
        stop = start + 2 * len(rates)
        piece[0, :, start:stop:2] = np.cos(angles)
        piece[0, :, start + 1 : stop : 2] = np.cos(angles)
        piece[1, :, start:stop:2] = -np.sin(angles)
        piece[2, :, start + 1 : stop : 2] = np.sin(angles)
        pieces.append(piece)
    begins = np.cumsum([0] + [piece.shape[1] for piece in pieces])
    return np.concatenate(pieces, axis=1), tuple(int(x) for x in begins[:3])


def local_table(plane, table_ref, begins, frames, rows, cols):
    frame_lo = begins[0] + lax.axis_index("ta") * frames
    row_lo = pl.multiple_of(begins[1] + lax.axis_index("ha") * rows, 8)
    col_lo = pl.multiple_of(begins[2] + lax.axis_index("wa") * cols, 8)
    row_part = table_ref[plane, pl.ds(row_lo, rows), :]
    col_part = table_ref[plane, pl.ds(col_lo, cols), :]
    grids = []
    for i in range(frames):
        lead = row_part + table_ref[plane, pl.ds(frame_lo + i, 1), :]
        grid = lead[:, None, :] + col_part[None, :, :]
        grids.append(grid.reshape(rows * cols, DH))
    return jnp.concatenate(grids, axis=0)


def turn(x, cosine, sin_even, sin_odd, sign):
    follow = pltpu.roll(x, DH - 1, 1)
    lead = pltpu.roll(x, 1, 1)
    return x * cosine + sign * (follow * sin_even + lead * sin_odd)


def head_slice(head):
    return slice(head * DH, (head + 1) * DH)


def rotate_kernel(
    dims, begins, q_hbm, k_hbm, v_hbm, g_hbm, table_hbm, kv_ref, qg_ref, rope_ref, q_ref, k_ref,
    table_ref, sems,
):
    moves = [
        (table_hbm, table_ref),
        (k_hbm, k_ref),
        (q_hbm, q_ref),
        (v_hbm, kv_ref.at[1]),
        (g_hbm, qg_ref.at[1]),
    ]
    copies = [pltpu.make_async_copy(*move, sems.at[i]) for i, move in enumerate(moves)]
    for copy in copies:
        copy.start()
    copies[0].wait()
    tables = [local_table(plane, table_ref, begins, *dims) for plane in range(3)]
    for plane in range(3):
        rope_ref[plane] = tables[plane]
    for copy, source, target in ((copies[1], k_ref, kv_ref), (copies[2], q_ref, qg_ref)):
        copy.wait()
        for head in range(HEADS):
            cut = head_slice(head)
            target[0, :, cut] = turn(source[:, cut].astype(F32), *tables, 1.0).astype(BF16)
    copies[3].wait()
    copies[4].wait()


def dot_nt(a, b):
    return lax.dot_general(a, b, (((1,), (1,)), ((), ())), preferred_element_type=F32)


def dot_nn(a, b):
    return lax.dot_general(a, b, (((1,), (0,)), ((), ())), preferred_element_type=F32)


def dot_tn(a, b):
    return lax.dot_general(a, b, (((0,), (0,)), ((), ())), preferred_element_type=F32)


def group_bias(flags, sizes):
    valid = None
    for axis, is_far in zip(("ha", "wa"), flags):
        if is_far:
            here = far_exists(axis, sizes[axis])
            valid = here if valid is None else valid & here
    return None if valid is None else jnp.where(valid, 0.0, NEGATIVE).astype(F32)


def frame_block(ref, distance):
    return ref.at[lax.axis_index("ta") ^ distance]


def forward_kernel(groups, sizes, cells, qg_ref, *refs):
    tile_count = sum(len(members) for _, members in groups)
    kv_refs = refs[:tile_count]
    o_refs = refs[tile_count : tile_count + 4]
    stat_ref, key_buf, value_buf = refs[tile_count + 4 :]
    at = 0
    spans = []
    for flags, members in groups:
        begin = at
        for member in members:
            key_buf[at : at + cells] = kv_refs[member][0]
            value_buf[at : at + cells] = kv_refs[member][1]
            at += cells
        spans.append((begin, at, group_bias(flags, sizes)))
    lane = lax.broadcasted_iota(jnp.int32, (2 * cells, DH), 1)
    for half in range(2):
        blocks = [frame_block(qg_ref, 2 * half + i) for i in range(2)]
        stat = jnp.zeros((2 * cells, DH), F32)
        for head in range(HEADS):
            cut = head_slice(head)
            query = jnp.concatenate([block[0, :, cut] for block in blocks], axis=0)
            grad = jnp.concatenate([block[1, :, cut] for block in blocks], axis=0)
            scores = [dot_nt(query, key_buf[lo:hi, cut]) for lo, hi, _ in spans]
            best = None
            for raw, (_, _, bias) in zip(scores, spans):
                top = jnp.max(raw, axis=1, keepdims=True) * SCALE_LOG2
                if bias is not None:
                    top = top + bias
                best = top if best is None else jnp.maximum(best, top)
            total = None
            out = None
            for raw, (lo, hi, bias) in zip(scores, spans):
                shift = best if bias is None else best - bias
                weights = jnp.exp2(raw * SCALE_LOG2 - shift)
                part = jnp.sum(weights, axis=1, keepdims=True)
                piece = dot_nn(weights.astype(BF16), value_buf[lo:hi, cut])
                total = part if total is None else total + part
                out = piece if out is None else out + piece
            out = out * (1.0 / total)
            dotted = jnp.sum(out * grad.astype(F32), axis=1, keepdims=True)
            out = out.astype(BF16)
            o_refs[2 * half][:, cut] = out[:cells]
            o_refs[2 * half + 1][:, cut] = out[cells:]
            stat = jnp.where(lane == head, best + jnp.log2(total), stat)
            stat = jnp.where(lane == HEADS + head, dotted, stat)
        stat_ref[half] = stat.T[: stat_ref.shape[1]]


def merged_stats(stat_ref, half, cells):
    parts = [
        frame_block(stat_ref, 0)[half],
        pltpu.roll(frame_block(stat_ref, 1)[half], cells, 1),
        frame_block(stat_ref, 2)[1 - half],
        pltpu.roll(frame_block(stat_ref, 3)[1 - half], cells, 1),
    ]
    top = functools.reduce(jnp.maximum, parts)
    shares = [jnp.exp2(part - top) for part in parts]
    total = functools.reduce(jnp.add, shares)
    lse = top + jnp.log2(total)
    shares = [share / total for share in shares]
    delta = functools.reduce(
        jnp.add,
        [share[:HEADS] * part[HEADS : 2 * HEADS] for share, part in zip(shares, parts)],
    )
    return lse[:HEADS], delta, shares


def gradient_blocks(cols, flags_of, sizes, key_buf, value_buf, queries, grads, lse, delta, span):
    dq = None
    results = []
    for slot, col in enumerate(cols):
        lo = slot * span
        key = key_buf[lo : lo + span]
        value = value_buf[lo : lo + span]
        raw = dot_nt(key, queries)
        prob_grad = dot_nt(value, grads)
        cells = span // len(flags_of)
        probs = []
        for row, row_far in enumerate(flags_of):
            bias = group_bias((row_far, col == 2), sizes)
            shift = lse if bias is None else lse - bias
            probs.append(jnp.exp2(raw[row * cells : (row + 1) * cells] * SCALE_LOG2 - shift))
        probs = jnp.concatenate(probs, axis=0)
        dscore = (probs * (prob_grad - delta)).astype(BF16)
        dv = dot_nn(probs.astype(BF16), grads)
        dk = dot_nn(dscore, queries) * SCALE
        results.append((dk, dv))
        part = dot_nn(key.T, dscore)
        dq = part if dq is None else dq + part
    return results, dq


def backward_kernel(cols, grid_rows, sizes, cells, last, qg_ref, *refs):
    tile_count = grid_rows * len(cols)
    kv_refs = refs[:tile_count]
    rest = refs[tile_count:]
    if last:
        lse_ref, delta_ref, share_ref, dq_ref = rest[:4]
        o_refs = rest[4:8]
        dq_outs, out_ref = rest[8:12], rest[12]
        col_refs = rest[13 : 13 + len(cols)]
        key_buf, value_buf = rest[13 + len(cols) :]
        lse, delta = lse_ref[...], delta_ref[...]
        for head in range(HEADS):
            cut = head_slice(head)
            out = None
            for d in range(4):
                weight = share_ref[:, 4 * head + d : 4 * head + d + 1]
                piece = o_refs[d][:, cut].astype(F32) * weight
                out = piece if out is None else out + piece
            out_ref[:, cut] = out.astype(BF16)
    else:
        stat_ref, lse_ref, delta_ref, share_ref, dq_ref = rest[:5]
        col_refs = rest[5 : 5 + len(cols)]
        key_buf, value_buf = rest[5 + len(cols) :]
        stats = [merged_stats(stat_ref, half, cells) for half in range(2)]
        lse = jnp.concatenate([stats[0][0], stats[1][0]], axis=1)
        delta = jnp.concatenate([stats[0][1], stats[1][1]], axis=1)
        lse_ref[...] = lse
        delta_ref[...] = delta
        shares = stats[0][2]
        rows = [shares[d][head : head + 1] for head in range(HEADS) for d in range(4)]
        wide = jnp.concatenate(rows + [jnp.zeros((DH - len(rows), 2 * cells), F32)], axis=0)
        share_ref[...] = wide.T[:cells]

    span = grid_rows * cells
    for i, ref in enumerate(kv_refs):
        key_buf[i * cells : (i + 1) * cells] = ref[0]
        value_buf[i * cells : (i + 1) * cells] = ref[1]
    row_flags = [row == 2 for row in range(grid_rows)]
    for head in range(HEADS):
        cut = head_slice(head)
        blocks = [frame_block(qg_ref, d) for d in range(4)]
        queries = jnp.concatenate([block[0, :, cut] for block in blocks], axis=0)
        grads = jnp.concatenate([block[1, :, cut] for block in blocks], axis=0)
        results, dq = gradient_blocks(
            cols, row_flags, sizes, key_buf.at[:, cut], value_buf.at[:, cut], queries, grads,
            lse[head : head + 1], delta[head : head + 1], span,
        )
        for (dk, dv), ref in zip(results, col_refs):
            for row in range(grid_rows):
                at = slice(row * cells, (row + 1) * cells)
                ref[row, 0, :, cut] = dk[at].astype(BF16)
                ref[row, 1, :, cut] = dv[at].astype(BF16)
        if last:
            dq = ((dq + dq_ref[head]) * SCALE).T.astype(BF16)
            for i, ref in enumerate(dq_outs):
                ref[:, cut] = dq[i * cells : (i + 1) * cells]
        else:
            dq_ref[head] = dq


def finish_query_kernel(*refs):
    dq_refs = refs[:4]
    rope_ref, dq_out = refs[4:]
    for head in range(HEADS):
        cut = head_slice(head)
        dq = functools.reduce(jnp.add, [ref[:, cut].astype(F32) for ref in dq_refs])
        dq_out[:, cut] = turn(dq, rope_ref[0], rope_ref[1], rope_ref[2], -1.0).astype(BF16)


def finish_key_kernel(cols, rows, *refs):
    col_refs, row_refs = refs[:cols], refs[cols : cols + rows]
    rope_ref, dk_out, dv_out = refs[cols + rows :]
    for head in range(HEADS):
        cut = head_slice(head)
        sums = []
        for which in range(2):
            terms = [ref[0, which, :, cut].astype(F32) for ref in col_refs]
            terms += [ref[which, :, cut].astype(F32) for ref in row_refs]
            sums.append(functools.reduce(jnp.add, terms))
        dk_out[:, cut] = turn(
            sums[0], rope_ref[0], rope_ref[1], rope_ref[2], -1.0
        ).astype(BF16)
        dv_out[:, cut] = sums[1].astype(BF16)


def call(kernel, out_shape, args, flops=0, exps=0, scratch=(), space=pltpu.VMEM, limit=VMEM_LIMIT):
    shapes = jax.tree.leaves(out_shape)
    flops *= 8
    moved = sum(math.prod(x.shape) * x.dtype.itemsize for x in list(args) + shapes)
    return pl.pallas_call(
        kernel,
        out_shape=out_shape,
        in_specs=[pl.BlockSpec(memory_space=space)] * len(args),
        scratch_shapes=list(scratch),
        compiler_params=pltpu.CompilerParams(vmem_limit_bytes=limit),
        cost_estimate=pl.CostEstimate(flops=flops, bytes_accessed=moved, transcendentals=exps),
    )(*args)


def shards(query_in, key_in, value_in, cotangent):
    frames, rows, cols, chan = query_in.shape
    cells = frames * rows * cols
    sizes = {axis: lax.axis_size(axis) for axis in ("ta", "ha", "wa")}
    assert rows == TILE_H and cols == TILE_W and chan == HEADS * DH
    assert TILE_T % frames == 0 and frames * sizes["ta"] <= 2 * TILE_T
    assert sizes["ta"] == 4 and sizes["ha"] % 2 == 0 and sizes["wa"] % 2 == 0
    dims = (frames, rows, cols)
    table, begins = rope_table(frames * sizes["ta"], rows * sizes["ha"], cols * sizes["wa"])
    flat = [x.reshape(cells, chan) for x in (query_in, key_in, value_in, cotangent)]
    pair = jax.ShapeDtypeStruct((2, cells, chan), BF16)
    plain = jax.ShapeDtypeStruct((cells, chan), BF16)

    def real(*shape):
        return jax.ShapeDtypeStruct(shape, F32)

    with jax.named_scope("rotate"):
        kv, qg, rope = call(
            functools.partial(rotate_kernel, dims, begins),
            (pair, pair, real(3, cells, DH)),
            [pltpu.with_memory_space_constraint(x, pltpu.HBM) for x in (*flat, jnp.asarray(table))],
            scratch=[pltpu.VMEM((cells, chan), BF16)] * 2
            + [pltpu.VMEM(table.shape, F32), pltpu.SemaphoreType.DMA((5,))],
            space=pltpu.HBM,
        )

    def other_frames(x, distance):
        return lax.ppermute(x, "ta", [(i, i ^ distance) for i in range(sizes["ta"])])

    row_sides = side_pairs(sizes["ha"])
    col_sides = side_pairs(sizes["wa"])
    with jax.named_scope("halo"):
        kv_rows = [kv] + [lax.ppermute(kv, "ha", pairs) for pairs in row_sides]
        gathered = lax.all_gather(qg, "ta")
        tiles = []
        for block in kv_rows:
            tiles.append([block] + [lax.ppermute(block, "wa", pairs) for pairs in col_sides])
    grid_rows, grid_cols = 1 + len(row_sides), 1 + len(col_sides)
    flat_tiles = [tiles[row][col] for row in range(grid_rows) for col in range(grid_cols)]
    groups = {}
    for row in range(grid_rows):
        for col in range(grid_cols):
            groups.setdefault((row == 2, col == 2), []).append(row * grid_cols + col)
    groups = list(groups.items())

    key_count = len(flat_tiles) * cells
    product = 2 * 4 * cells * key_count * DH * HEADS

    with jax.named_scope("attend"):
        *parts, stat = call(
            functools.partial(forward_kernel, groups, sizes, cells),
            (*[plain] * 4, real(2, 8, 2 * cells)),
            (gathered, *flat_tiles),
            2 * product,
            4 * cells * key_count * HEADS,
            [pltpu.VMEM((key_count, chan), BF16)] * 2,
        )
    with jax.named_scope("merge"):
        stats = lax.all_gather(stat, "ta")
        outs = [parts[0]] + [other_frames(parts[d], d) for d in (1, 2, 3)]

    col_shape = jax.ShapeDtypeStruct((grid_rows, 2, cells, chan), BF16)

    def gradients(which, last, extra_out, extra_in):
        count = len(which)
        return call(
            functools.partial(backward_kernel, which, grid_rows, sizes, cells, last),
            (*extra_out, *[col_shape] * count),
            (gathered, *[tiles[row][col] for col in which for row in range(grid_rows)], *extra_in),
            5 * product * count // grid_cols,
            4 * cells * key_count * HEADS * count // grid_cols,
            [pltpu.VMEM((count * grid_rows * cells, chan), BF16)] * 2,
        )

    with jax.named_scope("gradients"):
        lse, delta, shares, dq, *sides = gradients(
            tuple(range(1, grid_cols)),
            False,
            (
                real(HEADS, 4 * cells),
                real(HEADS, 4 * cells),
                real(cells, DH),
                real(HEADS, DH, 4 * cells),
            ),
            (stats,),
        )
        sides = [lax.ppermute(x, "wa", pairs) for x, pairs in zip(sides, col_sides)]
        d0, d1, d2, d3, attended, own = gradients(
            (0,), True, [plain] * 5, (lse, delta, shares, dq, *outs)
        )
    with jax.named_scope("return"):
        col_parts = [own, *sides]
        dqs = [d0] + [other_frames(x, d) for d, x in ((1, d1), (2, d2), (3, d3))]
        row_parts = []
        for row, pairs in enumerate(row_sides, start=1):
            partial_sum = sum(x[row].astype(F32) for x in col_parts).astype(BF16)
            row_parts.append(lax.ppermute(partial_sum, "ha", pairs))

    with jax.named_scope("finish"):
        grad_query = call(finish_query_kernel, plain, (*dqs, rope), 5 * product)
        grad_key, grad_value = call(
            functools.partial(finish_key_kernel, grid_cols, len(row_parts)),
            (plain, plain),
            (*col_parts, *row_parts, rope),
        )
    return tuple(x.reshape(query_in.shape) for x in (attended, grad_query, grad_key, grad_value))


def solution(mesh):
    spec = P("ta", "ha", "wa", None)
    return jax.shard_map(
        shards, mesh=mesh, in_specs=(spec,) * 4, out_specs=(spec,) * 4, check_vma=False
    )
```

```python
import functools
import math

import jax
import jax.numpy as jnp
import numpy as np
from jax import lax
from jax.experimental import pallas as pl
from jax.experimental.pallas import tpu as pltpu
from jax.sharding import PartitionSpec as P

DH = 128
HEADS = 2
TILE_T = 6
TILE_H = 8
TILE_W = 8

NEGATIVE = -1e30
SCALE = DH**-0.5
SCALE_LOG2 = SCALE * math.log2(math.e)
F32 = jnp.float32
BF16 = jnp.bfloat16
VMEM_LIMIT = 48 * 1024 * 1024


def near_pairs(count):
    return [(i, i ^ 1) for i in range(count)]


def far_pairs(count):
    pairs = []
    for i in range(count):
        j = i + 1 if i % 2 else i - 1
        pairs.append((i, j if 0 <= j < count else i))
    return pairs


def far_exists(axis, count):
    pos = lax.axis_index(axis)
    other = jnp.where(pos % 2 == 1, pos + 1, pos - 1)
    return (other >= 0) & (other < count)


def side_pairs(count):
    sides = []
    if count > 1:
        sides.append(near_pairs(count))
    if count > 2:
        sides.append(far_pairs(count))
    return sides


def rope_table(frame_total, row_total, col_total):
    time_dims = DH // 8
    space_dims = (DH - time_dims) // 2
    slower = 256.0 ** (-np.arange(0, time_dims, 2) / time_dims)
    faster = 256.0 ** (-np.arange(0, space_dims, 2) / space_dims)
    starts = (0, time_dims, time_dims + space_dims)
    pieces = []
    for total, rates, start in zip(
        (frame_total, row_total, col_total), (slower, faster, faster), starts
    ):
        padded = -(-total // 8) * 8
        piece = np.zeros((3, padded, DH), np.float32)
        angles = np.arange(padded)[:, None] * rates[None, :]
        stop = start + 2 * len(rates)
        piece[0, :, start:stop:2] = np.cos(angles)
        piece[0, :, start + 1 : stop : 2] = np.cos(angles)
        piece[1, :, start:stop:2] = -np.sin(angles)
        piece[2, :, start + 1 : stop : 2] = np.sin(angles)
        pieces.append(piece)
    begins = np.cumsum([0] + [piece.shape[1] for piece in pieces])
    return np.concatenate(pieces, axis=1), tuple(int(x) for x in begins[:3])


def local_table(plane, table_ref, begins, frames, rows, cols):
    frame_lo = begins[0] + lax.axis_index("ta") * frames
    row_lo = pl.multiple_of(begins[1] + lax.axis_index("ha") * rows, 8)
    col_lo = pl.multiple_of(begins[2] + lax.axis_index("wa") * cols, 8)
    row_part = table_ref[plane, pl.ds(row_lo, rows), :]
    col_part = table_ref[plane, pl.ds(col_lo, cols), :]
    grids = []
    for i in range(frames):
        lead = row_part + table_ref[plane, pl.ds(frame_lo + i, 1), :]
        grid = lead[:, None, :] + col_part[None, :, :]
        grids.append(grid.reshape(rows * cols, DH))
    return jnp.concatenate(grids, axis=0)


def turn(x, cosine, sin_even, sin_odd, sign):
    follow = pltpu.roll(x, DH - 1, 1)
    lead = pltpu.roll(x, 1, 1)
    return x * cosine + sign * (follow * sin_even + lead * sin_odd)


def head_slice(head):
    return slice(head * DH, (head + 1) * DH)


def rotate_kernel(
    dims, begins, q_hbm, k_hbm, v_hbm, g_hbm, table_hbm, kv_ref, qg_ref, rope_ref, q_ref, k_ref,
    table_ref, sems,
):
    moves = [
        (table_hbm, table_ref),
        (k_hbm, k_ref),
        (q_hbm, q_ref),
        (v_hbm, kv_ref.at[1]),
        (g_hbm, qg_ref.at[1]),
    ]
    copies = [pltpu.make_async_copy(*move, sems.at[i]) for i, move in enumerate(moves)]
    for copy in copies:
        copy.start()
    copies[0].wait()
    tables = [local_table(plane, table_ref, begins, *dims) for plane in range(3)]
    for plane in range(3):
        rope_ref[plane] = tables[plane]
    for copy, source, target in ((copies[1], k_ref, kv_ref), (copies[2], q_ref, qg_ref)):
        copy.wait()
        for head in range(HEADS):
            cut = head_slice(head)
            target[0, :, cut] = turn(source[:, cut].astype(F32), *tables, 1.0).astype(BF16)
    copies[3].wait()
    copies[4].wait()


def dot_nt(a, b):
    return lax.dot_general(a, b, (((1,), (1,)), ((), ())), preferred_element_type=F32)


def dot_nn(a, b):
    return lax.dot_general(a, b, (((1,), (0,)), ((), ())), preferred_element_type=F32)


def dot_tn(a, b):
    return lax.dot_general(a, b, (((0,), (0,)), ((), ())), preferred_element_type=F32)


def group_bias(flags, sizes):
    valid = None
    for axis, is_far in zip(("ha", "wa"), flags):
        if is_far:
            here = far_exists(axis, sizes[axis])
            valid = here if valid is None else valid & here
    return None if valid is None else jnp.where(valid, 0.0, NEGATIVE).astype(F32)


def forward_kernel(groups, sizes, cells, with_first, *refs):
    tile_count = sum(len(members) for _, members in groups)
    qa_ref, qb_ref = refs[0], refs[1]
    kv_refs = refs[2 : 2 + tile_count]
    rest = refs[2 + tile_count :]
    if with_first:
        first_ref, oa_ref, ob_ref, stat_ref, key_buf, value_buf = rest
    else:
        oa_ref, ob_ref, stat_ref, key_buf, value_buf = rest
    at = 0
    spans = []
    for flags, members in groups:
        begin = at
        for member in members:
            key_buf[at : at + cells] = kv_refs[member][0]
            value_buf[at : at + cells] = kv_refs[member][1]
            at += cells
        spans.append((begin, at, group_bias(flags, sizes)))
    lane = lax.broadcasted_iota(jnp.int32, (2 * cells, DH), 1)
    stat = jnp.zeros((2 * cells, DH), F32)
    for head in range(HEADS):
        cut = head_slice(head)
        query = jnp.concatenate([qa_ref[0, :, cut], qb_ref[0, :, cut]], axis=0)
        grad = jnp.concatenate([qa_ref[1, :, cut], qb_ref[1, :, cut]], axis=0)
        scores = [dot_nt(query, key_buf[lo:hi, cut]) for lo, hi, _ in spans]
        best = None
        for raw, (_, _, bias) in zip(scores, spans):
            top = jnp.max(raw, axis=1, keepdims=True) * SCALE_LOG2
            if bias is not None:
                top = top + bias
            best = top if best is None else jnp.maximum(best, top)
        total = None
        out = None
        for raw, (lo, hi, bias) in zip(scores, spans):
            shift = best if bias is None else best - bias
            weights = jnp.exp2(raw * SCALE_LOG2 - shift)
            part = jnp.sum(weights, axis=1, keepdims=True)
            piece = dot_nn(weights.astype(BF16), value_buf[lo:hi, cut])
            total = part if total is None else total + part
            out = piece if out is None else out + piece
        out = out * (1.0 / total)
        dotted = jnp.sum(out * grad.astype(F32), axis=1, keepdims=True)
        out = out.astype(BF16)
        oa_ref[:, cut] = out[:cells]
        ob_ref[:, cut] = out[cells:]
        stat = jnp.where(lane == head, best + jnp.log2(total), stat)
        stat = jnp.where(lane == HEADS + head, dotted, stat)
    flipped = stat.T[: stat_ref.shape[-2]]
    if with_first:
        stat_ref[0] = first_ref[...]
        stat_ref[1] = flipped
    else:
        stat_ref[...] = flipped


def merged_stats(own_ref, s1_ref, s2_ref, s3_ref, half, cells):
    parts = [
        own_ref[half],
        pltpu.roll(s1_ref[half], cells, 1),
        s2_ref[1 - half],
        pltpu.roll(s3_ref[1 - half], cells, 1),
    ]
    top = functools.reduce(jnp.maximum, parts)
    shares = [jnp.exp2(part - top) for part in parts]
    total = functools.reduce(jnp.add, shares)
    lse = top + jnp.log2(total)
    shares = [share / total for share in shares]
    delta = functools.reduce(
        jnp.add,
        [share[:HEADS] * part[HEADS : 2 * HEADS] for share, part in zip(shares, parts)],
    )
    return lse[:HEADS], delta, shares


def gradient_blocks(cols, flags_of, sizes, key_buf, value_buf, queries, grads, lse, delta, span):
    dq = None
    results = []
    for slot, col in enumerate(cols):
        lo = slot * span
        key = key_buf[lo : lo + span]
        value = value_buf[lo : lo + span]
        raw = dot_nt(key, queries)
        prob_grad = dot_nt(value, grads)
        cells = span // len(flags_of)
        probs = []
        for row, row_far in enumerate(flags_of):
            bias = group_bias((row_far, col == 2), sizes)
            shift = lse if bias is None else lse - bias
            probs.append(jnp.exp2(raw[row * cells : (row + 1) * cells] * SCALE_LOG2 - shift))
        probs = jnp.concatenate(probs, axis=0)
        dscore = (probs * (prob_grad - delta)).astype(BF16)
        dv = dot_nn(probs.astype(BF16), grads)
        dk = dot_nn(dscore, queries) * SCALE
        results.append((dk, dv))
        part = dot_nn(key.T, dscore)
        dq = part if dq is None else dq + part
    return results, dq


def backward_kernel(cols, grid_rows, sizes, cells, last, *refs):
    tile_count = grid_rows * len(cols)
    qg_refs = refs[:4]
    kv_refs = refs[4 : 4 + tile_count]
    rest = refs[4 + tile_count :]
    if last:
        lse_ref, delta_ref, share_ref, dq_ref = rest[:4]
        o_refs = rest[4:8]
        dq_outs, out_ref = rest[8:12], rest[12]
        col_refs = rest[13 : 13 + len(cols)]
        key_buf, value_buf = rest[13 + len(cols) :]
        lse, delta = lse_ref[...], delta_ref[...]
        for head in range(HEADS):
            cut = head_slice(head)
            out = None
            for d, o_ref in zip((0, 3, 2, 1), o_refs):
                weight = share_ref[:, 4 * head + d : 4 * head + d + 1]
                piece = o_ref[:, cut].astype(F32) * weight
                out = piece if out is None else out + piece
            out_ref[:, cut] = out.astype(BF16)
    else:
        stat_refs = rest[:4]
        lse_ref, delta_ref, share_ref, dq_ref = rest[4:8]
        col_refs = rest[8 : 8 + len(cols)]
        key_buf, value_buf = rest[8 + len(cols) :]
        stats = [merged_stats(*stat_refs, half, cells) for half in range(2)]
        lse = jnp.concatenate([stats[0][0], stats[1][0]], axis=1)
        delta = jnp.concatenate([stats[0][1], stats[1][1]], axis=1)
        lse_ref[...] = lse
        delta_ref[...] = delta
        shares = stats[0][2]
        rows = [shares[d][head : head + 1] for head in range(HEADS) for d in range(4)]
        wide = jnp.concatenate(rows + [jnp.zeros((DH - len(rows), 2 * cells), F32)], axis=0)
        share_ref[...] = wide.T[:cells]

    span = grid_rows * cells
    for i, ref in enumerate(kv_refs):
        key_buf[i * cells : (i + 1) * cells] = ref[0]
        value_buf[i * cells : (i + 1) * cells] = ref[1]
    row_flags = [row == 2 for row in range(grid_rows)]
    for head in range(HEADS):
        cut = head_slice(head)
        queries = jnp.concatenate([ref[0, :, cut] for ref in qg_refs], axis=0)
        grads = jnp.concatenate([ref[1, :, cut] for ref in qg_refs], axis=0)
        results, dq = gradient_blocks(
            cols, row_flags, sizes, key_buf.at[:, cut], value_buf.at[:, cut], queries, grads,
            lse[head : head + 1], delta[head : head + 1], span,
        )
        for (dk, dv), ref in zip(results, col_refs):
            for row in range(grid_rows):
                at = slice(row * cells, (row + 1) * cells)
                ref[row, 0, :, cut] = dk[at].astype(BF16)
                ref[row, 1, :, cut] = dv[at].astype(BF16)
        if last:
            dq = ((dq + dq_ref[head]) * SCALE).T.astype(BF16)
            for i, ref in enumerate(dq_outs):
                ref[:, cut] = dq[i * cells : (i + 1) * cells]
        else:
            dq_ref[head] = dq


def finish_query_kernel(*refs):
    dq_refs = refs[:4]
    rope_ref, dq_out = refs[4:]
    for head in range(HEADS):
        cut = head_slice(head)
        dq = functools.reduce(jnp.add, [ref[:, cut].astype(F32) for ref in dq_refs])
        dq_out[:, cut] = turn(dq, rope_ref[0], rope_ref[1], rope_ref[2], -1.0).astype(BF16)


def finish_key_kernel(cols, rows, *refs):
    col_refs, row_refs = refs[:cols], refs[cols : cols + rows]
    rope_ref, dk_out, dv_out = refs[cols + rows :]
    for head in range(HEADS):
        cut = head_slice(head)
        sums = []
        for which in range(2):
            terms = [ref[0, which, :, cut].astype(F32) for ref in col_refs]
            terms += [ref[which, :, cut].astype(F32) for ref in row_refs]
            sums.append(functools.reduce(jnp.add, terms))
        dk_out[:, cut] = turn(
            sums[0], rope_ref[0], rope_ref[1], rope_ref[2], -1.0
        ).astype(BF16)
        dv_out[:, cut] = sums[1].astype(BF16)


def call(kernel, out_shape, args, flops=0, exps=0, scratch=(), space=pltpu.VMEM, limit=VMEM_LIMIT):
    shapes = jax.tree.leaves(out_shape)
    flops *= 8
    moved = sum(math.prod(x.shape) * x.dtype.itemsize for x in list(args) + shapes)
    return pl.pallas_call(
        kernel,
        out_shape=out_shape,
        in_specs=[pl.BlockSpec(memory_space=space)] * len(args),
        scratch_shapes=list(scratch),
        compiler_params=pltpu.CompilerParams(vmem_limit_bytes=limit),
        cost_estimate=pl.CostEstimate(flops=flops, bytes_accessed=moved, transcendentals=exps),
    )(*args)


def shards(query_in, key_in, value_in, cotangent):
    frames, rows, cols, chan = query_in.shape
    cells = frames * rows * cols
    sizes = {axis: lax.axis_size(axis) for axis in ("ta", "ha", "wa")}
    assert rows == TILE_H and cols == TILE_W and chan == HEADS * DH
    assert TILE_T % frames == 0 and frames * sizes["ta"] <= 2 * TILE_T
    assert sizes["ta"] == 4 and sizes["ha"] % 2 == 0 and sizes["wa"] % 2 == 0
    dims = (frames, rows, cols)
    table, begins = rope_table(frames * sizes["ta"], rows * sizes["ha"], cols * sizes["wa"])
    flat = [x.reshape(cells, chan) for x in (query_in, key_in, value_in, cotangent)]
    pair = jax.ShapeDtypeStruct((2, cells, chan), BF16)
    plain = jax.ShapeDtypeStruct((cells, chan), BF16)

    def real(*shape):
        return jax.ShapeDtypeStruct(shape, F32)

    with jax.named_scope("rotate"):
        kv, qg, rope = call(
            functools.partial(rotate_kernel, dims, begins),
            (pair, pair, real(3, cells, DH)),
            [pltpu.with_memory_space_constraint(x, pltpu.HBM) for x in (*flat, jnp.asarray(table))],
            scratch=[pltpu.VMEM((cells, chan), BF16)] * 2
            + [pltpu.VMEM(table.shape, F32), pltpu.SemaphoreType.DMA((5,))],
            space=pltpu.HBM,
        )

    def other_frames(x, distance):
        return lax.ppermute(x, "ta", [(i, i ^ distance) for i in range(sizes["ta"])])

    row_sides = side_pairs(sizes["ha"])
    col_sides = side_pairs(sizes["wa"])
    with jax.named_scope("halo"):
        kv_rows = [kv] + [lax.ppermute(kv, "ha", pairs) for pairs in row_sides]
        qg2 = other_frames(qg, 2)
        qg1 = other_frames(qg, 1)
        tiles = []
        for block in kv_rows:
            tiles.append([block] + [lax.ppermute(block, "wa", pairs) for pairs in col_sides])
        qg3 = other_frames(qg2, 1)
    grid_rows, grid_cols = 1 + len(row_sides), 1 + len(col_sides)
    flat_tiles = [tiles[row][col] for row in range(grid_rows) for col in range(grid_cols)]
    groups = {}
    for row in range(grid_rows):
        for col in range(grid_cols):
            groups.setdefault((row == 2, col == 2), []).append(row * grid_cols + col)
    groups = list(groups.items())

    key_count = len(flat_tiles) * cells
    product = 2 * 2 * cells * key_count * DH * HEADS

    def forward(qa, qb, first):
        args = (qa, qb, *flat_tiles) + (() if first is None else (first,))
        stat = (8, 2 * cells) if first is None else (2, 8, 2 * cells)
        return call(
            functools.partial(forward_kernel, groups, sizes, cells, first is not None),
            (plain, plain, real(*stat)),
            args,
            2 * product,
            2 * cells * key_count * HEADS,
            [pltpu.VMEM((key_count, chan), BF16)] * 2,
        )

    with jax.named_scope("attend"):
        o0, o1, first = forward(qg, qg1, None)
        o2, o3, stat = forward(qg2, qg3, first)
    with jax.named_scope("merge"):
        stats = [stat] + [other_frames(stat, d) for d in (1, 2, 3)]
        outs = [o0] + [other_frames(o, d) for d, o in ((3, o3), (2, o2), (1, o1))]

    queries = (qg, qg1, qg2, qg3)
    col_shape = jax.ShapeDtypeStruct((grid_rows, 2, cells, chan), BF16)

    def gradients(which, last, extra_out, extra_in):
        count = len(which)
        return call(
            functools.partial(backward_kernel, which, grid_rows, sizes, cells, last),
            (*extra_out, *[col_shape] * count),
            (*queries, *[tiles[row][col] for col in which for row in range(grid_rows)], *extra_in),
            10 * product * count // grid_cols,
            4 * cells * key_count * HEADS * count // grid_cols,
            [pltpu.VMEM((count * grid_rows * cells, chan), BF16)] * 2,
        )

    with jax.named_scope("gradients"):
        lse, delta, shares, dq, *sides = gradients(
            tuple(range(1, grid_cols)),
            False,
            (
                real(HEADS, 4 * cells),
                real(HEADS, 4 * cells),
                real(cells, DH),
                real(HEADS, DH, 4 * cells),
            ),
            stats,
        )
        sides = [lax.ppermute(x, "wa", pairs) for x, pairs in zip(sides, col_sides)]
        d0, d1, d2, d3, attended, own = gradients(
            (0,), True, [plain] * 5, (lse, delta, shares, dq, *outs)
        )
    with jax.named_scope("return"):
        col_parts = [own, *sides]
        dqs = [d0] + [other_frames(x, d) for d, x in ((3, d3), (2, d2), (1, d1))]
        row_parts = []
        for row, pairs in enumerate(row_sides, start=1):
            partial_sum = sum(x[row].astype(F32) for x in col_parts).astype(BF16)
            row_parts.append(lax.ppermute(partial_sum, "ha", pairs))

    with jax.named_scope("finish"):
        grad_query = call(finish_query_kernel, plain, (*dqs, rope), 5 * product)
        grad_key, grad_value = call(
            functools.partial(finish_key_kernel, grid_cols, len(row_parts)),
            (plain, plain),
            (*col_parts, *row_parts, rope),
        )
    return tuple(x.reshape(query_in.shape) for x in (attended, grad_query, grad_key, grad_value))


def solution(mesh):
    spec = P("ta", "ha", "wa", None)
    return jax.shard_map(
        shards, mesh=mesh, in_specs=(spec,) * 4, out_specs=(spec,) * 4, check_vma=False
    )
```

```python
import functools
import math

import jax
import jax.numpy as jnp
import numpy as np
from jax import lax
from jax.experimental import pallas as pl
from jax.experimental.pallas import tpu as pltpu
from jax.sharding import PartitionSpec as P

DH = 128
HEADS = 2
TILE_T = 6
TILE_H = 8
TILE_W = 8

NEGATIVE = -1e30
SCALE = DH**-0.5
SCALE_LOG2 = SCALE * math.log2(math.e)
F32 = jnp.float32
BF16 = jnp.bfloat16
VMEM_LIMIT = 48 * 1024 * 1024


def near_pairs(count):
    return [(i, i ^ 1) for i in range(count)]


def far_pairs(count):
    pairs = []
    for i in range(count):
        j = i + 1 if i % 2 else i - 1
        pairs.append((i, j if 0 <= j < count else i))
    return pairs


def far_exists(axis, count):
    pos = lax.axis_index(axis)
    other = jnp.where(pos % 2 == 1, pos + 1, pos - 1)
    return (other >= 0) & (other < count)


def side_pairs(count):
    sides = []
    if count > 1:
        sides.append(near_pairs(count))
    if count > 2:
        sides.append(far_pairs(count))
    return sides


def rope_table(frame_total, row_total, col_total):
    time_dims = DH // 8
    space_dims = (DH - time_dims) // 2
    slower = 256.0 ** (-np.arange(0, time_dims, 2) / time_dims)
    faster = 256.0 ** (-np.arange(0, space_dims, 2) / space_dims)
    starts = (0, time_dims, time_dims + space_dims)
    pieces = []
    for total, rates, start in zip(
        (frame_total, row_total, col_total), (slower, faster, faster), starts
    ):
        padded = -(-total // 8) * 8
        piece = np.zeros((3, padded, DH), np.float32)
        angles = np.arange(padded)[:, None] * rates[None, :]
        stop = start + 2 * len(rates)
        piece[0, :, start:stop:2] = np.cos(angles)
        piece[0, :, start + 1 : stop : 2] = np.cos(angles)
        piece[1, :, start:stop:2] = -np.sin(angles)
        piece[2, :, start + 1 : stop : 2] = np.sin(angles)
        pieces.append(piece)
    begins = np.cumsum([0] + [piece.shape[1] for piece in pieces])
    return np.concatenate(pieces, axis=1), tuple(int(x) for x in begins[:3])


def local_table(plane, table_ref, begins, frames, rows, cols):
    frame_lo = begins[0] + lax.axis_index("ta") * frames
    row_lo = pl.multiple_of(begins[1] + lax.axis_index("ha") * rows, 8)
    col_lo = pl.multiple_of(begins[2] + lax.axis_index("wa") * cols, 8)
    row_part = table_ref[plane, pl.ds(row_lo, rows), :]
    col_part = table_ref[plane, pl.ds(col_lo, cols), :]
    grids = []
    for i in range(frames):
        lead = row_part + table_ref[plane, pl.ds(frame_lo + i, 1), :]
        grid = lead[:, None, :] + col_part[None, :, :]
        grids.append(grid.reshape(rows * cols, DH))
    return jnp.concatenate(grids, axis=0)


def turn(x, cosine, sin_even, sin_odd, sign):
    follow = pltpu.roll(x, DH - 1, 1)
    lead = pltpu.roll(x, 1, 1)
    return x * cosine + sign * (follow * sin_even + lead * sin_odd)


def head_slice(head):
    return slice(head * DH, (head + 1) * DH)


def rotate_kernel(
    dims, begins, q_hbm, k_hbm, v_hbm, g_hbm, table_hbm, kv_ref, qg_ref, rope_ref, q_ref, k_ref,
    table_ref, sems,
):
    moves = [
        (table_hbm, table_ref),
        (k_hbm, k_ref),
        (q_hbm, q_ref),
        (v_hbm, kv_ref.at[1]),
        (g_hbm, qg_ref.at[1]),
    ]
    copies = [pltpu.make_async_copy(*move, sems.at[i]) for i, move in enumerate(moves)]
    for copy in copies:
        copy.start()
    copies[0].wait()
    tables = [local_table(plane, table_ref, begins, *dims) for plane in range(3)]
    for plane in range(3):
        rope_ref[plane] = tables[plane]
    for copy, source, target in ((copies[1], k_ref, kv_ref), (copies[2], q_ref, qg_ref)):
        copy.wait()
        for head in range(HEADS):
            cut = head_slice(head)
            target[0, :, cut] = turn(source[:, cut].astype(F32), *tables, 1.0).astype(BF16)
    copies[3].wait()
    copies[4].wait()


def dot_nt(a, b):
    return lax.dot_general(a, b, (((1,), (1,)), ((), ())), preferred_element_type=F32)


def dot_nn(a, b):
    return lax.dot_general(a, b, (((1,), (0,)), ((), ())), preferred_element_type=F32)


def dot_tn(a, b):
    return lax.dot_general(a, b, (((0,), (0,)), ((), ())), preferred_element_type=F32)


def group_bias(flags, sizes):
    valid = None
    for axis, is_far in zip(("ha", "wa"), flags):
        if is_far:
            here = far_exists(axis, sizes[axis])
            valid = here if valid is None else valid & here
    return None if valid is None else jnp.where(valid, 0.0, NEGATIVE).astype(F32)


def forward_kernel(groups, sizes, cells, count, last, *refs):
    tile_count = sum(len(members) for _, members in groups)
    qg_refs = refs[:count]
    kv_refs = refs[count : count + tile_count]
    rest = refs[count + tile_count :]
    if last:
        first_ref, rest = rest[0], rest[1:]
    o_refs = rest[:count]
    stat_ref, key_buf, value_buf = rest[count:]
    at = 0
    spans = []
    for flags, members in groups:
        begin = at
        for member in members:
            key_buf[at : at + cells] = kv_refs[member][0]
            value_buf[at : at + cells] = kv_refs[member][1]
            at += cells
        spans.append((begin, at, group_bias(flags, sizes)))
    lane = lax.broadcasted_iota(jnp.int32, (cells, DH), 1)
    stats = []
    for qg_ref, o_ref in zip(qg_refs, o_refs):
        stat = jnp.zeros((cells, DH), F32)
        for head in range(HEADS):
            cut = head_slice(head)
            scores = [dot_nt(qg_ref[0, :, cut], key_buf[lo:hi, cut]) for lo, hi, _ in spans]
            best = None
            for raw, (_, _, bias) in zip(scores, spans):
                top = jnp.max(raw, axis=1, keepdims=True) * SCALE_LOG2
                if bias is not None:
                    top = top + bias
                best = top if best is None else jnp.maximum(best, top)
            total = None
            out = None
            for raw, (lo, hi, bias) in zip(scores, spans):
                shift = best if bias is None else best - bias
                weights = jnp.exp2(raw * SCALE_LOG2 - shift)
                part = jnp.sum(weights, axis=1, keepdims=True)
                piece = dot_nn(weights.astype(BF16), value_buf[lo:hi, cut])
                total = part if total is None else total + part
                out = piece if out is None else out + piece
            out = out * (1.0 / total)
            dotted = jnp.sum(out * qg_ref[1, :, cut].astype(F32), axis=1, keepdims=True)
            o_ref[:, cut] = out.astype(BF16)
            stat = jnp.where(lane == head, best + jnp.log2(total), stat)
            stat = jnp.where(lane == HEADS + head, dotted, stat)
        stats.append(stat)
    if last:
        whole = jnp.concatenate([first_ref[...]] + stats, axis=0)
        stat_ref[...] = whole.T[: stat_ref.shape[0]]
    else:
        for i, stat in enumerate(stats):
            stat_ref[i * cells : (i + 1) * cells] = stat


def seen_from(stat, distance, cells):
    if distance & 2:
        stat = pltpu.roll(stat, 2 * cells, 1)
    if distance & 1:
        lane = lax.broadcasted_iota(jnp.int32, stat.shape, 1)
        even = (lane < cells) | ((lane >= 2 * cells) & (lane < 3 * cells))
        stat = jnp.where(even, pltpu.roll(stat, 3 * cells, 1), pltpu.roll(stat, cells, 1))
    return stat


def merged_stats(stat_refs, cells):
    parts = [seen_from(ref[...], distance, cells) for distance, ref in enumerate(stat_refs)]
    top = functools.reduce(jnp.maximum, parts)
    shares = [jnp.exp2(part - top) for part in parts]
    total = functools.reduce(jnp.add, shares)
    lse = top + jnp.log2(total)
    shares = [share / total for share in shares]
    delta = functools.reduce(
        jnp.add,
        [share[:HEADS] * part[HEADS : 2 * HEADS] for share, part in zip(shares, parts)],
    )
    return lse[:HEADS], delta, shares


def gradient_blocks(cols, flags_of, sizes, key_buf, value_buf, queries, grads, lse, delta, span):
    dq = None
    results = []
    for slot, col in enumerate(cols):
        lo = slot * span
        key = key_buf[lo : lo + span]
        value = value_buf[lo : lo + span]
        raw = dot_nt(key, queries)
        prob_grad = dot_nt(value, grads)
        cells = span // len(flags_of)
        probs = []
        for row, row_far in enumerate(flags_of):
            bias = group_bias((row_far, col == 2), sizes)
            shift = lse if bias is None else lse - bias
            probs.append(jnp.exp2(raw[row * cells : (row + 1) * cells] * SCALE_LOG2 - shift))
        probs = jnp.concatenate(probs, axis=0)
        dscore = (probs * (prob_grad - delta)).astype(BF16)
        dv = dot_nn(probs.astype(BF16), grads)
        dk = dot_nn(dscore, queries) * SCALE
        results.append((dk, dv))
        part = dot_nn(key.T, dscore)
        dq = part if dq is None else dq + part
    return results, dq


def backward_kernel(cols, grid_rows, sizes, cells, first, last, *refs):
    tile_count = grid_rows * len(cols)
    qg_refs = refs[:4]
    kv_refs = refs[4 : 4 + tile_count]
    rest = refs[4 + tile_count :]
    if first:
        stat_refs, rest = rest[:4], rest[4:]
    else:
        (lse_ref, delta_ref, dq_ref), rest = rest[:3], rest[3:]
    if last:
        dq_outs, rest = rest[:4], rest[4:]
    else:
        dq_out, rest = rest[0], rest[1:]
    if first:
        (lse_ref, delta_ref, share_ref), rest = rest[:3], rest[3:]
        lse, delta, shares = merged_stats(stat_refs, cells)
        lse_ref[...] = lse
        delta_ref[...] = delta
        rows = [shares[d][head : head + 1, : 2 * cells] for head in range(HEADS) for d in range(4)]
        wide = jnp.concatenate(rows + [jnp.zeros((DH - len(rows), 2 * cells), F32)], axis=0)
        share_ref[...] = wide.T[:cells]
    else:
        lse, delta = lse_ref[...], delta_ref[...]
    col_refs = rest[: len(cols)]
    key_buf, value_buf = rest[len(cols) :]

    span = grid_rows * cells
    for i, ref in enumerate(kv_refs):
        key_buf[i * cells : (i + 1) * cells] = ref[0]
        value_buf[i * cells : (i + 1) * cells] = ref[1]
    row_flags = [row == 2 for row in range(grid_rows)]
    for head in range(HEADS):
        cut = head_slice(head)
        queries = jnp.concatenate([ref[0, :, cut] for ref in qg_refs], axis=0)
        grads = jnp.concatenate([ref[1, :, cut] for ref in qg_refs], axis=0)
        results, dq = gradient_blocks(
            cols, row_flags, sizes, key_buf.at[:, cut], value_buf.at[:, cut], queries, grads,
            lse[head : head + 1], delta[head : head + 1], span,
        )
        for (dk, dv), ref in zip(results, col_refs):
            for row in range(grid_rows):
                at = slice(row * cells, (row + 1) * cells)
                ref[row, 0, :, cut] = dk[at].astype(BF16)
                ref[row, 1, :, cut] = dv[at].astype(BF16)
        if not first:
            dq = dq + dq_ref[head]
        if last:
            dq = (dq * SCALE).T.astype(BF16)
            for i, ref in enumerate(dq_outs):
                ref[:, cut] = dq[i * cells : (i + 1) * cells]
        else:
            dq_out[head] = dq


def finish_query_kernel(*refs):
    o_refs, dq_refs = refs[:4], refs[4:8]
    share_ref, rope_ref, out_ref, dq_out = refs[8:]
    for head in range(HEADS):
        cut = head_slice(head)
        outs = []
        for d, o_ref in zip((0, 3, 2, 1), o_refs):
            weight = share_ref[:, 4 * head + d : 4 * head + d + 1]
            outs.append(o_ref[:, cut].astype(F32) * weight)
        out_ref[:, cut] = functools.reduce(jnp.add, outs).astype(BF16)
        dq = functools.reduce(jnp.add, [ref[:, cut].astype(F32) for ref in dq_refs])
        dq_out[:, cut] = turn(dq, rope_ref[0], rope_ref[1], rope_ref[2], -1.0).astype(BF16)


def finish_key_kernel(cols, rows, *refs):
    col_refs, row_refs = refs[:cols], refs[cols : cols + rows]
    rope_ref, dk_out, dv_out = refs[cols + rows :]
    for head in range(HEADS):
        cut = head_slice(head)
        sums = []
        for which in range(2):
            terms = [ref[0, which, :, cut].astype(F32) for ref in col_refs]
            terms += [ref[which, :, cut].astype(F32) for ref in row_refs]
            sums.append(functools.reduce(jnp.add, terms))
        dk_out[:, cut] = turn(
            sums[0], rope_ref[0], rope_ref[1], rope_ref[2], -1.0
        ).astype(BF16)
        dv_out[:, cut] = sums[1].astype(BF16)


def call(kernel, out_shape, args, flops=0, exps=0, scratch=(), space=pltpu.VMEM, limit=VMEM_LIMIT):
    shapes = jax.tree.leaves(out_shape)
    flops *= 8
    moved = sum(math.prod(x.shape) * x.dtype.itemsize for x in list(args) + shapes)
    return pl.pallas_call(
        kernel,
        out_shape=out_shape,
        in_specs=[pl.BlockSpec(memory_space=space)] * len(args),
        scratch_shapes=list(scratch),
        compiler_params=pltpu.CompilerParams(vmem_limit_bytes=limit),
        cost_estimate=pl.CostEstimate(flops=flops, bytes_accessed=moved, transcendentals=exps),
    )(*args)


def shards(query_in, key_in, value_in, cotangent):
    frames, rows, cols, chan = query_in.shape
    cells = frames * rows * cols
    sizes = {axis: lax.axis_size(axis) for axis in ("ta", "ha", "wa")}
    assert rows == TILE_H and cols == TILE_W and chan == HEADS * DH
    assert TILE_T % frames == 0 and frames * sizes["ta"] <= 2 * TILE_T
    assert sizes["ta"] == 4 and sizes["ha"] % 2 == 0 and sizes["wa"] % 2 == 0
    dims = (frames, rows, cols)
    table, begins = rope_table(frames * sizes["ta"], rows * sizes["ha"], cols * sizes["wa"])
    flat = [x.reshape(cells, chan) for x in (query_in, key_in, value_in, cotangent)]
    pair = jax.ShapeDtypeStruct((2, cells, chan), BF16)
    plain = jax.ShapeDtypeStruct((cells, chan), BF16)

    def real(*shape):
        return jax.ShapeDtypeStruct(shape, F32)

    with jax.named_scope("rotate"):
        kv, qg, rope = call(
            functools.partial(rotate_kernel, dims, begins),
            (pair, pair, real(3, cells, DH)),
            [pltpu.with_memory_space_constraint(x, pltpu.HBM) for x in (*flat, jnp.asarray(table))],
            scratch=[pltpu.VMEM((cells, chan), BF16)] * 2
            + [pltpu.VMEM(table.shape, F32), pltpu.SemaphoreType.DMA((5,))],
            space=pltpu.HBM,
        )

    def other_frames(x, distance):
        return lax.ppermute(x, "ta", [(i, i ^ distance) for i in range(sizes["ta"])])

    row_sides = side_pairs(sizes["ha"])
    col_sides = side_pairs(sizes["wa"])
    with jax.named_scope("halo"):
        kv_rows = [kv] + [lax.ppermute(kv, "ha", pairs) for pairs in row_sides]
        qg2 = other_frames(qg, 2)
        qg1 = other_frames(qg, 1)
        tiles = []
        for block in kv_rows:
            tiles.append([block] + [lax.ppermute(block, "wa", pairs) for pairs in col_sides])
        qg3 = other_frames(qg2, 1)
    grid_rows, grid_cols = 1 + len(row_sides), 1 + len(col_sides)
    flat_tiles = [tiles[row][col] for row in range(grid_rows) for col in range(grid_cols)]
    groups = {}
    for row in range(grid_rows):
        for col in range(grid_cols):
            groups.setdefault((row == 2, col == 2), []).append(row * grid_cols + col)
    groups = list(groups.items())

    key_count = len(flat_tiles) * cells
    product = 2 * cells * key_count * DH * HEADS

    def forward(blocks, first):
        count = len(blocks)
        stat = (count * cells, DH) if first is None else (8, 4 * cells)
        return call(
            functools.partial(forward_kernel, groups, sizes, cells, count, first is not None),
            (*[plain] * count, real(*stat)),
            (*blocks, *flat_tiles) + (() if first is None else (first,)),
            2 * product * count,
            cells * key_count * HEADS * count,
            [pltpu.VMEM((key_count, chan), BF16)] * 2,
        )

    with jax.named_scope("attend"):
        o0, o1, o2, first = forward((qg, qg1, qg2), None)
        o3, stat = forward((qg3,), first)
    with jax.named_scope("merge"):
        stats = [stat] + [other_frames(stat, d) for d in (1, 2, 3)]
        outs = [other_frames(o, d) for d, o in ((3, o3), (2, o2), (1, o1))]

    queries = (qg, qg1, qg2, qg3)
    col_shape = jax.ShapeDtypeStruct((grid_rows, 2, cells, chan), BF16)

    def gradients(which, carried):
        count = len(which)
        first, last = which[-1] == grid_cols - 1, which[0] == 0
        stat_outs = [real(HEADS, 4 * cells), real(HEADS, 4 * cells), real(cells, DH)]
        return call(
            functools.partial(backward_kernel, which, grid_rows, sizes, cells, first, last),
            (
                *([plain] * 4 if last else [real(HEADS, DH, 4 * cells)]),
                *(stat_outs if first else []),
                *[col_shape] * count,
            ),
            (*queries, *[tiles[row][col] for col in which for row in range(grid_rows)], *carried),
            20 * product * count // grid_cols,
            4 * cells * key_count * HEADS * count // grid_cols,
            [pltpu.VMEM((count * grid_rows * cells, chan), BF16)] * 2,
        )

    with jax.named_scope("gradients"):
        dq, lse, delta, shares, *sides = gradients(tuple(range(1, grid_cols)), stats)
        sides = [lax.ppermute(x, "wa", pairs) for x, pairs in zip(sides, col_sides)]
        d0, d1, d2, d3, own = gradients((0,), (lse, delta, dq))
    with jax.named_scope("return"):
        (d1, d2, d3), outs = lax.optimization_barrier(((d1, d2, d3), outs))
        col_parts = [own, *sides]
        dqs = [d0] + [other_frames(x, d) for d, x in ((3, d3), (2, d2), (1, d1))]
        row_parts = []
        for row, pairs in enumerate(row_sides, start=1):
            partial_sum = sum(x[row].astype(F32) for x in col_parts).astype(BF16)
            row_parts.append(lax.ppermute(partial_sum, "ha", pairs))

    with jax.named_scope("finish"):
        attended, grad_query = call(
            finish_query_kernel, (plain, plain), (o0, *outs, *dqs, shares, rope), 10 * product
        )
        grad_key, grad_value = call(
            functools.partial(finish_key_kernel, grid_cols, len(row_parts)),
            (plain, plain),
            (*col_parts, *row_parts, rope),
        )
    return tuple(x.reshape(query_in.shape) for x in (attended, grad_query, grad_key, grad_value))


def solution(mesh):
    spec = P("ta", "ha", "wa", None)
    return jax.shard_map(
        shards, mesh=mesh, in_specs=(spec,) * 4, out_specs=(spec,) * 4, check_vma=False
    )
```

```python
import functools
import math

import jax
import jax.numpy as jnp
import numpy as np
from jax import lax
from jax.experimental import pallas as pl
from jax.experimental.pallas import tpu as pltpu
from jax.sharding import PartitionSpec as P

DH = 128
HEADS = 2
TILE_T = 6
TILE_H = 8
TILE_W = 8

NEGATIVE = -1e30
SCALE = DH**-0.5
SCALE_LOG2 = SCALE * math.log2(math.e)
F32 = jnp.float32
BF16 = jnp.bfloat16
VMEM_LIMIT = 48 * 1024 * 1024


def near_pairs(count):
    return [(i, i ^ 1) for i in range(count)]


def far_pairs(count):
    pairs = []
    for i in range(count):
        j = i + 1 if i % 2 else i - 1
        pairs.append((i, j if 0 <= j < count else i))
    return pairs


def far_exists(axis, count):
    pos = lax.axis_index(axis)
    other = jnp.where(pos % 2 == 1, pos + 1, pos - 1)
    return (other >= 0) & (other < count)


def side_pairs(count):
    sides = []
    if count > 1:
        sides.append(near_pairs(count))
    if count > 2:
        sides.append(far_pairs(count))
    return sides


def rope_table(frame_total, row_total, col_total):
    time_dims = DH // 8
    space_dims = (DH - time_dims) // 2
    slower = 256.0 ** (-np.arange(0, time_dims, 2) / time_dims)
    faster = 256.0 ** (-np.arange(0, space_dims, 2) / space_dims)
    starts = (0, time_dims, time_dims + space_dims)
    pieces = []
    for total, rates, start in zip(
        (frame_total, row_total, col_total), (slower, faster, faster), starts
    ):
        padded = -(-total // 8) * 8
        piece = np.zeros((3, padded, DH), np.float32)
        angles = np.arange(padded)[:, None] * rates[None, :]
        stop = start + 2 * len(rates)
        piece[0, :, start:stop:2] = np.cos(angles)
        piece[0, :, start + 1 : stop : 2] = np.cos(angles)
        piece[1, :, start:stop:2] = -np.sin(angles)
        piece[2, :, start + 1 : stop : 2] = np.sin(angles)
        pieces.append(piece)
    begins = np.cumsum([0] + [piece.shape[1] for piece in pieces])
    return np.concatenate(pieces, axis=1), tuple(int(x) for x in begins[:3])


def local_table(plane, table_ref, begins, frames, rows, cols):
    frame_lo = begins[0] + lax.axis_index("ta") * frames
    row_lo = pl.multiple_of(begins[1] + lax.axis_index("ha") * rows, 8)
    col_lo = pl.multiple_of(begins[2] + lax.axis_index("wa") * cols, 8)
    row_part = table_ref[plane, pl.ds(row_lo, rows), :]
    col_part = table_ref[plane, pl.ds(col_lo, cols), :]
    grids = []
    for i in range(frames):
        lead = row_part + table_ref[plane, pl.ds(frame_lo + i, 1), :]
        grid = lead[:, None, :] + col_part[None, :, :]
        grids.append(grid.reshape(rows * cols, DH))
    return jnp.concatenate(grids, axis=0)


def turn(x, cosine, sin_even, sin_odd, sign):
    follow = pltpu.roll(x, DH - 1, 1)
    lead = pltpu.roll(x, 1, 1)
    return x * cosine + sign * (follow * sin_even + lead * sin_odd)


def head_slice(head):
    return slice(head * DH, (head + 1) * DH)


def rotate_kernel(
    dims, begins, q_hbm, k_hbm, v_hbm, g_hbm, table_hbm, kv_ref, qg_ref, rope_ref, q_ref, k_ref,
    table_ref, sems,
):
    moves = [
        (table_hbm, table_ref),
        (k_hbm, k_ref),
        (q_hbm, q_ref),
        (v_hbm, kv_ref.at[1]),
        (g_hbm, qg_ref.at[1]),
    ]
    copies = [pltpu.make_async_copy(*move, sems.at[i]) for i, move in enumerate(moves)]
    for copy in copies:
        copy.start()
    copies[0].wait()
    tables = [local_table(plane, table_ref, begins, *dims) for plane in range(3)]
    for plane in range(3):
        rope_ref[plane] = tables[plane]
    for copy, source, target in ((copies[1], k_ref, kv_ref), (copies[2], q_ref, qg_ref)):
        copy.wait()
        for head in range(HEADS):
            cut = head_slice(head)
            target[0, :, cut] = turn(source[:, cut].astype(F32), *tables, 1.0).astype(BF16)
    copies[3].wait()
    copies[4].wait()


def dot_nt(a, b):
    return lax.dot_general(a, b, (((1,), (1,)), ((), ())), preferred_element_type=F32)


def dot_nn(a, b):
    return lax.dot_general(a, b, (((1,), (0,)), ((), ())), preferred_element_type=F32)


def dot_tn(a, b):
    return lax.dot_general(a, b, (((0,), (0,)), ((), ())), preferred_element_type=F32)


def group_bias(flags, sizes):
    valid = None
    for axis, is_far in zip(("ha", "wa"), flags):
        if is_far:
            here = far_exists(axis, sizes[axis])
            valid = here if valid is None else valid & here
    return None if valid is None else jnp.where(valid, 0.0, NEGATIVE).astype(F32)


def forward_kernel(groups, sizes, cells, count, last, *refs):
    tile_count = sum(len(members) for _, members in groups)
    qg_refs = refs[:count]
    kv_refs = refs[count : count + tile_count]
    rest = refs[count + tile_count :]
    if last:
        first_ref, rest = rest[0], rest[1:]
    o_refs = rest[:count]
    stat_ref, key_buf, value_buf = rest[count:]
    at = 0
    spans = []
    for flags, members in groups:
        begin = at
        for member in members:
            key_buf[at : at + cells] = kv_refs[member][0]
            value_buf[at : at + cells] = kv_refs[member][1]
            at += cells
        spans.append((begin, at, group_bias(flags, sizes)))
    lane = lax.broadcasted_iota(jnp.int32, (cells, DH), 1)
    stats = []
    for qg_ref, o_ref in zip(qg_refs, o_refs):
        stat = jnp.zeros((cells, DH), F32)
        for head in range(HEADS):
            cut = head_slice(head)
            scores = [dot_nt(qg_ref[0, :, cut], key_buf[lo:hi, cut]) for lo, hi, _ in spans]
            best = None
            for raw, (_, _, bias) in zip(scores, spans):
                top = jnp.max(raw, axis=1, keepdims=True) * SCALE_LOG2
                if bias is not None:
                    top = top + bias
                best = top if best is None else jnp.maximum(best, top)
            total = None
            out = None
            for raw, (lo, hi, bias) in zip(scores, spans):
                shift = best if bias is None else best - bias
                weights = jnp.exp2(raw * SCALE_LOG2 - shift)
                part = jnp.sum(weights, axis=1, keepdims=True)
                piece = dot_nn(weights.astype(BF16), value_buf[lo:hi, cut])
                total = part if total is None else total + part
                out = piece if out is None else out + piece
            out = out * (1.0 / total)
            dotted = jnp.sum(out * qg_ref[1, :, cut].astype(F32), axis=1, keepdims=True)
            o_ref[:, cut] = out.astype(BF16)
            stat = jnp.where(lane == head, best + jnp.log2(total), stat)
            stat = jnp.where(lane == HEADS + head, dotted, stat)
        stats.append(stat)
    if last:
        whole = jnp.concatenate([first_ref[...]] + stats, axis=0)
        stat_ref[...] = whole.T[: stat_ref.shape[0]]
    else:
        for i, stat in enumerate(stats):
            stat_ref[i * cells : (i + 1) * cells] = stat


def seen_from(stat, distance, cells):
    if distance & 2:
        stat = pltpu.roll(stat, 2 * cells, 1)
    if distance & 1:
        lane = lax.broadcasted_iota(jnp.int32, stat.shape, 1)
        even = (lane < cells) | ((lane >= 2 * cells) & (lane < 3 * cells))
        stat = jnp.where(even, pltpu.roll(stat, 3 * cells, 1), pltpu.roll(stat, cells, 1))
    return stat


def merged_stats(stat_refs, cells):
    parts = [seen_from(ref[...], distance, cells) for distance, ref in enumerate(stat_refs)]
    top = functools.reduce(jnp.maximum, parts)
    shares = [jnp.exp2(part - top) for part in parts]
    total = functools.reduce(jnp.add, shares)
    lse = top + jnp.log2(total)
    shares = [share / total for share in shares]
    delta = functools.reduce(
        jnp.add,
        [share[:HEADS] * part[HEADS : 2 * HEADS] for share, part in zip(shares, parts)],
    )
    return lse[:HEADS], delta, shares


def gradient_blocks(cols, flags_of, sizes, key_buf, value_buf, queries, grads, lse, delta, span):
    dq = None
    results = []
    for slot, col in enumerate(cols):
        lo = slot * span
        key = key_buf[lo : lo + span]
        value = value_buf[lo : lo + span]
        raw = dot_nt(key, queries)
        prob_grad = dot_nt(value, grads)
        cells = span // len(flags_of)
        probs = []
        for row, row_far in enumerate(flags_of):
            bias = group_bias((row_far, col == 2), sizes)
            shift = lse if bias is None else lse - bias
            probs.append(jnp.exp2(raw[row * cells : (row + 1) * cells] * SCALE_LOG2 - shift))
        probs = jnp.concatenate(probs, axis=0)
        dscore = (probs * (prob_grad - delta)).astype(BF16)
        dv = dot_nn(probs.astype(BF16), grads)
        dk = dot_nn(dscore, queries) * SCALE
        results.append((dk, dv))
        part = dot_nn(key.T, dscore)
        dq = part if dq is None else dq + part
    return results, dq


def backward_kernel(cols, grid_rows, sizes, cells, first, last, *refs):
    tile_count = grid_rows * len(cols)
    qg_refs = refs[:4]
    kv_refs = refs[4 : 4 + tile_count]
    rest = refs[4 + tile_count :]
    if first:
        stat_refs, rest = rest[:4], rest[4:]
    else:
        (lse_ref, delta_ref, dq_ref), rest = rest[:3], rest[3:]
    if last:
        dq_outs, rest = rest[:4], rest[4:]
    else:
        dq_out, rest = rest[0], rest[1:]
    if first:
        (lse_ref, delta_ref, share_ref), rest = rest[:3], rest[3:]
        lse, delta, shares = merged_stats(stat_refs, cells)
        lse_ref[...] = lse
        delta_ref[...] = delta
        rows = [shares[d][head : head + 1, : 2 * cells] for head in range(HEADS) for d in range(4)]
        wide = jnp.concatenate(rows + [jnp.zeros((DH - len(rows), 2 * cells), F32)], axis=0)
        share_ref[...] = wide.T[:cells]
    else:
        lse, delta = lse_ref[...], delta_ref[...]
    col_refs = rest[: len(cols)]
    key_buf, value_buf = rest[len(cols) :]

    span = grid_rows * cells
    for i, ref in enumerate(kv_refs):
        key_buf[i * cells : (i + 1) * cells] = ref[0]
        value_buf[i * cells : (i + 1) * cells] = ref[1]
    row_flags = [row == 2 for row in range(grid_rows)]
    for head in range(HEADS):
        cut = head_slice(head)
        queries = jnp.concatenate([ref[0, :, cut] for ref in qg_refs], axis=0)
        grads = jnp.concatenate([ref[1, :, cut] for ref in qg_refs], axis=0)
        results, dq = gradient_blocks(
            cols, row_flags, sizes, key_buf.at[:, cut], value_buf.at[:, cut], queries, grads,
            lse[head : head + 1], delta[head : head + 1], span,
        )
        for (dk, dv), ref in zip(results, col_refs):
            for row in range(grid_rows):
                at = slice(row * cells, (row + 1) * cells)
                ref[row, 0, :, cut] = dk[at].astype(BF16)
                ref[row, 1, :, cut] = dv[at].astype(BF16)
        if not first:
            dq = dq + dq_ref[head]
        if last:
            dq = (dq * SCALE).T.astype(BF16)
            for i, ref in enumerate(dq_outs):
                ref[:, cut] = dq[i * cells : (i + 1) * cells]
        else:
            dq_out[head] = dq


def finish_query_kernel(*refs):
    o_refs, dq_refs = refs[:4], refs[4:8]
    share_ref, rope_ref, out_ref, dq_out = refs[8:]
    for head in range(HEADS):
        cut = head_slice(head)
        outs = []
        for d, o_ref in zip((0, 3, 2, 1), o_refs):
            weight = share_ref[:, 4 * head + d : 4 * head + d + 1]
            outs.append(o_ref[:, cut].astype(F32) * weight)
        out_ref[:, cut] = functools.reduce(jnp.add, outs).astype(BF16)
        dq = functools.reduce(jnp.add, [ref[:, cut].astype(F32) for ref in dq_refs])
        dq_out[:, cut] = turn(dq, rope_ref[0], rope_ref[1], rope_ref[2], -1.0).astype(BF16)


def finish_key_kernel(cols, rows, *refs):
    col_refs, row_refs = refs[:cols], refs[cols : cols + rows]
    rope_ref, dk_out, dv_out = refs[cols + rows :]
    for head in range(HEADS):
        cut = head_slice(head)
        sums = []
        for which in range(2):
            terms = [ref[0, which, :, cut].astype(F32) for ref in col_refs]
            terms += [ref[which, :, cut].astype(F32) for ref in row_refs]
            sums.append(functools.reduce(jnp.add, terms))
        dk_out[:, cut] = turn(
            sums[0], rope_ref[0], rope_ref[1], rope_ref[2], -1.0
        ).astype(BF16)
        dv_out[:, cut] = sums[1].astype(BF16)


def call(kernel, out_shape, args, flops=0, exps=0, scratch=(), space=pltpu.VMEM, limit=VMEM_LIMIT):
    shapes = jax.tree.leaves(out_shape)
    flops *= 8
    moved = sum(math.prod(x.shape) * x.dtype.itemsize for x in list(args) + shapes)
    return pl.pallas_call(
        kernel,
        out_shape=out_shape,
        in_specs=[pl.BlockSpec(memory_space=space)] * len(args),
        scratch_shapes=list(scratch),
        compiler_params=pltpu.CompilerParams(vmem_limit_bytes=limit),
        cost_estimate=pl.CostEstimate(flops=flops, bytes_accessed=moved, transcendentals=exps),
    )(*args)


def shards(query_in, key_in, value_in, cotangent):
    frames, rows, cols, chan = query_in.shape
    cells = frames * rows * cols
    sizes = {axis: lax.axis_size(axis) for axis in ("ta", "ha", "wa")}
    assert rows == TILE_H and cols == TILE_W and chan == HEADS * DH
    assert TILE_T % frames == 0 and frames * sizes["ta"] <= 2 * TILE_T
    assert sizes["ta"] == 4 and sizes["ha"] % 2 == 0 and sizes["wa"] % 2 == 0
    dims = (frames, rows, cols)
    table, begins = rope_table(frames * sizes["ta"], rows * sizes["ha"], cols * sizes["wa"])
    flat = [x.reshape(cells, chan) for x in (query_in, key_in, value_in, cotangent)]
    pair = jax.ShapeDtypeStruct((2, cells, chan), BF16)
    plain = jax.ShapeDtypeStruct((cells, chan), BF16)

    def real(*shape):
        return jax.ShapeDtypeStruct(shape, F32)

    with jax.named_scope("rotate"):
        kv, qg, rope = call(
            functools.partial(rotate_kernel, dims, begins),
            (pair, pair, real(3, cells, DH)),
            [pltpu.with_memory_space_constraint(x, pltpu.HBM) for x in (*flat, jnp.asarray(table))],
            scratch=[pltpu.VMEM((cells, chan), BF16)] * 2
            + [pltpu.VMEM(table.shape, F32), pltpu.SemaphoreType.DMA((5,))],
            space=pltpu.HBM,
        )

    def other_frames(x, distance):
        return lax.ppermute(x, "ta", [(i, i ^ distance) for i in range(sizes["ta"])])

    row_sides = side_pairs(sizes["ha"])
    col_sides = side_pairs(sizes["wa"])
    with jax.named_scope("halo"):
        kv_rows = [kv] + [lax.ppermute(kv, "ha", pairs) for pairs in row_sides]
        qg2 = other_frames(qg, 2)
        qg1 = other_frames(qg, 1)
        tiles = []
        for block in kv_rows:
            tiles.append([block] + [lax.ppermute(block, "wa", pairs) for pairs in col_sides])
        qg3 = other_frames(qg2, 1)
    grid_rows, grid_cols = 1 + len(row_sides), 1 + len(col_sides)
    flat_tiles = [tiles[row][col] for row in range(grid_rows) for col in range(grid_cols)]
    groups = {}
    for row in range(grid_rows):
        for col in range(grid_cols):
            groups.setdefault((row == 2, col == 2), []).append(row * grid_cols + col)
    groups = list(groups.items())

    key_count = len(flat_tiles) * cells
    product = 2 * cells * key_count * DH * HEADS

    def forward(blocks, first):
        count = len(blocks)
        stat = (count * cells, DH) if first is None else (8, 4 * cells)
        return call(
            functools.partial(forward_kernel, groups, sizes, cells, count, first is not None),
            (*[plain] * count, real(*stat)),
            (*blocks, *flat_tiles) + (() if first is None else (first,)),
            2 * product * count,
            cells * key_count * HEADS * count,
            [pltpu.VMEM((key_count, chan), BF16)] * 2,
        )

    with jax.named_scope("attend"):
        o0, o1, o2, first = forward((qg, qg1, qg2), None)
        o3, stat = forward((qg3,), first)
    with jax.named_scope("merge"):
        stats = [stat] + [other_frames(stat, d) for d in (1, 2, 3)]
        outs = [other_frames(o, d) for d, o in ((3, o3), (2, o2), (1, o1))]
        stats, outs[1:] = lax.optimization_barrier((stats, outs[1:]))

    queries = (qg, qg1, qg2, qg3)
    col_shape = jax.ShapeDtypeStruct((grid_rows, 2, cells, chan), BF16)

    def gradients(which, carried):
        count = len(which)
        first, last = which[-1] == grid_cols - 1, which[0] == 0
        stat_outs = [real(HEADS, 4 * cells), real(HEADS, 4 * cells), real(cells, DH)]
        return call(
            functools.partial(backward_kernel, which, grid_rows, sizes, cells, first, last),
            (
                *([plain] * 4 if last else [real(HEADS, DH, 4 * cells)]),
                *(stat_outs if first else []),
                *[col_shape] * count,
            ),
            (*queries, *[tiles[row][col] for col in which for row in range(grid_rows)], *carried),
            20 * product * count // grid_cols,
            4 * cells * key_count * HEADS * count // grid_cols,
            [pltpu.VMEM((count * grid_rows * cells, chan), BF16)] * 2,
        )

    with jax.named_scope("gradients"):
        dq, lse, delta, shares, *sides = gradients(tuple(range(1, grid_cols)), stats)
        sides = [lax.ppermute(x, "wa", pairs) for x, pairs in zip(sides, col_sides)]
        d0, d1, d2, d3, own = gradients((0,), (lse, delta, dq))
    with jax.named_scope("return"):
        (d1, d2, d3), outs = lax.optimization_barrier(((d1, d2, d3), outs))
        col_parts = [own, *sides]
        dqs = [d0] + [other_frames(x, d) for d, x in ((3, d3), (2, d2), (1, d1))]
        row_parts = []
        for row, pairs in enumerate(row_sides, start=1):
            partial_sum = sum(x[row].astype(F32) for x in col_parts).astype(BF16)
            row_parts.append(lax.ppermute(partial_sum, "ha", pairs))

    with jax.named_scope("finish"):
        attended, grad_query = call(
            finish_query_kernel, (plain, plain), (o0, *outs, *dqs, shares, rope), 10 * product
        )
        grad_key, grad_value = call(
            functools.partial(finish_key_kernel, grid_cols, len(row_parts)),
            (plain, plain),
            (*col_parts, *row_parts, rope),
        )
    return tuple(x.reshape(query_in.shape) for x in (attended, grad_query, grad_key, grad_value))


def solution(mesh):
    spec = P("ta", "ha", "wa", None)
    return jax.shard_map(
        shards, mesh=mesh, in_specs=(spec,) * 4, out_specs=(spec,) * 4, check_vma=False
    )
```

```python
import functools
import math

import jax
import jax.numpy as jnp
import numpy as np
from jax import lax
from jax.experimental import pallas as pl
from jax.experimental.pallas import tpu as pltpu
from jax.sharding import PartitionSpec as P

DH = 128
HEADS = 2
TILE_T = 6
TILE_H = 8
TILE_W = 8

NEGATIVE = -1e30
SCALE = DH**-0.5
SCALE_LOG2 = SCALE * math.log2(math.e)
F32 = jnp.float32
BF16 = jnp.bfloat16
VMEM_LIMIT = 48 * 1024 * 1024


def near_pairs(count):
    return [(i, i ^ 1) for i in range(count)]


def far_pairs(count):
    pairs = []
    for i in range(count):
        j = i + 1 if i % 2 else i - 1
        pairs.append((i, j if 0 <= j < count else i))
    return pairs


def far_exists(axis, count):
    pos = lax.axis_index(axis)
    other = jnp.where(pos % 2 == 1, pos + 1, pos - 1)
    return (other >= 0) & (other < count)


def side_pairs(count):
    sides = []
    if count > 1:
        sides.append(near_pairs(count))
    if count > 2:
        sides.append(far_pairs(count))
    return sides


def rope_table(frame_total, row_total, col_total):
    time_dims = DH // 8
    space_dims = (DH - time_dims) // 2
    slower = 256.0 ** (-np.arange(0, time_dims, 2) / time_dims)
    faster = 256.0 ** (-np.arange(0, space_dims, 2) / space_dims)
    starts = (0, time_dims, time_dims + space_dims)
    pieces = []
    for total, rates, start in zip(
        (frame_total, row_total, col_total), (slower, faster, faster), starts
    ):
        padded = -(-total // 8) * 8
        piece = np.zeros((3, padded, DH), np.float32)
        angles = np.arange(padded)[:, None] * rates[None, :]
        stop = start + 2 * len(rates)
        piece[0, :, start:stop:2] = np.cos(angles)
        piece[0, :, start + 1 : stop : 2] = np.cos(angles)
        piece[1, :, start:stop:2] = -np.sin(angles)
        piece[2, :, start + 1 : stop : 2] = np.sin(angles)
        pieces.append(piece)
    begins = np.cumsum([0] + [piece.shape[1] for piece in pieces])
    return np.concatenate(pieces, axis=1), tuple(int(x) for x in begins[:3])


def local_table(plane, table_ref, begins, frames, rows, cols):
    frame_lo = begins[0] + lax.axis_index("ta") * frames
    row_lo = pl.multiple_of(begins[1] + lax.axis_index("ha") * rows, 8)
    col_lo = pl.multiple_of(begins[2] + lax.axis_index("wa") * cols, 8)
    row_part = table_ref[plane, pl.ds(row_lo, rows), :]
    col_part = table_ref[plane, pl.ds(col_lo, cols), :]
    grids = []
    for i in range(frames):
        lead = row_part + table_ref[plane, pl.ds(frame_lo + i, 1), :]
        grid = lead[:, None, :] + col_part[None, :, :]
        grids.append(grid.reshape(rows * cols, DH))
    return jnp.concatenate(grids, axis=0)


def turn(x, cosine, sin_even, sin_odd, sign):
    follow = pltpu.roll(x, DH - 1, 1)
    lead = pltpu.roll(x, 1, 1)
    return x * cosine + sign * (follow * sin_even + lead * sin_odd)


def head_slice(head):
    return slice(head * DH, (head + 1) * DH)


def rotate_kernel(
    dims, begins, q_hbm, k_hbm, v_hbm, g_hbm, table_hbm, kv_ref, qg_ref, rope_ref, q_ref, k_ref,
    table_ref, sems,
):
    moves = [
        (table_hbm, table_ref),
        (k_hbm, k_ref),
        (q_hbm, q_ref),
        (v_hbm, kv_ref.at[1]),
        (g_hbm, qg_ref.at[1]),
    ]
    copies = [pltpu.make_async_copy(*move, sems.at[i]) for i, move in enumerate(moves)]
    for copy in copies:
        copy.start()
    copies[0].wait()
    tables = [local_table(plane, table_ref, begins, *dims) for plane in range(3)]
    for plane in range(3):
        rope_ref[plane] = tables[plane]
    for copy, source, target in ((copies[1], k_ref, kv_ref), (copies[2], q_ref, qg_ref)):
        copy.wait()
        for head in range(HEADS):
            cut = head_slice(head)
            target[0, :, cut] = turn(source[:, cut].astype(F32), *tables, 1.0).astype(BF16)
    copies[3].wait()
    copies[4].wait()


def dot_nt(a, b):
    return lax.dot_general(a, b, (((1,), (1,)), ((), ())), preferred_element_type=F32)


def dot_nn(a, b):
    return lax.dot_general(a, b, (((1,), (0,)), ((), ())), preferred_element_type=F32)


def dot_tn(a, b):
    return lax.dot_general(a, b, (((0,), (0,)), ((), ())), preferred_element_type=F32)


def group_bias(flags, sizes):
    valid = None
    for axis, is_far in zip(("ha", "wa"), flags):
        if is_far:
            here = far_exists(axis, sizes[axis])
            valid = here if valid is None else valid & here
    return None if valid is None else jnp.where(valid, 0.0, NEGATIVE).astype(F32)


def forward_kernel(groups, sizes, cells, count, last, *refs):
    tile_count = sum(len(members) for _, members in groups)
    qg_refs = refs[:count]
    kv_refs = refs[count : count + tile_count]
    rest = refs[count + tile_count :]
    if last:
        first_ref, rest = rest[0], rest[1:]
    o_refs = rest[:count]
    stat_ref, key_buf, value_buf = rest[count:]
    at = 0
    spans = []
    for flags, members in groups:
        begin = at
        for member in members:
            key_buf[at : at + cells] = kv_refs[member][0]
            value_buf[at : at + cells] = kv_refs[member][1]
            at += cells
        spans.append((begin, at, group_bias(flags, sizes)))
    lane = lax.broadcasted_iota(jnp.int32, (count * cells, DH), 1)
    stat = jnp.zeros((count * cells, DH), F32)

    def scores_of(head):
        cut = head_slice(head)
        query = jnp.concatenate([ref[0, :, cut] for ref in qg_refs], axis=0)
        return [dot_nt(query, key_buf[lo:hi, cut]) for lo, hi, _ in spans]

    ahead = scores_of(0)
    for head in range(HEADS):
        cut = head_slice(head)
        scores = ahead
        if head + 1 < HEADS:
            ahead = scores_of(head + 1)
        best = None
        for raw, (_, _, bias) in zip(scores, spans):
            top = jnp.max(raw, axis=1, keepdims=True) * SCALE_LOG2
            if bias is not None:
                top = top + bias
            best = top if best is None else jnp.maximum(best, top)
        total = None
        out = None
        for raw, (lo, hi, bias) in zip(scores, spans):
            shift = best if bias is None else best - bias
            weights = jnp.exp2(raw * SCALE_LOG2 - shift)
            part = jnp.sum(weights, axis=1, keepdims=True)
            piece = dot_nn(weights.astype(BF16), value_buf[lo:hi, cut])
            total = part if total is None else total + part
            out = piece if out is None else out + piece
        out = out * (1.0 / total)
        grad = jnp.concatenate([ref[1, :, cut] for ref in qg_refs], axis=0)
        dotted = jnp.sum(out * grad.astype(F32), axis=1, keepdims=True)
        out = out.astype(BF16)
        for i, o_ref in enumerate(o_refs):
            o_ref[:, cut] = out[i * cells : (i + 1) * cells]
        stat = jnp.where(lane == head, best + jnp.log2(total), stat)
        stat = jnp.where(lane == HEADS + head, dotted, stat)
    if last:
        whole = jnp.concatenate([first_ref[...], stat], axis=0)
        stat_ref[...] = whole.T[: stat_ref.shape[0]]
    else:
        stat_ref[...] = stat


def seen_from(stat, distance, cells):
    if distance & 2:
        stat = pltpu.roll(stat, 2 * cells, 1)
    if distance & 1:
        lane = lax.broadcasted_iota(jnp.int32, stat.shape, 1)
        even = (lane < cells) | ((lane >= 2 * cells) & (lane < 3 * cells))
        stat = jnp.where(even, pltpu.roll(stat, 3 * cells, 1), pltpu.roll(stat, cells, 1))
    return stat


def merged_stats(stat_refs, cells):
    parts = [seen_from(ref[...], distance, cells) for distance, ref in enumerate(stat_refs)]
    top = functools.reduce(jnp.maximum, parts)
    shares = [jnp.exp2(part - top) for part in parts]
    total = functools.reduce(jnp.add, shares)
    lse = top + jnp.log2(total)
    shares = [share / total for share in shares]
    delta = functools.reduce(
        jnp.add,
        [share[:HEADS] * part[HEADS : 2 * HEADS] for share, part in zip(shares, parts)],
    )
    return lse[:HEADS], delta, shares


def backward_kernel(cols, grid_rows, sizes, cells, first, last, *refs):
    tile_count = grid_rows * len(cols)
    qg_refs = refs[:4]
    kv_refs = refs[4 : 4 + tile_count]
    rest = refs[4 + tile_count :]
    if first:
        stat_refs, rest = rest[:4], rest[4:]
    else:
        (lse_ref, delta_ref, dq_ref), rest = rest[:3], rest[3:]
    if last:
        dq_outs, rest = rest[:4], rest[4:]
    else:
        dq_out, rest = rest[0], rest[1:]
    if first:
        (lse_ref, delta_ref, share_ref), rest = rest[:3], rest[3:]
        lse, delta, shares = merged_stats(stat_refs, cells)
        lse_ref[...] = lse
        delta_ref[...] = delta
        rows = [shares[d][head : head + 1, : 2 * cells] for head in range(HEADS) for d in range(4)]
        wide = jnp.concatenate(rows + [jnp.zeros((DH - len(rows), 2 * cells), F32)], axis=0)
        share_ref[...] = wide.T[:cells]
    else:
        lse, delta = lse_ref[...], delta_ref[...]
    col_refs = rest[: len(cols)]
    key_buf, value_buf = rest[len(cols) :]

    span = grid_rows * cells
    for i, ref in enumerate(kv_refs):
        key_buf[i * cells : (i + 1) * cells] = ref[0]
        value_buf[i * cells : (i + 1) * cells] = ref[1]
    blocks = [(head, slot) for head in range(HEADS) for slot in range(len(cols))]

    def products_of(head, slot):
        cut = head_slice(head)
        at = slice(slot * span, (slot + 1) * span)
        queries = jnp.concatenate([ref[0, :, cut] for ref in qg_refs], axis=0)
        grads = jnp.concatenate([ref[1, :, cut] for ref in qg_refs], axis=0)
        raw = dot_nt(key_buf[at, cut], queries)
        return raw, dot_nt(value_buf[at, cut], grads), queries, grads

    dqs = [None] * HEADS
    ahead = products_of(*blocks[0])
    for i, (head, slot) in enumerate(blocks):
        raw, prob_grad, queries, grads = ahead
        if i + 1 < len(blocks):
            ahead = products_of(*blocks[i + 1])
        cut = head_slice(head)
        probs = []
        for row in range(grid_rows):
            bias = group_bias((row == 2, cols[slot] == 2), sizes)
            shift = lse[head : head + 1]
            shift = shift if bias is None else shift - bias
            probs.append(jnp.exp2(raw[row * cells : (row + 1) * cells] * SCALE_LOG2 - shift))
        probs = jnp.concatenate(probs, axis=0)
        dscore = (probs * (prob_grad - delta[head : head + 1])).astype(BF16)
        dv = dot_nn(probs.astype(BF16), grads).astype(BF16)
        dk = (dot_nn(dscore, queries) * SCALE).astype(BF16)
        for row in range(grid_rows):
            at = slice(row * cells, (row + 1) * cells)
            col_refs[slot][row, 0, :, cut] = dk[at]
            col_refs[slot][row, 1, :, cut] = dv[at]
        part = dot_nn(key_buf[slot * span : (slot + 1) * span, cut].T, dscore)
        dqs[head] = part if dqs[head] is None else dqs[head] + part
    for head in range(HEADS):
        cut = head_slice(head)
        dq = dqs[head] if first else dqs[head] + dq_ref[head]
        if last:
            dq = (dq * SCALE).T.astype(BF16)
            for i, ref in enumerate(dq_outs):
                ref[:, cut] = dq[i * cells : (i + 1) * cells]
        else:
            dq_out[head] = dq


def finish_query_kernel(*refs):
    o_refs, dq_refs = refs[:4], refs[4:8]
    share_ref, rope_ref, out_ref, dq_out = refs[8:]
    for head in range(HEADS):
        cut = head_slice(head)
        outs = []
        for d, o_ref in zip((0, 3, 2, 1), o_refs):
            weight = share_ref[:, 4 * head + d : 4 * head + d + 1]
            outs.append(o_ref[:, cut].astype(F32) * weight)
        out_ref[:, cut] = functools.reduce(jnp.add, outs).astype(BF16)
        dq = functools.reduce(jnp.add, [ref[:, cut].astype(F32) for ref in dq_refs])
        dq_out[:, cut] = turn(dq, rope_ref[0], rope_ref[1], rope_ref[2], -1.0).astype(BF16)


def finish_key_kernel(cols, rows, *refs):
    col_refs, row_refs = refs[:cols], refs[cols : cols + rows]
    rope_ref, dk_out, dv_out = refs[cols + rows :]
    for head in range(HEADS):
        cut = head_slice(head)
        sums = []
        for which in range(2):
            terms = [ref[0, which, :, cut].astype(F32) for ref in col_refs]
            terms += [ref[which, :, cut].astype(F32) for ref in row_refs]
            sums.append(functools.reduce(jnp.add, terms))
        dk_out[:, cut] = turn(
            sums[0], rope_ref[0], rope_ref[1], rope_ref[2], -1.0
        ).astype(BF16)
        dv_out[:, cut] = sums[1].astype(BF16)


def call(kernel, out_shape, args, flops=0, exps=0, scratch=(), space=pltpu.VMEM, limit=VMEM_LIMIT):
    shapes = jax.tree.leaves(out_shape)
    flops *= 8
    moved = sum(math.prod(x.shape) * x.dtype.itemsize for x in list(args) + shapes)
    return pl.pallas_call(
        kernel,
        out_shape=out_shape,
        in_specs=[pl.BlockSpec(memory_space=space)] * len(args),
        scratch_shapes=list(scratch),
        compiler_params=pltpu.CompilerParams(vmem_limit_bytes=limit),
        cost_estimate=pl.CostEstimate(flops=flops, bytes_accessed=moved, transcendentals=exps),
    )(*args)


def shards(query_in, key_in, value_in, cotangent):
    frames, rows, cols, chan = query_in.shape
    cells = frames * rows * cols
    sizes = {axis: lax.axis_size(axis) for axis in ("ta", "ha", "wa")}
    assert rows == TILE_H and cols == TILE_W and chan == HEADS * DH
    assert TILE_T % frames == 0 and frames * sizes["ta"] <= 2 * TILE_T
    assert sizes["ta"] == 4 and sizes["ha"] % 2 == 0 and sizes["wa"] % 2 == 0
    dims = (frames, rows, cols)
    table, begins = rope_table(frames * sizes["ta"], rows * sizes["ha"], cols * sizes["wa"])
    flat = [x.reshape(cells, chan) for x in (query_in, key_in, value_in, cotangent)]
    pair = jax.ShapeDtypeStruct((2, cells, chan), BF16)
    plain = jax.ShapeDtypeStruct((cells, chan), BF16)

    def real(*shape):
        return jax.ShapeDtypeStruct(shape, F32)

    with jax.named_scope("rotate"):
        kv, qg, rope = call(
            functools.partial(rotate_kernel, dims, begins),
            (pair, pair, real(3, cells, DH)),
            [pltpu.with_memory_space_constraint(x, pltpu.HBM) for x in (*flat, jnp.asarray(table))],
            scratch=[pltpu.VMEM((cells, chan), BF16)] * 2
            + [pltpu.VMEM(table.shape, F32), pltpu.SemaphoreType.DMA((5,))],
            space=pltpu.HBM,
        )

    def other_frames(x, distance):
        return lax.ppermute(x, "ta", [(i, i ^ distance) for i in range(sizes["ta"])])

    row_sides = side_pairs(sizes["ha"])
    col_sides = side_pairs(sizes["wa"])
    with jax.named_scope("halo"):
        kv_rows = [kv] + [lax.ppermute(kv, "ha", pairs) for pairs in row_sides]
        qg2 = other_frames(qg, 2)
        qg1 = other_frames(qg, 1)
        tiles = []
        for block in kv_rows:
            tiles.append([block] + [lax.ppermute(block, "wa", pairs) for pairs in col_sides])
        qg3 = other_frames(qg2, 1)
    grid_rows, grid_cols = 1 + len(row_sides), 1 + len(col_sides)
    flat_tiles = [tiles[row][col] for row in range(grid_rows) for col in range(grid_cols)]
    groups = {}
    for row in range(grid_rows):
        for col in range(grid_cols):
            groups.setdefault((row == 2, col == 2), []).append(row * grid_cols + col)
    groups = list(groups.items())

    key_count = len(flat_tiles) * cells
    product = 2 * cells * key_count * DH * HEADS

    def forward(blocks, first):
        count = len(blocks)
        stat = (count * cells, DH) if first is None else (8, 4 * cells)
        return call(
            functools.partial(forward_kernel, groups, sizes, cells, count, first is not None),
            (*[plain] * count, real(*stat)),
            (*blocks, *flat_tiles) + (() if first is None else (first,)),
            2 * product * count,
            cells * key_count * HEADS * count,
            [pltpu.VMEM((key_count, chan), BF16)] * 2,
        )

    with jax.named_scope("attend"):
        o0, o1, o2, first = forward((qg, qg1, qg2), None)
        o3, stat = forward((qg3,), first)
    with jax.named_scope("merge"):
        stats = [stat] + [other_frames(stat, d) for d in (1, 2, 3)]
        outs = [other_frames(o, d) for d, o in ((3, o3), (2, o2), (1, o1))]
        stats, outs[1:] = lax.optimization_barrier((stats, outs[1:]))

    queries = (qg, qg1, qg2, qg3)
    col_shape = jax.ShapeDtypeStruct((grid_rows, 2, cells, chan), BF16)

    def gradients(which, carried):
        count = len(which)
        first, last = which[-1] == grid_cols - 1, which[0] == 0
        stat_outs = [real(HEADS, 4 * cells), real(HEADS, 4 * cells), real(cells, DH)]
        return call(
            functools.partial(backward_kernel, which, grid_rows, sizes, cells, first, last),
            (
                *([plain] * 4 if last else [real(HEADS, DH, 4 * cells)]),
                *(stat_outs if first else []),
                *[col_shape] * count,
            ),
            (*queries, *[tiles[row][col] for col in which for row in range(grid_rows)], *carried),
            20 * product * count // grid_cols,
            4 * cells * key_count * HEADS * count // grid_cols,
            [pltpu.VMEM((count * grid_rows * cells, chan), BF16)] * 2,
        )

    with jax.named_scope("gradients"):
        dq, lse, delta, shares, *sides = gradients(tuple(range(1, grid_cols)), stats)
        sides = [lax.ppermute(x, "wa", pairs) for x, pairs in zip(sides, col_sides)]
        d0, d1, d2, d3, own = gradients((0,), (lse, delta, dq))
    with jax.named_scope("return"):
        (d1, d2, d3), outs = lax.optimization_barrier(((d1, d2, d3), outs))
        col_parts = [own, *sides]
        dqs = [d0] + [other_frames(x, d) for d, x in ((3, d3), (2, d2), (1, d1))]
        row_parts = []
        for row, pairs in enumerate(row_sides, start=1):
            partial_sum = sum(x[row].astype(F32) for x in col_parts).astype(BF16)
            row_parts.append(lax.ppermute(partial_sum, "ha", pairs))

    with jax.named_scope("finish"):
        attended, grad_query = call(
            finish_query_kernel, (plain, plain), (o0, *outs, *dqs, shares, rope), 10 * product
        )
        grad_key, grad_value = call(
            functools.partial(finish_key_kernel, grid_cols, len(row_parts)),
            (plain, plain),
            (*col_parts, *row_parts, rope),
        )
    return tuple(x.reshape(query_in.shape) for x in (attended, grad_query, grad_key, grad_value))


def solution(mesh):
    spec = P("ta", "ha", "wa", None)
    return jax.shard_map(
        shards, mesh=mesh, in_specs=(spec,) * 4, out_specs=(spec,) * 4, check_vma=False
    )
```

```python
import functools
import math

import jax
import jax.numpy as jnp
import numpy as np
from jax import lax
from jax.experimental import pallas as pl
from jax.experimental.pallas import tpu as pltpu
from jax.sharding import PartitionSpec as P

DH = 128
HEADS = 2
TILE_T = 6
TILE_H = 8
TILE_W = 8

NEGATIVE = -1e30
SCALE = DH**-0.5
SCALE_LOG2 = SCALE * math.log2(math.e)
F32 = jnp.float32
BF16 = jnp.bfloat16
VMEM_LIMIT = 48 * 1024 * 1024


def near_pairs(count):
    return [(i, i ^ 1) for i in range(count)]


def far_pairs(count):
    pairs = []
    for i in range(count):
        j = i + 1 if i % 2 else i - 1
        pairs.append((i, j if 0 <= j < count else i))
    return pairs


def far_exists(axis, count):
    pos = lax.axis_index(axis)
    other = jnp.where(pos % 2 == 1, pos + 1, pos - 1)
    return (other >= 0) & (other < count)


def side_pairs(count):
    sides = []
    if count > 1:
        sides.append(near_pairs(count))
    if count > 2:
        sides.append(far_pairs(count))
    return sides


def rope_table(frame_total, row_total, col_total):
    time_dims = DH // 8
    space_dims = (DH - time_dims) // 2
    slower = 256.0 ** (-np.arange(0, time_dims, 2) / time_dims)
    faster = 256.0 ** (-np.arange(0, space_dims, 2) / space_dims)
    starts = (0, time_dims, time_dims + space_dims)
    pieces = []
    for total, rates, start in zip(
        (frame_total, row_total, col_total), (slower, faster, faster), starts
    ):
        padded = -(-total // 8) * 8
        piece = np.zeros((3, padded, DH), np.float32)
        angles = np.arange(padded)[:, None] * rates[None, :]
        stop = start + 2 * len(rates)
        piece[0, :, start:stop:2] = np.cos(angles)
        piece[0, :, start + 1 : stop : 2] = np.cos(angles)
        piece[1, :, start:stop:2] = -np.sin(angles)
        piece[2, :, start + 1 : stop : 2] = np.sin(angles)
        pieces.append(piece)
    begins = np.cumsum([0] + [piece.shape[1] for piece in pieces])
    return np.concatenate(pieces, axis=1), tuple(int(x) for x in begins[:3])


def local_table(plane, table_ref, begins, frames, rows, cols):
    frame_lo = begins[0] + lax.axis_index("ta") * frames
    row_lo = pl.multiple_of(begins[1] + lax.axis_index("ha") * rows, 8)
    col_lo = pl.multiple_of(begins[2] + lax.axis_index("wa") * cols, 8)
    row_part = table_ref[plane, pl.ds(row_lo, rows), :]
    col_part = table_ref[plane, pl.ds(col_lo, cols), :]
    grids = []
    for i in range(frames):
        lead = row_part + table_ref[plane, pl.ds(frame_lo + i, 1), :]
        grid = lead[:, None, :] + col_part[None, :, :]
        grids.append(grid.reshape(rows * cols, DH))
    return jnp.concatenate(grids, axis=0)


def turn(x, cosine, sin_even, sin_odd, sign):
    follow = pltpu.roll(x, DH - 1, 1)
    lead = pltpu.roll(x, 1, 1)
    return x * cosine + sign * (follow * sin_even + lead * sin_odd)


def head_slice(head):
    return slice(head * DH, (head + 1) * DH)


def rotate_kernel(
    dims, begins, q_hbm, k_hbm, v_hbm, g_hbm, table_hbm, kv_ref, qg_ref, turned_ref, rope_ref,
    q_ref, k_ref, table_ref, sems,
):
    moves = [
        (table_hbm, table_ref),
        (k_hbm, k_ref),
        (q_hbm, q_ref),
        (v_hbm, kv_ref.at[1]),
        (g_hbm, qg_ref.at[1]),
    ]
    copies = [pltpu.make_async_copy(*move, sems.at[i]) for i, move in enumerate(moves)]
    for copy in copies:
        copy.start()
    copies[0].wait()
    tables = [local_table(plane, table_ref, begins, *dims) for plane in range(3)]
    for plane in range(3):
        rope_ref[plane] = tables[plane]
    for copy, source, target in ((copies[1], k_ref, kv_ref), (copies[2], q_ref, qg_ref)):
        copy.wait()
        for head in range(HEADS):
            cut = head_slice(head)
            turned = turn(source[:, cut].astype(F32), *tables, 1.0).astype(BF16)
            target[0, :, cut] = turned
            if target is qg_ref:
                turned_ref[:, cut] = turned
    copies[3].wait()
    copies[4].wait()


def dot_nt(a, b):
    return lax.dot_general(a, b, (((1,), (1,)), ((), ())), preferred_element_type=F32)


def dot_nn(a, b):
    return lax.dot_general(a, b, (((1,), (0,)), ((), ())), preferred_element_type=F32)


def dot_tn(a, b):
    return lax.dot_general(a, b, (((0,), (0,)), ((), ())), preferred_element_type=F32)


def group_bias(flags, sizes):
    valid = None
    for axis, is_far in zip(("ha", "wa"), flags):
        if is_far:
            here = far_exists(axis, sizes[axis])
            valid = here if valid is None else valid & here
    return None if valid is None else jnp.where(valid, 0.0, NEGATIVE).astype(F32)


def query_views(refs):
    qg_ref, qg1_ref, q2_ref, g2_ref, q3_ref, g3_ref = refs
    return (
        [qg_ref.at[0], qg1_ref.at[0], q2_ref, q3_ref],
        [qg_ref.at[1], qg1_ref.at[1], g2_ref, g3_ref],
    )


def forward_kernel(groups, sizes, cells, count, last, *refs):
    tile_count = sum(len(members) for _, members in groups)
    if last:
        q_refs, g_refs, refs = refs[:1], refs[1:2], refs[2:]
    else:
        qg_ref, qg1_ref, q2_ref, g2_ref = refs[:4]
        q_refs = [qg_ref.at[0], qg1_ref.at[0], q2_ref]
        g_refs = [qg_ref.at[1], qg1_ref.at[1], g2_ref]
        refs = refs[4:]
    kv_refs, rest = refs[:tile_count], refs[tile_count:]
    if last:
        first_ref, rest = rest[0], rest[1:]
    o_refs = rest[:count]
    stat_ref, key_buf, value_buf = rest[count:]
    at = 0
    spans = []
    for flags, members in groups:
        begin = at
        for member in members:
            key_buf[at : at + cells] = kv_refs[member][0]
            value_buf[at : at + cells] = kv_refs[member][1]
            at += cells
        spans.append((begin, at, group_bias(flags, sizes)))
    lane = lax.broadcasted_iota(jnp.int32, (count * cells, DH), 1)
    stat = jnp.zeros((count * cells, DH), F32)

    def scores_of(head):
        cut = head_slice(head)
        query = jnp.concatenate([ref[:, cut] for ref in q_refs], axis=0)
        return [dot_nt(query, key_buf[lo:hi, cut]) for lo, hi, _ in spans]

    ahead = scores_of(0)
    for head in range(HEADS):
        cut = head_slice(head)
        scores = ahead
        if head + 1 < HEADS:
            ahead = scores_of(head + 1)
        best = None
        for raw, (_, _, bias) in zip(scores, spans):
            top = jnp.max(raw, axis=1, keepdims=True) * SCALE_LOG2
            if bias is not None:
                top = top + bias
            best = top if best is None else jnp.maximum(best, top)
        total = None
        out = None
        for raw, (lo, hi, bias) in zip(scores, spans):
            shift = best if bias is None else best - bias
            weights = jnp.exp2(raw * SCALE_LOG2 - shift)
            part = jnp.sum(weights, axis=1, keepdims=True)
            piece = dot_nn(weights.astype(BF16), value_buf[lo:hi, cut])
            total = part if total is None else total + part
            out = piece if out is None else out + piece
        out = out * (1.0 / total)
        grad = jnp.concatenate([ref[:, cut] for ref in g_refs], axis=0)
        dotted = jnp.sum(out * grad.astype(F32), axis=1, keepdims=True)
        out = out.astype(BF16)
        for i, o_ref in enumerate(o_refs):
            o_ref[:, cut] = out[i * cells : (i + 1) * cells]
        stat = jnp.where(lane == head, best + jnp.log2(total), stat)
        stat = jnp.where(lane == HEADS + head, dotted, stat)
    if last:
        whole = jnp.concatenate([first_ref[...], stat], axis=0)
        stat_ref[...] = whole.T[: stat_ref.shape[0]]
    else:
        stat_ref[...] = stat


def seen_from(stat, distance, cells):
    if distance & 2:
        stat = pltpu.roll(stat, 2 * cells, 1)
    if distance & 1:
        lane = lax.broadcasted_iota(jnp.int32, stat.shape, 1)
        even = (lane < cells) | ((lane >= 2 * cells) & (lane < 3 * cells))
        stat = jnp.where(even, pltpu.roll(stat, 3 * cells, 1), pltpu.roll(stat, cells, 1))
    return stat


def merged_stats(stat_refs, cells):
    parts = [seen_from(ref[...], distance, cells) for distance, ref in enumerate(stat_refs)]
    top = functools.reduce(jnp.maximum, parts)
    shares = [jnp.exp2(part - top) for part in parts]
    total = functools.reduce(jnp.add, shares)
    lse = top + jnp.log2(total)
    shares = [share / total for share in shares]
    delta = functools.reduce(
        jnp.add,
        [share[:HEADS] * part[HEADS : 2 * HEADS] for share, part in zip(shares, parts)],
    )
    return lse[:HEADS], delta, shares


def backward_kernel(cols, grid_rows, sizes, cells, first, last, *refs):
    tile_count = grid_rows * len(cols)
    q_refs, g_refs = query_views(refs[:6])
    kv_refs = refs[6 : 6 + tile_count]
    rest = refs[6 + tile_count :]
    if first:
        stat_refs, rest = rest[:4], rest[4:]
    else:
        (lse_ref, delta_ref, dq_ref), rest = rest[:3], rest[3:]
    if last:
        dq_outs, rest = rest[:4], rest[4:]
    else:
        dq_out, rest = rest[0], rest[1:]
    if first:
        (lse_ref, delta_ref, share_ref), rest = rest[:3], rest[3:]
        lse, delta, shares = merged_stats(stat_refs, cells)
        lse_ref[...] = lse
        delta_ref[...] = delta
        rows = [shares[d][head : head + 1, : 2 * cells] for head in range(HEADS) for d in range(4)]
        wide = jnp.concatenate(rows + [jnp.zeros((DH - len(rows), 2 * cells), F32)], axis=0)
        share_ref[...] = wide.T[:cells]
    else:
        lse, delta = lse_ref[...], delta_ref[...]
    col_refs = rest[: len(cols)]
    key_buf, value_buf = rest[len(cols) :]

    span = grid_rows * cells
    for i, ref in enumerate(kv_refs):
        key_buf[i * cells : (i + 1) * cells] = ref[0]
        value_buf[i * cells : (i + 1) * cells] = ref[1]
    blocks = [(head, slot) for head in range(HEADS) for slot in range(len(cols))]

    def products_of(head, slot):
        cut = head_slice(head)
        at = slice(slot * span, (slot + 1) * span)
        queries = jnp.concatenate([ref[:, cut] for ref in q_refs], axis=0)
        grads = jnp.concatenate([ref[:, cut] for ref in g_refs], axis=0)
        raw = dot_nt(key_buf[at, cut], queries)
        return raw, dot_nt(value_buf[at, cut], grads), queries, grads

    dqs = [None] * HEADS
    ahead = products_of(*blocks[0])
    for i, (head, slot) in enumerate(blocks):
        raw, prob_grad, queries, grads = ahead
        if i + 1 < len(blocks):
            ahead = products_of(*blocks[i + 1])
        cut = head_slice(head)
        probs = []
        for row in range(grid_rows):
            bias = group_bias((row == 2, cols[slot] == 2), sizes)
            shift = lse[head : head + 1]
            shift = shift if bias is None else shift - bias
            probs.append(jnp.exp2(raw[row * cells : (row + 1) * cells] * SCALE_LOG2 - shift))
        probs = jnp.concatenate(probs, axis=0)
        dscore = (probs * (prob_grad - delta[head : head + 1])).astype(BF16)
        dv = dot_nn(probs.astype(BF16), grads).astype(BF16)
        dk = (dot_nn(dscore, queries) * SCALE).astype(BF16)
        for row in range(grid_rows):
            at = slice(row * cells, (row + 1) * cells)
            col_refs[slot][row, 0, :, cut] = dk[at]
            col_refs[slot][row, 1, :, cut] = dv[at]
        part = dot_nn(key_buf[slot * span : (slot + 1) * span, cut].T, dscore)
        dqs[head] = part if dqs[head] is None else dqs[head] + part
    for head in range(HEADS):
        cut = head_slice(head)
        dq = dqs[head] if first else dqs[head] + dq_ref[head]
        if last:
            dq = (dq * SCALE).T.astype(BF16)
            for i, ref in enumerate(dq_outs):
                ref[:, cut] = dq[i * cells : (i + 1) * cells]
        else:
            dq_out[head] = dq


def finish_query_kernel(*refs):
    o_refs, dq_refs = refs[:4], refs[4:8]
    share_ref, rope_ref, out_ref, dq_out = refs[8:]
    for head in range(HEADS):
        cut = head_slice(head)
        outs = []
        for d, o_ref in zip((0, 3, 2, 1), o_refs):
            weight = share_ref[:, 4 * head + d : 4 * head + d + 1]
            outs.append(o_ref[:, cut].astype(F32) * weight)
        out_ref[:, cut] = functools.reduce(jnp.add, outs).astype(BF16)
        dq = functools.reduce(jnp.add, [ref[:, cut].astype(F32) for ref in dq_refs])
        dq_out[:, cut] = turn(dq, rope_ref[0], rope_ref[1], rope_ref[2], -1.0).astype(BF16)


def finish_key_kernel(cols, rows, *refs):
    col_refs, row_refs = refs[:cols], refs[cols : cols + rows]
    rope_ref, dk_out, dv_out = refs[cols + rows :]
    for head in range(HEADS):
        cut = head_slice(head)
        sums = []
        for which in range(2):
            terms = [ref[0, which, :, cut].astype(F32) for ref in col_refs]
            terms += [ref[which, :, cut].astype(F32) for ref in row_refs]
            sums.append(functools.reduce(jnp.add, terms))
        dk_out[:, cut] = turn(
            sums[0], rope_ref[0], rope_ref[1], rope_ref[2], -1.0
        ).astype(BF16)
        dv_out[:, cut] = sums[1].astype(BF16)


def call(kernel, out_shape, args, flops=0, exps=0, scratch=(), space=pltpu.VMEM, limit=VMEM_LIMIT):
    shapes = jax.tree.leaves(out_shape)
    flops *= 8
    moved = sum(math.prod(x.shape) * x.dtype.itemsize for x in list(args) + shapes)
    return pl.pallas_call(
        kernel,
        out_shape=out_shape,
        in_specs=[pl.BlockSpec(memory_space=space)] * len(args),
        scratch_shapes=list(scratch),
        compiler_params=pltpu.CompilerParams(vmem_limit_bytes=limit),
        cost_estimate=pl.CostEstimate(flops=flops, bytes_accessed=moved, transcendentals=exps),
    )(*args)


def shards(query_in, key_in, value_in, cotangent):
    frames, rows, cols, chan = query_in.shape
    cells = frames * rows * cols
    sizes = {axis: lax.axis_size(axis) for axis in ("ta", "ha", "wa")}
    assert rows == TILE_H and cols == TILE_W and chan == HEADS * DH
    assert TILE_T % frames == 0 and frames * sizes["ta"] <= 2 * TILE_T
    assert sizes["ta"] == 4 and sizes["ha"] % 2 == 0 and sizes["wa"] % 2 == 0
    dims = (frames, rows, cols)
    table, begins = rope_table(frames * sizes["ta"], rows * sizes["ha"], cols * sizes["wa"])
    flat = [x.reshape(cells, chan) for x in (query_in, key_in, value_in, cotangent)]
    pair = jax.ShapeDtypeStruct((2, cells, chan), BF16)
    plain = jax.ShapeDtypeStruct((cells, chan), BF16)

    def real(*shape):
        return jax.ShapeDtypeStruct(shape, F32)

    with jax.named_scope("rotate"):
        kv, qg, turned, rope = call(
            functools.partial(rotate_kernel, dims, begins),
            (pair, pair, plain, real(3, cells, DH)),
            [pltpu.with_memory_space_constraint(x, pltpu.HBM) for x in (*flat, jnp.asarray(table))],
            scratch=[pltpu.VMEM((cells, chan), BF16)] * 2
            + [pltpu.VMEM(table.shape, F32), pltpu.SemaphoreType.DMA((5,))],
            space=pltpu.HBM,
        )

    def other_frames(x, distance):
        return lax.ppermute(x, "ta", [(i, i ^ distance) for i in range(sizes["ta"])])

    row_sides = side_pairs(sizes["ha"])
    col_sides = side_pairs(sizes["wa"])
    with jax.named_scope("halo"):
        kv_rows = [kv] + [lax.ppermute(kv, "ha", pairs) for pairs in row_sides]
        g2 = other_frames(flat[3], 2)
        q2 = other_frames(turned, 2)
        qg1 = other_frames(qg, 1)
        tiles = []
        for block in kv_rows:
            tiles.append([block] + [lax.ppermute(block, "wa", pairs) for pairs in col_sides])
        g3 = other_frames(g2, 1)
        q3 = other_frames(q2, 1)
    grid_rows, grid_cols = 1 + len(row_sides), 1 + len(col_sides)
    flat_tiles = [tiles[row][col] for row in range(grid_rows) for col in range(grid_cols)]
    groups = {}
    for row in range(grid_rows):
        for col in range(grid_cols):
            groups.setdefault((row == 2, col == 2), []).append(row * grid_cols + col)
    groups = list(groups.items())

    key_count = len(flat_tiles) * cells
    product = 2 * cells * key_count * DH * HEADS

    def forward(blocks, first):
        count = 3 if first is None else 1
        stat = (count * cells, DH) if first is None else (8, 4 * cells)
        return call(
            functools.partial(forward_kernel, groups, sizes, cells, count, first is not None),
            (*[plain] * count, real(*stat)),
            (*blocks, *flat_tiles) + (() if first is None else (first,)),
            2 * product * count,
            cells * key_count * HEADS * count,
            [pltpu.VMEM((key_count, chan), BF16)] * 2,
        )

    with jax.named_scope("attend"):
        o0, o1, o2, first = forward((qg, qg1, q2, g2), None)
        o3, stat = forward((q3, g3), first)
    with jax.named_scope("merge"):
        stats = [stat] + [other_frames(stat, d) for d in (1, 2, 3)]
        outs = [other_frames(o, d) for d, o in ((3, o3), (2, o2), (1, o1))]

    queries = (qg, qg1, q2, g2, q3, g3)
    col_shape = jax.ShapeDtypeStruct((grid_rows, 2, cells, chan), BF16)

    def gradients(which, carried):
        count = len(which)
        first, last = which[-1] == grid_cols - 1, which[0] == 0
        stat_outs = [real(HEADS, 4 * cells), real(HEADS, 4 * cells), real(cells, DH)]
        return call(
            functools.partial(backward_kernel, which, grid_rows, sizes, cells, first, last),
            (
                *([plain] * 4 if last else [real(HEADS, DH, 4 * cells)]),
                *(stat_outs if first else []),
                *[col_shape] * count,
            ),
            (*queries, *[tiles[row][col] for col in which for row in range(grid_rows)], *carried),
            20 * product * count // grid_cols,
            4 * cells * key_count * HEADS * count // grid_cols,
            [pltpu.VMEM((count * grid_rows * cells, chan), BF16)] * 2,
        )

    with jax.named_scope("gradients"):
        dq, lse, delta, shares, *sides = gradients(tuple(range(1, grid_cols)), stats)
        sides = [lax.ppermute(x, "wa", pairs) for x, pairs in zip(sides, col_sides)]
        d0, d1, d2, d3, own = gradients((0,), (lse, delta, dq))
    with jax.named_scope("return"):
        (d1, d2, d3), outs = lax.optimization_barrier(((d1, d2, d3), outs))
        col_parts = [own, *sides]
        dqs = [d0] + [other_frames(x, d) for d, x in ((3, d3), (2, d2), (1, d1))]
        row_parts = []
        for row, pairs in enumerate(row_sides, start=1):
            partial_sum = sum(x[row].astype(F32) for x in col_parts).astype(BF16)
            row_parts.append(lax.ppermute(partial_sum, "ha", pairs))

    with jax.named_scope("finish"):
        attended, grad_query = call(
            finish_query_kernel, (plain, plain), (o0, *outs, *dqs, shares, rope), 10 * product
        )
        grad_key, grad_value = call(
            functools.partial(finish_key_kernel, grid_cols, len(row_parts)),
            (plain, plain),
            (*col_parts, *row_parts, rope),
        )
    return tuple(x.reshape(query_in.shape) for x in (attended, grad_query, grad_key, grad_value))


def solution(mesh):
    spec = P("ta", "ha", "wa", None)
    return jax.shard_map(
        shards, mesh=mesh, in_specs=(spec,) * 4, out_specs=(spec,) * 4, check_vma=False
    )
```

```python
import functools
import math

import jax
import jax.numpy as jnp
import numpy as np
from jax import lax
from jax.experimental import pallas as pl
from jax.experimental.pallas import tpu as pltpu
from jax.sharding import PartitionSpec as P

DH = 128
HEADS = 2
TILE_T = 6
TILE_H = 8
TILE_W = 8

NEGATIVE = -1e30
SCALE = DH**-0.5
SCALE_LOG2 = SCALE * math.log2(math.e)
F32 = jnp.float32
BF16 = jnp.bfloat16
STAT_ORDER = (1, 3, 2)
VMEM_LIMIT = 48 * 1024 * 1024


def near_pairs(count):
    return [(i, i ^ 1) for i in range(count)]


def far_pairs(count):
    pairs = []
    for i in range(count):
        j = i + 1 if i % 2 else i - 1
        pairs.append((i, j if 0 <= j < count else i))
    return pairs


def far_exists(axis, count):
    pos = lax.axis_index(axis)
    other = jnp.where(pos % 2 == 1, pos + 1, pos - 1)
    return (other >= 0) & (other < count)


def side_pairs(count):
    sides = []
    if count > 1:
        sides.append(near_pairs(count))
    if count > 2:
        sides.append(far_pairs(count))
    return sides


def rope_table(frame_total, row_total, col_total):
    time_dims = DH // 8
    space_dims = (DH - time_dims) // 2
    slower = 256.0 ** (-np.arange(0, time_dims, 2) / time_dims)
    faster = 256.0 ** (-np.arange(0, space_dims, 2) / space_dims)
    starts = (0, time_dims, time_dims + space_dims)
    pieces = []
    for total, rates, start in zip(
        (frame_total, row_total, col_total), (slower, faster, faster), starts
    ):
        padded = -(-total // 8) * 8
        piece = np.zeros((3, padded, DH), np.float32)
        angles = np.arange(padded)[:, None] * rates[None, :]
        stop = start + 2 * len(rates)
        piece[0, :, start:stop:2] = np.cos(angles)
        piece[0, :, start + 1 : stop : 2] = np.cos(angles)
        piece[1, :, start:stop:2] = -np.sin(angles)
        piece[2, :, start + 1 : stop : 2] = np.sin(angles)
        pieces.append(piece)
    begins = np.cumsum([0] + [piece.shape[1] for piece in pieces])
    return np.concatenate(pieces, axis=1), tuple(int(x) for x in begins[:3])


def local_table(plane, table_ref, begins, frames, rows, cols):
    frame_lo = begins[0] + lax.axis_index("ta") * frames
    row_lo = pl.multiple_of(begins[1] + lax.axis_index("ha") * rows, 8)
    col_lo = pl.multiple_of(begins[2] + lax.axis_index("wa") * cols, 8)
    row_part = table_ref[plane, pl.ds(row_lo, rows), :]
    col_part = table_ref[plane, pl.ds(col_lo, cols), :]
    grids = []
    for i in range(frames):
        lead = row_part + table_ref[plane, pl.ds(frame_lo + i, 1), :]
        grid = lead[:, None, :] + col_part[None, :, :]
        grids.append(grid.reshape(rows * cols, DH))
    return jnp.concatenate(grids, axis=0)


def turn(x, cosine, sin_even, sin_odd, sign):
    follow = pltpu.roll(x, DH - 1, 1)
    lead = pltpu.roll(x, 1, 1)
    return x * cosine + sign * (follow * sin_even + lead * sin_odd)


def head_slice(head):
    return slice(head * DH, (head + 1) * DH)


def rotate_kernel(
    dims, begins, q_hbm, k_hbm, v_hbm, g_hbm, table_hbm, kv_ref, qg_ref, rope_ref, q_ref, k_ref,
    table_ref, sems,
):
    moves = [
        (table_hbm, table_ref),
        (k_hbm, k_ref),
        (q_hbm, q_ref),
        (v_hbm, kv_ref.at[1]),
        (g_hbm, qg_ref.at[1]),
    ]
    copies = [pltpu.make_async_copy(*move, sems.at[i]) for i, move in enumerate(moves)]
    for copy in copies:
        copy.start()
    copies[0].wait()
    tables = [local_table(plane, table_ref, begins, *dims) for plane in range(3)]
    for plane in range(3):
        rope_ref[plane] = tables[plane]
    for copy, source, target in ((copies[1], k_ref, kv_ref), (copies[2], q_ref, qg_ref)):
        copy.wait()
        for head in range(HEADS):
            cut = head_slice(head)
            target[0, :, cut] = turn(source[:, cut].astype(F32), *tables, 1.0).astype(BF16)
    copies[3].wait()
    copies[4].wait()


def dot_nt(a, b):
    return lax.dot_general(a, b, (((1,), (1,)), ((), ())), preferred_element_type=F32)


def dot_nn(a, b):
    return lax.dot_general(a, b, (((1,), (0,)), ((), ())), preferred_element_type=F32)


def dot_tn(a, b):
    return lax.dot_general(a, b, (((0,), (0,)), ((), ())), preferred_element_type=F32)


def group_bias(flags, sizes):
    valid = None
    for axis, is_far in zip(("ha", "wa"), flags):
        if is_far:
            here = far_exists(axis, sizes[axis])
            valid = here if valid is None else valid & here
    return None if valid is None else jnp.where(valid, 0.0, NEGATIVE).astype(F32)


def forward_kernel(groups, sizes, cells, count, last, *refs):
    tile_count = sum(len(members) for _, members in groups)
    qg_refs = refs[:count]
    kv_refs = refs[count : count + tile_count]
    rest = refs[count + tile_count :]
    if last:
        first_ref, rest = rest[0], rest[1:]
    o_refs = rest[:count]
    stat_ref, key_buf, value_buf = rest[count:]
    at = 0
    spans = []
    for flags, members in groups:
        begin = at
        for member in members:
            key_buf[at : at + cells] = kv_refs[member][0]
            value_buf[at : at + cells] = kv_refs[member][1]
            at += cells
        spans.append((begin, at, group_bias(flags, sizes)))
    lane = lax.broadcasted_iota(jnp.int32, (count * cells, DH), 1)
    stat = jnp.zeros((count * cells, DH), F32)

    def scores_of(head):
        cut = head_slice(head)
        query = jnp.concatenate([ref[0, :, cut] for ref in qg_refs], axis=0)
        return [dot_nt(query, key_buf[lo:hi, cut]) for lo, hi, _ in spans]

    ahead = scores_of(0)
    for head in range(HEADS):
        cut = head_slice(head)
        scores = ahead
        if head + 1 < HEADS:
            ahead = scores_of(head + 1)
        best = None
        for raw, (_, _, bias) in zip(scores, spans):
            top = jnp.max(raw, axis=1, keepdims=True) * SCALE_LOG2
            if bias is not None:
                top = top + bias
            best = top if best is None else jnp.maximum(best, top)
        total = None
        out = None
        for raw, (lo, hi, bias) in zip(scores, spans):
            shift = best if bias is None else best - bias
            weights = jnp.exp2(raw * SCALE_LOG2 - shift)
            part = jnp.sum(weights, axis=1, keepdims=True)
            piece = dot_nn(weights.astype(BF16), value_buf[lo:hi, cut])
            total = part if total is None else total + part
            out = piece if out is None else out + piece
        out = out * (1.0 / total)
        grad = jnp.concatenate([ref[1, :, cut] for ref in qg_refs], axis=0)
        dotted = jnp.sum(out * grad.astype(F32), axis=1, keepdims=True)
        out = out.astype(BF16)
        for i, o_ref in enumerate(o_refs):
            o_ref[:, cut] = out[i * cells : (i + 1) * cells]
        stat = jnp.where(lane == head, best + jnp.log2(total), stat)
        stat = jnp.where(lane == HEADS + head, dotted, stat)
    if last:
        whole = jnp.concatenate([first_ref[...], stat], axis=0)
        stat_ref[...] = whole.T[: stat_ref.shape[0]]
    else:
        stat_ref[...] = stat


def seen_from(stat, distance, cells):
    if distance & 2:
        stat = pltpu.roll(stat, 2 * cells, 1)
    if distance & 1:
        lane = lax.broadcasted_iota(jnp.int32, stat.shape, 1)
        even = (lane < cells) | ((lane >= 2 * cells) & (lane < 3 * cells))
        stat = jnp.where(even, pltpu.roll(stat, 3 * cells, 1), pltpu.roll(stat, cells, 1))
    return stat


def merged_stats(stat_refs, cells):
    refs = dict(zip((0, *STAT_ORDER), stat_refs))
    parts = [seen_from(refs[distance][...], distance, cells) for distance in range(4)]
    top = functools.reduce(jnp.maximum, parts)
    shares = [jnp.exp2(part - top) for part in parts]
    total = functools.reduce(jnp.add, shares)
    lse = top + jnp.log2(total)
    shares = [share / total for share in shares]
    delta = functools.reduce(
        jnp.add,
        [share[:HEADS] * part[HEADS : 2 * HEADS] for share, part in zip(shares, parts)],
    )
    return lse[:HEADS], delta, shares


def backward_kernel(cols, grid_rows, sizes, cells, first, last, *refs):
    tile_count = grid_rows * len(cols)
    qg_refs = refs[:4]
    kv_refs = refs[4 : 4 + tile_count]
    rest = refs[4 + tile_count :]
    if first:
        stat_refs, rest = rest[:4], rest[4:]
    else:
        (lse_ref, delta_ref, dq_ref), rest = rest[:3], rest[3:]
    if last:
        dq_outs, rest = rest[:4], rest[4:]
    else:
        dq_out, rest = rest[0], rest[1:]
    if first:
        (lse_ref, delta_ref, share_ref), rest = rest[:3], rest[3:]
        lse, delta, shares = merged_stats(stat_refs, cells)
        lse_ref[...] = lse
        delta_ref[...] = delta
        rows = [shares[d][head : head + 1, : 2 * cells] for head in range(HEADS) for d in range(4)]
        wide = jnp.concatenate(rows + [jnp.zeros((DH - len(rows), 2 * cells), F32)], axis=0)
        share_ref[...] = wide.T[:cells]
    else:
        lse, delta = lse_ref[...], delta_ref[...]
    col_refs = rest[: len(cols)]
    key_buf, value_buf = rest[len(cols) :]

    span = grid_rows * cells
    for i, ref in enumerate(kv_refs):
        key_buf[i * cells : (i + 1) * cells] = ref[0]
        value_buf[i * cells : (i + 1) * cells] = ref[1]
    blocks = [(head, slot) for head in range(HEADS) for slot in range(len(cols))]

    def products_of(head, slot):
        cut = head_slice(head)
        at = slice(slot * span, (slot + 1) * span)
        queries = jnp.concatenate([ref[0, :, cut] for ref in qg_refs], axis=0)
        grads = jnp.concatenate([ref[1, :, cut] for ref in qg_refs], axis=0)
        raw = dot_nt(key_buf[at, cut], queries)
        return raw, dot_nt(value_buf[at, cut], grads), queries, grads

    dqs = [None] * HEADS
    ahead = products_of(*blocks[0])
    for i, (head, slot) in enumerate(blocks):
        raw, prob_grad, queries, grads = ahead
        if i + 1 < len(blocks):
            ahead = products_of(*blocks[i + 1])
        cut = head_slice(head)
        probs = []
        for row in range(grid_rows):
            bias = group_bias((row == 2, cols[slot] == 2), sizes)
            shift = lse[head : head + 1]
            shift = shift if bias is None else shift - bias
            probs.append(jnp.exp2(raw[row * cells : (row + 1) * cells] * SCALE_LOG2 - shift))
        probs = jnp.concatenate(probs, axis=0)
        dscore = (probs * (prob_grad - delta[head : head + 1])).astype(BF16)
        dv = dot_nn(probs.astype(BF16), grads).astype(BF16)
        dk = (dot_nn(dscore, queries) * SCALE).astype(BF16)
        for row in range(grid_rows):
            at = slice(row * cells, (row + 1) * cells)
            col_refs[slot][row, 0, :, cut] = dk[at]
            col_refs[slot][row, 1, :, cut] = dv[at]
        part = dot_nn(key_buf[slot * span : (slot + 1) * span, cut].T, dscore)
        dqs[head] = part if dqs[head] is None else dqs[head] + part
    for head in range(HEADS):
        cut = head_slice(head)
        dq = dqs[head] if first else dqs[head] + dq_ref[head]
        if last:
            dq = (dq * SCALE).T.astype(BF16)
            for i, ref in enumerate(dq_outs):
                ref[:, cut] = dq[i * cells : (i + 1) * cells]
        else:
            dq_out[head] = dq


def finish_query_kernel(*refs):
    o_refs, dq_refs = refs[:4], refs[4:8]
    share_ref, rope_ref, out_ref, dq_out = refs[8:]
    for head in range(HEADS):
        cut = head_slice(head)
        outs = []
        for d, o_ref in zip((0, 3, 2, 1), o_refs):
            weight = share_ref[:, 4 * head + d : 4 * head + d + 1]
            outs.append(o_ref[:, cut].astype(F32) * weight)
        out_ref[:, cut] = functools.reduce(jnp.add, outs).astype(BF16)
        dq = functools.reduce(jnp.add, [ref[:, cut].astype(F32) for ref in dq_refs])
        dq_out[:, cut] = turn(dq, rope_ref[0], rope_ref[1], rope_ref[2], -1.0).astype(BF16)


def finish_key_kernel(cols, rows, *refs):
    col_refs, row_refs = refs[:cols], refs[cols : cols + rows]
    rope_ref, dk_out, dv_out = refs[cols + rows :]
    for head in range(HEADS):
        cut = head_slice(head)
        sums = []
        for which in range(2):
            terms = [ref[0, which, :, cut].astype(F32) for ref in col_refs]
            terms += [ref[which, :, cut].astype(F32) for ref in row_refs]
            sums.append(functools.reduce(jnp.add, terms))
        dk_out[:, cut] = turn(
            sums[0], rope_ref[0], rope_ref[1], rope_ref[2], -1.0
        ).astype(BF16)
        dv_out[:, cut] = sums[1].astype(BF16)


def call(kernel, out_shape, args, flops=0, exps=0, scratch=(), space=pltpu.VMEM, limit=VMEM_LIMIT):
    shapes = jax.tree.leaves(out_shape)
    flops *= 8
    moved = sum(math.prod(x.shape) * x.dtype.itemsize for x in list(args) + shapes)
    return pl.pallas_call(
        kernel,
        out_shape=out_shape,
        in_specs=[pl.BlockSpec(memory_space=space)] * len(args),
        scratch_shapes=list(scratch),
        compiler_params=pltpu.CompilerParams(vmem_limit_bytes=limit),
        cost_estimate=pl.CostEstimate(flops=flops, bytes_accessed=moved, transcendentals=exps),
    )(*args)


def shards(query_in, key_in, value_in, cotangent):
    frames, rows, cols, chan = query_in.shape
    cells = frames * rows * cols
    sizes = {axis: lax.axis_size(axis) for axis in ("ta", "ha", "wa")}
    assert rows == TILE_H and cols == TILE_W and chan == HEADS * DH
    assert TILE_T % frames == 0 and frames * sizes["ta"] <= 2 * TILE_T
    assert sizes["ta"] == 4 and sizes["ha"] % 2 == 0 and sizes["wa"] % 2 == 0
    dims = (frames, rows, cols)
    table, begins = rope_table(frames * sizes["ta"], rows * sizes["ha"], cols * sizes["wa"])
    flat = [x.reshape(cells, chan) for x in (query_in, key_in, value_in, cotangent)]
    pair = jax.ShapeDtypeStruct((2, cells, chan), BF16)
    plain = jax.ShapeDtypeStruct((cells, chan), BF16)

    def real(*shape):
        return jax.ShapeDtypeStruct(shape, F32)

    with jax.named_scope("rotate"):
        kv, qg, rope = call(
            functools.partial(rotate_kernel, dims, begins),
            (pair, pair, real(3, cells, DH)),
            [pltpu.with_memory_space_constraint(x, pltpu.HBM) for x in (*flat, jnp.asarray(table))],
            scratch=[pltpu.VMEM((cells, chan), BF16)] * 2
            + [pltpu.VMEM(table.shape, F32), pltpu.SemaphoreType.DMA((5,))],
            space=pltpu.HBM,
        )

    def other_frames(x, distance):
        return lax.ppermute(x, "ta", [(i, i ^ distance) for i in range(sizes["ta"])])

    row_sides = side_pairs(sizes["ha"])
    col_sides = side_pairs(sizes["wa"])
    with jax.named_scope("halo"):
        kv_rows = [kv] + [lax.ppermute(kv, "ha", pairs) for pairs in row_sides]
        qg2 = other_frames(qg, 2)
        qg1 = other_frames(qg, 1)
        tiles = []
        for block in kv_rows:
            tiles.append([block] + [lax.ppermute(block, "wa", pairs) for pairs in col_sides])
        qg3 = other_frames(qg2, 1)
    grid_rows, grid_cols = 1 + len(row_sides), 1 + len(col_sides)
    flat_tiles = [tiles[row][col] for row in range(grid_rows) for col in range(grid_cols)]
    groups = {}
    for row in range(grid_rows):
        for col in range(grid_cols):
            groups.setdefault((row == 2, col == 2), []).append(row * grid_cols + col)
    groups = list(groups.items())

    key_count = len(flat_tiles) * cells
    product = 2 * cells * key_count * DH * HEADS

    def forward(blocks, first):
        count = len(blocks)
        stat = (count * cells, DH) if first is None else (8, 4 * cells)
        return call(
            functools.partial(forward_kernel, groups, sizes, cells, count, first is not None),
            (*[plain] * count, real(*stat)),
            (*blocks, *flat_tiles) + (() if first is None else (first,)),
            2 * product * count,
            cells * key_count * HEADS * count,
            [pltpu.VMEM((key_count, chan), BF16)] * 2,
        )

    with jax.named_scope("attend"):
        o0, o1, o2, first = forward((qg, qg1, qg2), None)
        o3, stat = forward((qg3,), first)
    with jax.named_scope("merge"):
        stats = [stat] + [other_frames(stat, d) for d in STAT_ORDER]
        outs = [other_frames(o, d) for d, o in ((3, o3), (2, o2), (1, o1))]

    queries = (qg, qg1, qg2, qg3)
    col_shape = jax.ShapeDtypeStruct((grid_rows, 2, cells, chan), BF16)

    def gradients(which, carried):
        count = len(which)
        first, last = which[-1] == grid_cols - 1, which[0] == 0
        stat_outs = [real(HEADS, 4 * cells), real(HEADS, 4 * cells), real(cells, DH)]
        return call(
            functools.partial(backward_kernel, which, grid_rows, sizes, cells, first, last),
            (
                *([plain] * 4 if last else [real(HEADS, DH, 4 * cells)]),
                *(stat_outs if first else []),
                *[col_shape] * count,
            ),
            (*queries, *[tiles[row][col] for col in which for row in range(grid_rows)], *carried),
            20 * product * count // grid_cols,
            4 * cells * key_count * HEADS * count // grid_cols,
            [pltpu.VMEM((count * grid_rows * cells, chan), BF16)] * 2,
        )

    with jax.named_scope("gradients"):
        dq, lse, delta, shares, *sides = gradients(tuple(range(1, grid_cols)), stats)
        sides = [lax.ppermute(x, "wa", pairs) for x, pairs in zip(sides, col_sides)]
        d0, d1, d2, d3, own = gradients((0,), (lse, delta, dq))
    with jax.named_scope("return"):
        (d1, d2, d3), outs = lax.optimization_barrier(((d1, d2, d3), outs))
        col_parts = [own, *sides]
        dqs = [d0] + [other_frames(x, d) for d, x in ((3, d3), (2, d2), (1, d1))]
        row_parts = []
        for row, pairs in enumerate(row_sides, start=1):
            partial_sum = sum(x[row].astype(F32) for x in col_parts).astype(BF16)
            row_parts.append(lax.ppermute(partial_sum, "ha", pairs))

    with jax.named_scope("finish"):
        attended, grad_query = call(
            finish_query_kernel, (plain, plain), (o0, *outs, *dqs, shares, rope), 10 * product
        )
        grad_key, grad_value = call(
            functools.partial(finish_key_kernel, grid_cols, len(row_parts)),
            (plain, plain),
            (*col_parts, *row_parts, rope),
        )
    return tuple(x.reshape(query_in.shape) for x in (attended, grad_query, grad_key, grad_value))


def solution(mesh):
    spec = P("ta", "ha", "wa", None)
    return jax.shard_map(
        shards, mesh=mesh, in_specs=(spec,) * 4, out_specs=(spec,) * 4, check_vma=False
    )
```

```python
import functools
import math

import jax
import jax.numpy as jnp
import numpy as np
from jax import lax
from jax.experimental import pallas as pl
from jax.experimental.pallas import tpu as pltpu
from jax.sharding import PartitionSpec as P

DH = 128
HEADS = 2
TILE_T = 6
TILE_H = 8
TILE_W = 8

NEGATIVE = -1e30
SCALE = DH**-0.5
SCALE_LOG2 = SCALE * math.log2(math.e)
F32 = jnp.float32
BF16 = jnp.bfloat16
VMEM_LIMIT = 48 * 1024 * 1024


def near_pairs(count):
    return [(i, i ^ 1) for i in range(count)]


def far_pairs(count):
    pairs = []
    for i in range(count):
        j = i + 1 if i % 2 else i - 1
        pairs.append((i, j if 0 <= j < count else i))
    return pairs


def far_exists(axis, count):
    pos = lax.axis_index(axis)
    other = jnp.where(pos % 2 == 1, pos + 1, pos - 1)
    return (other >= 0) & (other < count)


def side_pairs(count):
    sides = []
    if count > 1:
        sides.append(near_pairs(count))
    if count > 2:
        sides.append(far_pairs(count))
    return sides


def rope_table(frame_total, row_total, col_total):
    time_dims = DH // 8
    space_dims = (DH - time_dims) // 2
    slower = 256.0 ** (-np.arange(0, time_dims, 2) / time_dims)
    faster = 256.0 ** (-np.arange(0, space_dims, 2) / space_dims)
    starts = (0, time_dims, time_dims + space_dims)
    pieces = []
    for total, rates, start in zip(
        (frame_total, row_total, col_total), (slower, faster, faster), starts
    ):
        padded = -(-total // 8) * 8
        piece = np.zeros((3, padded, DH), np.float32)
        angles = np.arange(padded)[:, None] * rates[None, :]
        stop = start + 2 * len(rates)
        piece[0, :, start:stop:2] = np.cos(angles)
        piece[0, :, start + 1 : stop : 2] = np.cos(angles)
        piece[1, :, start:stop:2] = -np.sin(angles)
        piece[2, :, start + 1 : stop : 2] = np.sin(angles)
        pieces.append(piece)
    begins = np.cumsum([0] + [piece.shape[1] for piece in pieces])
    return np.concatenate(pieces, axis=1), tuple(int(x) for x in begins[:3])


def local_table(plane, table_ref, begins, frames, rows, cols):
    frame_lo = begins[0] + lax.axis_index("ta") * frames
    row_lo = pl.multiple_of(begins[1] + lax.axis_index("ha") * rows, 8)
    col_lo = pl.multiple_of(begins[2] + lax.axis_index("wa") * cols, 8)
    row_part = table_ref[plane, pl.ds(row_lo, rows), :]
    col_part = table_ref[plane, pl.ds(col_lo, cols), :]
    grids = []
    for i in range(frames):
        lead = row_part + table_ref[plane, pl.ds(frame_lo + i, 1), :]
        grid = lead[:, None, :] + col_part[None, :, :]
        grids.append(grid.reshape(rows * cols, DH))
    return jnp.concatenate(grids, axis=0)


def turn(x, cosine, sin_even, sin_odd, sign):
    follow = pltpu.roll(x, DH - 1, 1)
    lead = pltpu.roll(x, 1, 1)
    return x * cosine + sign * (follow * sin_even + lead * sin_odd)


def head_slice(head):
    return slice(head * DH, (head + 1) * DH)


def rotate_kernel(
    dims, begins, q_hbm, k_hbm, v_hbm, g_hbm, table_hbm, kv_ref, qg_ref, rope_ref, q_ref, k_ref,
    table_ref, sems,
):
    moves = [
        (table_hbm, table_ref),
        (k_hbm, k_ref),
        (q_hbm, q_ref),
        (v_hbm, kv_ref.at[1]),
        (g_hbm, qg_ref.at[1]),
    ]
    copies = [pltpu.make_async_copy(*move, sems.at[i]) for i, move in enumerate(moves)]
    for copy in copies:
        copy.start()
    copies[0].wait()
    tables = [local_table(plane, table_ref, begins, *dims) for plane in range(3)]
    for plane in range(3):
        rope_ref[plane] = tables[plane]
    for copy, source, target in ((copies[1], k_ref, kv_ref), (copies[2], q_ref, qg_ref)):
        copy.wait()
        for head in range(HEADS):
            cut = head_slice(head)
            target[0, :, cut] = turn(source[:, cut].astype(F32), *tables, 1.0).astype(BF16)
    copies[3].wait()
    copies[4].wait()


def dot_nt(a, b):
    return lax.dot_general(a, b, (((1,), (1,)), ((), ())), preferred_element_type=F32)


def dot_nn(a, b):
    return lax.dot_general(a, b, (((1,), (0,)), ((), ())), preferred_element_type=F32)


def dot_tn(a, b):
    return lax.dot_general(a, b, (((0,), (0,)), ((), ())), preferred_element_type=F32)


def group_bias(flags, sizes):
    valid = None
    for axis, is_far in zip(("ha", "wa"), flags):
        if is_far:
            here = far_exists(axis, sizes[axis])
            valid = here if valid is None else valid & here
    return None if valid is None else jnp.where(valid, 0.0, NEGATIVE).astype(F32)


def forward_kernel(groups, sizes, cells, count, last, *refs):
    tile_count = sum(len(members) for _, members in groups)
    qg_refs = refs[:count]
    kv_refs = refs[count : count + tile_count]
    rest = refs[count + tile_count :]
    if last:
        first_ref, rest = rest[0], rest[1:]
    o_refs = rest[:count]
    stat_ref, key_buf, value_buf = rest[count:]
    at = 0
    spans = []
    for flags, members in groups:
        begin = at
        for member in members:
            key_buf[at : at + cells] = kv_refs[member][0]
            value_buf[at : at + cells] = kv_refs[member][1]
            at += cells
        spans.append((begin, at, group_bias(flags, sizes)))
    lane = lax.broadcasted_iota(jnp.int32, (count * cells, DH), 1)
    stat = jnp.zeros((count * cells, DH), F32)

    def scores_of(head):
        cut = head_slice(head)
        query = jnp.concatenate([ref[0, :, cut] for ref in qg_refs], axis=0)
        return [dot_nt(query, key_buf[lo:hi, cut]) for lo, hi, _ in spans]

    ahead = scores_of(0)
    for head in range(HEADS):
        cut = head_slice(head)
        scores = ahead
        if head + 1 < HEADS:
            ahead = scores_of(head + 1)
        best = None
        for raw, (_, _, bias) in zip(scores, spans):
            top = jnp.max(raw, axis=1, keepdims=True) * SCALE_LOG2
            if bias is not None:
                top = top + bias
            best = top if best is None else jnp.maximum(best, top)
        total = None
        out = None
        for raw, (lo, hi, bias) in zip(scores, spans):
            shift = best if bias is None else best - bias
            weights = jnp.exp2(raw * SCALE_LOG2 - shift)
            part = jnp.sum(weights, axis=1, keepdims=True)
            piece = dot_nn(weights.astype(BF16), value_buf[lo:hi, cut])
            total = part if total is None else total + part
            out = piece if out is None else out + piece
        out = out * (1.0 / total)
        grad = jnp.concatenate([ref[1, :, cut] for ref in qg_refs], axis=0)
        dotted = jnp.sum(out * grad.astype(F32), axis=1, keepdims=True)
        out = out.astype(BF16)
        for i, o_ref in enumerate(o_refs):
            o_ref[:, cut] = out[i * cells : (i + 1) * cells]
        stat = jnp.where(lane == head, best + jnp.log2(total), stat)
        stat = jnp.where(lane == HEADS + head, dotted, stat)
    if last:
        whole = jnp.concatenate([first_ref[...], stat], axis=0)
        rows = whole.T[: stat_ref.shape[1]]
        for i in range(stat_ref.shape[0]):
            stat_ref[i] = rows
    else:
        stat_ref[...] = stat


def seen_from(stat, distance, cells):
    if distance & 2:
        stat = pltpu.roll(stat, 2 * cells, 1)
    if distance & 1:
        lane = lax.broadcasted_iota(jnp.int32, stat.shape, 1)
        even = (lane < cells) | ((lane >= 2 * cells) & (lane < 3 * cells))
        stat = jnp.where(even, pltpu.roll(stat, 3 * cells, 1), pltpu.roll(stat, cells, 1))
    return stat


def merged_stats(stat_ref, cells):
    here = lax.axis_index("ta")
    parts = [seen_from(stat_ref[here ^ distance], distance, cells) for distance in range(4)]
    top = functools.reduce(jnp.maximum, parts)
    shares = [jnp.exp2(part - top) for part in parts]
    total = functools.reduce(jnp.add, shares)
    lse = top + jnp.log2(total)
    shares = [share / total for share in shares]
    delta = functools.reduce(
        jnp.add,
        [share[:HEADS] * part[HEADS : 2 * HEADS] for share, part in zip(shares, parts)],
    )
    return lse[:HEADS], delta, shares


def backward_kernel(cols, grid_rows, sizes, cells, first, last, *refs):
    tile_count = grid_rows * len(cols)
    qg_refs = refs[:4]
    kv_refs = refs[4 : 4 + tile_count]
    rest = refs[4 + tile_count :]
    if first:
        stat_ref, rest = rest[0], rest[1:]
    else:
        (lse_ref, delta_ref, dq_ref), rest = rest[:3], rest[3:]
    if last:
        dq_outs, rest = rest[:4], rest[4:]
    else:
        dq_out, rest = rest[0], rest[1:]
    if first:
        (lse_ref, delta_ref, share_ref), rest = rest[:3], rest[3:]
        lse, delta, shares = merged_stats(stat_ref, cells)
        lse_ref[...] = lse
        delta_ref[...] = delta
        rows = [shares[d][head : head + 1, : 2 * cells] for head in range(HEADS) for d in range(4)]
        wide = jnp.concatenate(rows + [jnp.zeros((DH - len(rows), 2 * cells), F32)], axis=0)
        share_ref[...] = wide.T[:cells]
    else:
        lse, delta = lse_ref[...], delta_ref[...]
    col_refs = rest[: len(cols)]
    key_buf, value_buf = rest[len(cols) :]

    span = grid_rows * cells
    for i, ref in enumerate(kv_refs):
        key_buf[i * cells : (i + 1) * cells] = ref[0]
        value_buf[i * cells : (i + 1) * cells] = ref[1]
    blocks = [(head, slot) for head in range(HEADS) for slot in range(len(cols))]

    def products_of(head, slot):
        cut = head_slice(head)
        at = slice(slot * span, (slot + 1) * span)
        queries = jnp.concatenate([ref[0, :, cut] for ref in qg_refs], axis=0)
        grads = jnp.concatenate([ref[1, :, cut] for ref in qg_refs], axis=0)
        raw = dot_nt(key_buf[at, cut], queries)
        return raw, dot_nt(value_buf[at, cut], grads), queries, grads

    dqs = [None] * HEADS
    ahead = products_of(*blocks[0])
    for i, (head, slot) in enumerate(blocks):
        raw, prob_grad, queries, grads = ahead
        if i + 1 < len(blocks):
            ahead = products_of(*blocks[i + 1])
        cut = head_slice(head)
        probs = []
        for row in range(grid_rows):
            bias = group_bias((row == 2, cols[slot] == 2), sizes)
            shift = lse[head : head + 1]
            shift = shift if bias is None else shift - bias
            probs.append(jnp.exp2(raw[row * cells : (row + 1) * cells] * SCALE_LOG2 - shift))
        probs = jnp.concatenate(probs, axis=0)
        dscore = (probs * (prob_grad - delta[head : head + 1])).astype(BF16)
        dv = dot_nn(probs.astype(BF16), grads).astype(BF16)
        dk = (dot_nn(dscore, queries) * SCALE).astype(BF16)
        for row in range(grid_rows):
            at = slice(row * cells, (row + 1) * cells)
            col_refs[slot][row, 0, :, cut] = dk[at]
            col_refs[slot][row, 1, :, cut] = dv[at]
        part = dot_nn(key_buf[slot * span : (slot + 1) * span, cut].T, dscore)
        dqs[head] = part if dqs[head] is None else dqs[head] + part
    for head in range(HEADS):
        cut = head_slice(head)
        dq = dqs[head] if first else dqs[head] + dq_ref[head]
        if last:
            dq = (dq * SCALE).T.astype(BF16)
            for i, ref in enumerate(dq_outs):
                ref[:, cut] = dq[i * cells : (i + 1) * cells]
        else:
            dq_out[head] = dq


def finish_query_kernel(*refs):
    o_refs, dq_refs = refs[:4], refs[4:8]
    share_ref, rope_ref, out_ref, dq_out = refs[8:]
    for head in range(HEADS):
        cut = head_slice(head)
        outs = []
        for d, o_ref in zip((0, 3, 2, 1), o_refs):
            weight = share_ref[:, 4 * head + d : 4 * head + d + 1]
            outs.append(o_ref[:, cut].astype(F32) * weight)
        out_ref[:, cut] = functools.reduce(jnp.add, outs).astype(BF16)
        dq = functools.reduce(jnp.add, [ref[:, cut].astype(F32) for ref in dq_refs])
        dq_out[:, cut] = turn(dq, rope_ref[0], rope_ref[1], rope_ref[2], -1.0).astype(BF16)


def finish_key_kernel(cols, rows, *refs):
    col_refs, row_refs = refs[:cols], refs[cols : cols + rows]
    rope_ref, dk_out, dv_out = refs[cols + rows :]
    for head in range(HEADS):
        cut = head_slice(head)
        sums = []
        for which in range(2):
            terms = [ref[0, which, :, cut].astype(F32) for ref in col_refs]
            terms += [ref[which, :, cut].astype(F32) for ref in row_refs]
            sums.append(functools.reduce(jnp.add, terms))
        dk_out[:, cut] = turn(
            sums[0], rope_ref[0], rope_ref[1], rope_ref[2], -1.0
        ).astype(BF16)
        dv_out[:, cut] = sums[1].astype(BF16)


def call(kernel, out_shape, args, flops=0, exps=0, scratch=(), space=pltpu.VMEM, limit=VMEM_LIMIT):
    shapes = jax.tree.leaves(out_shape)
    flops *= 8
    moved = sum(math.prod(x.shape) * x.dtype.itemsize for x in list(args) + shapes)
    return pl.pallas_call(
        kernel,
        out_shape=out_shape,
        in_specs=[pl.BlockSpec(memory_space=space)] * len(args),
        scratch_shapes=list(scratch),
        compiler_params=pltpu.CompilerParams(vmem_limit_bytes=limit),
        cost_estimate=pl.CostEstimate(flops=flops, bytes_accessed=moved, transcendentals=exps),
    )(*args)


def shards(query_in, key_in, value_in, cotangent):
    frames, rows, cols, chan = query_in.shape
    cells = frames * rows * cols
    sizes = {axis: lax.axis_size(axis) for axis in ("ta", "ha", "wa")}
    assert rows == TILE_H and cols == TILE_W and chan == HEADS * DH
    assert TILE_T % frames == 0 and frames * sizes["ta"] <= 2 * TILE_T
    assert sizes["ta"] == 4 and sizes["ha"] % 2 == 0 and sizes["wa"] % 2 == 0
    dims = (frames, rows, cols)
    table, begins = rope_table(frames * sizes["ta"], rows * sizes["ha"], cols * sizes["wa"])
    flat = [x.reshape(cells, chan) for x in (query_in, key_in, value_in, cotangent)]
    pair = jax.ShapeDtypeStruct((2, cells, chan), BF16)
    plain = jax.ShapeDtypeStruct((cells, chan), BF16)

    def real(*shape):
        return jax.ShapeDtypeStruct(shape, F32)

    with jax.named_scope("rotate"):
        kv, qg, rope = call(
            functools.partial(rotate_kernel, dims, begins),
            (pair, pair, real(3, cells, DH)),
            [pltpu.with_memory_space_constraint(x, pltpu.HBM) for x in (*flat, jnp.asarray(table))],
            scratch=[pltpu.VMEM((cells, chan), BF16)] * 2
            + [pltpu.VMEM(table.shape, F32), pltpu.SemaphoreType.DMA((5,))],
            space=pltpu.HBM,
        )

    def other_frames(x, distance):
        return lax.ppermute(x, "ta", [(i, i ^ distance) for i in range(sizes["ta"])])

    row_sides = side_pairs(sizes["ha"])
    col_sides = side_pairs(sizes["wa"])
    with jax.named_scope("halo"):
        kv_rows = [kv] + [lax.ppermute(kv, "ha", pairs) for pairs in row_sides]
        qg2 = other_frames(qg, 2)
        qg1 = other_frames(qg, 1)
        tiles = []
        for block in kv_rows:
            tiles.append([block] + [lax.ppermute(block, "wa", pairs) for pairs in col_sides])
        qg3 = other_frames(qg2, 1)
    grid_rows, grid_cols = 1 + len(row_sides), 1 + len(col_sides)
    flat_tiles = [tiles[row][col] for row in range(grid_rows) for col in range(grid_cols)]
    groups = {}
    for row in range(grid_rows):
        for col in range(grid_cols):
            groups.setdefault((row == 2, col == 2), []).append(row * grid_cols + col)
    groups = list(groups.items())

    key_count = len(flat_tiles) * cells
    product = 2 * cells * key_count * DH * HEADS

    def forward(blocks, first):
        count = len(blocks)
        stat = (count * cells, DH) if first is None else (4, 8, 4 * cells)
        return call(
            functools.partial(forward_kernel, groups, sizes, cells, count, first is not None),
            (*[plain] * count, real(*stat)),
            (*blocks, *flat_tiles) + (() if first is None else (first,)),
            2 * product * count,
            cells * key_count * HEADS * count,
            [pltpu.VMEM((key_count, chan), BF16)] * 2,
        )

    with jax.named_scope("attend"):
        o0, o1, o2, first = forward((qg, qg1, qg2), None)
        o3, stat = forward((qg3,), first)
    with jax.named_scope("merge"):
        stats = [lax.all_to_all(stat, "ta", 0, 0)]
        outs = [other_frames(o, d) for d, o in ((3, o3), (2, o2), (1, o1))]

    queries = (qg, qg1, qg2, qg3)
    col_shape = jax.ShapeDtypeStruct((grid_rows, 2, cells, chan), BF16)

    def gradients(which, carried):
        count = len(which)
        first, last = which[-1] == grid_cols - 1, which[0] == 0
        stat_outs = [real(HEADS, 4 * cells), real(HEADS, 4 * cells), real(cells, DH)]
        return call(
            functools.partial(backward_kernel, which, grid_rows, sizes, cells, first, last),
            (
                *([plain] * 4 if last else [real(HEADS, DH, 4 * cells)]),
                *(stat_outs if first else []),
                *[col_shape] * count,
            ),
            (*queries, *[tiles[row][col] for col in which for row in range(grid_rows)], *carried),
            20 * product * count // grid_cols,
            4 * cells * key_count * HEADS * count // grid_cols,
            [pltpu.VMEM((count * grid_rows * cells, chan), BF16)] * 2,
        )

    with jax.named_scope("gradients"):
        dq, lse, delta, shares, *sides = gradients(tuple(range(1, grid_cols)), stats)
        sides = [lax.ppermute(x, "wa", pairs) for x, pairs in zip(sides, col_sides)]
        d0, d1, d2, d3, own = gradients((0,), (lse, delta, dq))
    with jax.named_scope("return"):
        (d1, d2, d3), outs = lax.optimization_barrier(((d1, d2, d3), outs))
        col_parts = [own, *sides]
        dqs = [d0] + [other_frames(x, d) for d, x in ((3, d3), (2, d2), (1, d1))]
        row_parts = []
        for row, pairs in enumerate(row_sides, start=1):
            partial_sum = sum(x[row].astype(F32) for x in col_parts).astype(BF16)
            row_parts.append(lax.ppermute(partial_sum, "ha", pairs))

    with jax.named_scope("finish"):
        attended, grad_query = call(
            finish_query_kernel, (plain, plain), (o0, *outs, *dqs, shares, rope), 10 * product
        )
        grad_key, grad_value = call(
            functools.partial(finish_key_kernel, grid_cols, len(row_parts)),
            (plain, plain),
            (*col_parts, *row_parts, rope),
        )
    return tuple(x.reshape(query_in.shape) for x in (attended, grad_query, grad_key, grad_value))


def solution(mesh):
    spec = P("ta", "ha", "wa", None)
    return jax.shard_map(
        shards, mesh=mesh, in_specs=(spec,) * 4, out_specs=(spec,) * 4, check_vma=False
    )
```

```python
import functools
import math

import jax
import jax.numpy as jnp
import numpy as np
from jax import lax
from jax.experimental import pallas as pl
from jax.experimental.pallas import tpu as pltpu
from jax.sharding import PartitionSpec as P

DH = 128
HEADS = 2
TILE_T = 6
TILE_H = 8
TILE_W = 8

NEGATIVE = -1e30
SCALE = DH**-0.5
SCALE_LOG2 = SCALE * math.log2(math.e)
F32 = jnp.float32
BF16 = jnp.bfloat16
NEAR = 1
VMEM_LIMIT = 48 * 1024 * 1024


def near_pairs(count):
    return [(i, i ^ 1) for i in range(count)]


def far_pairs(count):
    pairs = []
    for i in range(count):
        j = i + 1 if i % 2 else i - 1
        pairs.append((i, j if 0 <= j < count else i))
    return pairs


def far_exists(axis, count):
    pos = lax.axis_index(axis)
    other = jnp.where(pos % 2 == 1, pos + 1, pos - 1)
    return (other >= 0) & (other < count)


def side_pairs(count):
    sides = []
    if count > 1:
        sides.append(near_pairs(count))
    if count > 2:
        sides.append(far_pairs(count))
    return sides


def rope_table(frame_total, row_total, col_total):
    time_dims = DH // 8
    space_dims = (DH - time_dims) // 2
    slower = 256.0 ** (-np.arange(0, time_dims, 2) / time_dims)
    faster = 256.0 ** (-np.arange(0, space_dims, 2) / space_dims)
    starts = (0, time_dims, time_dims + space_dims)
    pieces = []
    for total, rates, start in zip(
        (frame_total, row_total, col_total), (slower, faster, faster), starts
    ):
        padded = -(-total // 8) * 8
        piece = np.zeros((3, padded, DH), np.float32)
        angles = np.arange(padded)[:, None] * rates[None, :]
        stop = start + 2 * len(rates)
        piece[0, :, start:stop:2] = np.cos(angles)
        piece[0, :, start + 1 : stop : 2] = np.cos(angles)
        piece[1, :, start:stop:2] = -np.sin(angles)
        piece[2, :, start + 1 : stop : 2] = np.sin(angles)
        pieces.append(piece)
    begins = np.cumsum([0] + [piece.shape[1] for piece in pieces])
    return np.concatenate(pieces, axis=1), tuple(int(x) for x in begins[:3])


def local_table(plane, table_ref, begins, frames, rows, cols):
    frame_lo = begins[0] + lax.axis_index("ta") * frames
    row_lo = pl.multiple_of(begins[1] + lax.axis_index("ha") * rows, 8)
    col_lo = pl.multiple_of(begins[2] + lax.axis_index("wa") * cols, 8)
    row_part = table_ref[plane, pl.ds(row_lo, rows), :]
    col_part = table_ref[plane, pl.ds(col_lo, cols), :]
    grids = []
    for i in range(frames):
        lead = row_part + table_ref[plane, pl.ds(frame_lo + i, 1), :]
        grid = lead[:, None, :] + col_part[None, :, :]
        grids.append(grid.reshape(rows * cols, DH))
    return jnp.concatenate(grids, axis=0)


def turn(x, cosine, sin_even, sin_odd, sign):
    follow = pltpu.roll(x, DH - 1, 1)
    lead = pltpu.roll(x, 1, 1)
    return x * cosine + sign * (follow * sin_even + lead * sin_odd)


def head_slice(head):
    return slice(head * DH, (head + 1) * DH)


def rotate_kernel(
    dims, begins, q_hbm, k_hbm, v_hbm, g_hbm, table_hbm, kv_ref, qg_ref, rope_ref, q_ref, k_ref,
    table_ref, sems,
):
    moves = [
        (table_hbm, table_ref),
        (k_hbm, k_ref),
        (q_hbm, q_ref),
        (v_hbm, kv_ref.at[1]),
        (g_hbm, qg_ref.at[1]),
    ]
    copies = [pltpu.make_async_copy(*move, sems.at[i]) for i, move in enumerate(moves)]
    for copy in copies:
        copy.start()
    copies[0].wait()
    tables = [local_table(plane, table_ref, begins, *dims) for plane in range(3)]
    for plane in range(3):
        rope_ref[plane] = tables[plane]
    for copy, source, target in ((copies[1], k_ref, kv_ref), (copies[2], q_ref, qg_ref)):
        copy.wait()
        for head in range(HEADS):
            cut = head_slice(head)
            target[0, :, cut] = turn(source[:, cut].astype(F32), *tables, 1.0).astype(BF16)
    copies[3].wait()
    copies[4].wait()


def dot_nt(a, b):
    return lax.dot_general(a, b, (((1,), (1,)), ((), ())), preferred_element_type=F32)


def dot_nn(a, b):
    return lax.dot_general(a, b, (((1,), (0,)), ((), ())), preferred_element_type=F32)


def dot_tn(a, b):
    return lax.dot_general(a, b, (((0,), (0,)), ((), ())), preferred_element_type=F32)


def group_bias(flags, sizes):
    valid = None
    for axis, is_far in zip(("ha", "wa"), flags):
        if is_far:
            here = far_exists(axis, sizes[axis])
            valid = here if valid is None else valid & here
    return None if valid is None else jnp.where(valid, 0.0, NEGATIVE).astype(F32)


def forward_kernel(groups, sizes, cells, count, last, *refs):
    tile_count = sum(len(members) for _, members in groups)
    qg_refs = refs[:count]
    kv_refs = refs[count : count + tile_count]
    rest = refs[count + tile_count :]
    if last:
        first_ref, rest = rest[0], rest[1:]
    o_refs = rest[:count]
    stat_ref, key_buf, value_buf = rest[count:]
    at = 0
    spans = []
    for flags, members in groups:
        begin = at
        for member in members:
            key_buf[at : at + cells] = kv_refs[member][0]
            value_buf[at : at + cells] = kv_refs[member][1]
            at += cells
        spans.append((begin, at, group_bias(flags, sizes)))
    lane = lax.broadcasted_iota(jnp.int32, (count * cells, DH), 1)
    stat = jnp.zeros((count * cells, DH), F32)

    def scores_of(head):
        cut = head_slice(head)
        query = jnp.concatenate([ref[0, :, cut] for ref in qg_refs], axis=0)
        return [dot_nt(query, key_buf[lo:hi, cut]) for lo, hi, _ in spans]

    ahead = scores_of(0)
    for head in range(HEADS):
        cut = head_slice(head)
        scores = ahead
        if head + 1 < HEADS:
            ahead = scores_of(head + 1)
        best = None
        for raw, (_, _, bias) in zip(scores, spans):
            top = jnp.max(raw, axis=1, keepdims=True) * SCALE_LOG2
            if bias is not None:
                top = top + bias
            best = top if best is None else jnp.maximum(best, top)
        total = None
        out = None
        for raw, (lo, hi, bias) in zip(scores, spans):
            shift = best if bias is None else best - bias
            weights = jnp.exp2(raw * SCALE_LOG2 - shift)
            part = jnp.sum(weights, axis=1, keepdims=True)
            piece = dot_nn(weights.astype(BF16), value_buf[lo:hi, cut])
            total = part if total is None else total + part
            out = piece if out is None else out + piece
        out = out * (1.0 / total)
        grad = jnp.concatenate([ref[1, :, cut] for ref in qg_refs], axis=0)
        dotted = jnp.sum(out * grad.astype(F32), axis=1, keepdims=True)
        out = out.astype(BF16)
        for i, o_ref in enumerate(o_refs):
            o_ref[:, cut] = out[i * cells : (i + 1) * cells]
        stat = jnp.where(lane == head, best + jnp.log2(total), stat)
        stat = jnp.where(lane == HEADS + head, dotted, stat)
    if last:
        whole = jnp.concatenate([first_ref[...], stat], axis=0)
        stat_ref[...] = whole.T[: stat_ref.shape[0]]
    else:
        stat_ref[...] = stat


def seen_from(stat, distance, cells):
    if distance & 2:
        stat = pltpu.roll(stat, 2 * cells, 1)
    if distance & 1:
        lane = lax.broadcasted_iota(jnp.int32, stat.shape, 1)
        even = (lane < cells) | ((lane >= 2 * cells) & (lane < 3 * cells))
        stat = jnp.where(even, pltpu.roll(stat, 3 * cells, 1), pltpu.roll(stat, cells, 1))
    return stat


def merged_stats(stat_refs, cells):
    parts = [seen_from(ref[...], distance, cells) for distance, ref in enumerate(stat_refs)]
    top = functools.reduce(jnp.maximum, parts)
    shares = [jnp.exp2(part - top) for part in parts]
    total = functools.reduce(jnp.add, shares)
    lse = top + jnp.log2(total)
    shares = [share / total for share in shares]
    delta = functools.reduce(
        jnp.add,
        [share[:HEADS] * part[HEADS : 2 * HEADS] for share, part in zip(shares, parts)],
    )
    return lse[:HEADS], delta, shares


def backward_kernel(cols, grid_rows, sizes, cells, first, last, *refs):
    tile_count = grid_rows * len(cols)
    qg_refs, refs = refs[:4], refs[4:]
    kv_refs, refs = refs[:tile_count], refs[tile_count:]
    if first:
        stat_refs, refs = refs[:4], refs[4:]
    else:
        (lse_ref, delta_ref, dq_ref), refs = refs[:3], refs[3:]
    if last:
        dq_outs, refs = refs[:4], refs[4:]
    else:
        dq_out, refs = refs[0], refs[1:]
    if first:
        (lse_ref, delta_ref, share_ref), refs = refs[:3], refs[3:]
        lse, delta, shares = merged_stats(stat_refs, cells)
        lse_ref[...] = lse
        delta_ref[...] = delta
        rows = [shares[d][head : head + 1, : 2 * cells] for head in range(HEADS) for d in range(4)]
        wide = jnp.concatenate(rows + [jnp.zeros((DH - len(rows), 2 * cells), F32)], axis=0)
        share_ref[...] = wide.T[:cells]
    else:
        lse, delta = lse_ref[...], delta_ref[...]
    own_refs, rest_refs = [], []
    for col in cols:
        own_refs.append(refs[0].at[0] if col == NEAR else refs[0])
        rest_refs.append(refs[0].at[pl.ds(1, grid_rows - 1)] if col == NEAR else refs[1])
        refs = refs[1:] if col == NEAR else refs[2:]
    key_buf, value_buf = refs
    for i, ref in enumerate(kv_refs):
        key_buf[i * cells : (i + 1) * cells] = ref[0]
        value_buf[i * cells : (i + 1) * cells] = ref[1]
    span = grid_rows * cells
    blocks = [(head, slot) for head in range(HEADS) for slot in range(len(cols))]
    heads = []
    for head in range(HEADS):
        cut = head_slice(head)
        heads.append(
            [jnp.concatenate([ref[i, :, cut] for ref in qg_refs], axis=0) for i in range(2)]
        )

    def products_of(head, slot):
        cut = head_slice(head)
        at = slice(slot * span, (slot + 1) * span)
        queries, grads = heads[head]
        return dot_nt(key_buf[at, cut], queries), dot_nt(value_buf[at, cut], grads)

    ahead = products_of(*blocks[0])
    dqs = [None] * HEADS
    for i, (head, slot) in enumerate(blocks):
        raw, prob_grad = ahead
        if i + 1 < len(blocks):
            ahead = products_of(*blocks[i + 1])
        cut = head_slice(head)
        queries, grads = heads[head]
        probs = []
        for row in range(grid_rows):
            bias = group_bias((row == 2, cols[slot] == 2), sizes)
            shift = lse[head : head + 1]
            shift = shift if bias is None else shift - bias
            probs.append(jnp.exp2(raw[row * cells : (row + 1) * cells] * SCALE_LOG2 - shift))
        probs = jnp.concatenate(probs, axis=0)
        dscore = (probs * (prob_grad - delta[head : head + 1])).astype(BF16)
        dv = dot_nn(probs.astype(BF16), grads).astype(BF16)
        dk = (dot_nn(dscore, queries) * SCALE).astype(BF16)
        for which, part in enumerate((dk, dv)):
            own_refs[slot][which, :, cut] = part[:cells]
            for row in range(1, grid_rows):
                rest_refs[slot][row - 1, which, :, cut] = part[row * cells : (row + 1) * cells]
        part = dot_nn(key_buf[slot * span : (slot + 1) * span, cut].T, dscore)
        dqs[head] = part if dqs[head] is None else dqs[head] + part
    for head in range(HEADS):
        cut = head_slice(head)
        dq = dqs[head] if first else dqs[head] + dq_ref[head]
        if last:
            dq = (dq * SCALE).T.astype(BF16)
            for i, ref in enumerate(dq_outs):
                ref[:, cut] = dq[i * cells : (i + 1) * cells]
        else:
            dq_out[head] = dq


def finish_query_kernel(*refs):
    o_refs, dq_refs = refs[:4], refs[4:8]
    share_ref, rope_ref, out_ref, dq_out = refs[8:]
    for head in range(HEADS):
        cut = head_slice(head)
        outs = []
        for d, o_ref in zip((0, 3, 2, 1), o_refs):
            weight = share_ref[:, 4 * head + d : 4 * head + d + 1]
            outs.append(o_ref[:, cut].astype(F32) * weight)
        out_ref[:, cut] = functools.reduce(jnp.add, outs).astype(BF16)
        dq = functools.reduce(jnp.add, [ref[:, cut].astype(F32) for ref in dq_refs])
        dq_out[:, cut] = turn(dq, rope_ref[0], rope_ref[1], rope_ref[2], -1.0).astype(BF16)


def finish_key_kernel(count, *refs):
    near_ref, own_ref, rope_ref, dk_out, dv_out = refs[count:]
    part_refs = [*refs[:count], near_ref.at[0], own_ref]
    for head in range(HEADS):
        cut = head_slice(head)
        sums = []
        for which in range(2):
            terms = [ref[which, :, cut].astype(F32) for ref in part_refs]
            sums.append(functools.reduce(jnp.add, terms))
        dk_out[:, cut] = turn(
            sums[0], rope_ref[0], rope_ref[1], rope_ref[2], -1.0
        ).astype(BF16)
        dv_out[:, cut] = sums[1].astype(BF16)


def call(kernel, out_shape, args, flops=0, exps=0, scratch=(), space=pltpu.VMEM, limit=VMEM_LIMIT):
    shapes = jax.tree.leaves(out_shape)
    flops *= 8
    moved = sum(math.prod(x.shape) * x.dtype.itemsize for x in list(args) + shapes)
    return pl.pallas_call(
        kernel,
        out_shape=out_shape,
        in_specs=[pl.BlockSpec(memory_space=space)] * len(args),
        scratch_shapes=list(scratch),
        compiler_params=pltpu.CompilerParams(vmem_limit_bytes=limit),
        cost_estimate=pl.CostEstimate(flops=flops, bytes_accessed=moved, transcendentals=exps),
    )(*args)


def shards(query_in, key_in, value_in, cotangent):
    frames, rows, cols, chan = query_in.shape
    cells = frames * rows * cols
    sizes = {axis: lax.axis_size(axis) for axis in ("ta", "ha", "wa")}
    assert rows == TILE_H and cols == TILE_W and chan == HEADS * DH
    assert TILE_T % frames == 0 and frames * sizes["ta"] <= 2 * TILE_T
    assert sizes["ta"] == 4 and sizes["ha"] % 2 == 0 and sizes["wa"] % 2 == 0
    dims = (frames, rows, cols)
    table, begins = rope_table(frames * sizes["ta"], rows * sizes["ha"], cols * sizes["wa"])
    flat = [x.reshape(cells, chan) for x in (query_in, key_in, value_in, cotangent)]
    pair = jax.ShapeDtypeStruct((2, cells, chan), BF16)
    plain = jax.ShapeDtypeStruct((cells, chan), BF16)

    def real(*shape):
        return jax.ShapeDtypeStruct(shape, F32)

    with jax.named_scope("rotate"):
        kv, qg, rope = call(
            functools.partial(rotate_kernel, dims, begins),
            (pair, pair, real(3, cells, DH)),
            [pltpu.with_memory_space_constraint(x, pltpu.HBM) for x in (*flat, jnp.asarray(table))],
            scratch=[pltpu.VMEM((cells, chan), BF16)] * 2
            + [pltpu.VMEM(table.shape, F32), pltpu.SemaphoreType.DMA((5,))],
            space=pltpu.HBM,
        )

    def other_frames(x, distance):
        return lax.ppermute(x, "ta", [(i, i ^ distance) for i in range(sizes["ta"])])

    row_sides = side_pairs(sizes["ha"])
    col_sides = side_pairs(sizes["wa"])
    with jax.named_scope("halo"):
        kv_rows = [kv] + [lax.ppermute(kv, "ha", pairs) for pairs in row_sides]
        qg2 = other_frames(qg, 2)
        qg1 = other_frames(qg, 1)
        tiles = []
        for block in kv_rows:
            tiles.append([block] + [lax.ppermute(block, "wa", pairs) for pairs in col_sides])
        qg3 = other_frames(qg2, 1)
    grid_rows, grid_cols = 1 + len(row_sides), 1 + len(col_sides)
    flat_tiles = [tiles[row][col] for row in range(grid_rows) for col in range(grid_cols)]
    groups = {}
    for row in range(grid_rows):
        for col in range(grid_cols):
            groups.setdefault((row == 2, col == 2), []).append(row * grid_cols + col)
    groups = list(groups.items())

    key_count = len(flat_tiles) * cells
    product = 2 * cells * key_count * DH * HEADS

    def forward(blocks, first):
        count = len(blocks)
        stat = (count * cells, DH) if first is None else (8, 4 * cells)
        return call(
            functools.partial(forward_kernel, groups, sizes, cells, count, first is not None),
            (*[plain] * count, real(*stat)),
            (*blocks, *flat_tiles) + (() if first is None else (first,)),
            2 * product * count,
            cells * key_count * HEADS * count,
            [pltpu.VMEM((key_count, chan), BF16)] * 2,
        )

    with jax.named_scope("attend"):
        o0, o1, o2, first = forward((qg, qg1, qg2), None)
        o3, stat = forward((qg3,), first)
    with jax.named_scope("merge"):
        stats = [stat] + [other_frames(stat, d) for d in (1, 2, 3)]
        outs = [other_frames(o, d) for d, o in ((3, o3), (2, o2), (1, o1))]
        stats, outs[1:] = lax.optimization_barrier((stats, outs[1:]))

    queries = (qg, qg1, qg2, qg3)
    whole = jax.ShapeDtypeStruct((grid_rows, 2, cells, chan), BF16)
    rest_shape = jax.ShapeDtypeStruct((grid_rows - 1, 2, cells, chan), BF16)

    def gradients(which, carried):
        count = len(which)
        first, last = which[-1] == grid_cols - 1, which[0] == 0
        stat_outs = [real(HEADS, 4 * cells), real(HEADS, 4 * cells), real(cells, DH)]
        return call(
            functools.partial(backward_kernel, which, grid_rows, sizes, cells, first, last),
            (
                *([plain] * 4 if last else [real(HEADS, DH, 4 * cells)]),
                *(stat_outs if first else []),
                *[x for col in which for x in ([whole] if col == NEAR else [pair, rest_shape])],
            ),
            (*queries, *[tiles[row][col] for col in which for row in range(grid_rows)], *carried),
            20 * product * count // grid_cols,
            4 * cells * key_count * HEADS * count // grid_cols,
            [pltpu.VMEM((count * grid_rows * cells, chan), BF16)] * 2,
        )

    with jax.named_scope("gradients"):
        dq, lse, delta, shares, near, *far = gradients(tuple(range(1, grid_cols)), stats)
        near = lax.ppermute(near, "wa", col_sides[0])
        rests = [near[1:]]
        if far:
            rests.append(lax.ppermute(far[1], "wa", col_sides[1]))
        d0, d1, d2, d3, own, rest = gradients((0,), (lse, delta, dq))
    with jax.named_scope("return"):
        (d1, d2, d3), outs = lax.optimization_barrier(((d1, d2, d3), outs))
        dqs = [d0] + [other_frames(x, d) for d, x in ((2, d2), (3, d3), (1, d1))]
        row_parts = []
        for row, pairs in enumerate(row_sides):
            partial_sum = sum(x[row].astype(F32) for x in (rest, *rests)).astype(BF16)
            far, partial_sum = lax.optimization_barrier((far, partial_sum))
            row_parts.append(lax.ppermute(partial_sum, "ha", pairs))
        far_parts = [lax.ppermute(far[0], "wa", col_sides[1])] if far else []

    with jax.named_scope("finish"):
        attended, grad_query = call(
            finish_query_kernel, (plain, plain), (o0, *outs, *dqs, shares, rope), 10 * product
        )
        grad_key, grad_value = call(
            functools.partial(finish_key_kernel, len(row_parts) + len(far_parts)),
            (plain, plain),
            (*row_parts, *far_parts, near, own, rope),
        )
    return tuple(x.reshape(query_in.shape) for x in (attended, grad_query, grad_key, grad_value))


def solution(mesh):
    spec = P("ta", "ha", "wa", None)
    return jax.shard_map(
        shards, mesh=mesh, in_specs=(spec,) * 4, out_specs=(spec,) * 4, check_vma=False
    )
```

```python
import functools
import math

import jax
import jax.numpy as jnp
import numpy as np
from jax import lax
from jax.experimental import pallas as pl
from jax.experimental.pallas import tpu as pltpu
from jax.sharding import PartitionSpec as P

DH = 128
HEADS = 2
TILE_T = 6
TILE_H = 8
TILE_W = 8

NEGATIVE = -1e30
SCALE = DH**-0.5
SCALE_LOG2 = SCALE * math.log2(math.e)
F32 = jnp.float32
BF16 = jnp.bfloat16
VMEM_LIMIT = 48 * 1024 * 1024


def near_pairs(count):
    return [(i, i ^ 1) for i in range(count)]


def far_pairs(count):
    pairs = []
    for i in range(count):
        j = i + 1 if i % 2 else i - 1
        pairs.append((i, j if 0 <= j < count else i))
    return pairs


def far_exists(axis, count):
    pos = lax.axis_index(axis)
    other = jnp.where(pos % 2 == 1, pos + 1, pos - 1)
    return (other >= 0) & (other < count)


def side_pairs(count):
    sides = []
    if count > 1:
        sides.append(near_pairs(count))
    if count > 2:
        sides.append(far_pairs(count))
    return sides


def rope_table(frame_total, row_total, col_total):
    time_dims = DH // 8
    space_dims = (DH - time_dims) // 2
    slower = 256.0 ** (-np.arange(0, time_dims, 2) / time_dims)
    faster = 256.0 ** (-np.arange(0, space_dims, 2) / space_dims)
    starts = (0, time_dims, time_dims + space_dims)
    pieces = []
    for total, rates, start in zip(
        (frame_total, row_total, col_total), (slower, faster, faster), starts
    ):
        padded = -(-total // 8) * 8
        piece = np.zeros((3, padded, DH), np.float32)
        angles = np.arange(padded)[:, None] * rates[None, :]
        stop = start + 2 * len(rates)
        piece[0, :, start:stop:2] = np.cos(angles)
        piece[0, :, start + 1 : stop : 2] = np.cos(angles)
        piece[1, :, start:stop:2] = -np.sin(angles)
        piece[2, :, start + 1 : stop : 2] = np.sin(angles)
        pieces.append(piece)
    begins = np.cumsum([0] + [piece.shape[1] for piece in pieces])
    return np.concatenate(pieces, axis=1), tuple(int(x) for x in begins[:3])


def local_table(plane, table_ref, begins, frames, rows, cols):
    frame_lo = begins[0] + lax.axis_index("ta") * frames
    row_lo = pl.multiple_of(begins[1] + lax.axis_index("ha") * rows, 8)
    col_lo = pl.multiple_of(begins[2] + lax.axis_index("wa") * cols, 8)
    row_part = table_ref[plane, pl.ds(row_lo, rows), :]
    col_part = table_ref[plane, pl.ds(col_lo, cols), :]
    grids = []
    for i in range(frames):
        lead = row_part + table_ref[plane, pl.ds(frame_lo + i, 1), :]
        grid = lead[:, None, :] + col_part[None, :, :]
        grids.append(grid.reshape(rows * cols, DH))
    return jnp.concatenate(grids, axis=0)


def turn(x, cosine, sin_even, sin_odd, sign):
    follow = pltpu.roll(x, DH - 1, 1)
    lead = pltpu.roll(x, 1, 1)
    return x * cosine + sign * (follow * sin_even + lead * sin_odd)


def head_slice(head):
    return slice(head * DH, (head + 1) * DH)


def rotate_kernel(
    dims, begins, q_hbm, k_hbm, v_hbm, g_hbm, table_hbm, kv_ref, qg_ref, rope_ref, q_ref, k_ref,
    table_ref, sems,
):
    moves = [
        (table_hbm, table_ref),
        (k_hbm, k_ref),
        (q_hbm, q_ref),
        (v_hbm, kv_ref.at[1]),
        (g_hbm, qg_ref.at[1]),
    ]
    copies = [pltpu.make_async_copy(*move, sems.at[i]) for i, move in enumerate(moves)]
    for copy in copies:
        copy.start()
    copies[0].wait()
    tables = [local_table(plane, table_ref, begins, *dims) for plane in range(3)]
    for plane in range(3):
        rope_ref[plane] = tables[plane]
    for copy, source, target in ((copies[1], k_ref, kv_ref), (copies[2], q_ref, qg_ref)):
        copy.wait()
        for head in range(HEADS):
            cut = head_slice(head)
            target[0, :, cut] = turn(source[:, cut].astype(F32), *tables, 1.0).astype(BF16)
    copies[3].wait()
    copies[4].wait()


def dot_nt(a, b):
    return lax.dot_general(a, b, (((1,), (1,)), ((), ())), preferred_element_type=F32)


def dot_nn(a, b):
    return lax.dot_general(a, b, (((1,), (0,)), ((), ())), preferred_element_type=F32)


def dot_tn(a, b):
    return lax.dot_general(a, b, (((0,), (0,)), ((), ())), preferred_element_type=F32)


def group_bias(flags, sizes):
    valid = None
    for axis, is_far in zip(("ha", "wa"), flags):
        if is_far:
            here = far_exists(axis, sizes[axis])
            valid = here if valid is None else valid & here
    return None if valid is None else jnp.where(valid, 0.0, NEGATIVE).astype(F32)


def forward_kernel(groups, sizes, cells, count, last, *refs):
    tile_count = sum(len(members) for _, members in groups)
    qg_refs = refs[:count]
    kv_refs = refs[count : count + tile_count]
    rest = refs[count + tile_count :]
    if last:
        first_ref, rest = rest[0], rest[1:]
    o_refs = rest[:count]
    stat_ref, key_buf, value_buf = rest[count:]
    at = 0
    spans = []
    for flags, members in groups:
        begin = at
        for member in members:
            key_buf[at : at + cells] = kv_refs[member][0]
            value_buf[at : at + cells] = kv_refs[member][1]
            at += cells
        spans.append((begin, at, group_bias(flags, sizes)))
    lane = lax.broadcasted_iota(jnp.int32, (count * cells, DH), 1)
    stat = jnp.zeros((count * cells, DH), F32)

    def scores_of(head):
        cut = head_slice(head)
        query = jnp.concatenate([ref[0, :, cut] for ref in qg_refs], axis=0)
        return [dot_nt(query, key_buf[lo:hi, cut]) for lo, hi, _ in spans]

    ahead = scores_of(0)
    for head in range(HEADS):
        cut = head_slice(head)
        scores = ahead
        if head + 1 < HEADS:
            ahead = scores_of(head + 1)
        best = None
        for raw, (_, _, bias) in zip(scores, spans):
            top = jnp.max(raw, axis=1, keepdims=True) * SCALE_LOG2
            if bias is not None:
                top = top + bias
            best = top if best is None else jnp.maximum(best, top)
        total = None
        out = None
        for raw, (lo, hi, bias) in zip(scores, spans):
            shift = best if bias is None else best - bias
            weights = jnp.exp2(raw * SCALE_LOG2 - shift)
            part = jnp.sum(weights, axis=1, keepdims=True)
            piece = dot_nn(weights.astype(BF16), value_buf[lo:hi, cut])
            total = part if total is None else total + part
            out = piece if out is None else out + piece
        out = out * (1.0 / total)
        grad = jnp.concatenate([ref[1, :, cut] for ref in qg_refs], axis=0)
        dotted = jnp.sum(out * grad.astype(F32), axis=1, keepdims=True)
        out = out.astype(BF16)
        for i, o_ref in enumerate(o_refs):
            o_ref[:, cut] = out[i * cells : (i + 1) * cells]
        stat = jnp.where(lane == head, best + jnp.log2(total), stat)
        stat = jnp.where(lane == HEADS + head, dotted, stat)
    if last:
        whole = jnp.concatenate([first_ref[...], stat], axis=0)
        stat_ref[...] = whole.T[: stat_ref.shape[0]]
    else:
        stat_ref[...] = stat


def seen_from(stat, distance, cells):
    if distance & 2:
        stat = pltpu.roll(stat, 2 * cells, 1)
    if distance & 1:
        lane = lax.broadcasted_iota(jnp.int32, stat.shape, 1)
        even = (lane < cells) | ((lane >= 2 * cells) & (lane < 3 * cells))
        stat = jnp.where(even, pltpu.roll(stat, 3 * cells, 1), pltpu.roll(stat, cells, 1))
    return stat


def merged_stats(stat_refs, cells):
    parts = [seen_from(ref[...], distance, cells) for distance, ref in enumerate(stat_refs)]
    top = functools.reduce(jnp.maximum, parts)
    shares = [jnp.exp2(part - top) for part in parts]
    total = functools.reduce(jnp.add, shares)
    lse = top + jnp.log2(total)
    shares = [share / total for share in shares]
    delta = functools.reduce(
        jnp.add,
        [share[:HEADS] * part[HEADS : 2 * HEADS] for share, part in zip(shares, parts)],
    )
    return lse[:HEADS], delta, shares


def backward_kernel(cols, grid_rows, sizes, cells, first, last, *refs):
    tile_count = grid_rows * len(cols)
    qg_refs = refs[:4]
    kv_refs = refs[4 : 4 + tile_count]
    rest = refs[4 + tile_count :]
    if first:
        stat_refs, rest = rest[:4], rest[4:]
    else:
        (lse_ref, delta_ref, dq_ref), rest = rest[:3], rest[3:]
    if last:
        dq_outs, rest = rest[:4], rest[4:]
    else:
        dq_out, rest = rest[0], rest[1:]
    if first:
        (lse_ref, delta_ref, share_ref), rest = rest[:3], rest[3:]
        lse, delta, shares = merged_stats(stat_refs, cells)
        lse_ref[...] = lse
        delta_ref[...] = delta
        rows = [shares[d][head : head + 1, : 2 * cells] for head in range(HEADS) for d in range(4)]
        wide = jnp.concatenate(rows + [jnp.zeros((DH - len(rows), 2 * cells), F32)], axis=0)
        share_ref[...] = wide.T[:cells]
    else:
        lse, delta = lse_ref[...], delta_ref[...]
    col_refs = rest[: len(cols)]
    key_buf, value_buf = rest[len(cols) :]

    span = grid_rows * cells
    for i, ref in enumerate(kv_refs):
        key_buf[i * cells : (i + 1) * cells] = ref[0]
        value_buf[i * cells : (i + 1) * cells] = ref[1]
    blocks = [(head, slot) for head in range(HEADS) for slot in range(len(cols))]

    def products_of(head, slot):
        cut = head_slice(head)
        at = slice(slot * span, (slot + 1) * span)
        queries = jnp.concatenate([ref[0, :, cut] for ref in qg_refs], axis=0)
        grads = jnp.concatenate([ref[1, :, cut] for ref in qg_refs], axis=0)
        raw = dot_nt(key_buf[at, cut], queries)
        return raw, dot_nt(value_buf[at, cut], grads), queries, grads

    dqs = [None] * HEADS
    ahead = products_of(*blocks[0])
    for i, (head, slot) in enumerate(blocks):
        raw, prob_grad, queries, grads = ahead
        if i + 1 < len(blocks):
            ahead = products_of(*blocks[i + 1])
        cut = head_slice(head)
        probs = []
        for row in range(grid_rows):
            bias = group_bias((row == 2, cols[slot] == 2), sizes)
            shift = lse[head : head + 1]
            shift = shift if bias is None else shift - bias
            probs.append(jnp.exp2(raw[row * cells : (row + 1) * cells] * SCALE_LOG2 - shift))
        probs = jnp.concatenate(probs, axis=0)
        dscore = (probs * (prob_grad - delta[head : head + 1])).astype(BF16)
        dv = dot_nn(probs.astype(BF16), grads).astype(BF16)
        dk = (dot_nn(dscore, queries) * SCALE).astype(BF16)
        for row in range(grid_rows):
            at = slice(row * cells, (row + 1) * cells)
            col_refs[slot][row, 0, :, cut] = dk[at]
            col_refs[slot][row, 1, :, cut] = dv[at]
        part = dot_nn(key_buf[slot * span : (slot + 1) * span, cut].T, dscore)
        dqs[head] = part if dqs[head] is None else dqs[head] + part
    for head in range(HEADS):
        cut = head_slice(head)
        dq = dqs[head] if first else dqs[head] + dq_ref[head]
        if last:
            dq = (dq * SCALE).T.astype(BF16)
            for i, ref in enumerate(dq_outs):
                ref[:, cut] = dq[i * cells : (i + 1) * cells]
        else:
            dq_out[head] = dq


def finish_query_kernel(*refs):
    o_refs, dq_refs = refs[:4], refs[4:8]
    share_ref, rope_ref, out_ref, dq_out = refs[8:]
    for head in range(HEADS):
        cut = head_slice(head)
        outs = []
        for d, o_ref in zip((0, 3, 2, 1), o_refs):
            weight = share_ref[:, 4 * head + d : 4 * head + d + 1]
            outs.append(o_ref[:, cut].astype(F32) * weight)
        out_ref[:, cut] = functools.reduce(jnp.add, outs).astype(BF16)
        dq = functools.reduce(jnp.add, [ref[:, cut].astype(F32) for ref in dq_refs])
        dq_out[:, cut] = turn(dq, rope_ref[0], rope_ref[1], rope_ref[2], -1.0).astype(BF16)


def finish_key_kernel(cols, rows, *refs):
    col_refs, row_refs = refs[:cols], refs[cols : cols + rows]
    rope_ref, dk_out, dv_out = refs[cols + rows :]
    for head in range(HEADS):
        cut = head_slice(head)
        sums = []
        for which in range(2):
            terms = [ref[0, which, :, cut].astype(F32) for ref in col_refs]
            terms += [ref[which, :, cut].astype(F32) for ref in row_refs]
            sums.append(functools.reduce(jnp.add, terms))
        dk_out[:, cut] = turn(
            sums[0], rope_ref[0], rope_ref[1], rope_ref[2], -1.0
        ).astype(BF16)
        dv_out[:, cut] = sums[1].astype(BF16)


def call(kernel, out_shape, args, flops=0, exps=0, scratch=(), space=pltpu.VMEM, limit=VMEM_LIMIT):
    shapes = jax.tree.leaves(out_shape)
    flops *= 8
    moved = sum(math.prod(x.shape) * x.dtype.itemsize for x in list(args) + shapes)
    return pl.pallas_call(
        kernel,
        out_shape=out_shape,
        in_specs=[pl.BlockSpec(memory_space=space)] * len(args),
        scratch_shapes=list(scratch),
        compiler_params=pltpu.CompilerParams(vmem_limit_bytes=limit),
        cost_estimate=pl.CostEstimate(flops=flops, bytes_accessed=moved, transcendentals=exps),
    )(*args)


def shards(query_in, key_in, value_in, cotangent):
    frames, rows, cols, chan = query_in.shape
    cells = frames * rows * cols
    sizes = {axis: lax.axis_size(axis) for axis in ("ta", "ha", "wa")}
    assert rows == TILE_H and cols == TILE_W and chan == HEADS * DH
    assert TILE_T % frames == 0 and frames * sizes["ta"] <= 2 * TILE_T
    assert sizes["ta"] == 4 and sizes["ha"] % 2 == 0 and sizes["wa"] % 2 == 0
    dims = (frames, rows, cols)
    table, begins = rope_table(frames * sizes["ta"], rows * sizes["ha"], cols * sizes["wa"])
    flat = [x.reshape(cells, chan) for x in (query_in, key_in, value_in, cotangent)]
    pair = jax.ShapeDtypeStruct((2, cells, chan), BF16)
    plain = jax.ShapeDtypeStruct((cells, chan), BF16)

    def real(*shape):
        return jax.ShapeDtypeStruct(shape, F32)

    with jax.named_scope("rotate"):
        kv, qg, rope = call(
            functools.partial(rotate_kernel, dims, begins),
            (pair, pair, real(3, cells, DH)),
            [pltpu.with_memory_space_constraint(x, pltpu.HBM) for x in (*flat, jnp.asarray(table))],
            scratch=[pltpu.VMEM((cells, chan), BF16)] * 2
            + [pltpu.VMEM(table.shape, F32), pltpu.SemaphoreType.DMA((5,))],
            space=pltpu.HBM,
        )

    def other_frames(x, distance):
        return lax.ppermute(x, "ta", [(i, i ^ distance) for i in range(sizes["ta"])])

    row_sides = side_pairs(sizes["ha"])
    col_sides = side_pairs(sizes["wa"])
    with jax.named_scope("halo"):
        kv_rows = [kv] + [lax.ppermute(kv, "ha", pairs) for pairs in row_sides]
        qg2 = other_frames(qg, 2)
        qg1 = other_frames(qg, 1)
        tiles = []
        for block in kv_rows:
            tiles.append([block] + [lax.ppermute(block, "wa", pairs) for pairs in col_sides])
        qg3 = other_frames(qg2, 1)
    grid_rows, grid_cols = 1 + len(row_sides), 1 + len(col_sides)
    flat_tiles = [tiles[row][col] for row in range(grid_rows) for col in range(grid_cols)]
    groups = {}
    for row in range(grid_rows):
        for col in range(grid_cols):
            groups.setdefault((row == 2, col == 2), []).append(row * grid_cols + col)
    groups = list(groups.items())

    key_count = len(flat_tiles) * cells
    product = 2 * cells * key_count * DH * HEADS

    def forward(blocks, first):
        count = len(blocks)
        stat = (count * cells, DH) if first is None else (8, 4 * cells)
        return call(
            functools.partial(forward_kernel, groups, sizes, cells, count, first is not None),
            (*[plain] * count, real(*stat)),
            (*blocks, *flat_tiles) + (() if first is None else (first,)),
            2 * product * count,
            cells * key_count * HEADS * count,
            [pltpu.VMEM((key_count, chan), BF16)] * 2,
        )

    with jax.named_scope("attend"):
        o0, o1, o2, first = forward((qg, qg1, qg2), None)
        o3, stat = forward((qg3,), first)
    with jax.named_scope("merge"):
        outs = [other_frames(o, d) for d, o in ((3, o3), (2, o2), (1, o1))]
        stat_near, outs[1:] = lax.optimization_barrier((stat, outs[1:]))
        stats = [stat, other_frames(stat_near, 1), other_frames(stat, 2), other_frames(stat, 3)]

    queries = (qg, qg1, qg2, qg3)
    col_shape = jax.ShapeDtypeStruct((grid_rows, 2, cells, chan), BF16)

    def gradients(which, carried):
        count = len(which)
        first, last = which[-1] == grid_cols - 1, which[0] == 0
        stat_outs = [real(HEADS, 4 * cells), real(HEADS, 4 * cells), real(cells, DH)]
        return call(
            functools.partial(backward_kernel, which, grid_rows, sizes, cells, first, last),
            (
                *([plain] * 4 if last else [real(HEADS, DH, 4 * cells)]),
                *(stat_outs if first else []),
                *[col_shape] * count,
            ),
            (*queries, *[tiles[row][col] for col in which for row in range(grid_rows)], *carried),
            20 * product * count // grid_cols,
            4 * cells * key_count * HEADS * count // grid_cols,
            [pltpu.VMEM((count * grid_rows * cells, chan), BF16)] * 2,
        )

    with jax.named_scope("gradients"):
        dq, lse, delta, shares, *sides = gradients(tuple(range(1, grid_cols)), stats)
        sides = [lax.ppermute(x, "wa", pairs) for x, pairs in zip(sides, col_sides)]
        d0, d1, d2, d3, own = gradients((0,), (lse, delta, dq))
    with jax.named_scope("return"):
        (d1, d2, d3), outs = lax.optimization_barrier(((d1, d2, d3), outs))
        col_parts = [own, *sides]
        dqs = [d0] + [other_frames(x, d) for d, x in ((3, d3), (2, d2), (1, d1))]
        row_parts = []
        for row, pairs in enumerate(row_sides, start=1):
            partial_sum = sum(x[row].astype(F32) for x in col_parts).astype(BF16)
            row_parts.append(lax.ppermute(partial_sum, "ha", pairs))

    with jax.named_scope("finish"):
        attended, grad_query = call(
            finish_query_kernel, (plain, plain), (o0, *outs, *dqs, shares, rope), 10 * product
        )
        grad_key, grad_value = call(
            functools.partial(finish_key_kernel, grid_cols, len(row_parts)),
            (plain, plain),
            (*col_parts, *row_parts, rope),
        )
    return tuple(x.reshape(query_in.shape) for x in (attended, grad_query, grad_key, grad_value))


def solution(mesh):
    spec = P("ta", "ha", "wa", None)
    return jax.shard_map(
        shards, mesh=mesh, in_specs=(spec,) * 4, out_specs=(spec,) * 4, check_vma=False
    )
```

```python
import functools
import math

import jax
import jax.numpy as jnp
import numpy as np
from jax import lax
from jax.experimental import pallas as pl
from jax.experimental.pallas import tpu as pltpu
from jax.sharding import PartitionSpec as P

DH = 128
HEADS = 2
TILE_T = 6
TILE_H = 8
TILE_W = 8

NEGATIVE = -1e30
SCALE = DH**-0.5
SCALE_LOG2 = SCALE * math.log2(math.e)
F32 = jnp.float32
BF16 = jnp.bfloat16
STAT_ORDER = (0, 1, 3, 2)
VMEM_LIMIT = 48 * 1024 * 1024


def near_pairs(count):
    return [(i, i ^ 1) for i in range(count)]


def far_pairs(count):
    pairs = []
    for i in range(count):
        j = i + 1 if i % 2 else i - 1
        pairs.append((i, j if 0 <= j < count else i))
    return pairs


def far_exists(axis, count):
    pos = lax.axis_index(axis)
    other = jnp.where(pos % 2 == 1, pos + 1, pos - 1)
    return (other >= 0) & (other < count)


def side_pairs(count):
    sides = []
    if count > 1:
        sides.append(near_pairs(count))
    if count > 2:
        sides.append(far_pairs(count))
    return sides


def rope_table(frame_total, row_total, col_total):
    time_dims = DH // 8
    space_dims = (DH - time_dims) // 2
    slower = 256.0 ** (-np.arange(0, time_dims, 2) / time_dims)
    faster = 256.0 ** (-np.arange(0, space_dims, 2) / space_dims)
    starts = (0, time_dims, time_dims + space_dims)
    pieces = []
    for total, rates, start in zip(
        (frame_total, row_total, col_total), (slower, faster, faster), starts
    ):
        padded = -(-total // 8) * 8
        piece = np.zeros((3, padded, DH), np.float32)
        angles = np.arange(padded)[:, None] * rates[None, :]
        stop = start + 2 * len(rates)
        piece[0, :, start:stop:2] = np.cos(angles)
        piece[0, :, start + 1 : stop : 2] = np.cos(angles)
        piece[1, :, start:stop:2] = -np.sin(angles)
        piece[2, :, start + 1 : stop : 2] = np.sin(angles)
        pieces.append(piece)
    begins = np.cumsum([0] + [piece.shape[1] for piece in pieces])
    return np.concatenate(pieces, axis=1), tuple(int(x) for x in begins[:3])


def local_table(plane, table_ref, begins, frames, rows, cols):
    frame_lo = begins[0] + lax.axis_index("ta") * frames
    row_lo = pl.multiple_of(begins[1] + lax.axis_index("ha") * rows, 8)
    col_lo = pl.multiple_of(begins[2] + lax.axis_index("wa") * cols, 8)
    row_part = table_ref[plane, pl.ds(row_lo, rows), :]
    col_part = table_ref[plane, pl.ds(col_lo, cols), :]
    grids = []
    for i in range(frames):
        lead = row_part + table_ref[plane, pl.ds(frame_lo + i, 1), :]
        grid = lead[:, None, :] + col_part[None, :, :]
        grids.append(grid.reshape(rows * cols, DH))
    return jnp.concatenate(grids, axis=0)


def turn(x, cosine, sin_even, sin_odd, sign):
    follow = pltpu.roll(x, DH - 1, 1)
    lead = pltpu.roll(x, 1, 1)
    return x * cosine + sign * (follow * sin_even + lead * sin_odd)


def head_slice(head):
    return slice(head * DH, (head + 1) * DH)


def rotate_kernel(
    dims, begins, q_hbm, k_hbm, v_hbm, g_hbm, table_hbm, kv_ref, qg_ref, rope_ref, q_ref, k_ref,
    table_ref, sems,
):
    moves = [
        (table_hbm, table_ref),
        (k_hbm, k_ref),
        (q_hbm, q_ref),
        (v_hbm, kv_ref.at[1]),
        (g_hbm, qg_ref.at[1]),
    ]
    copies = [pltpu.make_async_copy(*move, sems.at[i]) for i, move in enumerate(moves)]
    for copy in copies:
        copy.start()
    copies[0].wait()
    tables = [local_table(plane, table_ref, begins, *dims) for plane in range(3)]
    for plane in range(3):
        rope_ref[plane] = tables[plane]
    for copy, source, target in ((copies[1], k_ref, kv_ref), (copies[2], q_ref, qg_ref)):
        copy.wait()
        for head in range(HEADS):
            cut = head_slice(head)
            target[0, :, cut] = turn(source[:, cut].astype(F32), *tables, 1.0).astype(BF16)
    copies[3].wait()
    copies[4].wait()


def dot_nt(a, b):
    return lax.dot_general(a, b, (((1,), (1,)), ((), ())), preferred_element_type=F32)


def dot_nn(a, b):
    return lax.dot_general(a, b, (((1,), (0,)), ((), ())), preferred_element_type=F32)


def dot_tn(a, b):
    return lax.dot_general(a, b, (((0,), (0,)), ((), ())), preferred_element_type=F32)


def group_bias(flags, sizes):
    valid = None
    for axis, is_far in zip(("ha", "wa"), flags):
        if is_far:
            here = far_exists(axis, sizes[axis])
            valid = here if valid is None else valid & here
    return None if valid is None else jnp.where(valid, 0.0, NEGATIVE).astype(F32)


def forward_kernel(groups, sizes, cells, count, last, *refs):
    tile_count = sum(len(members) for _, members in groups)
    qg_refs = refs[:count]
    kv_refs = refs[count : count + tile_count]
    rest = refs[count + tile_count :]
    if last:
        first_ref, rest = rest[0], rest[1:]
    o_refs = rest[:count]
    stat_ref, key_buf, value_buf = rest[count:]
    at = 0
    spans = []
    for flags, members in groups:
        begin = at
        for member in members:
            key_buf[at : at + cells] = kv_refs[member][0]
            value_buf[at : at + cells] = kv_refs[member][1]
            at += cells
        spans.append((begin, at, group_bias(flags, sizes)))
    lane = lax.broadcasted_iota(jnp.int32, (count * cells, DH), 1)
    stat = jnp.zeros((count * cells, DH), F32)

    def scores_of(head):
        cut = head_slice(head)
        query = jnp.concatenate([ref[0, :, cut] for ref in qg_refs], axis=0)
        return [dot_nt(query, key_buf[lo:hi, cut]) for lo, hi, _ in spans]

    ahead = scores_of(0)
    for head in range(HEADS):
        cut = head_slice(head)
        scores = ahead
        if head + 1 < HEADS:
            ahead = scores_of(head + 1)
        best = None
        for raw, (_, _, bias) in zip(scores, spans):
            top = jnp.max(raw, axis=1, keepdims=True) * SCALE_LOG2
            if bias is not None:
                top = top + bias
            best = top if best is None else jnp.maximum(best, top)
        total = None
        out = None
        for raw, (lo, hi, bias) in zip(scores, spans):
            shift = best if bias is None else best - bias
            weights = jnp.exp2(raw * SCALE_LOG2 - shift)
            part = jnp.sum(weights, axis=1, keepdims=True)
            piece = dot_nn(weights.astype(BF16), value_buf[lo:hi, cut])
            total = part if total is None else total + part
            out = piece if out is None else out + piece
        out = out * (1.0 / total)
        grad = jnp.concatenate([ref[1, :, cut] for ref in qg_refs], axis=0)
        dotted = jnp.sum(out * grad.astype(F32), axis=1, keepdims=True)
        out = out.astype(BF16)
        for i, o_ref in enumerate(o_refs):
            o_ref[:, cut] = out[i * cells : (i + 1) * cells]
        stat = jnp.where(lane == head, best + jnp.log2(total), stat)
        stat = jnp.where(lane == HEADS + head, dotted, stat)
    if last:
        whole = jnp.concatenate([first_ref[...], stat], axis=0)
        stat_ref[...] = whole.T[: stat_ref.shape[0]]
    else:
        stat_ref[...] = stat


def seen_from(stat, distance, cells):
    if distance & 2:
        stat = pltpu.roll(stat, 2 * cells, 1)
    if distance & 1:
        lane = lax.broadcasted_iota(jnp.int32, stat.shape, 1)
        even = (lane < cells) | ((lane >= 2 * cells) & (lane < 3 * cells))
        stat = jnp.where(even, pltpu.roll(stat, 3 * cells, 1), pltpu.roll(stat, cells, 1))
    return stat


def merged_stats(stat_refs, cells):
    refs = dict(zip(STAT_ORDER, stat_refs))
    parts = [seen_from(refs[distance][...], distance, cells) for distance in range(4)]
    top = functools.reduce(jnp.maximum, parts)
    shares = [jnp.exp2(part - top) for part in parts]
    total = functools.reduce(jnp.add, shares)
    lse = top + jnp.log2(total)
    shares = [share / total for share in shares]
    delta = functools.reduce(
        jnp.add,
        [share[:HEADS] * part[HEADS : 2 * HEADS] for share, part in zip(shares, parts)],
    )
    return lse[:HEADS], delta, shares


def backward_kernel(cols, grid_rows, sizes, cells, first, last, *refs):
    tile_count = grid_rows * len(cols)
    qg_refs = refs[:4]
    kv_refs = refs[4 : 4 + tile_count]
    rest = refs[4 + tile_count :]
    if first:
        stat_refs, rest = rest[:4], rest[4:]
    else:
        (lse_ref, delta_ref, dq_ref), rest = rest[:3], rest[3:]
    if last:
        dq_outs, rest = rest[:4], rest[4:]
    else:
        dq_out, rest = rest[0], rest[1:]
    if first:
        (lse_ref, delta_ref, share_ref), rest = rest[:3], rest[3:]
        lse, delta, shares = merged_stats(stat_refs, cells)
        lse_ref[...] = lse
        delta_ref[...] = delta
        rows = [shares[d][head : head + 1, : 2 * cells] for head in range(HEADS) for d in range(4)]
        wide = jnp.concatenate(rows + [jnp.zeros((DH - len(rows), 2 * cells), F32)], axis=0)
        share_ref[...] = wide.T[:cells]
    else:
        lse, delta = lse_ref[...], delta_ref[...]
    col_refs = rest[: len(cols)]
    key_buf, value_buf = rest[len(cols) :]

    span = grid_rows * cells
    for i, ref in enumerate(kv_refs):
        key_buf[i * cells : (i + 1) * cells] = ref[0]
        value_buf[i * cells : (i + 1) * cells] = ref[1]
    blocks = [(head, slot) for head in range(HEADS) for slot in range(len(cols))]

    def products_of(head, slot):
        cut = head_slice(head)
        at = slice(slot * span, (slot + 1) * span)
        queries = jnp.concatenate([ref[0, :, cut] for ref in qg_refs], axis=0)
        grads = jnp.concatenate([ref[1, :, cut] for ref in qg_refs], axis=0)
        raw = dot_nt(key_buf[at, cut], queries)
        return raw, dot_nt(value_buf[at, cut], grads), queries, grads

    dqs = [None] * HEADS
    ahead = products_of(*blocks[0])
    for i, (head, slot) in enumerate(blocks):
        raw, prob_grad, queries, grads = ahead
        if i + 1 < len(blocks):
            ahead = products_of(*blocks[i + 1])
        cut = head_slice(head)
        probs = []
        for row in range(grid_rows):
            bias = group_bias((row == 2, cols[slot] == 2), sizes)
            shift = lse[head : head + 1]
            shift = shift if bias is None else shift - bias
            probs.append(jnp.exp2(raw[row * cells : (row + 1) * cells] * SCALE_LOG2 - shift))
        probs = jnp.concatenate(probs, axis=0)
        dscore = (probs * (prob_grad - delta[head : head + 1])).astype(BF16)
        dv = dot_nn(probs.astype(BF16), grads).astype(BF16)
        dk = (dot_nn(dscore, queries) * SCALE).astype(BF16)
        for row in range(grid_rows):
            at = slice(row * cells, (row + 1) * cells)
            col_refs[slot][row, 0, :, cut] = dk[at]
            col_refs[slot][row, 1, :, cut] = dv[at]
        part = dot_nn(key_buf[slot * span : (slot + 1) * span, cut].T, dscore)
        dqs[head] = part if dqs[head] is None else dqs[head] + part
    for head in range(HEADS):
        cut = head_slice(head)
        dq = dqs[head] if first else dqs[head] + dq_ref[head]
        if last:
            dq = (dq * SCALE).T.astype(BF16)
            for i, ref in enumerate(dq_outs):
                ref[:, cut] = dq[i * cells : (i + 1) * cells]
        else:
            dq_out[head] = dq


def finish_query_kernel(*refs):
    o_refs, dq_refs = refs[:4], refs[4:8]
    share_ref, rope_ref, out_ref, dq_out = refs[8:]
    for head in range(HEADS):
        cut = head_slice(head)
        outs = []
        for d, o_ref in zip((0, 3, 2, 1), o_refs):
            weight = share_ref[:, 4 * head + d : 4 * head + d + 1]
            outs.append(o_ref[:, cut].astype(F32) * weight)
        out_ref[:, cut] = functools.reduce(jnp.add, outs).astype(BF16)
        dq = functools.reduce(jnp.add, [ref[:, cut].astype(F32) for ref in dq_refs])
        dq_out[:, cut] = turn(dq, rope_ref[0], rope_ref[1], rope_ref[2], -1.0).astype(BF16)


def finish_key_kernel(cols, rows, *refs):
    col_refs, row_refs = refs[:cols], refs[cols : cols + rows]
    rope_ref, dk_out, dv_out = refs[cols + rows :]
    for head in range(HEADS):
        cut = head_slice(head)
        sums = []
        for which in range(2):
            terms = [ref[0, which, :, cut].astype(F32) for ref in col_refs]
            terms += [ref[which, :, cut].astype(F32) for ref in row_refs]
            sums.append(functools.reduce(jnp.add, terms))
        dk_out[:, cut] = turn(
            sums[0], rope_ref[0], rope_ref[1], rope_ref[2], -1.0
        ).astype(BF16)
        dv_out[:, cut] = sums[1].astype(BF16)


def call(kernel, out_shape, args, flops=0, exps=0, scratch=(), space=pltpu.VMEM, limit=VMEM_LIMIT):
    shapes = jax.tree.leaves(out_shape)
    flops *= 8
    moved = sum(math.prod(x.shape) * x.dtype.itemsize for x in list(args) + shapes)
    return pl.pallas_call(
        kernel,
        out_shape=out_shape,
        in_specs=[pl.BlockSpec(memory_space=space)] * len(args),
        scratch_shapes=list(scratch),
        compiler_params=pltpu.CompilerParams(vmem_limit_bytes=limit),
        cost_estimate=pl.CostEstimate(flops=flops, bytes_accessed=moved, transcendentals=exps),
    )(*args)


def shards(query_in, key_in, value_in, cotangent):
    frames, rows, cols, chan = query_in.shape
    cells = frames * rows * cols
    sizes = {axis: lax.axis_size(axis) for axis in ("ta", "ha", "wa")}
    assert rows == TILE_H and cols == TILE_W and chan == HEADS * DH
    assert TILE_T % frames == 0 and frames * sizes["ta"] <= 2 * TILE_T
    assert sizes["ta"] == 4 and sizes["ha"] % 2 == 0 and sizes["wa"] % 2 == 0
    dims = (frames, rows, cols)
    table, begins = rope_table(frames * sizes["ta"], rows * sizes["ha"], cols * sizes["wa"])
    flat = [x.reshape(cells, chan) for x in (query_in, key_in, value_in, cotangent)]
    pair = jax.ShapeDtypeStruct((2, cells, chan), BF16)
    plain = jax.ShapeDtypeStruct((cells, chan), BF16)

    def real(*shape):
        return jax.ShapeDtypeStruct(shape, F32)

    with jax.named_scope("rotate"):
        kv, qg, rope = call(
            functools.partial(rotate_kernel, dims, begins),
            (pair, pair, real(3, cells, DH)),
            [pltpu.with_memory_space_constraint(x, pltpu.HBM) for x in (*flat, jnp.asarray(table))],
            scratch=[pltpu.VMEM((cells, chan), BF16)] * 2
            + [pltpu.VMEM(table.shape, F32), pltpu.SemaphoreType.DMA((5,))],
            space=pltpu.HBM,
        )

    def other_frames(x, distance):
        return lax.ppermute(x, "ta", [(i, i ^ distance) for i in range(sizes["ta"])])

    row_sides = side_pairs(sizes["ha"])
    col_sides = side_pairs(sizes["wa"])
    with jax.named_scope("halo"):
        kv_rows = [kv] + [lax.ppermute(kv, "ha", pairs) for pairs in row_sides]
        qg2 = other_frames(qg, 2)
        qg1 = other_frames(qg, 1)
        tiles = []
        for block in kv_rows:
            tiles.append([block] + [lax.ppermute(block, "wa", pairs) for pairs in col_sides])
        qg3 = other_frames(qg2, 1)
    grid_rows, grid_cols = 1 + len(row_sides), 1 + len(col_sides)
    flat_tiles = [tiles[row][col] for row in range(grid_rows) for col in range(grid_cols)]
    groups = {}
    for row in range(grid_rows):
        for col in range(grid_cols):
            groups.setdefault((row == 2, col == 2), []).append(row * grid_cols + col)
    groups = list(groups.items())

    key_count = len(flat_tiles) * cells
    product = 2 * cells * key_count * DH * HEADS

    def forward(blocks, first):
        count = len(blocks)
        stat = (count * cells, DH) if first is None else (8, 4 * cells)
        return call(
            functools.partial(forward_kernel, groups, sizes, cells, count, first is not None),
            (*[plain] * count, real(*stat)),
            (*blocks, *flat_tiles) + (() if first is None else (first,)),
            2 * product * count,
            cells * key_count * HEADS * count,
            [pltpu.VMEM((key_count, chan), BF16)] * 2,
        )

    with jax.named_scope("attend"):
        o0, o1, o2, first = forward((qg, qg1, qg2), None)
        o3, stat = forward((qg3,), first)
    with jax.named_scope("merge"):
        outs = [other_frames(o, d) for d, o in ((3, o3), (2, o2), (1, o1))]
        stat_near, outs[1:] = lax.optimization_barrier((stat, outs[1:]))
        stats = [stat, other_frames(stat_near, 1), other_frames(stat, 3), other_frames(stat, 2)]

    queries = (qg, qg1, qg2, qg3)
    col_shape = jax.ShapeDtypeStruct((grid_rows, 2, cells, chan), BF16)

    def gradients(which, carried):
        count = len(which)
        first, last = which[-1] == grid_cols - 1, which[0] == 0
        stat_outs = [real(HEADS, 4 * cells), real(HEADS, 4 * cells), real(cells, DH)]
        return call(
            functools.partial(backward_kernel, which, grid_rows, sizes, cells, first, last),
            (
                *([plain] * 4 if last else [real(HEADS, DH, 4 * cells)]),
                *(stat_outs if first else []),
                *[col_shape] * count,
            ),
            (*queries, *[tiles[row][col] for col in which for row in range(grid_rows)], *carried),
            20 * product * count // grid_cols,
            4 * cells * key_count * HEADS * count // grid_cols,
            [pltpu.VMEM((count * grid_rows * cells, chan), BF16)] * 2,
        )

    with jax.named_scope("gradients"):
        dq, lse, delta, shares, *sides = gradients(tuple(range(1, grid_cols)), stats)
        sides = [lax.ppermute(x, "wa", pairs) for x, pairs in zip(sides, col_sides)]
        d0, d1, d2, d3, own = gradients((0,), (lse, delta, dq))
    with jax.named_scope("return"):
        (d1, d2, d3), outs = lax.optimization_barrier(((d1, d2, d3), outs))
        col_parts = [own, *sides]
        dqs = [d0] + [other_frames(x, d) for d, x in ((3, d3), (2, d2), (1, d1))]
        row_parts = []
        for row, pairs in enumerate(row_sides, start=1):
            partial_sum = sum(x[row].astype(F32) for x in col_parts).astype(BF16)
            row_parts.append(lax.ppermute(partial_sum, "ha", pairs))

    with jax.named_scope("finish"):
        attended, grad_query = call(
            finish_query_kernel, (plain, plain), (o0, *outs, *dqs, shares, rope), 10 * product
        )
        grad_key, grad_value = call(
            functools.partial(finish_key_kernel, grid_cols, len(row_parts)),
            (plain, plain),
            (*col_parts, *row_parts, rope),
        )
    return tuple(x.reshape(query_in.shape) for x in (attended, grad_query, grad_key, grad_value))


def solution(mesh):
    spec = P("ta", "ha", "wa", None)
    return jax.shard_map(
        shards, mesh=mesh, in_specs=(spec,) * 4, out_specs=(spec,) * 4, check_vma=False
    )
```

```python
import functools
import math

import jax
import jax.numpy as jnp
import numpy as np
from jax import lax
from jax.experimental import pallas as pl
from jax.experimental.pallas import tpu as pltpu
from jax.sharding import PartitionSpec as P

DH = 128
HEADS = 2
TILE_T = 6
TILE_H = 8
TILE_W = 8

NEGATIVE = -1e30
SCALE = DH**-0.5
SCALE_LOG2 = SCALE * math.log2(math.e)
F32 = jnp.float32
BF16 = jnp.bfloat16
STAT_ORDER = (0, 1, 3, 2)
VMEM_LIMIT = 48 * 1024 * 1024


def near_pairs(count):
    return [(i, i ^ 1) for i in range(count)]


def far_pairs(count):
    pairs = []
    for i in range(count):
        j = i + 1 if i % 2 else i - 1
        pairs.append((i, j if 0 <= j < count else i))
    return pairs


def far_exists(axis, count):
    pos = lax.axis_index(axis)
    other = jnp.where(pos % 2 == 1, pos + 1, pos - 1)
    return (other >= 0) & (other < count)


def side_pairs(count):
    sides = []
    if count > 1:
        sides.append(near_pairs(count))
    if count > 2:
        sides.append(far_pairs(count))
    return sides


def rope_table(frame_total, row_total, col_total):
    time_dims = DH // 8
    space_dims = (DH - time_dims) // 2
    slower = 256.0 ** (-np.arange(0, time_dims, 2) / time_dims)
    faster = 256.0 ** (-np.arange(0, space_dims, 2) / space_dims)
    starts = (0, time_dims, time_dims + space_dims)
    pieces = []
    for total, rates, start in zip(
        (frame_total, row_total, col_total), (slower, faster, faster), starts
    ):
        padded = -(-total // 8) * 8
        piece = np.zeros((3, padded, DH), np.float32)
        angles = np.arange(padded)[:, None] * rates[None, :]
        stop = start + 2 * len(rates)
        piece[0, :, start:stop:2] = np.cos(angles)
        piece[0, :, start + 1 : stop : 2] = np.cos(angles)
        piece[1, :, start:stop:2] = -np.sin(angles)
        piece[2, :, start + 1 : stop : 2] = np.sin(angles)
        pieces.append(piece)
    begins = np.cumsum([0] + [piece.shape[1] for piece in pieces])
    return np.concatenate(pieces, axis=1), tuple(int(x) for x in begins[:3])


def local_table(plane, table_ref, begins, frames, rows, cols):
    frame_lo = begins[0] + lax.axis_index("ta") * frames
    row_lo = pl.multiple_of(begins[1] + lax.axis_index("ha") * rows, 8)
    col_lo = pl.multiple_of(begins[2] + lax.axis_index("wa") * cols, 8)
    row_part = table_ref[plane, pl.ds(row_lo, rows), :]
    col_part = table_ref[plane, pl.ds(col_lo, cols), :]
    grids = []
    for i in range(frames):
        lead = row_part + table_ref[plane, pl.ds(frame_lo + i, 1), :]
        grid = lead[:, None, :] + col_part[None, :, :]
        grids.append(grid.reshape(rows * cols, DH))
    return jnp.concatenate(grids, axis=0)


def turn(x, cosine, sin_even, sin_odd, sign):
    follow = pltpu.roll(x, DH - 1, 1)
    lead = pltpu.roll(x, 1, 1)
    return x * cosine + sign * (follow * sin_even + lead * sin_odd)


def head_slice(head):
    return slice(head * DH, (head + 1) * DH)


def rotate_kernel(
    dims, begins, q_hbm, k_hbm, v_hbm, g_hbm, table_hbm, kv_ref, qg_ref, rope_ref, q_ref, k_ref,
    table_ref, sems,
):
    moves = [
        (table_hbm, table_ref),
        (k_hbm, k_ref),
        (q_hbm, q_ref),
        (v_hbm, kv_ref.at[1]),
        (g_hbm, qg_ref.at[1]),
    ]
    copies = [pltpu.make_async_copy(*move, sems.at[i]) for i, move in enumerate(moves)]
    for copy in copies:
        copy.start()
    copies[0].wait()
    tables = [local_table(plane, table_ref, begins, *dims) for plane in range(3)]
    for plane in range(3):
        rope_ref[plane] = tables[plane]
    for copy, source, target in ((copies[1], k_ref, kv_ref), (copies[2], q_ref, qg_ref)):
        copy.wait()
        for head in range(HEADS):
            cut = head_slice(head)
            target[0, :, cut] = turn(source[:, cut].astype(F32), *tables, 1.0).astype(BF16)
    copies[3].wait()
    copies[4].wait()


def dot_nt(a, b):
    return lax.dot_general(a, b, (((1,), (1,)), ((), ())), preferred_element_type=F32)


def dot_nn(a, b):
    return lax.dot_general(a, b, (((1,), (0,)), ((), ())), preferred_element_type=F32)


def dot_tn(a, b):
    return lax.dot_general(a, b, (((0,), (0,)), ((), ())), preferred_element_type=F32)


def group_bias(flags, sizes):
    valid = None
    for axis, is_far in zip(("ha", "wa"), flags):
        if is_far:
            here = far_exists(axis, sizes[axis])
            valid = here if valid is None else valid & here
    return None if valid is None else jnp.where(valid, 0.0, NEGATIVE).astype(F32)


def forward_kernel(groups, sizes, cells, count, last, *refs):
    tile_count = sum(len(members) for _, members in groups)
    qg_refs = refs[:count]
    kv_refs = refs[count : count + tile_count]
    rest = refs[count + tile_count :]
    if last:
        first_ref, rest = rest[0], rest[1:]
    o_refs = rest[:count]
    stat_ref, key_buf, value_buf = rest[count:]
    at = 0
    spans = []
    for flags, members in groups:
        begin = at
        for member in members:
            key_buf[at : at + cells] = kv_refs[member][0]
            value_buf[at : at + cells] = kv_refs[member][1]
            at += cells
        spans.append((begin, at, group_bias(flags, sizes)))
    lane = lax.broadcasted_iota(jnp.int32, (count * cells, DH), 1)
    stat = jnp.zeros((count * cells, DH), F32)

    def scores_of(head):
        cut = head_slice(head)
        query = jnp.concatenate([ref[0, :, cut] for ref in qg_refs], axis=0)
        return [dot_nt(query, key_buf[lo:hi, cut]) for lo, hi, _ in spans]

    ahead = scores_of(0)
    for head in range(HEADS):
        cut = head_slice(head)
        scores = ahead
        if head + 1 < HEADS:
            ahead = scores_of(head + 1)
        best = None
        for raw, (_, _, bias) in zip(scores, spans):
            top = jnp.max(raw, axis=1, keepdims=True) * SCALE_LOG2
            if bias is not None:
                top = top + bias
            best = top if best is None else jnp.maximum(best, top)
        total = None
        out = None
        for raw, (lo, hi, bias) in zip(scores, spans):
            shift = best if bias is None else best - bias
            weights = jnp.exp2(raw * SCALE_LOG2 - shift)
            part = jnp.sum(weights, axis=1, keepdims=True)
            piece = dot_nn(weights.astype(BF16), value_buf[lo:hi, cut])
            total = part if total is None else total + part
            out = piece if out is None else out + piece
        out = out * (1.0 / total)
        grad = jnp.concatenate([ref[1, :, cut] for ref in qg_refs], axis=0)
        dotted = jnp.sum(out * grad.astype(F32), axis=1, keepdims=True)
        out = out.astype(BF16)
        for i, o_ref in enumerate(o_refs):
            o_ref[:, cut] = out[i * cells : (i + 1) * cells]
        stat = jnp.where(lane == head, best + jnp.log2(total), stat)
        stat = jnp.where(lane == HEADS + head, dotted, stat)
    if last:
        whole = jnp.concatenate([first_ref[...], stat], axis=0)
        stat_ref[...] = whole.T[: stat_ref.shape[0]]
    else:
        stat_ref[...] = stat


def seen_from(stat, distance, cells):
    if distance & 2:
        stat = pltpu.roll(stat, 2 * cells, 1)
    if distance & 1:
        lane = lax.broadcasted_iota(jnp.int32, stat.shape, 1)
        even = (lane < cells) | ((lane >= 2 * cells) & (lane < 3 * cells))
        stat = jnp.where(even, pltpu.roll(stat, 3 * cells, 1), pltpu.roll(stat, cells, 1))
    return stat


def merged_stats(stat_refs, cells):
    refs = dict(zip(STAT_ORDER, stat_refs))
    parts = [seen_from(refs[distance][...], distance, cells) for distance in range(4)]
    top = functools.reduce(jnp.maximum, parts)
    shares = [jnp.exp2(part - top) for part in parts]
    total = functools.reduce(jnp.add, shares)
    lse = top + jnp.log2(total)
    shares = [share / total for share in shares]
    delta = functools.reduce(
        jnp.add,
        [share[:HEADS] * part[HEADS : 2 * HEADS] for share, part in zip(shares, parts)],
    )
    return lse[:HEADS], delta, shares


def backward_kernel(cols, grid_rows, sizes, cells, first, last, *refs):
    tile_count = grid_rows * len(cols)
    qg_refs = refs[:4]
    kv_refs = refs[4 : 4 + tile_count]
    rest = refs[4 + tile_count :]
    if first:
        stat_refs, rest = rest[:4], rest[4:]
    else:
        (lse_ref, delta_ref, dq_ref), rest = rest[:3], rest[3:]
    if last:
        dq_outs, rest = rest[:4], rest[4:]
    else:
        dq_out, rest = rest[0], rest[1:]
    if first:
        (lse_ref, delta_ref, share_ref), rest = rest[:3], rest[3:]
        lse, delta, shares = merged_stats(stat_refs, cells)
        lse_ref[...] = lse
        delta_ref[...] = delta
        rows = [shares[d][head : head + 1, : 2 * cells] for head in range(HEADS) for d in range(4)]
        wide = jnp.concatenate(rows + [jnp.zeros((DH - len(rows), 2 * cells), F32)], axis=0)
        share_ref[...] = wide.T[:cells]
    else:
        lse, delta = lse_ref[...], delta_ref[...]
    col_refs = rest[: len(cols)]
    key_buf, value_buf = rest[len(cols) :]

    span = grid_rows * cells
    for i, ref in enumerate(kv_refs):
        key_buf[i * cells : (i + 1) * cells] = ref[0]
        value_buf[i * cells : (i + 1) * cells] = ref[1]
    blocks = [(head, slot) for head in range(HEADS) for slot in range(len(cols))]

    def products_of(head, slot):
        cut = head_slice(head)
        at = slice(slot * span, (slot + 1) * span)
        queries = jnp.concatenate([ref[0, :, cut] for ref in qg_refs], axis=0)
        grads = jnp.concatenate([ref[1, :, cut] for ref in qg_refs], axis=0)
        raw = dot_nt(key_buf[at, cut], queries)
        return raw, dot_nt(value_buf[at, cut], grads), queries, grads

    dqs = [None] * HEADS
    ahead = products_of(*blocks[0])
    for i, (head, slot) in enumerate(blocks):
        raw, prob_grad, queries, grads = ahead
        if i + 1 < len(blocks):
            ahead = products_of(*blocks[i + 1])
        cut = head_slice(head)
        probs = []
        for row in range(grid_rows):
            bias = group_bias((row == 2, cols[slot] == 2), sizes)
            shift = lse[head : head + 1]
            shift = shift if bias is None else shift - bias
            probs.append(jnp.exp2(raw[row * cells : (row + 1) * cells] * SCALE_LOG2 - shift))
        probs = jnp.concatenate(probs, axis=0)
        dscore = (probs * (prob_grad - delta[head : head + 1])).astype(BF16)
        dv = dot_nn(probs.astype(BF16), grads).astype(BF16)
        dk = (dot_nn(dscore, queries) * SCALE).astype(BF16)
        for row in range(grid_rows):
            at = slice(row * cells, (row + 1) * cells)
            col_refs[slot][row, 0, :, cut] = dk[at]
            col_refs[slot][row, 1, :, cut] = dv[at]
        part = dot_nn(key_buf[slot * span : (slot + 1) * span, cut].T, dscore)
        dqs[head] = part if dqs[head] is None else dqs[head] + part
    for head in range(HEADS):
        cut = head_slice(head)
        dq = dqs[head] if first else dqs[head] + dq_ref[head]
        if last:
            dq = (dq * SCALE).T.astype(BF16)
            for i, ref in enumerate(dq_outs):
                ref[:, cut] = dq[i * cells : (i + 1) * cells]
        else:
            dq_out[head] = dq


def finish_query_kernel(*refs):
    o_refs, dq_refs = refs[:4], refs[4:8]
    share_ref, rope_ref, out_ref, dq_out = refs[8:]
    for head in range(HEADS):
        cut = head_slice(head)
        outs = []
        for d, o_ref in zip((0, 3, 2, 1), o_refs):
            weight = share_ref[:, 4 * head + d : 4 * head + d + 1]
            outs.append(o_ref[:, cut].astype(F32) * weight)
        out_ref[:, cut] = functools.reduce(jnp.add, outs).astype(BF16)
        dq = functools.reduce(jnp.add, [ref[:, cut].astype(F32) for ref in dq_refs])
        dq_out[:, cut] = turn(dq, rope_ref[0], rope_ref[1], rope_ref[2], -1.0).astype(BF16)


def finish_key_kernel(cols, rows, *refs):
    col_refs, row_refs = refs[:cols], refs[cols : cols + rows]
    rope_ref, dk_out, dv_out = refs[cols + rows :]
    for head in range(HEADS):
        cut = head_slice(head)
        sums = []
        for which in range(2):
            terms = [ref[0, which, :, cut].astype(F32) for ref in col_refs]
            terms += [ref[which, :, cut].astype(F32) for ref in row_refs]
            sums.append(functools.reduce(jnp.add, terms))
        dk_out[:, cut] = turn(
            sums[0], rope_ref[0], rope_ref[1], rope_ref[2], -1.0
        ).astype(BF16)
        dv_out[:, cut] = sums[1].astype(BF16)


def call(kernel, out_shape, args, flops=0, exps=0, scratch=(), space=pltpu.VMEM, limit=VMEM_LIMIT):
    shapes = jax.tree.leaves(out_shape)
    flops *= 8
    moved = sum(math.prod(x.shape) * x.dtype.itemsize for x in list(args) + shapes)
    return pl.pallas_call(
        kernel,
        out_shape=out_shape,
        in_specs=[pl.BlockSpec(memory_space=space)] * len(args),
        scratch_shapes=list(scratch),
        compiler_params=pltpu.CompilerParams(vmem_limit_bytes=limit),
        cost_estimate=pl.CostEstimate(flops=flops, bytes_accessed=moved, transcendentals=exps),
    )(*args)


def shards(query_in, key_in, value_in, cotangent):
    frames, rows, cols, chan = query_in.shape
    cells = frames * rows * cols
    sizes = {axis: lax.axis_size(axis) for axis in ("ta", "ha", "wa")}
    assert rows == TILE_H and cols == TILE_W and chan == HEADS * DH
    assert TILE_T % frames == 0 and frames * sizes["ta"] <= 2 * TILE_T
    assert sizes["ta"] == 4 and sizes["ha"] % 2 == 0 and sizes["wa"] % 2 == 0
    dims = (frames, rows, cols)
    table, begins = rope_table(frames * sizes["ta"], rows * sizes["ha"], cols * sizes["wa"])
    flat = [x.reshape(cells, chan) for x in (query_in, key_in, value_in, cotangent)]
    pair = jax.ShapeDtypeStruct((2, cells, chan), BF16)
    plain = jax.ShapeDtypeStruct((cells, chan), BF16)

    def real(*shape):
        return jax.ShapeDtypeStruct(shape, F32)

    with jax.named_scope("rotate"):
        kv, qg, rope = call(
            functools.partial(rotate_kernel, dims, begins),
            (pair, pair, real(3, cells, DH)),
            [pltpu.with_memory_space_constraint(x, pltpu.HBM) for x in (*flat, jnp.asarray(table))],
            scratch=[pltpu.VMEM((cells, chan), BF16)] * 2
            + [pltpu.VMEM(table.shape, F32), pltpu.SemaphoreType.DMA((5,))],
            space=pltpu.HBM,
        )

    def other_frames(x, distance):
        return lax.ppermute(x, "ta", [(i, i ^ distance) for i in range(sizes["ta"])])

    row_sides = side_pairs(sizes["ha"])
    col_sides = side_pairs(sizes["wa"])
    with jax.named_scope("halo"):
        kv_rows = [kv] + [lax.ppermute(kv, "ha", pairs) for pairs in row_sides]
        qg2 = other_frames(qg, 2)
        qg1 = other_frames(qg, 1)
        tiles = []
        for block in kv_rows:
            tiles.append([block] + [lax.ppermute(block, "wa", pairs) for pairs in col_sides])
        qg3 = other_frames(qg2, 1)
    grid_rows, grid_cols = 1 + len(row_sides), 1 + len(col_sides)
    flat_tiles = [tiles[row][col] for row in range(grid_rows) for col in range(grid_cols)]
    groups = {}
    for row in range(grid_rows):
        for col in range(grid_cols):
            groups.setdefault((row == 2, col == 2), []).append(row * grid_cols + col)
    groups = list(groups.items())

    key_count = len(flat_tiles) * cells
    product = 2 * cells * key_count * DH * HEADS

    def forward(blocks, first):
        count = len(blocks)
        stat = (count * cells, DH) if first is None else (8, 4 * cells)
        return call(
            functools.partial(forward_kernel, groups, sizes, cells, count, first is not None),
            (*[plain] * count, real(*stat)),
            (*blocks, *flat_tiles) + (() if first is None else (first,)),
            2 * product * count,
            cells * key_count * HEADS * count,
            [pltpu.VMEM((key_count, chan), BF16)] * 2,
        )

    with jax.named_scope("attend"):
        o0, o1, o2, first = forward((qg, qg1, qg2), None)
        o3, stat = forward((qg3,), first)
    with jax.named_scope("merge"):
        outs = [other_frames(o, d) for d, o in ((3, o3), (2, o2), (1, o1))]
        stat_near, outs[1] = lax.optimization_barrier((stat, outs[1]))
        stats = [stat, other_frames(stat_near, 1), other_frames(stat, 3), other_frames(stat, 2)]

    queries = (qg, qg1, qg2, qg3)
    col_shape = jax.ShapeDtypeStruct((grid_rows, 2, cells, chan), BF16)

    def gradients(which, carried):
        count = len(which)
        first, last = which[-1] == grid_cols - 1, which[0] == 0
        stat_outs = [real(HEADS, 4 * cells), real(HEADS, 4 * cells), real(cells, DH)]
        return call(
            functools.partial(backward_kernel, which, grid_rows, sizes, cells, first, last),
            (
                *([plain] * 4 if last else [real(HEADS, DH, 4 * cells)]),
                *(stat_outs if first else []),
                *[col_shape] * count,
            ),
            (*queries, *[tiles[row][col] for col in which for row in range(grid_rows)], *carried),
            20 * product * count // grid_cols,
            4 * cells * key_count * HEADS * count // grid_cols,
            [pltpu.VMEM((count * grid_rows * cells, chan), BF16)] * 2,
        )

    with jax.named_scope("gradients"):
        dq, lse, delta, shares, *sides = gradients(tuple(range(1, grid_cols)), stats)
        sides = [lax.ppermute(x, "wa", pairs) for x, pairs in zip(sides, col_sides)]
        d0, d1, d2, d3, own = gradients((0,), (lse, delta, dq))
    with jax.named_scope("return"):
        (d1, d2, d3), outs = lax.optimization_barrier(((d1, d2, d3), outs))
        col_parts = [own, *sides]
        dqs = [d0] + [other_frames(x, d) for d, x in ((3, d3), (2, d2), (1, d1))]
        row_parts = []
        for row, pairs in enumerate(row_sides, start=1):
            partial_sum = sum(x[row].astype(F32) for x in col_parts).astype(BF16)
            row_parts.append(lax.ppermute(partial_sum, "ha", pairs))

    with jax.named_scope("finish"):
        attended, grad_query = call(
            finish_query_kernel, (plain, plain), (o0, *outs, *dqs, shares, rope), 10 * product
        )
        grad_key, grad_value = call(
            functools.partial(finish_key_kernel, grid_cols, len(row_parts)),
            (plain, plain),
            (*col_parts, *row_parts, rope),
        )
    return tuple(x.reshape(query_in.shape) for x in (attended, grad_query, grad_key, grad_value))


def solution(mesh):
    spec = P("ta", "ha", "wa", None)
    return jax.shard_map(
        shards, mesh=mesh, in_specs=(spec,) * 4, out_specs=(spec,) * 4, check_vma=False
    )
```

```python
import functools
import math

import jax
import jax.numpy as jnp
import numpy as np
from jax import lax
from jax.experimental import pallas as pl
from jax.experimental.pallas import tpu as pltpu
from jax.sharding import PartitionSpec as P

DH = 128
HEADS = 2
TILE_T = 6
TILE_H = 8
TILE_W = 8

NEGATIVE = -1e30
SCALE = DH**-0.5
SCALE_LOG2 = SCALE * math.log2(math.e)
F32 = jnp.float32
BF16 = jnp.bfloat16
STAT_ORDER = (0, 1, 3, 2)
VMEM_LIMIT = 48 * 1024 * 1024


def near_pairs(count):
    return [(i, i ^ 1) for i in range(count)]


def far_pairs(count):
    pairs = []
    for i in range(count):
        j = i + 1 if i % 2 else i - 1
        pairs.append((i, j if 0 <= j < count else i))
    return pairs


def far_exists(axis, count):
    pos = lax.axis_index(axis)
    other = jnp.where(pos % 2 == 1, pos + 1, pos - 1)
    return (other >= 0) & (other < count)


def side_pairs(count):
    sides = []
    if count > 1:
        sides.append(near_pairs(count))
    if count > 2:
        sides.append(far_pairs(count))
    return sides


def rope_table(frame_total, row_total, col_total):
    time_dims = DH // 8
    space_dims = (DH - time_dims) // 2
    slower = 256.0 ** (-np.arange(0, time_dims, 2) / time_dims)
    faster = 256.0 ** (-np.arange(0, space_dims, 2) / space_dims)
    starts = (0, time_dims, time_dims + space_dims)
    pieces = []
    for total, rates, start in zip(
        (frame_total, row_total, col_total), (slower, faster, faster), starts
    ):
        padded = -(-total // 8) * 8
        piece = np.zeros((3, padded, DH), np.float32)
        angles = np.arange(padded)[:, None] * rates[None, :]
        stop = start + 2 * len(rates)
        piece[0, :, start:stop:2] = np.cos(angles)
        piece[0, :, start + 1 : stop : 2] = np.cos(angles)
        piece[1, :, start:stop:2] = -np.sin(angles)
        piece[2, :, start + 1 : stop : 2] = np.sin(angles)
        pieces.append(piece)
    begins = np.cumsum([0] + [piece.shape[1] for piece in pieces])
    return np.concatenate(pieces, axis=1), tuple(int(x) for x in begins[:3])


def local_table(plane, table_ref, begins, frames, rows, cols):
    frame_lo = begins[0] + lax.axis_index("ta") * frames
    row_lo = pl.multiple_of(begins[1] + lax.axis_index("ha") * rows, 8)
    col_lo = pl.multiple_of(begins[2] + lax.axis_index("wa") * cols, 8)
    row_part = table_ref[plane, pl.ds(row_lo, rows), :]
    col_part = table_ref[plane, pl.ds(col_lo, cols), :]
    grids = []
    for i in range(frames):
        lead = row_part + table_ref[plane, pl.ds(frame_lo + i, 1), :]
        grid = lead[:, None, :] + col_part[None, :, :]
        grids.append(grid.reshape(rows * cols, DH))
    return jnp.concatenate(grids, axis=0)


def turn(x, cosine, sin_even, sin_odd, sign):
    follow = pltpu.roll(x, DH - 1, 1)
    lead = pltpu.roll(x, 1, 1)
    return x * cosine + sign * (follow * sin_even + lead * sin_odd)


def head_slice(head):
    return slice(head * DH, (head + 1) * DH)


def rotate_kernel(
    dims, begins, q_hbm, k_hbm, v_hbm, g_hbm, table_hbm, kv_ref, qg_ref, rope_ref, q_ref, k_ref,
    table_ref, sems,
):
    moves = [
        (table_hbm, table_ref),
        (k_hbm, k_ref),
        (q_hbm, q_ref),
        (v_hbm, kv_ref.at[1]),
        (g_hbm, qg_ref.at[1]),
    ]
    copies = [pltpu.make_async_copy(*move, sems.at[i]) for i, move in enumerate(moves)]
    for copy in copies:
        copy.start()
    copies[0].wait()
    tables = [local_table(plane, table_ref, begins, *dims) for plane in range(3)]
    for plane in range(3):
        rope_ref[plane] = tables[plane]
    for copy, source, target in ((copies[1], k_ref, kv_ref), (copies[2], q_ref, qg_ref)):
        copy.wait()
        for head in range(HEADS):
            cut = head_slice(head)
            target[0, :, cut] = turn(source[:, cut].astype(F32), *tables, 1.0).astype(BF16)
    copies[3].wait()
    copies[4].wait()


def dot_nt(a, b):
    return lax.dot_general(a, b, (((1,), (1,)), ((), ())), preferred_element_type=F32)


def dot_nn(a, b):
    return lax.dot_general(a, b, (((1,), (0,)), ((), ())), preferred_element_type=F32)


def dot_tn(a, b):
    return lax.dot_general(a, b, (((0,), (0,)), ((), ())), preferred_element_type=F32)


def group_bias(flags, sizes):
    valid = None
    for axis, is_far in zip(("ha", "wa"), flags):
        if is_far:
            here = far_exists(axis, sizes[axis])
            valid = here if valid is None else valid & here
    return None if valid is None else jnp.where(valid, 0.0, NEGATIVE).astype(F32)


def forward_kernel(groups, sizes, cells, count, last, *refs):
    tile_count = sum(len(members) for _, members in groups)
    qg_refs = refs[:count]
    kv_refs = refs[count : count + tile_count]
    rest = refs[count + tile_count :]
    if last:
        first_ref, rest = rest[0], rest[1:]
    o_refs = rest[:count]
    stat_ref, key_buf, value_buf = rest[count:]
    at = 0
    spans = []
    for flags, members in groups:
        begin = at
        for member in members:
            key_buf[at : at + cells] = kv_refs[member][0]
            value_buf[at : at + cells] = kv_refs[member][1]
            at += cells
        spans.append((begin, at, group_bias(flags, sizes)))
    lane = lax.broadcasted_iota(jnp.int32, (count * cells, DH), 1)
    stat = jnp.zeros((count * cells, DH), F32)

    def scores_of(head):
        cut = head_slice(head)
        query = jnp.concatenate([ref[0, :, cut] for ref in qg_refs], axis=0)
        return [dot_nt(query, key_buf[lo:hi, cut]) for lo, hi, _ in spans]

    ahead = scores_of(0)
    for head in range(HEADS):
        cut = head_slice(head)
        scores = ahead
        if head + 1 < HEADS:
            ahead = scores_of(head + 1)
        best = None
        for raw, (_, _, bias) in zip(scores, spans):
            top = jnp.max(raw, axis=1, keepdims=True) * SCALE_LOG2
            if bias is not None:
                top = top + bias
            best = top if best is None else jnp.maximum(best, top)
        total = None
        out = None
        for raw, (lo, hi, bias) in zip(scores, spans):
            shift = best if bias is None else best - bias
            weights = jnp.exp2(raw * SCALE_LOG2 - shift)
            part = jnp.sum(weights, axis=1, keepdims=True)
            piece = dot_nn(weights.astype(BF16), value_buf[lo:hi, cut])
            total = part if total is None else total + part
            out = piece if out is None else out + piece
        out = out * (1.0 / total)
        grad = jnp.concatenate([ref[1, :, cut] for ref in qg_refs], axis=0)
        dotted = jnp.sum(out * grad.astype(F32), axis=1, keepdims=True)
        out = out.astype(BF16)
        for i, o_ref in enumerate(o_refs):
            o_ref[:, cut] = out[i * cells : (i + 1) * cells]
        stat = jnp.where(lane == head, best + jnp.log2(total), stat)
        stat = jnp.where(lane == HEADS + head, dotted, stat)
    if last:
        whole = jnp.concatenate([first_ref[...], stat], axis=0)
        stat_ref[...] = whole.T[: stat_ref.shape[0]]
    else:
        stat_ref[...] = stat


def seen_from(stat, distance, cells):
    if distance & 2:
        stat = pltpu.roll(stat, 2 * cells, 1)
    if distance & 1:
        lane = lax.broadcasted_iota(jnp.int32, stat.shape, 1)
        even = (lane < cells) | ((lane >= 2 * cells) & (lane < 3 * cells))
        stat = jnp.where(even, pltpu.roll(stat, 3 * cells, 1), pltpu.roll(stat, cells, 1))
    return stat


def merged_stats(stat_refs, cells):
    refs = dict(zip(STAT_ORDER, stat_refs))
    parts = [seen_from(refs[distance][...], distance, cells) for distance in range(4)]
    top = functools.reduce(jnp.maximum, parts)
    shares = [jnp.exp2(part - top) for part in parts]
    total = functools.reduce(jnp.add, shares)
    lse = top + jnp.log2(total)
    shares = [share / total for share in shares]
    delta = functools.reduce(
        jnp.add,
        [share[:HEADS] * part[HEADS : 2 * HEADS] for share, part in zip(shares, parts)],
    )
    return lse[:HEADS], delta, shares


def backward_kernel(cols, grid_rows, sizes, cells, first, last, *refs):
    tile_count = grid_rows * len(cols)
    qg_refs = refs[:4]
    kv_refs = refs[4 : 4 + tile_count]
    rest = refs[4 + tile_count :]
    if first:
        stat_refs, rest = rest[:4], rest[4:]
    else:
        (lse_ref, delta_ref, dq_ref), rest = rest[:3], rest[3:]
    if last:
        dq_outs, rest = rest[:4], rest[4:]
    else:
        dq_out, rest = rest[0], rest[1:]
    if first:
        (lse_ref, delta_ref, share_ref), rest = rest[:3], rest[3:]
        lse, delta, shares = merged_stats(stat_refs, cells)
        lse_ref[...] = lse
        delta_ref[...] = delta
        rows = [shares[d][head : head + 1, : 2 * cells] for head in range(HEADS) for d in range(4)]
        wide = jnp.concatenate(rows + [jnp.zeros((DH - len(rows), 2 * cells), F32)], axis=0)
        share_ref[...] = wide.T[:cells]
    else:
        lse, delta = lse_ref[...], delta_ref[...]
    col_refs = rest[: len(cols)]
    key_buf, value_buf = rest[len(cols) :]

    span = grid_rows * cells
    for i, ref in enumerate(kv_refs):
        key_buf[i * cells : (i + 1) * cells] = ref[0]
        value_buf[i * cells : (i + 1) * cells] = ref[1]
    blocks = [(head, slot) for head in range(HEADS) for slot in range(len(cols))]

    def products_of(head, slot):
        cut = head_slice(head)
        at = slice(slot * span, (slot + 1) * span)
        queries = jnp.concatenate([ref[0, :, cut] for ref in qg_refs], axis=0)
        grads = jnp.concatenate([ref[1, :, cut] for ref in qg_refs], axis=0)
        raw = dot_nt(key_buf[at, cut], queries)
        return raw, dot_nt(value_buf[at, cut], grads), queries, grads

    dqs = [None] * HEADS
    ahead = products_of(*blocks[0])
    for i, (head, slot) in enumerate(blocks):
        raw, prob_grad, queries, grads = ahead
        if i + 1 < len(blocks):
            ahead = products_of(*blocks[i + 1])
        cut = head_slice(head)
        probs = []
        for row in range(grid_rows):
            bias = group_bias((row == 2, cols[slot] == 2), sizes)
            shift = lse[head : head + 1]
            shift = shift if bias is None else shift - bias
            probs.append(jnp.exp2(raw[row * cells : (row + 1) * cells] * SCALE_LOG2 - shift))
        probs = jnp.concatenate(probs, axis=0)
        dscore = (probs * (prob_grad - delta[head : head + 1])).astype(BF16)
        dv = dot_nn(probs.astype(BF16), grads).astype(BF16)
        dk = (dot_nn(dscore, queries) * SCALE).astype(BF16)
        for row in range(grid_rows):
            at = slice(row * cells, (row + 1) * cells)
            col_refs[slot][row, 0, :, cut] = dk[at]
            col_refs[slot][row, 1, :, cut] = dv[at]
        part = dot_nn(key_buf[slot * span : (slot + 1) * span, cut].T, dscore)
        dqs[head] = part if dqs[head] is None else dqs[head] + part
    for head in range(HEADS):
        cut = head_slice(head)
        dq = dqs[head] if first else dqs[head] + dq_ref[head]
        if last:
            dq = (dq * SCALE).T.astype(BF16)
            for i, ref in enumerate(dq_outs):
                ref[:, cut] = dq[i * cells : (i + 1) * cells]
        else:
            dq_out[head] = dq


def finish_query_kernel(*refs):
    o_refs, dq_refs = refs[:4], refs[4:8]
    share_ref, rope_ref, out_ref, dq_out = refs[8:]
    for head in range(HEADS):
        cut = head_slice(head)
        outs = []
        for d, o_ref in zip((0, 3, 2, 1), o_refs):
            weight = share_ref[:, 4 * head + d : 4 * head + d + 1]
            outs.append(o_ref[:, cut].astype(F32) * weight)
        out_ref[:, cut] = functools.reduce(jnp.add, outs).astype(BF16)
        dq = functools.reduce(jnp.add, [ref[:, cut].astype(F32) for ref in dq_refs])
        dq_out[:, cut] = turn(dq, rope_ref[0], rope_ref[1], rope_ref[2], -1.0).astype(BF16)


def finish_key_kernel(cols, rows, *refs):
    col_refs, row_refs = refs[:cols], refs[cols : cols + rows]
    rope_ref, dk_out, dv_out = refs[cols + rows :]
    for head in range(HEADS):
        cut = head_slice(head)
        sums = []
        for which in range(2):
            terms = [ref[0, which, :, cut].astype(F32) for ref in col_refs]
            terms += [ref[which, :, cut].astype(F32) for ref in row_refs]
            sums.append(functools.reduce(jnp.add, terms))
        dk_out[:, cut] = turn(
            sums[0], rope_ref[0], rope_ref[1], rope_ref[2], -1.0
        ).astype(BF16)
        dv_out[:, cut] = sums[1].astype(BF16)


def call(kernel, out_shape, args, flops=0, exps=0, scratch=(), space=pltpu.VMEM, limit=VMEM_LIMIT):
    shapes = jax.tree.leaves(out_shape)
    flops *= 8
    moved = sum(math.prod(x.shape) * x.dtype.itemsize for x in list(args) + shapes)
    return pl.pallas_call(
        kernel,
        out_shape=out_shape,
        in_specs=[pl.BlockSpec(memory_space=space)] * len(args),
        scratch_shapes=list(scratch),
        compiler_params=pltpu.CompilerParams(vmem_limit_bytes=limit),
        cost_estimate=pl.CostEstimate(flops=flops, bytes_accessed=moved, transcendentals=exps),
    )(*args)


def shards(query_in, key_in, value_in, cotangent):
    frames, rows, cols, chan = query_in.shape
    cells = frames * rows * cols
    sizes = {axis: lax.axis_size(axis) for axis in ("ta", "ha", "wa")}
    assert rows == TILE_H and cols == TILE_W and chan == HEADS * DH
    assert TILE_T % frames == 0 and frames * sizes["ta"] <= 2 * TILE_T
    assert sizes["ta"] == 4 and sizes["ha"] % 2 == 0 and sizes["wa"] % 2 == 0
    dims = (frames, rows, cols)
    table, begins = rope_table(frames * sizes["ta"], rows * sizes["ha"], cols * sizes["wa"])
    flat = [x.reshape(cells, chan) for x in (query_in, key_in, value_in, cotangent)]
    pair = jax.ShapeDtypeStruct((2, cells, chan), BF16)
    plain = jax.ShapeDtypeStruct((cells, chan), BF16)

    def real(*shape):
        return jax.ShapeDtypeStruct(shape, F32)

    with jax.named_scope("rotate"):
        kv, qg, rope = call(
            functools.partial(rotate_kernel, dims, begins),
            (pair, pair, real(3, cells, DH)),
            [pltpu.with_memory_space_constraint(x, pltpu.HBM) for x in (*flat, jnp.asarray(table))],
            scratch=[pltpu.VMEM((cells, chan), BF16)] * 2
            + [pltpu.VMEM(table.shape, F32), pltpu.SemaphoreType.DMA((5,))],
            space=pltpu.HBM,
        )

    def other_frames(x, distance):
        return lax.ppermute(x, "ta", [(i, i ^ distance) for i in range(sizes["ta"])])

    row_sides = side_pairs(sizes["ha"])
    col_sides = side_pairs(sizes["wa"])
    with jax.named_scope("halo"):
        kv_rows = [kv] + [lax.ppermute(kv, "ha", pairs) for pairs in row_sides]
        qg2 = other_frames(qg, 2)
        qg1 = other_frames(qg, 1)
        tiles = []
        for block in kv_rows:
            tiles.append([block] + [lax.ppermute(block, "wa", pairs) for pairs in col_sides])
        qg3 = other_frames(qg2, 1)
    grid_rows, grid_cols = 1 + len(row_sides), 1 + len(col_sides)
    flat_tiles = [tiles[row][col] for row in range(grid_rows) for col in range(grid_cols)]
    groups = {}
    for row in range(grid_rows):
        for col in range(grid_cols):
            groups.setdefault((row == 2, col == 2), []).append(row * grid_cols + col)
    groups = list(groups.items())

    key_count = len(flat_tiles) * cells
    product = 2 * cells * key_count * DH * HEADS

    def forward(blocks, first):
        count = len(blocks)
        stat = (count * cells, DH) if first is None else (8, 4 * cells)
        return call(
            functools.partial(forward_kernel, groups, sizes, cells, count, first is not None),
            (*[plain] * count, real(*stat)),
            (*blocks, *flat_tiles) + (() if first is None else (first,)),
            2 * product * count,
            cells * key_count * HEADS * count,
            [pltpu.VMEM((key_count, chan), BF16)] * 2,
        )

    with jax.named_scope("attend"):
        o0, o1, o2, first = forward((qg, qg1, qg2), None)
        o3, stat = forward((qg3,), first)
    with jax.named_scope("merge"):
        outs = [other_frames(o, d) for d, o in ((3, o3), (2, o2), (1, o1))]
        stat_near, outs[1:] = lax.optimization_barrier((stat, outs[1:]))
        stats = [stat, other_frames(stat_near, 1), other_frames(stat, 3), other_frames(stat, 2)]

    queries = (qg, qg1, qg2, qg3)
    col_shape = jax.ShapeDtypeStruct((grid_rows, 2, cells, chan), BF16)

    def gradients(which, carried):
        count = len(which)
        first, last = which[-1] == grid_cols - 1, which[0] == 0
        stat_outs = [real(HEADS, 4 * cells), real(HEADS, 4 * cells), real(cells, DH)]
        return call(
            functools.partial(backward_kernel, which, grid_rows, sizes, cells, first, last),
            (
                *([plain] * 4 if last else [real(HEADS, DH, 4 * cells)]),
                *(stat_outs if first else []),
                *[col_shape] * count,
            ),
            (*queries, *[tiles[row][col] for col in which for row in range(grid_rows)], *carried),
            20 * product * count // grid_cols,
            4 * cells * key_count * HEADS * count // grid_cols,
            [pltpu.VMEM((count * grid_rows * cells, chan), BF16)] * 2,
        )

    with jax.named_scope("gradients"):
        dq, lse, delta, shares, *sides = gradients(tuple(range(1, grid_cols)), stats)
        sides = [lax.ppermute(x, "wa", pairs) for x, pairs in zip(sides, col_sides)]
        d0, d1, d2, d3, own = gradients((0,), (lse, delta, dq))
    with jax.named_scope("return"):
        (d1, d2, d3), outs = lax.optimization_barrier(((d1, d2, d3), outs))
        col_parts = [own, *sides]
        dqs = [d0] + [other_frames(x, d) for d, x in ((2, d2), (3, d3), (1, d1))]
        row_parts = []
        for row, pairs in enumerate(row_sides, start=1):
            partial_sum = sum(x[row].astype(F32) for x in col_parts).astype(BF16)
            row_parts.append(lax.ppermute(partial_sum, "ha", pairs))

    with jax.named_scope("finish"):
        attended, grad_query = call(
            finish_query_kernel, (plain, plain), (o0, *outs, *dqs, shares, rope), 10 * product
        )
        grad_key, grad_value = call(
            functools.partial(finish_key_kernel, grid_cols, len(row_parts)),
            (plain, plain),
            (*col_parts, *row_parts, rope),
        )
    return tuple(x.reshape(query_in.shape) for x in (attended, grad_query, grad_key, grad_value))


def solution(mesh):
    spec = P("ta", "ha", "wa", None)
    return jax.shard_map(
        shards, mesh=mesh, in_specs=(spec,) * 4, out_specs=(spec,) * 4, check_vma=False
    )
```

```python
import functools
import math

import jax
import jax.numpy as jnp
import numpy as np
from jax import lax
from jax.experimental import pallas as pl
from jax.experimental.pallas import tpu as pltpu
from jax.sharding import PartitionSpec as P

DH = 128
HEADS = 2
TILE_T = 6
TILE_H = 8
TILE_W = 8

NEGATIVE = -1e30
SCALE = DH**-0.5
SCALE_LOG2 = SCALE * math.log2(math.e)
F32 = jnp.float32
BF16 = jnp.bfloat16
STAT_ORDER = (0, 1, 3, 2)
VMEM_LIMIT = 48 * 1024 * 1024


def near_pairs(count):
    return [(i, i ^ 1) for i in range(count)]


def far_pairs(count):
    pairs = []
    for i in range(count):
        j = i + 1 if i % 2 else i - 1
        pairs.append((i, j if 0 <= j < count else i))
    return pairs


def far_exists(axis, count):
    pos = lax.axis_index(axis)
    other = jnp.where(pos % 2 == 1, pos + 1, pos - 1)
    return (other >= 0) & (other < count)


def side_pairs(count):
    sides = []
    if count > 1:
        sides.append(near_pairs(count))
    if count > 2:
        sides.append(far_pairs(count))
    return sides


def rope_table(frame_total, row_total, col_total):
    time_dims = DH // 8
    space_dims = (DH - time_dims) // 2
    slower = 256.0 ** (-np.arange(0, time_dims, 2) / time_dims)
    faster = 256.0 ** (-np.arange(0, space_dims, 2) / space_dims)
    starts = (0, time_dims, time_dims + space_dims)
    pieces = []
    for total, rates, start in zip(
        (frame_total, row_total, col_total), (slower, faster, faster), starts
    ):
        padded = -(-total // 8) * 8
        piece = np.zeros((3, padded, DH), np.float32)
        angles = np.arange(padded)[:, None] * rates[None, :]
        stop = start + 2 * len(rates)
        piece[0, :, start:stop:2] = np.cos(angles)
        piece[0, :, start + 1 : stop : 2] = np.cos(angles)
        piece[1, :, start:stop:2] = -np.sin(angles)
        piece[2, :, start + 1 : stop : 2] = np.sin(angles)
        pieces.append(piece)
    begins = np.cumsum([0] + [piece.shape[1] for piece in pieces])
    return np.concatenate(pieces, axis=1), tuple(int(x) for x in begins[:3])


def local_table(plane, table_ref, begins, frames, rows, cols):
    frame_lo = begins[0] + lax.axis_index("ta") * frames
    row_lo = pl.multiple_of(begins[1] + lax.axis_index("ha") * rows, 8)
    col_lo = pl.multiple_of(begins[2] + lax.axis_index("wa") * cols, 8)
    row_part = table_ref[plane, pl.ds(row_lo, rows), :]
    col_part = table_ref[plane, pl.ds(col_lo, cols), :]
    grids = []
    for i in range(frames):
        lead = row_part + table_ref[plane, pl.ds(frame_lo + i, 1), :]
        grid = lead[:, None, :] + col_part[None, :, :]
        grids.append(grid.reshape(rows * cols, DH))
    return jnp.concatenate(grids, axis=0)


def turn(x, cosine, sin_even, sin_odd, sign):
    follow = pltpu.roll(x, DH - 1, 1)
    lead = pltpu.roll(x, 1, 1)
    return x * cosine + sign * (follow * sin_even + lead * sin_odd)


def head_slice(head):
    return slice(head * DH, (head + 1) * DH)


def rotate_kernel(
    dims, begins, q_hbm, k_hbm, v_hbm, g_hbm, table_hbm, kv_ref, qg_ref, rope_ref, q_ref, k_ref,
    table_ref, sems,
):
    moves = [
        (table_hbm, table_ref),
        (k_hbm, k_ref),
        (q_hbm, q_ref),
        (v_hbm, kv_ref.at[1]),
        (g_hbm, qg_ref.at[1]),
    ]
    copies = [pltpu.make_async_copy(*move, sems.at[i]) for i, move in enumerate(moves)]
    for copy in copies:
        copy.start()
    copies[0].wait()
    tables = [local_table(plane, table_ref, begins, *dims) for plane in range(3)]
    for plane in range(3):
        rope_ref[plane] = tables[plane]
    for copy, source, target in ((copies[1], k_ref, kv_ref), (copies[2], q_ref, qg_ref)):
        copy.wait()
        for head in range(HEADS):
            cut = head_slice(head)
            target[0, :, cut] = turn(source[:, cut].astype(F32), *tables, 1.0).astype(BF16)
    copies[3].wait()
    copies[4].wait()


def dot_nt(a, b):
    return lax.dot_general(a, b, (((1,), (1,)), ((), ())), preferred_element_type=F32)


def dot_nn(a, b):
    return lax.dot_general(a, b, (((1,), (0,)), ((), ())), preferred_element_type=F32)


def dot_tn(a, b):
    return lax.dot_general(a, b, (((0,), (0,)), ((), ())), preferred_element_type=F32)


def group_bias(flags, sizes):
    valid = None
    for axis, is_far in zip(("ha", "wa"), flags):
        if is_far:
            here = far_exists(axis, sizes[axis])
            valid = here if valid is None else valid & here
    return None if valid is None else jnp.where(valid, 0.0, NEGATIVE).astype(F32)


def forward_kernel(groups, sizes, cells, count, last, *refs):
    tile_count = sum(len(members) for _, members in groups)
    qg_refs = refs[:count]
    kv_refs = refs[count : count + tile_count]
    rest = refs[count + tile_count :]
    if last:
        first_ref, rest = rest[0], rest[1:]
    o_refs = rest[:count]
    stat_ref, key_buf, value_buf = rest[count:]
    at = 0
    spans = []
    for flags, members in groups:
        begin = at
        for member in members:
            key_buf[at : at + cells] = kv_refs[member][0]
            value_buf[at : at + cells] = kv_refs[member][1]
            at += cells
        spans.append((begin, at, group_bias(flags, sizes)))
    lane = lax.broadcasted_iota(jnp.int32, (count * cells, DH), 1)
    stat = jnp.zeros((count * cells, DH), F32)

    def scores_of(head):
        cut = head_slice(head)
        query = jnp.concatenate([ref[0, :, cut] for ref in qg_refs], axis=0)
        return [dot_nt(query, key_buf[lo:hi, cut]) for lo, hi, _ in spans]

    ahead = scores_of(0)
    for head in range(HEADS):
        cut = head_slice(head)
        scores = ahead
        if head + 1 < HEADS:
            ahead = scores_of(head + 1)
        best = None
        for raw, (_, _, bias) in zip(scores, spans):
            top = jnp.max(raw, axis=1, keepdims=True) * SCALE_LOG2
            if bias is not None:
                top = top + bias
            best = top if best is None else jnp.maximum(best, top)
        total = None
        out = None
        for raw, (lo, hi, bias) in zip(scores, spans):
            shift = best if bias is None else best - bias
            weights = jnp.exp2(raw * SCALE_LOG2 - shift)
            part = jnp.sum(weights, axis=1, keepdims=True)
            piece = dot_nn(weights.astype(BF16), value_buf[lo:hi, cut])
            total = part if total is None else total + part
            out = piece if out is None else out + piece
        out = out * (1.0 / total)
        grad = jnp.concatenate([ref[1, :, cut] for ref in qg_refs], axis=0)
        dotted = jnp.sum(out * grad.astype(F32), axis=1, keepdims=True)
        out = out.astype(BF16)
        for i, o_ref in enumerate(o_refs):
            o_ref[:, cut] = out[i * cells : (i + 1) * cells]
        stat = jnp.where(lane == head, best + jnp.log2(total), stat)
        stat = jnp.where(lane == HEADS + head, dotted, stat)
    if last:
        whole = jnp.concatenate([first_ref[...], stat], axis=0)
        stat_ref[...] = whole.T[: stat_ref.shape[0]]
    else:
        stat_ref[...] = stat


def seen_from(stat, distance, cells):
    if distance & 2:
        stat = pltpu.roll(stat, 2 * cells, 1)
    if distance & 1:
        lane = lax.broadcasted_iota(jnp.int32, stat.shape, 1)
        even = (lane < cells) | ((lane >= 2 * cells) & (lane < 3 * cells))
        stat = jnp.where(even, pltpu.roll(stat, 3 * cells, 1), pltpu.roll(stat, cells, 1))
    return stat


def merged_stats(stat_refs, cells):
    refs = dict(zip(STAT_ORDER, stat_refs))
    parts = [seen_from(refs[distance][...], distance, cells) for distance in range(4)]
    top = functools.reduce(jnp.maximum, parts)
    shares = [jnp.exp2(part - top) for part in parts]
    total = functools.reduce(jnp.add, shares)
    lse = top + jnp.log2(total)
    shares = [share / total for share in shares]
    delta = functools.reduce(
        jnp.add,
        [share[:HEADS] * part[HEADS : 2 * HEADS] for share, part in zip(shares, parts)],
    )
    return lse[:HEADS], delta, shares


def backward_kernel(cols, grid_rows, sizes, cells, first, last, *refs):
    tile_count = grid_rows * len(cols)
    qg_refs = refs[:4]
    kv_refs = refs[4 : 4 + tile_count]
    rest = refs[4 + tile_count :]
    if first:
        stat_refs, rest = rest[:4], rest[4:]
    else:
        (lse_ref, delta_ref, dq_ref), rest = rest[:3], rest[3:]
    if last:
        dq_outs, rest = rest[:4], rest[4:]
    else:
        dq_out, rest = rest[0], rest[1:]
    if first:
        (lse_ref, delta_ref, share_ref), rest = rest[:3], rest[3:]
        lse, delta, shares = merged_stats(stat_refs, cells)
        lse_ref[...] = lse
        delta_ref[...] = delta
        rows = [shares[d][head : head + 1, : 2 * cells] for head in range(HEADS) for d in range(4)]
        wide = jnp.concatenate(rows + [jnp.zeros((DH - len(rows), 2 * cells), F32)], axis=0)
        share_ref[...] = wide.T[:cells]
    else:
        lse, delta = lse_ref[...], delta_ref[...]
    col_refs = rest[: len(cols)]
    key_buf, value_buf = rest[len(cols) :]

    span = grid_rows * cells
    for i, ref in enumerate(kv_refs):
        key_buf[i * cells : (i + 1) * cells] = ref[0]
        value_buf[i * cells : (i + 1) * cells] = ref[1]
    blocks = [(head, slot) for head in range(HEADS) for slot in range(len(cols))]

    def products_of(head, slot):
        cut = head_slice(head)
        at = slice(slot * span, (slot + 1) * span)
        queries = jnp.concatenate([ref[0, :, cut] for ref in qg_refs], axis=0)
        grads = jnp.concatenate([ref[1, :, cut] for ref in qg_refs], axis=0)
        raw = dot_nt(key_buf[at, cut], queries)
        return raw, dot_nt(value_buf[at, cut], grads), queries, grads

    dqs = [None] * HEADS
    ahead = products_of(*blocks[0])
    for i, (head, slot) in enumerate(blocks):
        raw, prob_grad, queries, grads = ahead
        if i + 1 < len(blocks):
            ahead = products_of(*blocks[i + 1])
        cut = head_slice(head)
        probs = []
        for row in range(grid_rows):
            bias = group_bias((row == 2, cols[slot] == 2), sizes)
            shift = lse[head : head + 1]
            shift = shift if bias is None else shift - bias
            probs.append(jnp.exp2(raw[row * cells : (row + 1) * cells] * SCALE_LOG2 - shift))
        probs = jnp.concatenate(probs, axis=0)
        dscore = (probs * (prob_grad - delta[head : head + 1])).astype(BF16)
        dv = dot_nn(probs.astype(BF16), grads).astype(BF16)
        dk = (dot_nn(dscore, queries) * SCALE).astype(BF16)
        for row in range(grid_rows):
            at = slice(row * cells, (row + 1) * cells)
            col_refs[slot][row, 0, :, cut] = dk[at]
            col_refs[slot][row, 1, :, cut] = dv[at]
        part = dot_nn(key_buf[slot * span : (slot + 1) * span, cut].T, dscore)
        dqs[head] = part if dqs[head] is None else dqs[head] + part
    for head in range(HEADS):
        cut = head_slice(head)
        dq = dqs[head] if first else dqs[head] + dq_ref[head]
        if last:
            dq = (dq * SCALE).T.astype(BF16)
            for i, ref in enumerate(dq_outs):
                ref[:, cut] = dq[i * cells : (i + 1) * cells]
        else:
            dq_out[head] = dq


def finish_kernel(cols, rows, *refs):
    o_refs, dq_refs, refs = refs[:4], refs[4:8], refs[8:]
    col_refs, row_refs = refs[:cols], refs[cols : cols + 2 * rows]
    share_ref, rope_ref, out_ref, dq_out, dk_out, dv_out = refs[cols + 2 * rows :]
    tables = [rope_ref[plane] for plane in range(3)]
    for head in range(HEADS):
        cut = head_slice(head)
        outs = []
        for d, o_ref in zip((0, 3, 2, 1), o_refs):
            weight = share_ref[:, 4 * head + d : 4 * head + d + 1]
            outs.append(o_ref[:, cut].astype(F32) * weight)
        out_ref[:, cut] = functools.reduce(jnp.add, outs).astype(BF16)
        dq = functools.reduce(jnp.add, [ref[:, cut].astype(F32) for ref in dq_refs])
        dq_out[:, cut] = turn(dq, *tables, -1.0).astype(BF16)
        sums = []
        for which in range(2):
            terms = [ref[0, which, :, cut].astype(F32) for ref in col_refs]
            terms += [ref[:, cut].astype(F32) for ref in row_refs[which::2]]
            sums.append(functools.reduce(jnp.add, terms))
        dk_out[:, cut] = turn(sums[0], *tables, -1.0).astype(BF16)
        dv_out[:, cut] = sums[1].astype(BF16)


def call(kernel, out_shape, args, flops=0, exps=0, scratch=(), space=pltpu.VMEM, limit=VMEM_LIMIT):
    shapes = jax.tree.leaves(out_shape)
    flops *= 8
    moved = sum(math.prod(x.shape) * x.dtype.itemsize for x in list(args) + shapes)
    return pl.pallas_call(
        kernel,
        out_shape=out_shape,
        in_specs=[pl.BlockSpec(memory_space=space)] * len(args),
        scratch_shapes=list(scratch),
        compiler_params=pltpu.CompilerParams(vmem_limit_bytes=limit),
        cost_estimate=pl.CostEstimate(flops=flops, bytes_accessed=moved, transcendentals=exps),
    )(*args)


def shards(query_in, key_in, value_in, cotangent):
    frames, rows, cols, chan = query_in.shape
    cells = frames * rows * cols
    sizes = {axis: lax.axis_size(axis) for axis in ("ta", "ha", "wa")}
    assert rows == TILE_H and cols == TILE_W and chan == HEADS * DH
    assert TILE_T % frames == 0 and frames * sizes["ta"] <= 2 * TILE_T
    assert sizes["ta"] == 4 and sizes["ha"] % 2 == 0 and sizes["wa"] % 2 == 0
    dims = (frames, rows, cols)
    table, begins = rope_table(frames * sizes["ta"], rows * sizes["ha"], cols * sizes["wa"])
    flat = [x.reshape(cells, chan) for x in (query_in, key_in, value_in, cotangent)]
    pair = jax.ShapeDtypeStruct((2, cells, chan), BF16)
    plain = jax.ShapeDtypeStruct((cells, chan), BF16)

    def real(*shape):
        return jax.ShapeDtypeStruct(shape, F32)

    with jax.named_scope("rotate"):
        kv, qg, rope = call(
            functools.partial(rotate_kernel, dims, begins),
            (pair, pair, real(3, cells, DH)),
            [pltpu.with_memory_space_constraint(x, pltpu.HBM) for x in (*flat, jnp.asarray(table))],
            scratch=[pltpu.VMEM((cells, chan), BF16)] * 2
            + [pltpu.VMEM(table.shape, F32), pltpu.SemaphoreType.DMA((5,))],
            space=pltpu.HBM,
        )

    def other_frames(x, distance):
        return lax.ppermute(x, "ta", [(i, i ^ distance) for i in range(sizes["ta"])])

    row_sides = side_pairs(sizes["ha"])
    col_sides = side_pairs(sizes["wa"])
    with jax.named_scope("halo"):
        kv_rows = [kv] + [lax.ppermute(kv, "ha", pairs) for pairs in row_sides]
        qg2 = other_frames(qg, 2)
        qg1 = other_frames(qg, 1)
        tiles = []
        for block in kv_rows:
            tiles.append([block] + [lax.ppermute(block, "wa", pairs) for pairs in col_sides])
        qg3 = other_frames(qg2, 1)
    grid_rows, grid_cols = 1 + len(row_sides), 1 + len(col_sides)
    flat_tiles = [tiles[row][col] for row in range(grid_rows) for col in range(grid_cols)]
    groups = {}
    for row in range(grid_rows):
        for col in range(grid_cols):
            groups.setdefault((row == 2, col == 2), []).append(row * grid_cols + col)
    groups = list(groups.items())

    key_count = len(flat_tiles) * cells
    product = 2 * cells * key_count * DH * HEADS

    def forward(blocks, first):
        count = len(blocks)
        stat = (count * cells, DH) if first is None else (8, 4 * cells)
        return call(
            functools.partial(forward_kernel, groups, sizes, cells, count, first is not None),
            (*[plain] * count, real(*stat)),
            (*blocks, *flat_tiles) + (() if first is None else (first,)),
            2 * product * count,
            cells * key_count * HEADS * count,
            [pltpu.VMEM((key_count, chan), BF16)] * 2,
        )

    with jax.named_scope("attend"):
        o0, o1, o2, first = forward((qg, qg1, qg2), None)
        o3, stat = forward((qg3,), first)
    with jax.named_scope("merge"):
        outs = [other_frames(o, d) for d, o in ((3, o3), (2, o2), (1, o1))]
        stat_near, outs[1:] = lax.optimization_barrier((stat, outs[1:]))
        stats = [stat, other_frames(stat_near, 1), other_frames(stat, 3), other_frames(stat, 2)]

    queries = (qg, qg1, qg2, qg3)
    col_shape = jax.ShapeDtypeStruct((grid_rows, 2, cells, chan), BF16)

    def gradients(which, carried):
        count = len(which)
        first, last = which[-1] == grid_cols - 1, which[0] == 0
        stat_outs = [real(HEADS, 4 * cells), real(HEADS, 4 * cells), real(cells, DH)]
        return call(
            functools.partial(backward_kernel, which, grid_rows, sizes, cells, first, last),
            (
                *([plain] * 4 if last else [real(HEADS, DH, 4 * cells)]),
                *(stat_outs if first else []),
                *[col_shape] * count,
            ),
            (*queries, *[tiles[row][col] for col in which for row in range(grid_rows)], *carried),
            20 * product * count // grid_cols,
            4 * cells * key_count * HEADS * count // grid_cols,
            [pltpu.VMEM((count * grid_rows * cells, chan), BF16)] * 2,
        )

    with jax.named_scope("gradients"):
        dq, lse, delta, shares, *sides = gradients(tuple(range(1, grid_cols)), stats)
        sides = [lax.ppermute(x, "wa", pairs) for x, pairs in zip(sides, col_sides)]
        d0, d1, d2, d3, own = gradients((0,), (lse, delta, dq))
    with jax.named_scope("return"):
        (d1, d2, d3), outs = lax.optimization_barrier(((d1, d2, d3), outs))
        col_parts = [own, *sides]
        dqs = [d0] + [other_frames(x, d) for d, x in ((2, d2), (3, d3), (1, d1))]
        row_parts = []
        for row, pairs in enumerate(row_sides, start=1):
            for which in range(2):
                partial_sum = sum(x[row, which].astype(F32) for x in col_parts).astype(BF16)
                row_parts.append(lax.ppermute(partial_sum, "ha", pairs))

    with jax.named_scope("finish"):
        results = call(
            functools.partial(finish_kernel, grid_cols, len(row_parts) // 2),
            [plain] * 4,
            (o0, *outs, *dqs, *col_parts, *row_parts, shares, rope),
        )
    return tuple(x.reshape(query_in.shape) for x in results)


def solution(mesh):
    spec = P("ta", "ha", "wa", None)
    return jax.shard_map(
        shards, mesh=mesh, in_specs=(spec,) * 4, out_specs=(spec,) * 4, check_vma=False
    )
```

```python
import functools
import math

import jax
import jax.numpy as jnp
import numpy as np
from jax import lax
from jax.experimental import pallas as pl
from jax.experimental.pallas import tpu as pltpu
from jax.sharding import PartitionSpec as P

DH = 128
HEADS = 2
TILE_T = 6
TILE_H = 8
TILE_W = 8

NEGATIVE = -1e30
SCALE = DH**-0.5
SCALE_LOG2 = SCALE * math.log2(math.e)
F32 = jnp.float32
BF16 = jnp.bfloat16
STAT_ORDER = (0, 1, 3, 2)
VMEM_LIMIT = 48 * 1024 * 1024


def near_pairs(count):
    return [(i, i ^ 1) for i in range(count)]


def far_pairs(count):
    pairs = []
    for i in range(count):
        j = i + 1 if i % 2 else i - 1
        pairs.append((i, j if 0 <= j < count else i))
    return pairs


def far_exists(axis, count):
    pos = lax.axis_index(axis)
    other = jnp.where(pos % 2 == 1, pos + 1, pos - 1)
    return (other >= 0) & (other < count)


def side_pairs(count):
    sides = []
    if count > 1:
        sides.append(near_pairs(count))
    if count > 2:
        sides.append(far_pairs(count))
    return sides


def rope_table(frame_total, row_total, col_total):
    time_dims = DH // 8
    space_dims = (DH - time_dims) // 2
    slower = 256.0 ** (-np.arange(0, time_dims, 2) / time_dims)
    faster = 256.0 ** (-np.arange(0, space_dims, 2) / space_dims)
    starts = (0, time_dims, time_dims + space_dims)
    pieces = []
    for total, rates, start in zip(
        (frame_total, row_total, col_total), (slower, faster, faster), starts
    ):
        padded = -(-total // 8) * 8
        piece = np.zeros((3, padded, DH), np.float32)
        angles = np.arange(padded)[:, None] * rates[None, :]
        stop = start + 2 * len(rates)
        piece[0, :, start:stop:2] = np.cos(angles)
        piece[0, :, start + 1 : stop : 2] = np.cos(angles)
        piece[1, :, start:stop:2] = -np.sin(angles)
        piece[2, :, start + 1 : stop : 2] = np.sin(angles)
        pieces.append(piece)
    begins = np.cumsum([0] + [piece.shape[1] for piece in pieces])
    return np.concatenate(pieces, axis=1), tuple(int(x) for x in begins[:3])


def local_table(plane, table_ref, begins, frames, rows, cols):
    frame_lo = begins[0] + lax.axis_index("ta") * frames
    row_lo = pl.multiple_of(begins[1] + lax.axis_index("ha") * rows, 8)
    col_lo = pl.multiple_of(begins[2] + lax.axis_index("wa") * cols, 8)
    row_part = table_ref[plane, pl.ds(row_lo, rows), :]
    col_part = table_ref[plane, pl.ds(col_lo, cols), :]
    grids = []
    for i in range(frames):
        lead = row_part + table_ref[plane, pl.ds(frame_lo + i, 1), :]
        grid = lead[:, None, :] + col_part[None, :, :]
        grids.append(grid.reshape(rows * cols, DH))
    return jnp.concatenate(grids, axis=0)


def turn(x, cosine, sin_even, sin_odd, sign):
    follow = pltpu.roll(x, DH - 1, 1)
    lead = pltpu.roll(x, 1, 1)
    return x * cosine + sign * (follow * sin_even + lead * sin_odd)


def head_slice(head):
    return slice(head * DH, (head + 1) * DH)


def rotate_kernel(
    dims, begins, q_hbm, k_hbm, v_hbm, g_hbm, table_hbm, kv_ref, qg_ref, rope_ref, q_ref, k_ref,
    table_ref, sems,
):
    moves = [
        (table_hbm, table_ref),
        (k_hbm, k_ref),
        (q_hbm, q_ref),
        (v_hbm, kv_ref.at[1]),
        (g_hbm, qg_ref.at[1]),
    ]
    copies = [pltpu.make_async_copy(*move, sems.at[i]) for i, move in enumerate(moves)]
    for copy in copies:
        copy.start()
    copies[0].wait()
    tables = [local_table(plane, table_ref, begins, *dims) for plane in range(3)]
    for plane in range(3):
        rope_ref[plane] = tables[plane]
    for copy, source, target in ((copies[1], k_ref, kv_ref), (copies[2], q_ref, qg_ref)):
        copy.wait()
        for head in range(HEADS):
            cut = head_slice(head)
            target[0, :, cut] = turn(source[:, cut].astype(F32), *tables, 1.0).astype(BF16)
    copies[3].wait()
    copies[4].wait()


def dot_nt(a, b):
    return lax.dot_general(a, b, (((1,), (1,)), ((), ())), preferred_element_type=F32)


def dot_nn(a, b):
    return lax.dot_general(a, b, (((1,), (0,)), ((), ())), preferred_element_type=F32)


def dot_tn(a, b):
    return lax.dot_general(a, b, (((0,), (0,)), ((), ())), preferred_element_type=F32)


def group_bias(flags, sizes):
    valid = None
    for axis, is_far in zip(("ha", "wa"), flags):
        if is_far:
            here = far_exists(axis, sizes[axis])
            valid = here if valid is None else valid & here
    return None if valid is None else jnp.where(valid, 0.0, NEGATIVE).astype(F32)


def forward_kernel(groups, sizes, cells, count, last, *refs):
    tile_count = sum(len(members) for _, members in groups)
    qg_refs = refs[:count]
    kv_refs = refs[count : count + tile_count]
    rest = refs[count + tile_count :]
    if last:
        first_ref, rest = rest[0], rest[1:]
    o_refs = rest[:count]
    stat_ref, key_buf, value_buf = rest[count:]
    at = 0
    spans = []
    for flags, members in groups:
        begin = at
        for member in members:
            key_buf[at : at + cells] = kv_refs[member][0]
            value_buf[at : at + cells] = kv_refs[member][1]
            at += cells
        spans.append((begin, at, group_bias(flags, sizes)))
    lane = lax.broadcasted_iota(jnp.int32, (count * cells, DH), 1)
    stat = jnp.zeros((count * cells, DH), F32)

    def scores_of(head):
        cut = head_slice(head)
        query = jnp.concatenate([ref[0, :, cut] for ref in qg_refs], axis=0)
        return [dot_nt(query, key_buf[lo:hi, cut]) for lo, hi, _ in spans]

    ahead = scores_of(0)
    for head in range(HEADS):
        cut = head_slice(head)
        scores = ahead
        if head + 1 < HEADS:
            ahead = scores_of(head + 1)
        best = None
        for raw, (_, _, bias) in zip(scores, spans):
            top = jnp.max(raw, axis=1, keepdims=True) * SCALE_LOG2
            if bias is not None:
                top = top + bias
            best = top if best is None else jnp.maximum(best, top)
        total = None
        out = None
        for raw, (lo, hi, bias) in zip(scores, spans):
            shift = best if bias is None else best - bias
            weights = jnp.exp2(raw * SCALE_LOG2 - shift)
            part = jnp.sum(weights, axis=1, keepdims=True)
            piece = dot_nn(weights.astype(BF16), value_buf[lo:hi, cut])
            total = part if total is None else total + part
            out = piece if out is None else out + piece
        out = out * (1.0 / total)
        grad = jnp.concatenate([ref[1, :, cut] for ref in qg_refs], axis=0)
        dotted = jnp.sum(out * grad.astype(F32), axis=1, keepdims=True)
        out = out.astype(BF16)
        for i, o_ref in enumerate(o_refs):
            o_ref[:, cut] = out[i * cells : (i + 1) * cells]
        stat = jnp.where(lane == head, best + jnp.log2(total), stat)
        stat = jnp.where(lane == HEADS + head, dotted, stat)
    if last:
        whole = jnp.concatenate([first_ref[...], stat], axis=0)
        stat_ref[...] = whole.T[: stat_ref.shape[0]]
    else:
        stat_ref[...] = stat


def seen_from(stat, distance, cells):
    if distance & 2:
        stat = pltpu.roll(stat, 2 * cells, 1)
    if distance & 1:
        lane = lax.broadcasted_iota(jnp.int32, stat.shape, 1)
        even = (lane < cells) | ((lane >= 2 * cells) & (lane < 3 * cells))
        stat = jnp.where(even, pltpu.roll(stat, 3 * cells, 1), pltpu.roll(stat, cells, 1))
    return stat


def merged_stats(stat_refs, cells):
    refs = dict(zip(STAT_ORDER, stat_refs))
    parts = [seen_from(refs[distance][...], distance, cells) for distance in range(4)]
    top = functools.reduce(jnp.maximum, parts)
    shares = [jnp.exp2(part - top) for part in parts]
    total = functools.reduce(jnp.add, shares)
    lse = top + jnp.log2(total)
    shares = [share / total for share in shares]
    delta = functools.reduce(
        jnp.add,
        [share[:HEADS] * part[HEADS : 2 * HEADS] for share, part in zip(shares, parts)],
    )
    return lse[:HEADS], delta, shares


def backward_kernel(cols, grid_rows, sizes, cells, first, last, *refs):
    tile_count = grid_rows * len(cols)
    qg_refs = refs[:4]
    kv_refs = refs[4 : 4 + tile_count]
    rest = refs[4 + tile_count :]
    if first:
        stat_refs, rest = rest[:4], rest[4:]
    else:
        (lse_ref, delta_ref, dq_ref), rest = rest[:3], rest[3:]
    if last:
        dq_outs, rest = rest[:4], rest[4:]
    else:
        dq_out, rest = rest[0], rest[1:]
    if first:
        (lse_ref, delta_ref, share_ref), rest = rest[:3], rest[3:]
        lse, delta, shares = merged_stats(stat_refs, cells)
        lse_ref[...] = lse
        delta_ref[...] = delta
        rows = [shares[d][head : head + 1, : 2 * cells] for head in range(HEADS) for d in range(4)]
        wide = jnp.concatenate(rows + [jnp.zeros((DH - len(rows), 2 * cells), F32)], axis=0)
        share_ref[...] = wide.T[:cells]
    else:
        lse, delta = lse_ref[...], delta_ref[...]
    col_refs = rest[: len(cols)]
    key_buf, value_buf = rest[len(cols) :]

    span = grid_rows * cells
    for i, ref in enumerate(kv_refs):
        key_buf[i * cells : (i + 1) * cells] = ref[0]
        value_buf[i * cells : (i + 1) * cells] = ref[1]
    blocks = [(head, slot) for head in range(HEADS) for slot in range(len(cols))]

    def products_of(head, slot):
        cut = head_slice(head)
        at = slice(slot * span, (slot + 1) * span)
        queries = jnp.concatenate([ref[0, :, cut] for ref in qg_refs], axis=0)
        grads = jnp.concatenate([ref[1, :, cut] for ref in qg_refs], axis=0)
        raw = dot_nt(key_buf[at, cut], queries)
        return raw, dot_nt(value_buf[at, cut], grads), queries, grads

    dscores = [[] for _ in range(HEADS)]
    ahead = products_of(*blocks[0])
    for i, (head, slot) in enumerate(blocks):
        raw, prob_grad, queries, grads = ahead
        if i + 1 < len(blocks):
            ahead = products_of(*blocks[i + 1])
        cut = head_slice(head)
        probs = []
        for row in range(grid_rows):
            bias = group_bias((row == 2, cols[slot] == 2), sizes)
            shift = lse[head : head + 1]
            shift = shift if bias is None else shift - bias
            probs.append(jnp.exp2(raw[row * cells : (row + 1) * cells] * SCALE_LOG2 - shift))
        probs = jnp.concatenate(probs, axis=0)
        dscore = (probs * (prob_grad - delta[head : head + 1])).astype(BF16)
        dv = dot_nn(probs.astype(BF16), grads).astype(BF16)
        dk = (dot_nn(dscore, queries) * SCALE).astype(BF16)
        for row in range(grid_rows):
            at = slice(row * cells, (row + 1) * cells)
            col_refs[slot][row, 0, :, cut] = dk[at]
            col_refs[slot][row, 1, :, cut] = dv[at]
        dscores[head].append(dscore)
    for head in range(HEADS):
        cut = head_slice(head)
        dq = dot_nn(key_buf[:, cut].T, jnp.concatenate(dscores[head], axis=0))
        dq = dq if first else dq + dq_ref[head]
        if last:
            dq = (dq * SCALE).T.astype(BF16)
            for i, ref in enumerate(dq_outs):
                ref[:, cut] = dq[i * cells : (i + 1) * cells]
        else:
            dq_out[head] = dq


def finish_kernel(cols, rows, *refs):
    o_refs, dq_refs, refs = refs[:4], refs[4:8], refs[8:]
    col_refs, row_refs = refs[:cols], refs[cols : cols + 2 * rows]
    share_ref, rope_ref, *outs, made_ref, sems = refs[cols + 2 * rows :]
    copies = [
        pltpu.make_async_copy(made_ref.at[i], out, sems.at[i]) for i, out in enumerate(outs)
    ]
    tables = [rope_ref[plane] for plane in range(3)]
    cuts = [head_slice(head) for head in range(HEADS)]

    def summed(parts):
        return functools.reduce(jnp.add, [part.astype(F32) for part in parts])

    def returned(which, cut):
        return summed(
            [ref[0, which, :, cut] for ref in col_refs] + [ref[:, cut] for ref in row_refs[which::2]]
        )

    for head, cut in enumerate(cuts):
        weighted = []
        for d, o_ref in zip((0, 3, 2, 1), o_refs):
            weight = share_ref[:, 4 * head + d : 4 * head + d + 1]
            weighted.append(o_ref[:, cut].astype(F32) * weight)
        made_ref[0, :, cut] = functools.reduce(jnp.add, weighted).astype(BF16)
    copies[0].start()
    for cut in cuts:
        made_ref[3, :, cut] = returned(1, cut).astype(BF16)
    copies[3].start()
    for cut in cuts:
        dq = summed([ref[:, cut] for ref in dq_refs])
        made_ref[1, :, cut] = turn(dq, *tables, -1.0).astype(BF16)
    copies[1].start()
    for cut in cuts:
        made_ref[2, :, cut] = turn(returned(0, cut), *tables, -1.0).astype(BF16)
    copies[2].start()
    for copy in copies:
        copy.wait()


def call(kernel, out_shape, args, flops=0, exps=0, scratch=(), space=pltpu.VMEM, out_space=pltpu.VMEM):
    shapes = jax.tree.leaves(out_shape)
    flops *= 8
    moved = sum(math.prod(x.shape) * x.dtype.itemsize for x in list(args) + shapes)
    return pl.pallas_call(
        kernel,
        out_shape=out_shape,
        in_specs=[pl.BlockSpec(memory_space=space)] * len(args),
        out_specs=jax.tree.map(lambda _: pl.BlockSpec(memory_space=out_space), out_shape),
        scratch_shapes=list(scratch),
        compiler_params=pltpu.CompilerParams(vmem_limit_bytes=VMEM_LIMIT),
        cost_estimate=pl.CostEstimate(flops=flops, bytes_accessed=moved, transcendentals=exps),
    )(*args)


def shards(query_in, key_in, value_in, cotangent):
    frames, rows, cols, chan = query_in.shape
    cells = frames * rows * cols
    sizes = {axis: lax.axis_size(axis) for axis in ("ta", "ha", "wa")}
    assert rows == TILE_H and cols == TILE_W and chan == HEADS * DH
    assert TILE_T % frames == 0 and frames * sizes["ta"] <= 2 * TILE_T
    assert sizes["ta"] == 4 and sizes["ha"] % 2 == 0 and sizes["wa"] % 2 == 0
    dims = (frames, rows, cols)
    table, begins = rope_table(frames * sizes["ta"], rows * sizes["ha"], cols * sizes["wa"])
    flat = [x.reshape(cells, chan) for x in (query_in, key_in, value_in, cotangent)]
    pair = jax.ShapeDtypeStruct((2, cells, chan), BF16)
    plain = jax.ShapeDtypeStruct((cells, chan), BF16)

    def real(*shape):
        return jax.ShapeDtypeStruct(shape, F32)

    with jax.named_scope("rotate"):
        kv, qg, rope = call(
            functools.partial(rotate_kernel, dims, begins),
            (pair, pair, real(3, cells, DH)),
            [pltpu.with_memory_space_constraint(x, pltpu.HBM) for x in (*flat, jnp.asarray(table))],
            scratch=[pltpu.VMEM((cells, chan), BF16)] * 2
            + [pltpu.VMEM(table.shape, F32), pltpu.SemaphoreType.DMA((5,))],
            space=pltpu.HBM,
        )

    def other_frames(x, distance):
        return lax.ppermute(x, "ta", [(i, i ^ distance) for i in range(sizes["ta"])])

    row_sides = side_pairs(sizes["ha"])
    col_sides = side_pairs(sizes["wa"])
    with jax.named_scope("halo"):
        kv_rows = [kv] + [lax.ppermute(kv, "ha", pairs) for pairs in row_sides]
        qg2 = other_frames(qg, 2)
        qg1 = other_frames(qg, 1)
        tiles = []
        for block in kv_rows:
            tiles.append([block] + [lax.ppermute(block, "wa", pairs) for pairs in col_sides])
        qg3 = other_frames(qg2, 1)
    grid_rows, grid_cols = 1 + len(row_sides), 1 + len(col_sides)
    flat_tiles = [tiles[row][col] for row in range(grid_rows) for col in range(grid_cols)]
    groups = {}
    for row in range(grid_rows):
        for col in range(grid_cols):
            groups.setdefault((row == 2, col == 2), []).append(row * grid_cols + col)
    groups = list(groups.items())

    key_count = len(flat_tiles) * cells
    product = 2 * cells * key_count * DH * HEADS

    def forward(blocks, first):
        count = len(blocks)
        stat = (count * cells, DH) if first is None else (8, 4 * cells)
        return call(
            functools.partial(forward_kernel, groups, sizes, cells, count, first is not None),
            (*[plain] * count, real(*stat)),
            (*blocks, *flat_tiles) + (() if first is None else (first,)),
            2 * product * count,
            cells * key_count * HEADS * count,
            [pltpu.VMEM((key_count, chan), BF16)] * 2,
        )

    with jax.named_scope("attend"):
        o0, o1, o2, first = forward((qg, qg1, qg2), None)
        o3, stat = forward((qg3,), first)
    with jax.named_scope("merge"):
        outs = [other_frames(o, d) for d, o in ((3, o3), (2, o2), (1, o1))]
        stat_near, outs[1:] = lax.optimization_barrier((stat, outs[1:]))
        stats = [stat, other_frames(stat_near, 1), other_frames(stat, 3), other_frames(stat, 2)]

    queries = (qg, qg1, qg2, qg3)
    col_shape = jax.ShapeDtypeStruct((grid_rows, 2, cells, chan), BF16)

    def gradients(which, carried):
        count = len(which)
        first, last = which[-1] == grid_cols - 1, which[0] == 0
        stat_outs = [real(HEADS, 4 * cells), real(HEADS, 4 * cells), real(cells, DH)]
        return call(
            functools.partial(backward_kernel, which, grid_rows, sizes, cells, first, last),
            (
                *([plain] * 4 if last else [real(HEADS, DH, 4 * cells)]),
                *(stat_outs if first else []),
                *[col_shape] * count,
            ),
            (*queries, *[tiles[row][col] for col in which for row in range(grid_rows)], *carried),
            20 * product * count // grid_cols,
            4 * cells * key_count * HEADS * count // grid_cols,
            [pltpu.VMEM((count * grid_rows * cells, chan), BF16)] * 2,
        )

    with jax.named_scope("gradients"):
        dq, lse, delta, shares, *sides = gradients(tuple(range(1, grid_cols)), stats)
        sides = [lax.ppermute(x, "wa", pairs) for x, pairs in zip(sides, col_sides)]
        d0, d1, d2, d3, own = gradients((0,), (lse, delta, dq))
    with jax.named_scope("return"):
        (d1, d2, d3), outs = lax.optimization_barrier(((d1, d2, d3), outs))
        col_parts = [own, *sides]
        dqs = [d0] + [other_frames(x, d) for d, x in ((2, d2), (3, d3), (1, d1))]
        row_parts = []
        for row, pairs in enumerate(row_sides, start=1):
            for which in range(2):
                partial_sum = sum(x[row, which].astype(F32) for x in col_parts).astype(BF16)
                row_parts.append(lax.ppermute(partial_sum, "ha", pairs))

    with jax.named_scope("finish"):
        results = call(
            functools.partial(finish_kernel, grid_cols, len(row_parts) // 2),
            [plain] * 4,
            (o0, *outs, *dqs, *col_parts, *row_parts, shares, rope),
            scratch=[pltpu.VMEM((4, cells, chan), BF16), pltpu.SemaphoreType.DMA((4,))],
            out_space=pltpu.HBM,
        )
    return tuple(x.reshape(query_in.shape) for x in results)


def solution(mesh):
    spec = P("ta", "ha", "wa", None)
    return jax.shard_map(
        shards, mesh=mesh, in_specs=(spec,) * 4, out_specs=(spec,) * 4, check_vma=False
    )
```

```python
import functools
import math

import jax
import jax.numpy as jnp
import numpy as np
from jax import lax
from jax.experimental import pallas as pl
from jax.experimental.pallas import tpu as pltpu
from jax.sharding import PartitionSpec as P

DH = 128
HEADS = 2
TILE_T = 6
TILE_H = 8
TILE_W = 8

NEGATIVE = -1e30
SCALE = DH**-0.5
SCALE_LOG2 = SCALE * math.log2(math.e)
F32 = jnp.float32
BF16 = jnp.bfloat16
STAT_ORDER = (0, 1, 3, 2)
VMEM_LIMIT = 48 * 1024 * 1024


def near_pairs(count):
    return [(i, i ^ 1) for i in range(count)]


def far_pairs(count):
    pairs = []
    for i in range(count):
        j = i + 1 if i % 2 else i - 1
        pairs.append((i, j if 0 <= j < count else i))
    return pairs


def far_exists(axis, count):
    pos = lax.axis_index(axis)
    other = jnp.where(pos % 2 == 1, pos + 1, pos - 1)
    return (other >= 0) & (other < count)


def side_pairs(count):
    sides = []
    if count > 1:
        sides.append(near_pairs(count))
    if count > 2:
        sides.append(far_pairs(count))
    return sides


def rope_table(frame_total, row_total, col_total):
    time_dims = DH // 8
    space_dims = (DH - time_dims) // 2
    slower = 256.0 ** (-np.arange(0, time_dims, 2) / time_dims)
    faster = 256.0 ** (-np.arange(0, space_dims, 2) / space_dims)
    starts = (0, time_dims, time_dims + space_dims)
    pieces = []
    for total, rates, start in zip(
        (frame_total, row_total, col_total), (slower, faster, faster), starts
    ):
        padded = -(-total // 8) * 8
        piece = np.zeros((3, padded, DH), np.float32)
        angles = np.arange(padded)[:, None] * rates[None, :]
        stop = start + 2 * len(rates)
        piece[0, :, start:stop:2] = np.cos(angles)
        piece[0, :, start + 1 : stop : 2] = np.cos(angles)
        piece[1, :, start:stop:2] = -np.sin(angles)
        piece[2, :, start + 1 : stop : 2] = np.sin(angles)
        pieces.append(piece)
    begins = np.cumsum([0] + [piece.shape[1] for piece in pieces])
    return np.concatenate(pieces, axis=1), tuple(int(x) for x in begins[:3])


def local_table(plane, table_ref, begins, frames, rows, cols):
    frame_lo = begins[0] + lax.axis_index("ta") * frames
    row_lo = pl.multiple_of(begins[1] + lax.axis_index("ha") * rows, 8)
    col_lo = pl.multiple_of(begins[2] + lax.axis_index("wa") * cols, 8)
    row_part = table_ref[plane, pl.ds(row_lo, rows), :]
    col_part = table_ref[plane, pl.ds(col_lo, cols), :]
    grids = []
    for i in range(frames):
        lead = row_part + table_ref[plane, pl.ds(frame_lo + i, 1), :]
        grid = lead[:, None, :] + col_part[None, :, :]
        grids.append(grid.reshape(rows * cols, DH))
    return jnp.concatenate(grids, axis=0)


def turn(x, cosine, sin_even, sin_odd, sign):
    follow = pltpu.roll(x, DH - 1, 1)
    lead = pltpu.roll(x, 1, 1)
    return x * cosine + sign * (follow * sin_even + lead * sin_odd)


def head_slice(head):
    return slice(head * DH, (head + 1) * DH)


def rotate_kernel(
    dims, begins, q_hbm, k_hbm, v_hbm, g_hbm, table_hbm, kv_ref, qg_ref, rope_ref, q_ref, k_ref,
    table_ref, sems,
):
    moves = [
        (table_hbm, table_ref),
        (k_hbm, k_ref),
        (q_hbm, q_ref),
        (v_hbm, kv_ref.at[1]),
        (g_hbm, qg_ref.at[1]),
    ]
    copies = [pltpu.make_async_copy(*move, sems.at[i]) for i, move in enumerate(moves)]
    for copy in copies:
        copy.start()
    copies[0].wait()
    tables = [local_table(plane, table_ref, begins, *dims) for plane in range(3)]
    for plane in range(3):
        rope_ref[plane] = tables[plane]
    for copy, source, target in ((copies[1], k_ref, kv_ref), (copies[2], q_ref, qg_ref)):
        copy.wait()
        for head in range(HEADS):
            cut = head_slice(head)
            target[0, :, cut] = turn(source[:, cut].astype(F32), *tables, 1.0).astype(BF16)
    copies[3].wait()
    copies[4].wait()


def dot_nt(a, b):
    return lax.dot_general(a, b, (((1,), (1,)), ((), ())), preferred_element_type=F32)


def dot_nn(a, b):
    return lax.dot_general(a, b, (((1,), (0,)), ((), ())), preferred_element_type=F32)


def dot_tn(a, b):
    return lax.dot_general(a, b, (((0,), (0,)), ((), ())), preferred_element_type=F32)


def group_bias(flags, sizes):
    valid = None
    for axis, is_far in zip(("ha", "wa"), flags):
        if is_far:
            here = far_exists(axis, sizes[axis])
            valid = here if valid is None else valid & here
    return None if valid is None else jnp.where(valid, 0.0, NEGATIVE).astype(F32)


def forward_kernel(groups, sizes, cells, count, last, *refs):
    tile_count = sum(len(members) for _, members in groups)
    qg_refs = refs[:count]
    kv_refs = refs[count : count + tile_count]
    rest = refs[count + tile_count :]
    if last:
        first_ref, rest = rest[0], rest[1:]
    o_refs, stat_ref = rest[:count], rest[count]
    spans = [(members, group_bias(flags, sizes)) for flags, members in groups]

    def joined(members, which, cut):
        return jnp.concatenate([kv_refs[i][which, :, cut] for i in members], axis=0)

    lane = lax.broadcasted_iota(jnp.int32, (count * cells, DH), 1)
    stat = jnp.zeros((count * cells, DH), F32)

    def scores_of(head):
        cut = head_slice(head)
        query = jnp.concatenate([ref[0, :, cut] for ref in qg_refs], axis=0)
        return [dot_nt(query, joined(members, 0, cut)) for members, _ in spans]

    ahead = scores_of(0)
    for head in range(HEADS):
        cut = head_slice(head)
        scores = ahead
        if head + 1 < HEADS:
            ahead = scores_of(head + 1)
        best = None
        for raw, (_, bias) in zip(scores, spans):
            top = jnp.max(raw, axis=1, keepdims=True) * SCALE_LOG2
            if bias is not None:
                top = top + bias
            best = top if best is None else jnp.maximum(best, top)
        total = None
        out = None
        for raw, (members, bias) in zip(scores, spans):
            shift = best if bias is None else best - bias
            weights = jnp.exp2(raw * SCALE_LOG2 - shift)
            part = jnp.sum(weights, axis=1, keepdims=True)
            piece = dot_nn(weights.astype(BF16), joined(members, 1, cut))
            total = part if total is None else total + part
            out = piece if out is None else out + piece
        out = out * (1.0 / total)
        grad = jnp.concatenate([ref[1, :, cut] for ref in qg_refs], axis=0)
        dotted = jnp.sum(out * grad.astype(F32), axis=1, keepdims=True)
        out = out.astype(BF16)
        for i, o_ref in enumerate(o_refs):
            o_ref[:, cut] = out[i * cells : (i + 1) * cells]
        stat = jnp.where(lane == head, best + jnp.log2(total), stat)
        stat = jnp.where(lane == HEADS + head, dotted, stat)
    if last:
        whole = jnp.concatenate([first_ref[...], stat], axis=0)
        stat_ref[...] = whole.T[: stat_ref.shape[0]]
    else:
        stat_ref[...] = stat


def seen_from(stat, distance, cells):
    if distance & 2:
        stat = pltpu.roll(stat, 2 * cells, 1)
    if distance & 1:
        lane = lax.broadcasted_iota(jnp.int32, stat.shape, 1)
        even = (lane < cells) | ((lane >= 2 * cells) & (lane < 3 * cells))
        stat = jnp.where(even, pltpu.roll(stat, 3 * cells, 1), pltpu.roll(stat, cells, 1))
    return stat


def merged_stats(stat_refs, cells):
    refs = dict(zip(STAT_ORDER, stat_refs))
    parts = [seen_from(refs[distance][...], distance, cells) for distance in range(4)]
    top = functools.reduce(jnp.maximum, parts)
    shares = [jnp.exp2(part - top) for part in parts]
    total = functools.reduce(jnp.add, shares)
    lse = top + jnp.log2(total)
    shares = [share / total for share in shares]
    delta = functools.reduce(
        jnp.add,
        [share[:HEADS] * part[HEADS : 2 * HEADS] for share, part in zip(shares, parts)],
    )
    return lse[:HEADS], delta, shares


def backward_kernel(cols, grid_rows, sizes, cells, first, last, *refs):
    tile_count = grid_rows * len(cols)
    qg_refs = refs[:4]
    kv_refs = refs[4 : 4 + tile_count]
    rest = refs[4 + tile_count :]
    if first:
        stat_refs, rest = rest[:4], rest[4:]
    else:
        (lse_ref, delta_ref, dq_ref), rest = rest[:3], rest[3:]
    if last:
        dq_outs, rest = rest[:4], rest[4:]
    else:
        dq_out, rest = rest[0], rest[1:]
    if first:
        (lse_ref, delta_ref, share_ref), rest = rest[:3], rest[3:]
        lse, delta, shares = merged_stats(stat_refs, cells)
        lse_ref[...] = lse
        delta_ref[...] = delta
        rows = [shares[d][head : head + 1, : 2 * cells] for head in range(HEADS) for d in range(4)]
        wide = jnp.concatenate(rows + [jnp.zeros((DH - len(rows), 2 * cells), F32)], axis=0)
        share_ref[...] = wide.T[:cells]
    else:
        lse, delta = lse_ref[...], delta_ref[...]
    col_refs = rest
    blocks = [(head, slot) for head in range(HEADS) for slot in range(len(cols))]

    def joined(slots, which, cut):
        picked = [kv_refs[slot * grid_rows + row] for slot in slots for row in range(grid_rows)]
        return jnp.concatenate([ref[which, :, cut] for ref in picked], axis=0)

    def products_of(head, slot):
        cut = head_slice(head)
        queries = jnp.concatenate([ref[0, :, cut] for ref in qg_refs], axis=0)
        grads = jnp.concatenate([ref[1, :, cut] for ref in qg_refs], axis=0)
        raw = dot_nt(joined([slot], 0, cut), queries)
        return raw, dot_nt(joined([slot], 1, cut), grads), queries, grads

    dscores = [[] for _ in range(HEADS)]
    ahead = products_of(*blocks[0])
    for i, (head, slot) in enumerate(blocks):
        raw, prob_grad, queries, grads = ahead
        if i + 1 < len(blocks):
            ahead = products_of(*blocks[i + 1])
        cut = head_slice(head)
        probs = []
        for row in range(grid_rows):
            bias = group_bias((row == 2, cols[slot] == 2), sizes)
            shift = lse[head : head + 1]
            shift = shift if bias is None else shift - bias
            probs.append(jnp.exp2(raw[row * cells : (row + 1) * cells] * SCALE_LOG2 - shift))
        probs = jnp.concatenate(probs, axis=0)
        dscore = (probs * (prob_grad - delta[head : head + 1])).astype(BF16)
        dv = dot_nn(probs.astype(BF16), grads).astype(BF16)
        dk = (dot_nn(dscore, queries) * SCALE).astype(BF16)
        for row in range(grid_rows):
            at = slice(row * cells, (row + 1) * cells)
            col_refs[slot][row, 0, :, cut] = dk[at]
            col_refs[slot][row, 1, :, cut] = dv[at]
        dscores[head].append(dscore)
    for head in range(HEADS):
        cut = head_slice(head)
        dq = dot_nn(joined(range(len(cols)), 0, cut).T, jnp.concatenate(dscores[head], axis=0))
        dq = dq if first else dq + dq_ref[head]
        if last:
            dq = (dq * SCALE).T.astype(BF16)
            for i, ref in enumerate(dq_outs):
                ref[:, cut] = dq[i * cells : (i + 1) * cells]
        else:
            dq_out[head] = dq


def finish_kernel(cols, rows, *refs):
    o_refs, dq_refs, refs = refs[:4], refs[4:8], refs[8:]
    col_refs, row_refs = refs[:cols], refs[cols : cols + 2 * rows]
    share_ref, rope_ref, *outs, made_ref, sems = refs[cols + 2 * rows :]
    copies = [
        pltpu.make_async_copy(made_ref.at[i], out, sems.at[i]) for i, out in enumerate(outs)
    ]
    tables = [rope_ref[plane] for plane in range(3)]
    cuts = [head_slice(head) for head in range(HEADS)]

    def summed(parts):
        return functools.reduce(jnp.add, [part.astype(F32) for part in parts])

    def returned(which, cut):
        return summed(
            [ref[0, which, :, cut] for ref in col_refs] + [ref[:, cut] for ref in row_refs[which::2]]
        )

    for head, cut in enumerate(cuts):
        weighted = []
        for d, o_ref in zip((0, 3, 2, 1), o_refs):
            weight = share_ref[:, 4 * head + d : 4 * head + d + 1]
            weighted.append(o_ref[:, cut].astype(F32) * weight)
        made_ref[0, :, cut] = functools.reduce(jnp.add, weighted).astype(BF16)
    copies[0].start()
    for cut in cuts:
        made_ref[3, :, cut] = returned(1, cut).astype(BF16)
    copies[3].start()
    for cut in cuts:
        dq = summed([ref[:, cut] for ref in dq_refs])
        made_ref[1, :, cut] = turn(dq, *tables, -1.0).astype(BF16)
    copies[1].start()
    for cut in cuts:
        made_ref[2, :, cut] = turn(returned(0, cut), *tables, -1.0).astype(BF16)
    copies[2].start()
    for copy in copies:
        copy.wait()


def call(kernel, out_shape, args, flops=0, exps=0, scratch=(), space=pltpu.VMEM, out_space=pltpu.VMEM):
    shapes = jax.tree.leaves(out_shape)
    flops *= 8
    moved = sum(math.prod(x.shape) * x.dtype.itemsize for x in list(args) + shapes)
    return pl.pallas_call(
        kernel,
        out_shape=out_shape,
        in_specs=[pl.BlockSpec(memory_space=space)] * len(args),
        out_specs=jax.tree.map(lambda _: pl.BlockSpec(memory_space=out_space), out_shape),
        scratch_shapes=list(scratch),
        compiler_params=pltpu.CompilerParams(vmem_limit_bytes=VMEM_LIMIT),
        cost_estimate=pl.CostEstimate(flops=flops, bytes_accessed=moved, transcendentals=exps),
    )(*args)


def shards(query_in, key_in, value_in, cotangent):
    frames, rows, cols, chan = query_in.shape
    cells = frames * rows * cols
    sizes = {axis: lax.axis_size(axis) for axis in ("ta", "ha", "wa")}
    assert rows == TILE_H and cols == TILE_W and chan == HEADS * DH
    assert TILE_T % frames == 0 and frames * sizes["ta"] <= 2 * TILE_T
    assert sizes["ta"] == 4 and sizes["ha"] % 2 == 0 and sizes["wa"] % 2 == 0
    dims = (frames, rows, cols)
    table, begins = rope_table(frames * sizes["ta"], rows * sizes["ha"], cols * sizes["wa"])
    flat = [x.reshape(cells, chan) for x in (query_in, key_in, value_in, cotangent)]
    pair = jax.ShapeDtypeStruct((2, cells, chan), BF16)
    plain = jax.ShapeDtypeStruct((cells, chan), BF16)

    def real(*shape):
        return jax.ShapeDtypeStruct(shape, F32)

    with jax.named_scope("rotate"):
        kv, qg, rope = call(
            functools.partial(rotate_kernel, dims, begins),
            (pair, pair, real(3, cells, DH)),
            [pltpu.with_memory_space_constraint(x, pltpu.HBM) for x in (*flat, jnp.asarray(table))],
            scratch=[pltpu.VMEM((cells, chan), BF16)] * 2
            + [pltpu.VMEM(table.shape, F32), pltpu.SemaphoreType.DMA((5,))],
            space=pltpu.HBM,
        )

    def other_frames(x, distance):
        return lax.ppermute(x, "ta", [(i, i ^ distance) for i in range(sizes["ta"])])

    row_sides = side_pairs(sizes["ha"])
    col_sides = side_pairs(sizes["wa"])
    with jax.named_scope("halo"):
        kv_rows = [kv] + [lax.ppermute(kv, "ha", pairs) for pairs in row_sides]
        qg2 = other_frames(qg, 2)
        qg1 = other_frames(qg, 1)
        tiles = []
        for block in kv_rows:
            tiles.append([block] + [lax.ppermute(block, "wa", pairs) for pairs in col_sides])
        qg3 = other_frames(qg2, 1)
    grid_rows, grid_cols = 1 + len(row_sides), 1 + len(col_sides)
    flat_tiles = [tiles[row][col] for row in range(grid_rows) for col in range(grid_cols)]
    groups = {}
    for row in range(grid_rows):
        for col in range(grid_cols):
            groups.setdefault((row == 2, col == 2), []).append(row * grid_cols + col)
    groups = list(groups.items())

    key_count = len(flat_tiles) * cells
    product = 2 * cells * key_count * DH * HEADS

    def forward(blocks, first):
        count = len(blocks)
        stat = (count * cells, DH) if first is None else (8, 4 * cells)
        return call(
            functools.partial(forward_kernel, groups, sizes, cells, count, first is not None),
            (*[plain] * count, real(*stat)),
            (*blocks, *flat_tiles) + (() if first is None else (first,)),
            2 * product * count,
            cells * key_count * HEADS * count,
        )

    with jax.named_scope("attend"):
        o0, o1, o2, first = forward((qg, qg1, qg2), None)
        o3, stat = forward((qg3,), first)
    with jax.named_scope("merge"):
        outs = [other_frames(o, d) for d, o in ((3, o3), (2, o2), (1, o1))]
        stat_near, outs[1:] = lax.optimization_barrier((stat, outs[1:]))
        stats = [stat, other_frames(stat_near, 1), other_frames(stat, 3), other_frames(stat, 2)]

    queries = (qg, qg1, qg2, qg3)
    col_shape = jax.ShapeDtypeStruct((grid_rows, 2, cells, chan), BF16)

    def gradients(which, carried):
        count = len(which)
        first, last = which[-1] == grid_cols - 1, which[0] == 0
        stat_outs = [real(HEADS, 4 * cells), real(HEADS, 4 * cells), real(cells, DH)]
        return call(
            functools.partial(backward_kernel, which, grid_rows, sizes, cells, first, last),
            (
                *([plain] * 4 if last else [real(HEADS, DH, 4 * cells)]),
                *(stat_outs if first else []),
                *[col_shape] * count,
            ),
            (*queries, *[tiles[row][col] for col in which for row in range(grid_rows)], *carried),
            20 * product * count // grid_cols,
            4 * cells * key_count * HEADS * count // grid_cols,
        )

    with jax.named_scope("gradients"):
        dq, lse, delta, shares, *sides = gradients(tuple(range(1, grid_cols)), stats)
        sides = [lax.ppermute(x, "wa", pairs) for x, pairs in zip(sides, col_sides)]
        d0, d1, d2, d3, own = gradients((0,), (lse, delta, dq))
    with jax.named_scope("return"):
        (d1, d2, d3), outs = lax.optimization_barrier(((d1, d2, d3), outs))
        col_parts = [own, *sides]
        dqs = [d0] + [other_frames(x, d) for d, x in ((2, d2), (3, d3), (1, d1))]
        row_parts = []
        for row, pairs in enumerate(row_sides, start=1):
            for which in range(2):
                partial_sum = sum(x[row, which].astype(F32) for x in col_parts).astype(BF16)
                row_parts.append(lax.ppermute(partial_sum, "ha", pairs))

    with jax.named_scope("finish"):
        results = call(
            functools.partial(finish_kernel, grid_cols, len(row_parts) // 2),
            [plain] * 4,
            (o0, *outs, *dqs, *col_parts, *row_parts, shares, rope),
            scratch=[pltpu.VMEM((4, cells, chan), BF16), pltpu.SemaphoreType.DMA((4,))],
            out_space=pltpu.HBM,
        )
    return tuple(x.reshape(query_in.shape) for x in results)


def solution(mesh):
    spec = P("ta", "ha", "wa", None)
    return jax.shard_map(
        shards, mesh=mesh, in_specs=(spec,) * 4, out_specs=(spec,) * 4, check_vma=False
    )
```

```python
import functools
import math

import jax
import jax.numpy as jnp
import numpy as np
from jax import lax
from jax.experimental import pallas as pl
from jax.experimental.pallas import tpu as pltpu
from jax.sharding import PartitionSpec as P

DH = 128
HEADS = 2
TILE_T = 6
TILE_H = 8
TILE_W = 8

NEGATIVE = -1e30
SCALE = DH**-0.5
SCALE_LOG2 = SCALE * math.log2(math.e)
F32 = jnp.float32
BF16 = jnp.bfloat16
STAT_ORDER = (0, 1, 3, 2)
VMEM_LIMIT = 48 * 1024 * 1024


def near_pairs(count):
    return [(i, i ^ 1) for i in range(count)]


def far_pairs(count):
    pairs = []
    for i in range(count):
        j = i + 1 if i % 2 else i - 1
        pairs.append((i, j if 0 <= j < count else i))
    return pairs


def far_exists(axis, count):
    pos = lax.axis_index(axis)
    other = jnp.where(pos % 2 == 1, pos + 1, pos - 1)
    return (other >= 0) & (other < count)


def side_pairs(count):
    sides = []
    if count > 1:
        sides.append(near_pairs(count))
    if count > 2:
        sides.append(far_pairs(count))
    return sides


def rope_table(frame_total, row_total, col_total):
    time_dims = DH // 8
    space_dims = (DH - time_dims) // 2
    slower = 256.0 ** (-np.arange(0, time_dims, 2) / time_dims)
    faster = 256.0 ** (-np.arange(0, space_dims, 2) / space_dims)
    starts = (0, time_dims, time_dims + space_dims)
    pieces = []
    for total, rates, start in zip(
        (frame_total, row_total, col_total), (slower, faster, faster), starts
    ):
        padded = -(-total // 8) * 8
        piece = np.zeros((3, padded, DH), np.float32)
        angles = np.arange(padded)[:, None] * rates[None, :]
        stop = start + 2 * len(rates)
        piece[0, :, start:stop:2] = np.cos(angles)
        piece[0, :, start + 1 : stop : 2] = np.cos(angles)
        piece[1, :, start:stop:2] = -np.sin(angles)
        piece[2, :, start + 1 : stop : 2] = np.sin(angles)
        pieces.append(piece)
    begins = np.cumsum([0] + [piece.shape[1] for piece in pieces])
    return np.concatenate(pieces, axis=1), tuple(int(x) for x in begins[:3])


def local_table(plane, table_ref, begins, frames, rows, cols):
    frame_lo = begins[0] + lax.axis_index("ta") * frames
    row_lo = pl.multiple_of(begins[1] + lax.axis_index("ha") * rows, 8)
    col_lo = pl.multiple_of(begins[2] + lax.axis_index("wa") * cols, 8)
    row_part = table_ref[plane, pl.ds(row_lo, rows), :]
    col_part = table_ref[plane, pl.ds(col_lo, cols), :]
    grids = []
    for i in range(frames):
        lead = row_part + table_ref[plane, pl.ds(frame_lo + i, 1), :]
        grid = lead[:, None, :] + col_part[None, :, :]
        grids.append(grid.reshape(rows * cols, DH))
    return jnp.concatenate(grids, axis=0)


def turn(x, cosine, sin_even, sin_odd, sign):
    follow = pltpu.roll(x, DH - 1, 1)
    lead = pltpu.roll(x, 1, 1)
    return x * cosine + sign * (follow * sin_even + lead * sin_odd)


def head_slice(head):
    return slice(head * DH, (head + 1) * DH)


def rotate_kernel(
    dims, begins, q_hbm, k_hbm, v_hbm, g_hbm, table_hbm, kv_ref, qg_ref, rope_ref, q_ref, k_ref,
    table_ref, sems,
):
    moves = [
        (table_hbm, table_ref),
        (k_hbm, k_ref),
        (q_hbm, q_ref),
        (v_hbm, kv_ref.at[1]),
        (g_hbm, qg_ref.at[1]),
    ]
    copies = [pltpu.make_async_copy(*move, sems.at[i]) for i, move in enumerate(moves)]
    for copy in copies:
        copy.start()
    copies[0].wait()
    tables = [local_table(plane, table_ref, begins, *dims) for plane in range(3)]
    for plane in range(3):
        rope_ref[plane] = tables[plane]
    for copy, source, target in ((copies[1], k_ref, kv_ref), (copies[2], q_ref, qg_ref)):
        copy.wait()
        for head in range(HEADS):
            cut = head_slice(head)
            target[0, :, cut] = turn(source[:, cut].astype(F32), *tables, 1.0).astype(BF16)
    copies[3].wait()
    copies[4].wait()


def dot_nt(a, b):
    return lax.dot_general(a, b, (((1,), (1,)), ((), ())), preferred_element_type=F32)


def dot_nn(a, b):
    return lax.dot_general(a, b, (((1,), (0,)), ((), ())), preferred_element_type=F32)


def dot_tn(a, b):
    return lax.dot_general(a, b, (((0,), (0,)), ((), ())), preferred_element_type=F32)


def group_bias(flags, sizes):
    valid = None
    for axis, is_far in zip(("ha", "wa"), flags):
        if is_far:
            here = far_exists(axis, sizes[axis])
            valid = here if valid is None else valid & here
    return None if valid is None else jnp.where(valid, 0.0, NEGATIVE).astype(F32)


def forward_kernel(groups, sizes, cells, count, last, *refs):
    tile_count = sum(len(members) for _, members in groups)
    qg_refs = refs[:count]
    kv_refs = refs[count : count + tile_count]
    rest = refs[count + tile_count :]
    if last:
        first_ref, rest = rest[0], rest[1:]
    o_refs, stat_ref = rest[:count], rest[count]
    spans = [(members, group_bias(flags, sizes)) for flags, members in groups]

    def joined(members, which, cut):
        return jnp.concatenate([kv_refs[i][which, :, cut] for i in members], axis=0)

    lane = lax.broadcasted_iota(jnp.int32, (count * cells, DH), 1)
    stat = jnp.zeros((count * cells, DH), F32)

    def scores_of(head):
        cut = head_slice(head)
        query = jnp.concatenate([ref[0, :, cut] for ref in qg_refs], axis=0)
        return [dot_nt(query, joined(members, 0, cut)) for members, _ in spans]

    ahead = scores_of(0)
    for head in range(HEADS):
        cut = head_slice(head)
        scores = ahead
        if head + 1 < HEADS:
            ahead = scores_of(head + 1)
        best = None
        for raw, (_, bias) in zip(scores, spans):
            top = jnp.max(raw, axis=1, keepdims=True) * SCALE_LOG2
            if bias is not None:
                top = top + bias
            best = top if best is None else jnp.maximum(best, top)
        total = None
        out = None
        for raw, (members, bias) in zip(scores, spans):
            shift = best if bias is None else best - bias
            weights = jnp.exp2(raw * SCALE_LOG2 - shift)
            part = jnp.sum(weights, axis=1, keepdims=True)
            piece = dot_nn(weights.astype(BF16), joined(members, 1, cut))
            total = part if total is None else total + part
            out = piece if out is None else out + piece
        out = out * (1.0 / total)
        grad = jnp.concatenate([ref[1, :, cut] for ref in qg_refs], axis=0)
        dotted = jnp.sum(out * grad.astype(F32), axis=1, keepdims=True)
        out = out.astype(BF16)
        for i, o_ref in enumerate(o_refs):
            o_ref[:, cut] = out[i * cells : (i + 1) * cells]
        stat = jnp.where(lane == head, best + jnp.log2(total), stat)
        stat = jnp.where(lane == HEADS + head, dotted, stat)
    if last:
        whole = jnp.concatenate([first_ref[...], stat], axis=0)
        stat_ref[...] = whole.T[: stat_ref.shape[0]]
    else:
        stat_ref[...] = stat


def seen_from(stat, distance, cells):
    if distance & 2:
        stat = pltpu.roll(stat, 2 * cells, 1)
    if distance & 1:
        lane = lax.broadcasted_iota(jnp.int32, stat.shape, 1)
        even = (lane < cells) | ((lane >= 2 * cells) & (lane < 3 * cells))
        stat = jnp.where(even, pltpu.roll(stat, 3 * cells, 1), pltpu.roll(stat, cells, 1))
    return stat


def merged_stats(stat_refs, cells):
    refs = dict(zip(STAT_ORDER, stat_refs))
    parts = [seen_from(refs[distance][...], distance, cells) for distance in range(4)]
    top = functools.reduce(jnp.maximum, parts)
    shares = [jnp.exp2(part - top) for part in parts]
    total = functools.reduce(jnp.add, shares)
    lse = top + jnp.log2(total)
    shares = [share / total for share in shares]
    delta = functools.reduce(
        jnp.add,
        [share[:HEADS] * part[HEADS : 2 * HEADS] for share, part in zip(shares, parts)],
    )
    return lse[:HEADS], delta, shares


def backward_kernel(cols, grid_rows, sizes, cells, first, last, *refs):
    tile_count = grid_rows * len(cols)
    qg_refs = refs[:4]
    kv_refs = refs[4 : 4 + tile_count]
    rest = refs[4 + tile_count :]
    if first:
        stat_refs, rest = rest[:4], rest[4:]
    else:
        (lse_ref, delta_ref, dq_ref), rest = rest[:3], rest[3:]
    if last:
        dq_outs, rest = rest[:4], rest[4:]
    else:
        dq_out, rest = rest[0], rest[1:]
    if first:
        (lse_ref, delta_ref, share_ref), rest = rest[:3], rest[3:]
        lse, delta, shares = merged_stats(stat_refs, cells)
        lse_ref[...] = lse
        delta_ref[...] = delta
        rows = [shares[d][head : head + 1, : 2 * cells] for head in range(HEADS) for d in range(4)]
        wide = jnp.concatenate(rows + [jnp.zeros((DH - len(rows), 2 * cells), F32)], axis=0)
        share_ref[...] = wide.T[:cells]
    else:
        lse, delta = lse_ref[...], delta_ref[...]
    col_refs = rest
    blocks = [(head, slot) for head in range(HEADS) for slot in range(len(cols))]

    def joined(slots, which, cut):
        picked = [kv_refs[slot * grid_rows + row] for slot in slots for row in range(grid_rows)]
        return jnp.concatenate([ref[which, :, cut] for ref in picked], axis=0)

    def products_of(head, slot):
        cut = head_slice(head)
        queries = jnp.concatenate([ref[0, :, cut] for ref in qg_refs], axis=0)
        grads = jnp.concatenate([ref[1, :, cut] for ref in qg_refs], axis=0)
        raw = dot_nt(joined([slot], 0, cut), queries)
        return raw, dot_nt(joined([slot], 1, cut), grads), queries, grads

    dscores = [[] for _ in range(HEADS)]
    ahead = products_of(*blocks[0])
    for i, (head, slot) in enumerate(blocks):
        raw, prob_grad, queries, grads = ahead
        if i + 1 < len(blocks):
            ahead = products_of(*blocks[i + 1])
        cut = head_slice(head)
        probs = []
        for row in range(grid_rows):
            bias = group_bias((row == 2, cols[slot] == 2), sizes)
            shift = lse[head : head + 1]
            shift = shift if bias is None else shift - bias
            probs.append(jnp.exp2(raw[row * cells : (row + 1) * cells] * SCALE_LOG2 - shift))
        probs = jnp.concatenate(probs, axis=0)
        dscore = (probs * (prob_grad - delta[head : head + 1])).astype(BF16)
        dv = dot_nn(probs.astype(BF16), grads).astype(BF16)
        dk = (dot_nn(dscore, queries) * SCALE).astype(BF16)
        for row in range(grid_rows):
            at = slice(row * cells, (row + 1) * cells)
            col_refs[slot][row, 0, :, cut] = dk[at]
            col_refs[slot][row, 1, :, cut] = dv[at]
        dscores[head].append(dscore)
    for head in range(HEADS):
        cut = head_slice(head)
        dq = dot_nn(joined(range(len(cols)), 0, cut).T, jnp.concatenate(dscores[head], axis=0))
        dq = dq if first else dq + dq_ref[head]
        if last:
            dq = (dq * SCALE).T.astype(BF16)
            for i, ref in enumerate(dq_outs):
                ref[:, cut] = dq[i * cells : (i + 1) * cells]
        else:
            dq_out[head] = dq


def summed(parts):
    return functools.reduce(jnp.add, [part.astype(F32) for part in parts])


def gather_kernel(cols, *refs):
    o_refs, col_refs = refs[:4], refs[4 : 4 + cols]
    share_ref, out_ref, sum_ref = refs[4 + cols :]
    for head in range(HEADS):
        cut = head_slice(head)
        weighted = []
        for d, o_ref in zip((0, 3, 2, 1), o_refs):
            weight = share_ref[:, 4 * head + d : 4 * head + d + 1]
            weighted.append(o_ref[:, cut].astype(F32) * weight)
        out_ref[:, cut] = functools.reduce(jnp.add, weighted).astype(BF16)
        for which in range(2):
            sum_ref[which, :, cut] = summed([ref[0, which, :, cut] for ref in col_refs])


def finish_kernel(rows, *refs):
    dq_refs, row_refs = refs[:4], refs[4 : 4 + 2 * rows]
    sum_ref, rope_ref, dq_out, dk_out, dv_out = refs[4 + 2 * rows :]
    tables = [rope_ref[plane] for plane in range(3)]
    for head in range(HEADS):
        cut = head_slice(head)
        dq = summed([ref[:, cut] for ref in dq_refs])
        dq_out[:, cut] = turn(dq, *tables, -1.0).astype(BF16)
        dk, dv = [
            summed([sum_ref[which, :, cut]] + [ref[:, cut] for ref in row_refs[which::2]])
            for which in range(2)
        ]
        dk_out[:, cut] = turn(dk, *tables, -1.0).astype(BF16)
        dv_out[:, cut] = dv.astype(BF16)


def call(kernel, out_shape, args, flops=0, exps=0, scratch=(), space=pltpu.VMEM):
    shapes = jax.tree.leaves(out_shape)
    flops *= 8
    moved = sum(math.prod(x.shape) * x.dtype.itemsize for x in list(args) + shapes)
    return pl.pallas_call(
        kernel,
        out_shape=out_shape,
        in_specs=[pl.BlockSpec(memory_space=space)] * len(args),
        scratch_shapes=list(scratch),
        compiler_params=pltpu.CompilerParams(vmem_limit_bytes=VMEM_LIMIT),
        cost_estimate=pl.CostEstimate(flops=flops, bytes_accessed=moved, transcendentals=exps),
    )(*args)


def shards(query_in, key_in, value_in, cotangent):
    frames, rows, cols, chan = query_in.shape
    cells = frames * rows * cols
    sizes = {axis: lax.axis_size(axis) for axis in ("ta", "ha", "wa")}
    assert rows == TILE_H and cols == TILE_W and chan == HEADS * DH
    assert TILE_T % frames == 0 and frames * sizes["ta"] <= 2 * TILE_T
    assert sizes["ta"] == 4 and sizes["ha"] % 2 == 0 and sizes["wa"] % 2 == 0
    dims = (frames, rows, cols)
    table, begins = rope_table(frames * sizes["ta"], rows * sizes["ha"], cols * sizes["wa"])
    flat = [x.reshape(cells, chan) for x in (query_in, key_in, value_in, cotangent)]
    pair = jax.ShapeDtypeStruct((2, cells, chan), BF16)
    plain = jax.ShapeDtypeStruct((cells, chan), BF16)

    def real(*shape):
        return jax.ShapeDtypeStruct(shape, F32)

    with jax.named_scope("rotate"):
        kv, qg, rope = call(
            functools.partial(rotate_kernel, dims, begins),
            (pair, pair, real(3, cells, DH)),
            [pltpu.with_memory_space_constraint(x, pltpu.HBM) for x in (*flat, jnp.asarray(table))],
            scratch=[pltpu.VMEM((cells, chan), BF16)] * 2
            + [pltpu.VMEM(table.shape, F32), pltpu.SemaphoreType.DMA((5,))],
            space=pltpu.HBM,
        )

    def other_frames(x, distance):
        return lax.ppermute(x, "ta", [(i, i ^ distance) for i in range(sizes["ta"])])

    row_sides = side_pairs(sizes["ha"])
    col_sides = side_pairs(sizes["wa"])
    with jax.named_scope("halo"):
        kv_rows = [kv] + [lax.ppermute(kv, "ha", pairs) for pairs in row_sides]
        qg2 = other_frames(qg, 2)
        qg1 = other_frames(qg, 1)
        tiles = []
        for block in kv_rows:
            tiles.append([block] + [lax.ppermute(block, "wa", pairs) for pairs in col_sides])
        qg3 = other_frames(qg2, 1)
    grid_rows, grid_cols = 1 + len(row_sides), 1 + len(col_sides)
    flat_tiles = [tiles[row][col] for row in range(grid_rows) for col in range(grid_cols)]
    groups = {}
    for row in range(grid_rows):
        for col in range(grid_cols):
            groups.setdefault((row == 2, col == 2), []).append(row * grid_cols + col)
    groups = list(groups.items())

    key_count = len(flat_tiles) * cells
    product = 2 * cells * key_count * DH * HEADS

    def forward(blocks, first):
        count = len(blocks)
        stat = (count * cells, DH) if first is None else (8, 4 * cells)
        return call(
            functools.partial(forward_kernel, groups, sizes, cells, count, first is not None),
            (*[plain] * count, real(*stat)),
            (*blocks, *flat_tiles) + (() if first is None else (first,)),
            2 * product * count,
            cells * key_count * HEADS * count,
        )

    with jax.named_scope("attend"):
        o0, o1, o2, first = forward((qg, qg1, qg2), None)
        o3, stat = forward((qg3,), first)
    with jax.named_scope("merge"):
        outs = [other_frames(o, d) for d, o in ((3, o3), (2, o2), (1, o1))]
        stat_near, outs[1:] = lax.optimization_barrier((stat, outs[1:]))
        stats = [stat, other_frames(stat_near, 1), other_frames(stat, 3), other_frames(stat, 2)]

    queries = (qg, qg1, qg2, qg3)
    col_shape = jax.ShapeDtypeStruct((grid_rows, 2, cells, chan), BF16)

    def gradients(which, carried):
        count = len(which)
        first, last = which[-1] == grid_cols - 1, which[0] == 0
        stat_outs = [real(HEADS, 4 * cells), real(HEADS, 4 * cells), real(cells, DH)]
        return call(
            functools.partial(backward_kernel, which, grid_rows, sizes, cells, first, last),
            (
                *([plain] * 4 if last else [real(HEADS, DH, 4 * cells)]),
                *(stat_outs if first else []),
                *[col_shape] * count,
            ),
            (*queries, *[tiles[row][col] for col in which for row in range(grid_rows)], *carried),
            20 * product * count // grid_cols,
            4 * cells * key_count * HEADS * count // grid_cols,
        )

    with jax.named_scope("gradients"):
        dq, lse, delta, shares, *sides = gradients(tuple(range(1, grid_cols)), stats)
        sides = [lax.ppermute(x, "wa", pairs) for x, pairs in zip(sides, col_sides)]
        d0, d1, d2, d3, own = gradients((0,), (lse, delta, dq))
    with jax.named_scope("return"):
        (d1, d2, d3), outs = lax.optimization_barrier(((d1, d2, d3), outs))
        col_parts = [own, *sides]
        dqs = [d0] + [other_frames(x, d) for d, x in ((2, d2), (3, d3), (1, d1))]
        row_parts = []
        for row, pairs in enumerate(row_sides, start=1):
            for which in range(2):
                partial_sum = sum(x[row, which].astype(F32) for x in col_parts).astype(BF16)
                row_parts.append(lax.ppermute(partial_sum, "ha", pairs))

    with jax.named_scope("finish"):
        attended, sums = call(
            functools.partial(gather_kernel, grid_cols),
            (plain, real(2, cells, chan)),
            (o0, *outs, *col_parts, shares),
        )
        results = call(
            functools.partial(finish_kernel, len(row_parts) // 2),
            [plain] * 3,
            (*dqs, *row_parts, sums, rope),
        )
    return tuple(x.reshape(query_in.shape) for x in (attended, *results))


def solution(mesh):
    spec = P("ta", "ha", "wa", None)
    return jax.shard_map(
        shards, mesh=mesh, in_specs=(spec,) * 4, out_specs=(spec,) * 4, check_vma=False
    )
```

```python
import functools
import math

import jax
import jax.numpy as jnp
import numpy as np
from jax import lax
from jax.experimental import pallas as pl
from jax.experimental.pallas import tpu as pltpu
from jax.sharding import PartitionSpec as P

DH = 128
HEADS = 2
TILE_T = 6
TILE_H = 8
TILE_W = 8

NEGATIVE = -1e30
SCALE = DH**-0.5
SCALE_LOG2 = SCALE * math.log2(math.e)
F32 = jnp.float32
BF16 = jnp.bfloat16
STAT_ORDER = (0, 1, 3, 2)
VMEM_LIMIT = 48 * 1024 * 1024


def near_pairs(count):
    return [(i, i ^ 1) for i in range(count)]


def far_pairs(count):
    pairs = []
    for i in range(count):
        j = i + 1 if i % 2 else i - 1
        pairs.append((i, j if 0 <= j < count else i))
    return pairs


def far_exists(axis, count):
    pos = lax.axis_index(axis)
    other = jnp.where(pos % 2 == 1, pos + 1, pos - 1)
    return (other >= 0) & (other < count)


def side_pairs(count):
    sides = []
    if count > 1:
        sides.append(near_pairs(count))
    if count > 2:
        sides.append(far_pairs(count))
    return sides


def rope_table(frame_total, row_total, col_total):
    time_dims = DH // 8
    space_dims = (DH - time_dims) // 2
    slower = 256.0 ** (-np.arange(0, time_dims, 2) / time_dims)
    faster = 256.0 ** (-np.arange(0, space_dims, 2) / space_dims)
    starts = (0, time_dims, time_dims + space_dims)
    pieces = []
    for total, rates, start in zip(
        (frame_total, row_total, col_total), (slower, faster, faster), starts
    ):
        padded = -(-total // 8) * 8
        piece = np.zeros((3, padded, DH), np.float32)
        angles = np.arange(padded)[:, None] * rates[None, :]
        stop = start + 2 * len(rates)
        piece[0, :, start:stop:2] = np.cos(angles)
        piece[0, :, start + 1 : stop : 2] = np.cos(angles)
        piece[1, :, start:stop:2] = -np.sin(angles)
        piece[2, :, start + 1 : stop : 2] = np.sin(angles)
        pieces.append(piece)
    begins = np.cumsum([0] + [piece.shape[1] for piece in pieces])
    return np.concatenate(pieces, axis=1), tuple(int(x) for x in begins[:3])


def local_table(plane, table_ref, begins, frames, rows, cols):
    frame_lo = begins[0] + lax.axis_index("ta") * frames
    row_lo = pl.multiple_of(begins[1] + lax.axis_index("ha") * rows, 8)
    col_lo = pl.multiple_of(begins[2] + lax.axis_index("wa") * cols, 8)
    row_part = table_ref[plane, pl.ds(row_lo, rows), :]
    col_part = table_ref[plane, pl.ds(col_lo, cols), :]
    grids = []
    for i in range(frames):
        lead = row_part + table_ref[plane, pl.ds(frame_lo + i, 1), :]
        grid = lead[:, None, :] + col_part[None, :, :]
        grids.append(grid.reshape(rows * cols, DH))
    return jnp.concatenate(grids, axis=0)


def turn(x, cosine, sin_even, sin_odd, sign):
    follow = pltpu.roll(x, DH - 1, 1)
    lead = pltpu.roll(x, 1, 1)
    return x * cosine + sign * (follow * sin_even + lead * sin_odd)


def head_slice(head):
    return slice(head * DH, (head + 1) * DH)


def rotate_kernel(
    dims, begins, q_hbm, k_hbm, v_hbm, g_hbm, table_hbm, kv_ref, qg_ref, rope_ref, q_ref, k_ref,
    table_ref, sems,
):
    moves = [
        (table_hbm, table_ref),
        (k_hbm, k_ref),
        (q_hbm, q_ref),
        (v_hbm, kv_ref.at[1]),
        (g_hbm, qg_ref.at[1]),
    ]
    copies = [pltpu.make_async_copy(*move, sems.at[i]) for i, move in enumerate(moves)]
    for copy in copies:
        copy.start()
    copies[0].wait()
    tables = [local_table(plane, table_ref, begins, *dims) for plane in range(3)]
    for plane in range(3):
        rope_ref[plane] = tables[plane]
    for copy, source, target in ((copies[1], k_ref, kv_ref), (copies[2], q_ref, qg_ref)):
        copy.wait()
        for head in range(HEADS):
            cut = head_slice(head)
            target[0, :, cut] = turn(source[:, cut].astype(F32), *tables, 1.0).astype(BF16)
    copies[3].wait()
    copies[4].wait()


def dot_nt(a, b):
    return lax.dot_general(a, b, (((1,), (1,)), ((), ())), preferred_element_type=F32)


def dot_nn(a, b):
    return lax.dot_general(a, b, (((1,), (0,)), ((), ())), preferred_element_type=F32)


def dot_tn(a, b):
    return lax.dot_general(a, b, (((0,), (0,)), ((), ())), preferred_element_type=F32)


def group_bias(flags, sizes):
    valid = None
    for axis, is_far in zip(("ha", "wa"), flags):
        if is_far:
            here = far_exists(axis, sizes[axis])
            valid = here if valid is None else valid & here
    return None if valid is None else jnp.where(valid, 0.0, NEGATIVE).astype(F32)


def forward_kernel(groups, sizes, cells, count, last, *refs):
    tile_count = sum(len(members) for _, members in groups)
    qg_refs = refs[:count]
    kv_refs = refs[count : count + tile_count]
    rest = refs[count + tile_count :]
    if last:
        first_ref, rest = rest[0], rest[1:]
    o_refs, stat_ref = rest[:count], rest[count]
    spans = [(members, group_bias(flags, sizes)) for flags, members in groups]

    def joined(members, which, cut):
        return jnp.concatenate([kv_refs[i][which, :, cut] for i in members], axis=0)

    lane = lax.broadcasted_iota(jnp.int32, (count * cells, DH), 1)
    stat = jnp.zeros((count * cells, DH), F32)

    def scores_of(head):
        cut = head_slice(head)
        query = jnp.concatenate([ref[0, :, cut] for ref in qg_refs], axis=0)
        return [dot_nt(query, joined(members, 0, cut)) for members, _ in spans]

    ahead = scores_of(0)
    for head in range(HEADS):
        cut = head_slice(head)
        scores = ahead
        if head + 1 < HEADS:
            ahead = scores_of(head + 1)
        best = None
        for raw, (_, bias) in zip(scores, spans):
            top = jnp.max(raw, axis=1, keepdims=True) * SCALE_LOG2
            if bias is not None:
                top = top + bias
            best = top if best is None else jnp.maximum(best, top)
        total = None
        out = None
        for raw, (members, bias) in zip(scores, spans):
            shift = best if bias is None else best - bias
            weights = jnp.exp2(raw * SCALE_LOG2 - shift)
            part = jnp.sum(weights, axis=1, keepdims=True)
            piece = dot_nn(weights.astype(BF16), joined(members, 1, cut))
            total = part if total is None else total + part
            out = piece if out is None else out + piece
        out = out * (1.0 / total)
        grad = jnp.concatenate([ref[1, :, cut] for ref in qg_refs], axis=0)
        dotted = jnp.sum(out * grad.astype(F32), axis=1, keepdims=True)
        out = out.astype(BF16)
        for i, o_ref in enumerate(o_refs):
            o_ref[:, cut] = out[i * cells : (i + 1) * cells]
        stat = jnp.where(lane == head, best + jnp.log2(total), stat)
        stat = jnp.where(lane == HEADS + head, dotted, stat)
    if last:
        whole = jnp.concatenate([first_ref[...], stat], axis=0)
        stat_ref[...] = whole.T[: stat_ref.shape[0]]
    else:
        stat_ref[...] = stat


def seen_from(stat, distance, cells):
    if distance & 2:
        stat = pltpu.roll(stat, 2 * cells, 1)
    if distance & 1:
        lane = lax.broadcasted_iota(jnp.int32, stat.shape, 1)
        even = (lane < cells) | ((lane >= 2 * cells) & (lane < 3 * cells))
        stat = jnp.where(even, pltpu.roll(stat, 3 * cells, 1), pltpu.roll(stat, cells, 1))
    return stat


def merged_stats(stat_refs, cells):
    refs = dict(zip(STAT_ORDER, stat_refs))
    parts = [seen_from(refs[distance][...], distance, cells) for distance in range(4)]
    top = functools.reduce(jnp.maximum, parts)
    shares = [jnp.exp2(part - top) for part in parts]
    total = functools.reduce(jnp.add, shares)
    lse = top + jnp.log2(total)
    shares = [share / total for share in shares]
    delta = functools.reduce(
        jnp.add,
        [share[:HEADS] * part[HEADS : 2 * HEADS] for share, part in zip(shares, parts)],
    )
    return lse[:HEADS], delta, shares


def backward_kernel(cols, grid_rows, sizes, cells, first, last, *refs):
    tile_count = grid_rows * len(cols)
    qg_refs = refs[:4]
    kv_refs = refs[4 : 4 + tile_count]
    rest = refs[4 + tile_count :]
    if first:
        stat_refs, rest = rest[:4], rest[4:]
    else:
        (lse_ref, delta_ref, dq_ref), rest = rest[:3], rest[3:]
    if last:
        dq_outs, rest = rest[:4], rest[4:]
    else:
        dq_out, rest = rest[0], rest[1:]
    if first:
        (lse_ref, delta_ref, share_ref), rest = rest[:3], rest[3:]
        lse, delta, shares = merged_stats(stat_refs, cells)
        lse_ref[...] = lse
        delta_ref[...] = delta
        rows = [shares[d][head : head + 1, : 2 * cells] for head in range(HEADS) for d in range(4)]
        wide = jnp.concatenate(rows + [jnp.zeros((DH - len(rows), 2 * cells), F32)], axis=0)
        share_ref[...] = wide.T[:cells]
    else:
        lse, delta = lse_ref[...], delta_ref[...]
    col_refs = rest
    blocks = [(head, slot) for head in range(HEADS) for slot in range(len(cols))]

    def joined(slots, which, cut):
        picked = [kv_refs[slot * grid_rows + row] for slot in slots for row in range(grid_rows)]
        return jnp.concatenate([ref[which, :, cut] for ref in picked], axis=0)

    def products_of(head, slot):
        cut = head_slice(head)
        queries = jnp.concatenate([ref[0, :, cut] for ref in qg_refs], axis=0)
        grads = jnp.concatenate([ref[1, :, cut] for ref in qg_refs], axis=0)
        raw = dot_nt(joined([slot], 0, cut), queries)
        return raw, dot_nt(joined([slot], 1, cut), grads), queries, grads

    dscores = [[] for _ in range(HEADS)]
    ahead = products_of(*blocks[0])
    for i, (head, slot) in enumerate(blocks):
        raw, prob_grad, queries, grads = ahead
        if i + 1 < len(blocks):
            ahead = products_of(*blocks[i + 1])
        cut = head_slice(head)
        probs = []
        for row in range(grid_rows):
            bias = group_bias((row == 2, cols[slot] == 2), sizes)
            shift = lse[head : head + 1]
            shift = shift if bias is None else shift - bias
            probs.append(jnp.exp2(raw[row * cells : (row + 1) * cells] * SCALE_LOG2 - shift))
        probs = jnp.concatenate(probs, axis=0)
        dscore = (probs * (prob_grad - delta[head : head + 1])).astype(BF16)
        dv = dot_nn(probs.astype(BF16), grads).astype(BF16)
        dk = (dot_nn(dscore, queries) * SCALE).astype(BF16)
        for row in range(grid_rows):
            at = slice(row * cells, (row + 1) * cells)
            col_refs[slot][row, 0, :, cut] = dk[at]
            col_refs[slot][row, 1, :, cut] = dv[at]
        dscores[head].append(dscore)
    for head in range(HEADS):
        cut = head_slice(head)
        dq = dot_nn(joined(range(len(cols)), 0, cut).T, jnp.concatenate(dscores[head], axis=0))
        dq = dq if first else dq + dq_ref[head]
        if last:
            dq = (dq * SCALE).T.astype(BF16)
            for i, ref in enumerate(dq_outs):
                ref[:, cut] = dq[i * cells : (i + 1) * cells]
        else:
            dq_out[head] = dq


def summed(parts):
    return functools.reduce(jnp.add, [part.astype(F32) for part in parts])


def gather_kernel(cols, *refs):
    o_refs, col_refs = refs[:4], refs[4 : 4 + cols]
    share_ref, out_ref, sum_ref = refs[4 + cols :]
    for head in range(HEADS):
        cut = head_slice(head)
        weighted = []
        for d, o_ref in zip((0, 3, 2, 1), o_refs):
            weight = share_ref[:, 4 * head + d : 4 * head + d + 1]
            weighted.append(o_ref[:, cut].astype(F32) * weight)
        out_ref[:, cut] = functools.reduce(jnp.add, weighted).astype(BF16)
        for which in range(2):
            sum_ref[which, :, cut] = summed([ref[0, which, :, cut] for ref in col_refs])


def finish_kernel(rows, *refs):
    dq_refs, row_refs = refs[:4], refs[4 : 4 + 2 * rows]
    sum_ref, rope_ref, dq_out, dk_out, dv_out = refs[4 + 2 * rows :]
    tables = [rope_ref[plane] for plane in range(3)]
    for head in range(HEADS):
        cut = head_slice(head)
        dq = summed([ref[:, cut] for ref in dq_refs])
        dq_out[:, cut] = turn(dq, *tables, -1.0).astype(BF16)
        dk, dv = [
            summed([sum_ref[which, :, cut]] + [ref[:, cut] for ref in row_refs[which::2]])
            for which in range(2)
        ]
        dk_out[:, cut] = turn(dk, *tables, -1.0).astype(BF16)
        dv_out[:, cut] = dv.astype(BF16)


def call(kernel, out_shape, args, flops=0, exps=0, scratch=(), space=pltpu.VMEM):
    shapes = jax.tree.leaves(out_shape)
    flops *= 8
    moved = sum(math.prod(x.shape) * x.dtype.itemsize for x in list(args) + shapes)
    return pl.pallas_call(
        kernel,
        out_shape=out_shape,
        in_specs=[pl.BlockSpec(memory_space=space)] * len(args),
        scratch_shapes=list(scratch),
        compiler_params=pltpu.CompilerParams(vmem_limit_bytes=VMEM_LIMIT),
        cost_estimate=pl.CostEstimate(flops=flops, bytes_accessed=moved, transcendentals=exps),
    )(*args)


def shards(query_in, key_in, value_in, cotangent):
    frames, rows, cols, chan = query_in.shape
    cells = frames * rows * cols
    sizes = {axis: lax.axis_size(axis) for axis in ("ta", "ha", "wa")}
    assert rows == TILE_H and cols == TILE_W and chan == HEADS * DH
    assert TILE_T % frames == 0 and frames * sizes["ta"] <= 2 * TILE_T
    assert sizes["ta"] == 4 and sizes["ha"] % 2 == 0 and sizes["wa"] % 2 == 0
    dims = (frames, rows, cols)
    table, begins = rope_table(frames * sizes["ta"], rows * sizes["ha"], cols * sizes["wa"])
    flat = [x.reshape(cells, chan) for x in (query_in, key_in, value_in, cotangent)]
    pair = jax.ShapeDtypeStruct((2, cells, chan), BF16)
    plain = jax.ShapeDtypeStruct((cells, chan), BF16)

    def real(*shape):
        return jax.ShapeDtypeStruct(shape, F32)

    with jax.named_scope("rotate"):
        kv, qg, rope = call(
            functools.partial(rotate_kernel, dims, begins),
            (pair, pair, real(3, cells, DH)),
            [pltpu.with_memory_space_constraint(x, pltpu.HBM) for x in (*flat, jnp.asarray(table))],
            scratch=[pltpu.VMEM((cells, chan), BF16)] * 2
            + [pltpu.VMEM(table.shape, F32), pltpu.SemaphoreType.DMA((5,))],
            space=pltpu.HBM,
        )

    def other_frames(x, distance):
        return lax.ppermute(x, "ta", [(i, i ^ distance) for i in range(sizes["ta"])])

    row_sides = side_pairs(sizes["ha"])
    col_sides = side_pairs(sizes["wa"])
    with jax.named_scope("halo"):
        kv_rows = [kv] + [lax.ppermute(kv, "ha", pairs) for pairs in row_sides]
        qg2 = other_frames(qg, 2)
        qg1 = other_frames(qg, 1)
        tiles = []
        for block in kv_rows:
            tiles.append([block] + [lax.ppermute(block, "wa", pairs) for pairs in col_sides])
        qg3 = other_frames(qg2, 1)
    grid_rows, grid_cols = 1 + len(row_sides), 1 + len(col_sides)
    flat_tiles = [tiles[row][col] for row in range(grid_rows) for col in range(grid_cols)]
    groups = {}
    for row in range(grid_rows):
        for col in range(grid_cols):
            groups.setdefault((row == 2, col == 2), []).append(row * grid_cols + col)
    groups = list(groups.items())

    key_count = len(flat_tiles) * cells
    product = 2 * cells * key_count * DH * HEADS

    def forward(blocks, first):
        count = len(blocks)
        stat = (count * cells, DH) if first is None else (8, 4 * cells)
        return call(
            functools.partial(forward_kernel, groups, sizes, cells, count, first is not None),
            (*[plain] * count, real(*stat)),
            (*blocks, *flat_tiles) + (() if first is None else (first,)),
            2 * product * count,
            cells * key_count * HEADS * count,
        )

    with jax.named_scope("attend"):
        o0, o1, o2, first = forward((qg, qg1, qg2), None)
        o3, stat = forward((qg3,), first)
    with jax.named_scope("merge"):
        outs = [other_frames(o, d) for d, o in ((3, o3), (2, o2), (1, o1))]
        stat_near, outs[2] = lax.optimization_barrier((stat, outs[2]))
        stats = [stat, other_frames(stat_near, 1), other_frames(stat, 3), other_frames(stat, 2)]
        stats, outs[1] = lax.optimization_barrier((stats, outs[1]))

    queries = (qg, qg1, qg2, qg3)
    col_shape = jax.ShapeDtypeStruct((grid_rows, 2, cells, chan), BF16)

    def gradients(which, carried):
        count = len(which)
        first, last = which[-1] == grid_cols - 1, which[0] == 0
        stat_outs = [real(HEADS, 4 * cells), real(HEADS, 4 * cells), real(cells, DH)]
        return call(
            functools.partial(backward_kernel, which, grid_rows, sizes, cells, first, last),
            (
                *([plain] * 4 if last else [real(HEADS, DH, 4 * cells)]),
                *(stat_outs if first else []),
                *[col_shape] * count,
            ),
            (*queries, *[tiles[row][col] for col in which for row in range(grid_rows)], *carried),
            20 * product * count // grid_cols,
            4 * cells * key_count * HEADS * count // grid_cols,
        )

    with jax.named_scope("gradients"):
        dq, lse, delta, shares, *sides = gradients(tuple(range(1, grid_cols)), stats)
        sides = [lax.ppermute(x, "wa", pairs) for x, pairs in zip(sides, col_sides)]
        d0, d1, d2, d3, own = gradients((0,), (lse, delta, dq))
    with jax.named_scope("return"):
        (d1, d2, d3), outs = lax.optimization_barrier(((d1, d2, d3), outs))
        col_parts = [own, *sides]
        dqs = [d0] + [other_frames(x, d) for d, x in ((2, d2), (3, d3), (1, d1))]
        row_parts = []
        for row, pairs in enumerate(row_sides, start=1):
            for which in range(2):
                partial_sum = sum(x[row, which].astype(F32) for x in col_parts).astype(BF16)
                row_parts.append(lax.ppermute(partial_sum, "ha", pairs))

    with jax.named_scope("finish"):
        attended, sums = call(
            functools.partial(gather_kernel, grid_cols),
            (plain, real(2, cells, chan)),
            (o0, *outs, *col_parts, shares),
        )
        results = call(
            functools.partial(finish_kernel, len(row_parts) // 2),
            [plain] * 3,
            (*dqs, *row_parts, sums, rope),
        )
    return tuple(x.reshape(query_in.shape) for x in (attended, *results))


def solution(mesh):
    spec = P("ta", "ha", "wa", None)
    return jax.shard_map(
        shards, mesh=mesh, in_specs=(spec,) * 4, out_specs=(spec,) * 4, check_vma=False
    )
```

```python
import functools
import math

import jax
import jax.numpy as jnp
import numpy as np
from jax import lax
from jax.experimental import pallas as pl
from jax.experimental.pallas import tpu as pltpu
from jax.sharding import PartitionSpec as P

DH = 128
HEADS = 2
TILE_T = 6
TILE_H = 8
TILE_W = 8

NEGATIVE = -1e30
SCALE = DH**-0.5
SCALE_LOG2 = SCALE * math.log2(math.e)
F32 = jnp.float32
BF16 = jnp.bfloat16
STAT_ORDER = (0, 1, 3, 2)
VMEM_LIMIT = 48 * 1024 * 1024


def near_pairs(count):
    return [(i, i ^ 1) for i in range(count)]


def far_pairs(count):
    pairs = []
    for i in range(count):
        j = i + 1 if i % 2 else i - 1
        pairs.append((i, j if 0 <= j < count else i))
    return pairs


def far_exists(axis, count):
    pos = lax.axis_index(axis)
    other = jnp.where(pos % 2 == 1, pos + 1, pos - 1)
    return (other >= 0) & (other < count)


def side_pairs(count):
    sides = []
    if count > 1:
        sides.append(near_pairs(count))
    if count > 2:
        sides.append(far_pairs(count))
    return sides


def rope_table(frame_total, row_total, col_total):
    time_dims = DH // 8
    space_dims = (DH - time_dims) // 2
    slower = 256.0 ** (-np.arange(0, time_dims, 2) / time_dims)
    faster = 256.0 ** (-np.arange(0, space_dims, 2) / space_dims)
    starts = (0, time_dims, time_dims + space_dims)
    pieces = []
    for total, rates, start in zip(
        (frame_total, row_total, col_total), (slower, faster, faster), starts
    ):
        padded = -(-total // 8) * 8
        piece = np.zeros((3, padded, DH), np.float32)
        angles = np.arange(padded)[:, None] * rates[None, :]
        stop = start + 2 * len(rates)
        piece[0, :, start:stop:2] = np.cos(angles)
        piece[0, :, start + 1 : stop : 2] = np.cos(angles)
        piece[1, :, start:stop:2] = -np.sin(angles)
        piece[2, :, start + 1 : stop : 2] = np.sin(angles)
        pieces.append(piece)
    begins = np.cumsum([0] + [piece.shape[1] for piece in pieces])
    return np.concatenate(pieces, axis=1), tuple(int(x) for x in begins[:3])


def local_table(plane, table_ref, begins, frames, rows, cols):
    frame_lo = begins[0] + lax.axis_index("ta") * frames
    row_lo = pl.multiple_of(begins[1] + lax.axis_index("ha") * rows, 8)
    col_lo = pl.multiple_of(begins[2] + lax.axis_index("wa") * cols, 8)
    row_part = table_ref[plane, pl.ds(row_lo, rows), :]
    col_part = table_ref[plane, pl.ds(col_lo, cols), :]
    grids = []
    for i in range(frames):
        lead = row_part + table_ref[plane, pl.ds(frame_lo + i, 1), :]
        grid = lead[:, None, :] + col_part[None, :, :]
        grids.append(grid.reshape(rows * cols, DH))
    return jnp.concatenate(grids, axis=0)


def turn(x, cosine, sin_even, sin_odd, sign):
    follow = pltpu.roll(x, DH - 1, 1)
    lead = pltpu.roll(x, 1, 1)
    return x * cosine + sign * (follow * sin_even + lead * sin_odd)


def head_slice(head):
    return slice(head * DH, (head + 1) * DH)


def rotate_kernel(
    dims, begins, q_hbm, k_hbm, v_hbm, g_hbm, table_hbm, kv_ref, qg_ref, rope_ref, q_ref, k_ref,
    table_ref, sems,
):
    moves = [
        (table_hbm, table_ref),
        (k_hbm, k_ref),
        (q_hbm, q_ref),
        (v_hbm, kv_ref.at[1]),
        (g_hbm, qg_ref.at[1]),
    ]
    copies = [pltpu.make_async_copy(*move, sems.at[i]) for i, move in enumerate(moves)]
    for copy in copies:
        copy.start()
    copies[0].wait()
    tables = [local_table(plane, table_ref, begins, *dims) for plane in range(3)]
    for plane in range(3):
        rope_ref[plane] = tables[plane]
    for copy, source, target in ((copies[1], k_ref, kv_ref), (copies[2], q_ref, qg_ref)):
        copy.wait()
        for head in range(HEADS):
            cut = head_slice(head)
            target[0, :, cut] = turn(source[:, cut].astype(F32), *tables, 1.0).astype(BF16)
    copies[3].wait()
    copies[4].wait()


def dot_nt(a, b):
    return lax.dot_general(a, b, (((1,), (1,)), ((), ())), preferred_element_type=F32)


def dot_nn(a, b):
    return lax.dot_general(a, b, (((1,), (0,)), ((), ())), preferred_element_type=F32)


def dot_tn(a, b):
    return lax.dot_general(a, b, (((0,), (0,)), ((), ())), preferred_element_type=F32)


def group_bias(flags, sizes):
    valid = None
    for axis, is_far in zip(("ha", "wa"), flags):
        if is_far:
            here = far_exists(axis, sizes[axis])
            valid = here if valid is None else valid & here
    return None if valid is None else jnp.where(valid, 0.0, NEGATIVE).astype(F32)


def forward_kernel(groups, sizes, cells, count, last, *refs):
    tile_count = sum(len(members) for _, members in groups)
    qg_refs = refs[:count]
    kv_refs = refs[count : count + tile_count]
    rest = refs[count + tile_count :]
    if last:
        first_ref, rest = rest[0], rest[1:]
    o_refs, stat_ref = rest[:count], rest[count]
    spans = [(members, group_bias(flags, sizes)) for flags, members in groups]

    def joined(members, which, cut):
        return jnp.concatenate([kv_refs[i][which, :, cut] for i in members], axis=0)

    lane = lax.broadcasted_iota(jnp.int32, (count * cells, DH), 1)
    stat = jnp.zeros((count * cells, DH), F32)

    def scores_of(head):
        cut = head_slice(head)
        query = jnp.concatenate([ref[0, :, cut] for ref in qg_refs], axis=0)
        return [dot_nt(query, joined(members, 0, cut)) for members, _ in spans]

    ahead = scores_of(0)
    for head in range(HEADS):
        cut = head_slice(head)
        scores = ahead
        if head + 1 < HEADS:
            ahead = scores_of(head + 1)
        best = None
        for raw, (_, bias) in zip(scores, spans):
            top = jnp.max(raw, axis=1, keepdims=True) * SCALE_LOG2
            if bias is not None:
                top = top + bias
            best = top if best is None else jnp.maximum(best, top)
        total = None
        out = None
        for raw, (members, bias) in zip(scores, spans):
            shift = best if bias is None else best - bias
            weights = jnp.exp2(raw * SCALE_LOG2 - shift)
            part = jnp.sum(weights, axis=1, keepdims=True)
            piece = dot_nn(weights.astype(BF16), joined(members, 1, cut))
            total = part if total is None else total + part
            out = piece if out is None else out + piece
        out = out * (1.0 / total)
        grad = jnp.concatenate([ref[1, :, cut] for ref in qg_refs], axis=0)
        dotted = jnp.sum(out * grad.astype(F32), axis=1, keepdims=True)
        out = out.astype(BF16)
        for i, o_ref in enumerate(o_refs):
            o_ref[:, cut] = out[i * cells : (i + 1) * cells]
        stat = jnp.where(lane == head, best + jnp.log2(total), stat)
        stat = jnp.where(lane == HEADS + head, dotted, stat)
    if last:
        whole = jnp.concatenate([first_ref[...], stat], axis=0)
        stat_ref[...] = whole.T[: stat_ref.shape[0]]
    else:
        stat_ref[...] = stat


def seen_from(stat, distance, cells):
    if distance & 2:
        stat = pltpu.roll(stat, 2 * cells, 1)
    if distance & 1:
        lane = lax.broadcasted_iota(jnp.int32, stat.shape, 1)
        even = (lane < cells) | ((lane >= 2 * cells) & (lane < 3 * cells))
        stat = jnp.where(even, pltpu.roll(stat, 3 * cells, 1), pltpu.roll(stat, cells, 1))
    return stat


def merged_stats(stat_refs, cells):
    refs = dict(zip(STAT_ORDER, stat_refs))
    parts = [seen_from(refs[distance][...], distance, cells) for distance in range(4)]
    top = functools.reduce(jnp.maximum, parts)
    shares = [jnp.exp2(part - top) for part in parts]
    total = functools.reduce(jnp.add, shares)
    lse = top + jnp.log2(total)
    shares = [share / total for share in shares]
    delta = functools.reduce(
        jnp.add,
        [share[:HEADS] * part[HEADS : 2 * HEADS] for share, part in zip(shares, parts)],
    )
    return lse[:HEADS], delta, shares


def backward_kernel(cols, grid_rows, sizes, cells, first, last, *refs):
    tile_count = grid_rows * len(cols)
    qg_refs = refs[:4]
    kv_refs = refs[4 : 4 + tile_count]
    rest = refs[4 + tile_count :]
    if first:
        stat_refs, rest = rest[:4], rest[4:]
    else:
        (lse_ref, delta_ref, dq_ref), rest = rest[:3], rest[3:]
    if last:
        dq_outs, rest = rest[:4], rest[4:]
    else:
        dq_out, rest = rest[0], rest[1:]
    if first:
        (lse_ref, delta_ref, share_ref), rest = rest[:3], rest[3:]
        lse, delta, shares = merged_stats(stat_refs, cells)
        lse_ref[...] = lse
        delta_ref[...] = delta
        rows = [shares[d][head : head + 1, : 2 * cells] for head in range(HEADS) for d in range(4)]
        wide = jnp.concatenate(rows + [jnp.zeros((DH - len(rows), 2 * cells), F32)], axis=0)
        share_ref[...] = wide.T[:cells]
    else:
        lse, delta = lse_ref[...], delta_ref[...]
    col_refs = rest
    blocks = [(head, slot) for head in range(HEADS) for slot in range(len(cols))]

    def joined(slots, which, cut):
        picked = [kv_refs[slot * grid_rows + row] for slot in slots for row in range(grid_rows)]
        return jnp.concatenate([ref[which, :, cut] for ref in picked], axis=0)

    def products_of(head, slot):
        cut = head_slice(head)
        queries = jnp.concatenate([ref[0, :, cut] for ref in qg_refs], axis=0)
        grads = jnp.concatenate([ref[1, :, cut] for ref in qg_refs], axis=0)
        raw = dot_nt(joined([slot], 0, cut), queries)
        return raw, dot_nt(joined([slot], 1, cut), grads), queries, grads

    dscores = [[] for _ in range(HEADS)]
    ahead = products_of(*blocks[0])
    for i, (head, slot) in enumerate(blocks):
        raw, prob_grad, queries, grads = ahead
        if i + 1 < len(blocks):
            ahead = products_of(*blocks[i + 1])
        cut = head_slice(head)
        probs = []
        for row in range(grid_rows):
            bias = group_bias((row == 2, cols[slot] == 2), sizes)
            shift = lse[head : head + 1]
            shift = shift if bias is None else shift - bias
            probs.append(jnp.exp2(raw[row * cells : (row + 1) * cells] * SCALE_LOG2 - shift))
        probs = jnp.concatenate(probs, axis=0)
        dscore = (probs * (prob_grad - delta[head : head + 1])).astype(BF16)
        dv = dot_nn(probs.astype(BF16), grads).astype(BF16)
        dk = (dot_nn(dscore, queries) * SCALE).astype(BF16)
        for row in range(grid_rows):
            at = slice(row * cells, (row + 1) * cells)
            col_refs[slot][row, 0, :, cut] = dk[at]
            col_refs[slot][row, 1, :, cut] = dv[at]
        dscores[head].append(dscore)
    for head in range(HEADS):
        cut = head_slice(head)
        dq = dot_nn(joined(range(len(cols)), 0, cut).T, jnp.concatenate(dscores[head], axis=0))
        dq = dq if first else dq + dq_ref[head]
        if last:
            dq = (dq * SCALE).T.astype(BF16)
            for i, ref in enumerate(dq_outs):
                ref[:, cut] = dq[i * cells : (i + 1) * cells]
        else:
            dq_out[head] = dq


def summed(parts):
    return functools.reduce(jnp.add, [part.astype(F32) for part in parts])


def gather_kernel(cols, *refs):
    o_refs, col_refs = refs[:4], refs[4 : 4 + cols]
    share_ref, out_ref, sum_ref = refs[4 + cols :]
    for head in range(HEADS):
        cut = head_slice(head)
        weighted = []
        for d, o_ref in zip((0, 3, 2, 1), o_refs):
            weight = share_ref[:, 4 * head + d : 4 * head + d + 1]
            weighted.append(o_ref[:, cut].astype(F32) * weight)
        out_ref[:, cut] = functools.reduce(jnp.add, weighted).astype(BF16)
        for which in range(2):
            sum_ref[which, :, cut] = summed([ref[0, which, :, cut] for ref in col_refs])


def finish_kernel(rows, *refs):
    dq_refs, row_refs = refs[:4], refs[4 : 4 + 2 * rows]
    sum_ref, rope_ref, dq_out, dk_out, dv_out = refs[4 + 2 * rows :]
    tables = [rope_ref[plane] for plane in range(3)]
    for head in range(HEADS):
        cut = head_slice(head)
        dq = summed([ref[:, cut] for ref in dq_refs])
        dq_out[:, cut] = turn(dq, *tables, -1.0).astype(BF16)
        dk, dv = [
            summed([sum_ref[which, :, cut]] + [ref[:, cut] for ref in row_refs[which::2]])
            for which in range(2)
        ]
        dk_out[:, cut] = turn(dk, *tables, -1.0).astype(BF16)
        dv_out[:, cut] = dv.astype(BF16)


def call(kernel, out_shape, args, flops=0, exps=0, scratch=(), space=pltpu.VMEM):
    shapes = jax.tree.leaves(out_shape)
    flops *= 8
    moved = sum(math.prod(x.shape) * x.dtype.itemsize for x in list(args) + shapes)
    return pl.pallas_call(
        kernel,
        out_shape=out_shape,
        in_specs=[pl.BlockSpec(memory_space=space)] * len(args),
        scratch_shapes=list(scratch),
        compiler_params=pltpu.CompilerParams(vmem_limit_bytes=VMEM_LIMIT),
        cost_estimate=pl.CostEstimate(flops=flops, bytes_accessed=moved, transcendentals=exps),
    )(*args)


def shards(query_in, key_in, value_in, cotangent):
    frames, rows, cols, chan = query_in.shape
    cells = frames * rows * cols
    sizes = {axis: lax.axis_size(axis) for axis in ("ta", "ha", "wa")}
    assert rows == TILE_H and cols == TILE_W and chan == HEADS * DH
    assert TILE_T % frames == 0 and frames * sizes["ta"] <= 2 * TILE_T
    assert sizes["ta"] == 4 and sizes["ha"] % 2 == 0 and sizes["wa"] % 2 == 0
    dims = (frames, rows, cols)
    table, begins = rope_table(frames * sizes["ta"], rows * sizes["ha"], cols * sizes["wa"])
    flat = [x.reshape(cells, chan) for x in (query_in, key_in, value_in, cotangent)]
    pair = jax.ShapeDtypeStruct((2, cells, chan), BF16)
    plain = jax.ShapeDtypeStruct((cells, chan), BF16)

    def real(*shape):
        return jax.ShapeDtypeStruct(shape, F32)

    with jax.named_scope("rotate"):
        kv, qg, rope = call(
            functools.partial(rotate_kernel, dims, begins),
            (pair, pair, real(3, cells, DH)),
            [pltpu.with_memory_space_constraint(x, pltpu.HBM) for x in (*flat, jnp.asarray(table))],
            scratch=[pltpu.VMEM((cells, chan), BF16)] * 2
            + [pltpu.VMEM(table.shape, F32), pltpu.SemaphoreType.DMA((5,))],
            space=pltpu.HBM,
        )

    def other_frames(x, distance):
        return lax.ppermute(x, "ta", [(i, i ^ distance) for i in range(sizes["ta"])])

    row_sides = side_pairs(sizes["ha"])
    col_sides = side_pairs(sizes["wa"])
    with jax.named_scope("halo"):
        kv_rows = [kv] + [lax.ppermute(kv, "ha", pairs) for pairs in row_sides]
        qg2 = other_frames(qg, 2)
        qg1 = other_frames(qg, 1)
        tiles = []
        for block in kv_rows:
            tiles.append([block] + [lax.ppermute(block, "wa", pairs) for pairs in col_sides])
        qg3 = other_frames(qg2, 1)
    grid_rows, grid_cols = 1 + len(row_sides), 1 + len(col_sides)
    flat_tiles = [tiles[row][col] for row in range(grid_rows) for col in range(grid_cols)]
    groups = {}
    for row in range(grid_rows):
        for col in range(grid_cols):
            groups.setdefault((row == 2, col == 2), []).append(row * grid_cols + col)
    groups = list(groups.items())

    key_count = len(flat_tiles) * cells
    product = 2 * cells * key_count * DH * HEADS

    def forward(blocks, first):
        count = len(blocks)
        stat = (count * cells, DH) if first is None else (8, 4 * cells)
        return call(
            functools.partial(forward_kernel, groups, sizes, cells, count, first is not None),
            (*[plain] * count, real(*stat)),
            (*blocks, *flat_tiles) + (() if first is None else (first,)),
            2 * product * count,
            cells * key_count * HEADS * count,
        )

    with jax.named_scope("attend"):
        o0, o1, o2, first = forward((qg, qg1, qg2), None)
        o3, stat = forward((qg3,), first)
    with jax.named_scope("merge"):
        outs = [other_frames(o, d) for d, o in ((3, o3), (2, o2), (1, o1))]
        stat_near, outs[1:] = lax.optimization_barrier((stat, outs[1:]))
        stats = [stat, other_frames(stat_near, 1), other_frames(stat, 3), other_frames(stat, 2)]

    queries = (qg, qg1, qg2, qg3)
    col_shape = jax.ShapeDtypeStruct((grid_rows, 2, cells, chan), BF16)

    def gradients(which, carried):
        count = len(which)
        first, last = which[-1] == grid_cols - 1, which[0] == 0
        stat_outs = [real(HEADS, 4 * cells), real(HEADS, 4 * cells), real(cells, DH)]
        return call(
            functools.partial(backward_kernel, which, grid_rows, sizes, cells, first, last),
            (
                *([plain] * 4 if last else [real(HEADS, DH, 4 * cells)]),
                *(stat_outs if first else []),
                *[col_shape] * count,
            ),
            (*queries, *[tiles[row][col] for col in which for row in range(grid_rows)], *carried),
            20 * product * count // grid_cols,
            4 * cells * key_count * HEADS * count // grid_cols,
        )

    with jax.named_scope("gradients"):
        dq, lse, delta, shares, *sides = gradients(tuple(range(1, grid_cols)), stats)
        sides = [lax.ppermute(x, "wa", pairs) for x, pairs in zip(sides, col_sides)]
        d0, d1, d2, d3, own = gradients((0,), (lse, delta, dq))
    with jax.named_scope("return"):
        (d1, d2, d3), outs = lax.optimization_barrier(((d1, d2, d3), outs))
        col_parts = [own, *sides]
        dqs = [d0] + [other_frames(x, d) for d, x in ((2, d2), (1, d1), (3, d3))]
        row_parts = []
        for row, pairs in enumerate(row_sides, start=1):
            for which in range(2):
                partial_sum = sum(x[row, which].astype(F32) for x in col_parts).astype(BF16)
                row_parts.append(lax.ppermute(partial_sum, "ha", pairs))

    with jax.named_scope("finish"):
        attended, sums = call(
            functools.partial(gather_kernel, grid_cols),
            (plain, real(2, cells, chan)),
            (o0, *outs, *col_parts, shares),
        )
        results = call(
            functools.partial(finish_kernel, len(row_parts) // 2),
            [plain] * 3,
            (*dqs, *row_parts, sums, rope),
        )
    return tuple(x.reshape(query_in.shape) for x in (attended, *results))


def solution(mesh):
    spec = P("ta", "ha", "wa", None)
    return jax.shard_map(
        shards, mesh=mesh, in_specs=(spec,) * 4, out_specs=(spec,) * 4, check_vma=False
    )
```

```python
import functools
import math

import jax
import jax.numpy as jnp
import numpy as np
from jax import lax
from jax.experimental import pallas as pl
from jax.experimental.pallas import tpu as pltpu
from jax.sharding import PartitionSpec as P

DH = 128
HEADS = 2
TILE_T = 6
TILE_H = 8
TILE_W = 8

NEGATIVE = -1e30
SCALE = DH**-0.5
SCALE_LOG2 = SCALE * math.log2(math.e)
F32 = jnp.float32
BF16 = jnp.bfloat16
STAT_ORDER = (0, 1, 3, 2)
VMEM_LIMIT = 48 * 1024 * 1024


def near_pairs(count):
    return [(i, i ^ 1) for i in range(count)]


def far_pairs(count):
    pairs = []
    for i in range(count):
        j = i + 1 if i % 2 else i - 1
        pairs.append((i, j if 0 <= j < count else i))
    return pairs


def far_exists(axis, count):
    pos = lax.axis_index(axis)
    other = jnp.where(pos % 2 == 1, pos + 1, pos - 1)
    return (other >= 0) & (other < count)


def side_pairs(count):
    sides = []
    if count > 1:
        sides.append(near_pairs(count))
    if count > 2:
        sides.append(far_pairs(count))
    return sides


def rope_table(frame_total, row_total, col_total):
    time_dims = DH // 8
    space_dims = (DH - time_dims) // 2
    slower = 256.0 ** (-np.arange(0, time_dims, 2) / time_dims)
    faster = 256.0 ** (-np.arange(0, space_dims, 2) / space_dims)
    starts = (0, time_dims, time_dims + space_dims)
    pieces = []
    for total, rates, start in zip(
        (frame_total, row_total, col_total), (slower, faster, faster), starts
    ):
        padded = -(-total // 8) * 8
        piece = np.zeros((3, padded, DH), np.float32)
        angles = np.arange(padded)[:, None] * rates[None, :]
        stop = start + 2 * len(rates)
        piece[0, :, start:stop:2] = np.cos(angles)
        piece[0, :, start + 1 : stop : 2] = np.cos(angles)
        piece[1, :, start:stop:2] = -np.sin(angles)
        piece[2, :, start + 1 : stop : 2] = np.sin(angles)
        pieces.append(piece)
    begins = np.cumsum([0] + [piece.shape[1] for piece in pieces])
    return np.concatenate(pieces, axis=1), tuple(int(x) for x in begins[:3])


def local_table(plane, table_ref, begins, frames, rows, cols):
    frame_lo = begins[0] + lax.axis_index("ta") * frames
    row_lo = pl.multiple_of(begins[1] + lax.axis_index("ha") * rows, 8)
    col_lo = pl.multiple_of(begins[2] + lax.axis_index("wa") * cols, 8)
    row_part = table_ref[plane, pl.ds(row_lo, rows), :]
    col_part = table_ref[plane, pl.ds(col_lo, cols), :]
    grids = []
    for i in range(frames):
        lead = row_part + table_ref[plane, pl.ds(frame_lo + i, 1), :]
        grid = lead[:, None, :] + col_part[None, :, :]
        grids.append(grid.reshape(rows * cols, DH))
    return jnp.concatenate(grids, axis=0)


def turn(x, cosine, sin_even, sin_odd, sign):
    follow = pltpu.roll(x, DH - 1, 1)
    lead = pltpu.roll(x, 1, 1)
    return x * cosine + sign * (follow * sin_even + lead * sin_odd)


def head_slice(head):
    return slice(head * DH, (head + 1) * DH)


def rotate_kernel(
    dims, begins, q_hbm, k_hbm, v_hbm, g_hbm, table_hbm, kv_ref, qg_ref, rope_ref, q_ref, k_ref,
    table_ref, sems,
):
    moves = [
        (table_hbm, table_ref),
        (k_hbm, k_ref),
        (q_hbm, q_ref),
        (v_hbm, kv_ref.at[1]),
        (g_hbm, qg_ref.at[1]),
    ]
    copies = [pltpu.make_async_copy(*move, sems.at[i]) for i, move in enumerate(moves)]
    for copy in copies:
        copy.start()
    copies[0].wait()
    tables = [local_table(plane, table_ref, begins, *dims) for plane in range(3)]
    for plane in range(3):
        rope_ref[plane] = tables[plane]
    for copy, source, target in ((copies[1], k_ref, kv_ref), (copies[2], q_ref, qg_ref)):
        copy.wait()
        for head in range(HEADS):
            cut = head_slice(head)
            target[0, :, cut] = turn(source[:, cut].astype(F32), *tables, 1.0).astype(BF16)
    copies[3].wait()
    copies[4].wait()


def dot_nt(a, b):
    return lax.dot_general(a, b, (((1,), (1,)), ((), ())), preferred_element_type=F32)


def dot_nn(a, b):
    return lax.dot_general(a, b, (((1,), (0,)), ((), ())), preferred_element_type=F32)


def dot_tn(a, b):
    return lax.dot_general(a, b, (((0,), (0,)), ((), ())), preferred_element_type=F32)


def group_bias(flags, sizes):
    valid = None
    for axis, is_far in zip(("ha", "wa"), flags):
        if is_far:
            here = far_exists(axis, sizes[axis])
            valid = here if valid is None else valid & here
    return None if valid is None else jnp.where(valid, 0.0, NEGATIVE).astype(F32)


def forward_kernel(groups, sizes, cells, count, last, *refs):
    tile_count = sum(len(members) for _, members in groups)
    qg_refs = refs[:count]
    kv_refs = refs[count : count + tile_count]
    rest = refs[count + tile_count :]
    if last:
        first_ref, rest = rest[0], rest[1:]
    o_refs, stat_ref = rest[:count], rest[count]
    spans = [(members, group_bias(flags, sizes)) for flags, members in groups]

    def joined(members, which, cut):
        return jnp.concatenate([kv_refs[i][which, :, cut] for i in members], axis=0)

    lane = lax.broadcasted_iota(jnp.int32, (count * cells, DH), 1)
    stat = jnp.zeros((count * cells, DH), F32)

    def scores_of(head):
        cut = head_slice(head)
        query = jnp.concatenate([ref[0, :, cut] for ref in qg_refs], axis=0)
        return [dot_nt(query, joined(members, 0, cut)) for members, _ in spans]

    ahead = scores_of(0)
    for head in range(HEADS):
        cut = head_slice(head)
        scores = ahead
        if head + 1 < HEADS:
            ahead = scores_of(head + 1)
        best = None
        for raw, (_, bias) in zip(scores, spans):
            top = jnp.max(raw, axis=1, keepdims=True) * SCALE_LOG2
            if bias is not None:
                top = top + bias
            best = top if best is None else jnp.maximum(best, top)
        total = None
        out = None
        for raw, (members, bias) in zip(scores, spans):
            shift = best if bias is None else best - bias
            weights = jnp.exp2(raw * SCALE_LOG2 - shift)
            values = joined(members, 1, cut)
            wide = jnp.concatenate([values, jnp.ones_like(values)], axis=1)
            both = dot_nn(weights.astype(BF16), wide)
            piece, part = both[:, :DH], both[:, DH : DH + 1]
            total = part if total is None else total + part
            out = piece if out is None else out + piece
        out = out * (1.0 / total)
        grad = jnp.concatenate([ref[1, :, cut] for ref in qg_refs], axis=0)
        dotted = jnp.sum(out * grad.astype(F32), axis=1, keepdims=True)
        out = out.astype(BF16)
        for i, o_ref in enumerate(o_refs):
            o_ref[:, cut] = out[i * cells : (i + 1) * cells]
        stat = jnp.where(lane == head, best + jnp.log2(total), stat)
        stat = jnp.where(lane == HEADS + head, dotted, stat)
    if last:
        whole = jnp.concatenate([first_ref[...], stat], axis=0)
        stat_ref[...] = whole.T[: stat_ref.shape[0]]
    else:
        stat_ref[...] = stat


def seen_from(stat, distance, cells):
    if distance & 2:
        stat = pltpu.roll(stat, 2 * cells, 1)
    if distance & 1:
        lane = lax.broadcasted_iota(jnp.int32, stat.shape, 1)
        even = (lane < cells) | ((lane >= 2 * cells) & (lane < 3 * cells))
        stat = jnp.where(even, pltpu.roll(stat, 3 * cells, 1), pltpu.roll(stat, cells, 1))
    return stat


def merged_stats(stat_refs, cells):
    refs = dict(zip(STAT_ORDER, stat_refs))
    parts = [seen_from(refs[distance][...], distance, cells) for distance in range(4)]
    top = functools.reduce(jnp.maximum, parts)
    shares = [jnp.exp2(part - top) for part in parts]
    total = functools.reduce(jnp.add, shares)
    lse = top + jnp.log2(total)
    shares = [share / total for share in shares]
    delta = functools.reduce(
        jnp.add,
        [share[:HEADS] * part[HEADS : 2 * HEADS] for share, part in zip(shares, parts)],
    )
    return lse[:HEADS], delta, shares


def backward_kernel(cols, grid_rows, sizes, cells, first, last, *refs):
    tile_count = grid_rows * len(cols)
    qg_refs = refs[:4]
    kv_refs = refs[4 : 4 + tile_count]
    rest = refs[4 + tile_count :]
    if first:
        stat_refs, rest = rest[:4], rest[4:]
    else:
        (lse_ref, delta_ref, dq_ref), rest = rest[:3], rest[3:]
    if last:
        dq_outs, rest = rest[:4], rest[4:]
    else:
        dq_out, rest = rest[0], rest[1:]
    if first:
        (lse_ref, delta_ref, share_ref), rest = rest[:3], rest[3:]
        lse, delta, shares = merged_stats(stat_refs, cells)
        lse_ref[...] = lse
        delta_ref[...] = delta
        rows = [shares[d][head : head + 1, : 2 * cells] for head in range(HEADS) for d in range(4)]
        wide = jnp.concatenate(rows + [jnp.zeros((DH - len(rows), 2 * cells), F32)], axis=0)
        share_ref[...] = wide.T[:cells]
    else:
        lse, delta = lse_ref[...], delta_ref[...]
    col_refs = rest
    blocks = [(head, slot) for head in range(HEADS) for slot in range(len(cols))]

    def joined(slots, which, cut):
        picked = [kv_refs[slot * grid_rows + row] for slot in slots for row in range(grid_rows)]
        return jnp.concatenate([ref[which, :, cut] for ref in picked], axis=0)

    def products_of(head, slot):
        cut = head_slice(head)
        queries = jnp.concatenate([ref[0, :, cut] for ref in qg_refs], axis=0)
        grads = jnp.concatenate([ref[1, :, cut] for ref in qg_refs], axis=0)
        raw = dot_nt(joined([slot], 0, cut), queries)
        return raw, dot_nt(joined([slot], 1, cut), grads), queries, grads

    dscores = [[] for _ in range(HEADS)]
    ahead = products_of(*blocks[0])
    for i, (head, slot) in enumerate(blocks):
        raw, prob_grad, queries, grads = ahead
        if i + 1 < len(blocks):
            ahead = products_of(*blocks[i + 1])
        cut = head_slice(head)
        probs = []
        for row in range(grid_rows):
            bias = group_bias((row == 2, cols[slot] == 2), sizes)
            shift = lse[head : head + 1]
            shift = shift if bias is None else shift - bias
            probs.append(jnp.exp2(raw[row * cells : (row + 1) * cells] * SCALE_LOG2 - shift))
        probs = jnp.concatenate(probs, axis=0)
        dscore = (probs * (prob_grad - delta[head : head + 1])).astype(BF16)
        dv = dot_nn(probs.astype(BF16), grads).astype(BF16)
        dk = (dot_nn(dscore, queries) * SCALE).astype(BF16)
        for row in range(grid_rows):
            at = slice(row * cells, (row + 1) * cells)
            col_refs[slot][row, 0, :, cut] = dk[at]
            col_refs[slot][row, 1, :, cut] = dv[at]
        dscores[head].append(dscore)
    for head in range(HEADS):
        cut = head_slice(head)
        dq = dot_nn(joined(range(len(cols)), 0, cut).T, jnp.concatenate(dscores[head], axis=0))
        dq = dq if first else dq + dq_ref[head]
        if last:
            dq = (dq * SCALE).T.astype(BF16)
            for i, ref in enumerate(dq_outs):
                ref[:, cut] = dq[i * cells : (i + 1) * cells]
        else:
            dq_out[head] = dq


def summed(parts):
    return functools.reduce(jnp.add, [part.astype(F32) for part in parts])


def gather_kernel(cols, *refs):
    o_refs, col_refs = refs[:4], refs[4 : 4 + cols]
    share_ref, out_ref, sum_ref = refs[4 + cols :]
    for head in range(HEADS):
        cut = head_slice(head)
        weighted = []
        for d, o_ref in zip((0, 3, 2, 1), o_refs):
            weight = share_ref[:, 4 * head + d : 4 * head + d + 1]
            weighted.append(o_ref[:, cut].astype(F32) * weight)
        out_ref[:, cut] = functools.reduce(jnp.add, weighted).astype(BF16)
        for which in range(2):
            sum_ref[which, :, cut] = summed([ref[0, which, :, cut] for ref in col_refs])


def finish_kernel(rows, *refs):
    dq_refs, row_refs = refs[:4], refs[4 : 4 + 2 * rows]
    sum_ref, rope_ref, dq_out, dk_out, dv_out = refs[4 + 2 * rows :]
    tables = [rope_ref[plane] for plane in range(3)]
    for head in range(HEADS):
        cut = head_slice(head)
        dq = summed([ref[:, cut] for ref in dq_refs])
        dq_out[:, cut] = turn(dq, *tables, -1.0).astype(BF16)
        dk, dv = [
            summed([sum_ref[which, :, cut]] + [ref[:, cut] for ref in row_refs[which::2]])
            for which in range(2)
        ]
        dk_out[:, cut] = turn(dk, *tables, -1.0).astype(BF16)
        dv_out[:, cut] = dv.astype(BF16)


def call(kernel, out_shape, args, flops=0, exps=0, scratch=(), space=pltpu.VMEM):
    shapes = jax.tree.leaves(out_shape)
    flops *= 8
    moved = sum(math.prod(x.shape) * x.dtype.itemsize for x in list(args) + shapes)
    return pl.pallas_call(
        kernel,
        out_shape=out_shape,
        in_specs=[pl.BlockSpec(memory_space=space)] * len(args),
        scratch_shapes=list(scratch),
        compiler_params=pltpu.CompilerParams(vmem_limit_bytes=VMEM_LIMIT),
        cost_estimate=pl.CostEstimate(flops=flops, bytes_accessed=moved, transcendentals=exps),
    )(*args)


def shards(query_in, key_in, value_in, cotangent):
    frames, rows, cols, chan = query_in.shape
    cells = frames * rows * cols
    sizes = {axis: lax.axis_size(axis) for axis in ("ta", "ha", "wa")}
    assert rows == TILE_H and cols == TILE_W and chan == HEADS * DH
    assert TILE_T % frames == 0 and frames * sizes["ta"] <= 2 * TILE_T
    assert sizes["ta"] == 4 and sizes["ha"] % 2 == 0 and sizes["wa"] % 2 == 0
    dims = (frames, rows, cols)
    table, begins = rope_table(frames * sizes["ta"], rows * sizes["ha"], cols * sizes["wa"])
    flat = [x.reshape(cells, chan) for x in (query_in, key_in, value_in, cotangent)]
    pair = jax.ShapeDtypeStruct((2, cells, chan), BF16)
    plain = jax.ShapeDtypeStruct((cells, chan), BF16)

    def real(*shape):
        return jax.ShapeDtypeStruct(shape, F32)

    with jax.named_scope("rotate"):
        kv, qg, rope = call(
            functools.partial(rotate_kernel, dims, begins),
            (pair, pair, real(3, cells, DH)),
            [pltpu.with_memory_space_constraint(x, pltpu.HBM) for x in (*flat, jnp.asarray(table))],
            scratch=[pltpu.VMEM((cells, chan), BF16)] * 2
            + [pltpu.VMEM(table.shape, F32), pltpu.SemaphoreType.DMA((5,))],
            space=pltpu.HBM,
        )

    def other_frames(x, distance):
        return lax.ppermute(x, "ta", [(i, i ^ distance) for i in range(sizes["ta"])])

    row_sides = side_pairs(sizes["ha"])
    col_sides = side_pairs(sizes["wa"])
    with jax.named_scope("halo"):
        kv_rows = [kv] + [lax.ppermute(kv, "ha", pairs) for pairs in row_sides]
        qg2 = other_frames(qg, 2)
        qg1 = other_frames(qg, 1)
        tiles = []
        for block in kv_rows:
            tiles.append([block] + [lax.ppermute(block, "wa", pairs) for pairs in col_sides])
        qg3 = other_frames(qg2, 1)
    grid_rows, grid_cols = 1 + len(row_sides), 1 + len(col_sides)
    flat_tiles = [tiles[row][col] for row in range(grid_rows) for col in range(grid_cols)]
    groups = {}
    for row in range(grid_rows):
        for col in range(grid_cols):
            groups.setdefault((row == 2, col == 2), []).append(row * grid_cols + col)
    groups = list(groups.items())

    key_count = len(flat_tiles) * cells
    product = 2 * cells * key_count * DH * HEADS

    def forward(blocks, first):
        count = len(blocks)
        stat = (count * cells, DH) if first is None else (8, 4 * cells)
        return call(
            functools.partial(forward_kernel, groups, sizes, cells, count, first is not None),
            (*[plain] * count, real(*stat)),
            (*blocks, *flat_tiles) + (() if first is None else (first,)),
            2 * product * count,
            cells * key_count * HEADS * count,
        )

    with jax.named_scope("attend"):
        o0, o1, o2, first = forward((qg, qg1, qg2), None)
        o3, stat = forward((qg3,), first)
    with jax.named_scope("merge"):
        outs = [other_frames(o, d) for d, o in ((3, o3), (2, o2), (1, o1))]
        stat_near, outs[1:] = lax.optimization_barrier((stat, outs[1:]))
        stats = [stat, other_frames(stat_near, 1), other_frames(stat, 3), other_frames(stat, 2)]

    queries = (qg, qg1, qg2, qg3)
    col_shape = jax.ShapeDtypeStruct((grid_rows, 2, cells, chan), BF16)

    def gradients(which, carried):
        count = len(which)
        first, last = which[-1] == grid_cols - 1, which[0] == 0
        stat_outs = [real(HEADS, 4 * cells), real(HEADS, 4 * cells), real(cells, DH)]
        return call(
            functools.partial(backward_kernel, which, grid_rows, sizes, cells, first, last),
            (
                *([plain] * 4 if last else [real(HEADS, DH, 4 * cells)]),
                *(stat_outs if first else []),
                *[col_shape] * count,
            ),
            (*queries, *[tiles[row][col] for col in which for row in range(grid_rows)], *carried),
            20 * product * count // grid_cols,
            4 * cells * key_count * HEADS * count // grid_cols,
        )

    with jax.named_scope("gradients"):
        dq, lse, delta, shares, *sides = gradients(tuple(range(1, grid_cols)), stats)
        sides = [lax.ppermute(x, "wa", pairs) for x, pairs in zip(sides, col_sides)]
        d0, d1, d2, d3, own = gradients((0,), (lse, delta, dq))
    with jax.named_scope("return"):
        (d1, d2, d3), outs = lax.optimization_barrier(((d1, d2, d3), outs))
        col_parts = [own, *sides]
        dqs = [d0] + [other_frames(x, d) for d, x in ((2, d2), (3, d3), (1, d1))]
        row_parts = []
        for row, pairs in enumerate(row_sides, start=1):
            for which in range(2):
                partial_sum = sum(x[row, which].astype(F32) for x in col_parts).astype(BF16)
                row_parts.append(lax.ppermute(partial_sum, "ha", pairs))

    with jax.named_scope("finish"):
        attended, sums = call(
            functools.partial(gather_kernel, grid_cols),
            (plain, real(2, cells, chan)),
            (o0, *outs, *col_parts, shares),
        )
        results = call(
            functools.partial(finish_kernel, len(row_parts) // 2),
            [plain] * 3,
            (*dqs, *row_parts, sums, rope),
        )
    return tuple(x.reshape(query_in.shape) for x in (attended, *results))


def solution(mesh):
    spec = P("ta", "ha", "wa", None)
    return jax.shard_map(
        shards, mesh=mesh, in_specs=(spec,) * 4, out_specs=(spec,) * 4, check_vma=False
    )
```
